128 devices in a mesh: rep: 16 (over y_lo, x, core), shard: 8 (over z, y_hi).
Axes of the slice: x: 4, y: 4 (y_hi: 2, y_lo: 2; y = y_hi * 2 + y_lo), z: 4, core: 2. Of those that a mesh axis runs over, the one named last changes fastest.
Arguments:
- tokens: bfloat16 [16, 1024, 1536], P('rep', 'shard'), may hold values from -6 to 6
- lengths: int32 [16], P('rep'), may hold values from 256 to 1024, as said below
- grad_output: bfloat16 [16, 1024, 1536], P('rep', 'shard'), may hold values from -6 to 6
- norm_attn_one: bfloat16 [1536], P('shard'), may hold values from 0.099609375 to 1.8984375
- w_query_one: bfloat16 [1536, 1536], P('shard'), may hold values from -0.15625 to 0.15625
- w_key_one: bfloat16 [1536, 768], P('shard'), may hold values from -0.15625 to 0.15625
- w_value_one: bfloat16 [1536, 768], P('shard'), may hold values from -0.15625 to 0.15625
- w_out_one: bfloat16 [1536, 1536], P('shard'), may hold values from -0.4375 to 0.4375
- norm_mlp_one: bfloat16 [1536], P('shard'), may hold values from 0.099609375 to 1.8984375
- w_gate_one: bfloat16 [1536, 4096], P('shard'), may hold values from -0.15625 to 0.15625
- w_up_one: bfloat16 [1536, 4096], P('shard'), may hold values from -0.15625 to 0.15625
- w_down_one: bfloat16 [4096, 1536], P('shard'), may hold values from -0.09375 to 0.09375
- norm_attn_two: bfloat16 [1536], P('shard'), may hold values from 0.099609375 to 1.8984375
- w_query_two: bfloat16 [1536, 1536], P('shard'), may hold values from -0.15625 to 0.15625
- w_key_two: bfloat16 [1536, 768], P('shard'), may hold values from -0.15625 to 0.15625
- w_value_two: bfloat16 [1536, 768], P('shard'), may hold values from -0.15625 to 0.15625
- w_out_two: bfloat16 [1536, 1536], P('shard'), may hold values from -0.4375 to 0.4375
- norm_mlp_two: bfloat16 [1536], P('shard'), may hold values from 0.099609375 to 1.8984375
- w_gate_two: bfloat16 [1536, 4096], P('shard'), may hold values from -0.15625 to 0.15625
- w_up_two: bfloat16 [1536, 4096], P('shard'), may hold values from -0.15625 to 0.15625
- w_down_two: bfloat16 [4096, 1536], P('shard'), may hold values from -0.09375 to 0.09375
Outputs:
- output: bfloat16 [16, 1024, 1536], P('rep', 'shard')
- input_grad: float32 [16, 1024, 1536], P('rep', 'shard')
- grad_norm_attn_one: float32 [1536], P('shard')
- grad_query_one: float32 [1536, 1536], P('shard')
- grad_key_one: float32 [1536, 768], P('shard')
- grad_value_one: float32 [1536, 768], P('shard')
- grad_out_one: float32 [1536, 1536], P('shard')
- grad_norm_mlp_one: float32 [1536], P('shard')
- grad_gate_one: float32 [1536, 4096], P('shard')
- grad_up_one: float32 [1536, 4096], P('shard')
- grad_down_one: float32 [4096, 1536], P('shard')
- grad_norm_attn_two: float32 [1536], P('shard')
- grad_query_two: float32 [1536, 1536], P('shard')
- grad_key_two: float32 [1536, 768], P('shard')
- grad_value_two: float32 [1536, 768], P('shard')
- grad_out_two: float32 [1536, 1536], P('shard')
- grad_norm_mlp_two: float32 [1536], P('shard')
- grad_gate_two: float32 [1536, 4096], P('shard')
- grad_up_two: float32 [1536, 4096], P('shard')
- grad_down_two: float32 [4096, 1536], P('shard')
The draws below stay inside these ranges and needn't reach their ends.
Inputs may be any that keep to these rules, and one draw needn't show every extreme that they name: `lengths`: every draw has slots of length exactly 1024 and one of length exactly 256.
All inputs are finite; a program needn't handle non-finite values.
Results may differ from the reference program's by a relative error of at most 0.028.
Values may be sent and summed in bfloat16 or wider, within the bound.
No kernel may reach another device: no remote copies, remote signals or barrier semaphores. Data moves between devices by JAX's collectives and lax.ppermute only.
A program may use at most 256 MiB of HBM per device.

```python
import jax
import jax.numpy as jnp
from jax import lax

D = 1536
HEADS = 16
KV_HEADS = 8
HEAD_DIM = 96
FF = 4096
SLOT_LEN = 1024
MIN_LEN = 256
WINDOW = 512
SLOTS = 16


def draw_lengths(key, part):
    key = jax.random.fold_in(key, 11)
    first, second = jax.random.split(key)
    order = jax.random.permutation(first, SLOTS)
    spread = jax.random.randint(second, (SLOTS,), MIN_LEN, SLOT_LEN + 1)
    full = order < (SLOTS + 1) // 2
    shortest = order == SLOTS - 1
    return jnp.where(full, SLOT_LEN, jnp.where(shortest, MIN_LEN, spread)).astype(jnp.int32)


def levels(rng, extent, cuts, least, top_value):
    loudness = 1.0
    for position, shards_of in cuts:
        steps = jax.random.uniform(jax.random.fold_in(jax.random.fold_in(rng, 6), position), (shards_of,), jnp.float32, least / len(cuts), top_value / len(cuts))
        loudness = loudness * jnp.repeat(jnp.exp(steps), extent[position] // shards_of).reshape((-1,) + (1,) * (len(extent) - 1 - position))
    return loudness


def noise(rng, dims, deviation, limit, cuts=(), kind=jnp.bfloat16):
    values = deviation * jax.random.normal(rng, dims, jnp.float32)
    if cuts:
        values = values * levels(rng, dims, cuts, -0.22, 0.18)
    return jnp.clip(values, -limit, limit).astype(kind)


def setup_inputs(seed: int = 0) -> dict:
    streams_of = jax.random.split(jax.random.key(seed), 22)
    tokens = noise(streams_of[0], (SLOTS, SLOT_LEN, D), 1.0, 6.0, ((0, 16), (1, 8)))
    lengths = draw_lengths(jax.random.fold_in(streams_of[21], 71), 0)
    grad_output = noise(streams_of[2], (SLOTS, SLOT_LEN, D), 1.0, 6.0, ((0, 16), (1, 8)))
    norm_attn_one = jnp.clip(1.0 + 0.18 * jax.random.normal(streams_of[3], (D,), jnp.float32), 0.099609375, 1.8984375).astype(jnp.bfloat16)
    w_query_one = noise(streams_of[4], (D, HEADS * HEAD_DIM), D ** -0.5, 0.15625, ((0, 8),))
    w_key_one = noise(streams_of[5], (D, KV_HEADS * HEAD_DIM), D ** -0.5, 0.15625, ((0, 8),))
    w_value_one = noise(streams_of[6], (D, KV_HEADS * HEAD_DIM), D ** -0.5, 0.15625, ((0, 8),))
    w_out_one = noise(streams_of[7], (HEADS * HEAD_DIM, D), (max(HEADS * HEAD_DIM // 8, 1)) ** -0.5, 0.4375, ((0, 8),))
    norm_mlp_one = jnp.clip(1.0 + 0.18 * jax.random.normal(streams_of[8], (D,), jnp.float32), 0.099609375, 1.8984375).astype(jnp.bfloat16)
    w_gate_one = noise(streams_of[9], (D, FF), D ** -0.5, 0.15625, ((0, 8),))
    w_up_one = noise(streams_of[10], (D, FF), D ** -0.5, 0.15625, ((0, 8),))
    w_down_one = noise(streams_of[11], (FF, D), FF ** -0.5, 0.09375, ((0, 8),))
    norm_attn_two = jnp.clip(1.0 + 0.18 * jax.random.normal(streams_of[12], (D,), jnp.float32), 0.099609375, 1.8984375).astype(jnp.bfloat16)
    w_query_two = noise(streams_of[13], (D, HEADS * HEAD_DIM), D ** -0.5, 0.15625, ((0, 8),))
    w_key_two = noise(streams_of[14], (D, KV_HEADS * HEAD_DIM), D ** -0.5, 0.15625, ((0, 8),))
    w_value_two = noise(streams_of[15], (D, KV_HEADS * HEAD_DIM), D ** -0.5, 0.15625, ((0, 8),))
    w_out_two = noise(streams_of[16], (HEADS * HEAD_DIM, D), (max(HEADS * HEAD_DIM // 8, 1)) ** -0.5, 0.4375, ((0, 8),))
    norm_mlp_two = jnp.clip(1.0 + 0.18 * jax.random.normal(streams_of[17], (D,), jnp.float32), 0.099609375, 1.8984375).astype(jnp.bfloat16)
    w_gate_two = noise(streams_of[18], (D, FF), D ** -0.5, 0.15625, ((0, 8),))
    w_up_two = noise(streams_of[19], (D, FF), D ** -0.5, 0.15625, ((0, 8),))
    w_down_two = noise(streams_of[20], (FF, D), FF ** -0.5, 0.09375, ((0, 8),))
    return dict(tokens=tokens, lengths=lengths, grad_output=grad_output, norm_attn_one=norm_attn_one, w_query_one=w_query_one, w_key_one=w_key_one, w_value_one=w_value_one, w_out_one=w_out_one, norm_mlp_one=norm_mlp_one, w_gate_one=w_gate_one, w_up_one=w_up_one, w_down_one=w_down_one, norm_attn_two=norm_attn_two, w_query_two=w_query_two, w_key_two=w_key_two, w_value_two=w_value_two, w_out_two=w_out_two, norm_mlp_two=norm_mlp_two, w_gate_two=w_gate_two, w_up_two=w_up_two, w_down_two=w_down_two)


EPSILON = 1e-05
ROPE_BASE = 100000.0
NEGATIVE = -1e+30

@jax.custom_vjp
def low(v):
    return lax.optimization_barrier(v.astype(jnp.bfloat16)).astype(jnp.float32)

@jax.custom_vjp
def low_back(v):
    return v

def low_keep(v):
    return (low(v), None)

def low_pass(kept, grad):
    return (grad,)

def back_keep(v):
    return (v, None)

def back_low(kept, grad):
    return (low(grad),)
low.defvjp(low_keep, low_pass)
low_back.defvjp(back_keep, back_low)

def product(left, right):
    return jnp.dot(left, right, precision=lax.Precision.HIGHEST, preferred_element_type=jnp.float32)

def rms_norm(values, gain):
    return values * lax.rsqrt(lax.optimization_barrier(jnp.mean(values * values, axis=-1, keepdims=True)) + EPSILON) * gain

def rotate(tensor, places):
    half = tensor.shape[-1] // 2
    freq = ROPE_BASE ** (-jnp.arange(half, dtype=jnp.float32) * (2.0 / tensor.shape[-1]))
    angle = places.astype(jnp.float32)[:, None] * freq[None, :]
    cosine = jnp.cos(angle)[:, None, :]
    sine = jnp.sin(angle)[:, None, :]
    first = tensor[..., :half]
    second = tensor[..., half:]
    return jnp.concatenate([first * cosine - second * sine, second * cosine + first * sine], axis=-1)

def attention(state, length, weights, window):
    gain, w_query, w_key, w_value, w_out = weights
    total = state.shape[0]
    places = jnp.arange(total, dtype=jnp.int32)
    normed = low(rms_norm(state, gain))
    queries = low(rotate(low_back(product(normed, w_query)).reshape(total, HEADS, HEAD_DIM), places))
    keys = low(rotate(low_back(product(normed, w_key)).reshape(total, KV_HEADS, HEAD_DIM), places))
    values = low(low_back(product(normed, w_value))).reshape(total, KV_HEADS, HEAD_DIM)
    grouped = queries.reshape(total, KV_HEADS, HEADS // KV_HEADS, HEAD_DIM)
    raw = low_back(jnp.einsum('qkgd,pkd->kgqp', grouped, keys, precision=lax.Precision.HIGHEST))
    scores = raw * HEAD_DIM ** (-0.5)
    gap = places[:, None] - places[None, :]
    allowed = (gap >= 0) & (gap < window) & (places[None, :] < length) | (gap == 0)
    masked = jnp.where(allowed, scores, NEGATIVE)
    peak = lax.optimization_barrier(jnp.max(masked, axis=-1, keepdims=True))
    shifted = jnp.where(allowed, jnp.exp(masked - peak), 0.0)
    probs = low(shifted / lax.optimization_barrier(jnp.sum(shifted, axis=-1, keepdims=True)))
    mixed = jnp.einsum('kgqp,pkd->qkgd', probs, values, precision=lax.Precision.HIGHEST)
    mixed = low(low_back(mixed.reshape(total, HEADS * HEAD_DIM)))
    return state + low_back(product(mixed, w_out))

def feed_forward(state, weights):
    gain, w_gate, w_up, w_down = weights
    normed = low(rms_norm(state, gain))
    gate = low_back(product(normed, w_gate))
    lifted = low_back(product(normed, w_up))
    hidden = low(jax.nn.silu(gate) * lifted)
    return state + low_back(product(hidden, w_down))

def reference(tokens, lengths, grad_output, norm_attn_one, w_query_one, w_key_one, w_value_one, w_out_one, norm_mlp_one, w_gate_one, w_up_one, w_down_one, norm_attn_two, w_query_two, w_key_two, w_value_two, w_out_two, norm_mlp_two, w_gate_two, w_up_two, w_down_two):
    params = tuple((item.astype(jnp.float32) for item in (norm_attn_one, w_query_one, w_key_one, w_value_one, w_out_one, norm_mlp_one, w_gate_one, w_up_one, w_down_one, norm_attn_two, w_query_two, w_key_two, w_value_two, w_out_two, norm_mlp_two, w_gate_two, w_up_two, w_down_two)))
    inputs = tokens.astype(jnp.float32)

    def forward(inputs, params):

        def one_slot(pair):
            state, length = pair
            state = attention(state, length, params[0:5], WINDOW)
            state = feed_forward(state, params[5:9])
            state = attention(state, length, params[9:14], SLOT_LEN)
            state = feed_forward(state, params[14:18])
            return state
        return lax.map(jax.checkpoint(one_slot), (inputs, lengths))
    result, pullback = jax.vjp(forward, inputs, params)
    places = jnp.arange(SLOT_LEN, dtype=jnp.int32)
    valid = (places[None, :] < lengths[:, None]).astype(jnp.float32)
    cotangent = grad_output.astype(jnp.float32) * valid[:, :, None]
    grad_inputs, grads = pullback(cotangent)
    return (result.astype(jnp.bfloat16), grad_inputs, grads[0], grads[1], grads[2], grads[3], grads[4], grads[5], grads[6], grads[7], grads[8], grads[9], grads[10], grads[11], grads[12], grads[13], grads[14], grads[15], grads[16], grads[17])
```

```python
import jax
import jax.numpy as jnp
from jax import lax
from jax.sharding import Mesh
from jax.sharding import PartitionSpec as P

HEAD_DIM = 96
WINDOW = 512
EPSILON = 1e-05
ROPE_BASE = 100000.0
NEGATIVE = -1e30

F32 = jnp.float32
BF16 = jnp.bfloat16

AXES = ("ylo", "x", "core", "z", "yhi")
SIZES = (2, 4, 2, 4, 2)
REP = ("ylo", "x", "core")
SHARD = ("z", "yhi")
SPREAD = ("z", "yhi", "core")

RIGHT = [(i, (i + 1) % 4) for i in range(4)]
LEFT = [(i, (i - 1) % 4) for i in range(4)]
SWAP = [(0, 1), (1, 0)]


def number(ylo, x, core, z, yhi):
    return (((ylo * 4 + x) * 2 + core) * 4 + z) * 2 + yhi


def permutation(place):
    pairs = []
    for ylo in range(2):
        for x in range(4):
            for core in range(2):
                for z in range(4):
                    for yhi in range(2):
                        pairs.append(
                            (number(ylo, x, core, z, yhi), number(ylo, *place(x, core, z, yhi)))
                        )
    return pairs


def inverse(pairs):
    return [(there, here) for here, there in pairs]


LINES = [permutation(lambda x, c, z, h, k=k: ((z + k) % 4, h, x, c)) for k in range(4)]
ROWS = permutation(lambda x, c, z, h: (z, c, 2 * h + x // 2, x % 2))


def to_lines(block, z):
    part = block.shape[0] // 4
    out = []
    for k in range(4):
        piece = lax.dynamic_slice_in_dim(block, ((z + k) % 4) * part, part, axis=0)
        out.append(lax.ppermute(piece, AXES, LINES[k]))
    return jnp.concatenate(out, axis=0)


def from_lines(block, z):
    part = block.shape[0] // 4
    out = jnp.zeros_like(block)
    for k in range(4):
        piece = lax.ppermute(block[part * k : part * (k + 1)], AXES, inverse(LINES[k]))
        out = lax.dynamic_update_slice_in_dim(out, piece, ((z + k) % 4) * part, axis=0)
    return out


def ring_gather(block):
    half = block.shape[0] // 2
    from_left = lax.ppermute(block, "x", RIGHT)
    from_right = lax.ppermute(block, "x", LEFT)
    far_first = lax.ppermute(from_left[:half], "x", RIGHT)
    far_second = lax.ppermute(from_right[half:], "x", LEFT)
    return jnp.concatenate([block, from_left, from_right, far_first, far_second], axis=0)


def ring_scatter(partial):
    rows = partial.shape[0] // 4
    half = rows // 2
    own = partial[:rows]
    left = partial[rows : 2 * rows]
    right = partial[2 * rows : 3 * rows]
    far = partial[3 * rows :].astype(BF16)
    first = lax.ppermute(far[:half], "x", RIGHT).astype(F32)
    second = lax.ppermute(far[half:], "x", LEFT).astype(F32)
    right = jnp.concatenate([right[:half] + first, right[half:]], axis=0).astype(BF16)
    left = jnp.concatenate([left[:half], left[half:] + second], axis=0).astype(BF16)
    from_left = lax.ppermute(right, "x", RIGHT).astype(F32)
    from_right = lax.ppermute(left, "x", LEFT).astype(F32)
    return own + from_left + from_right


def rms_norm(values, gain):
    return values * lax.rsqrt(jnp.mean(values * values, axis=-1, keepdims=True) + EPSILON) * gain


def turn(tensor, cosine, sine):
    half = tensor.shape[-1] // 2
    first = tensor[..., :half]
    second = tensor[..., half:]
    return jnp.concatenate(
        [first * cosine - second * sine, second * cosine + first * sine], axis=-1
    )


def masked_scores(queries, keys, context, window):
    places, key_places, length = context[0], context[1], context[2]
    raw = jnp.einsum("qkgd,pkd->kgqp", queries, keys, preferred_element_type=F32)
    gap = places[:, None] - key_places[None, :]
    allowed = ((key_places[None, :] < length) & (gap >= 0) & (gap < window)) | (gap == 0)
    return raw * HEAD_DIM ** (-0.5), allowed[None, None]


def attention_forward(state, weights, context, window):
    gain, w_qkv, w_out = weights
    cosine, sine = context[3], context[4]
    normed = rms_norm(state, gain).astype(BF16)
    flat = ring_gather(normed)
    rows = flat.shape[0]
    raw = jnp.dot(flat, w_qkv, preferred_element_type=F32)
    kv_here = w_qkv.shape[1] // (4 * HEAD_DIM)
    span = kv_here * HEAD_DIM
    queries = turn(raw[:, : 2 * span].reshape(rows, 2 * kv_here, HEAD_DIM), cosine, sine)
    queries = queries.astype(BF16).reshape(rows, kv_here, 2, HEAD_DIM)
    keys = turn(raw[:, 2 * span : 3 * span].reshape(rows, kv_here, HEAD_DIM), cosine, sine)
    both = jnp.concatenate([keys.reshape(rows, span), raw[:, 3 * span :]], axis=1).astype(BF16)
    both = jnp.concatenate([both, lax.ppermute(both, "core", SWAP)], axis=0)
    keys = both[:, :span].reshape(2 * rows, kv_here, HEAD_DIM)
    values = both[:, span:].reshape(2 * rows, kv_here, HEAD_DIM)
    scores, allowed = masked_scores(queries, keys, context, window)
    masked = jnp.where(allowed, scores, NEGATIVE)
    peak = jnp.max(masked, axis=-1, keepdims=True)
    shifted = jnp.where(allowed, jnp.exp(masked - peak), 0.0)
    totals = jnp.sum(shifted, axis=-1, keepdims=True)
    probs = (shifted / totals).astype(BF16)
    mixed = jnp.einsum("kgqp,pkd->qkgd", probs, values, preferred_element_type=F32)
    mixed = mixed.reshape(rows, 2 * span).astype(BF16)
    partial = jnp.dot(mixed, w_out, preferred_element_type=F32)
    result = state + ring_scatter(partial)
    return result, (state, flat, queries, keys, values, peak + jnp.log(totals), mixed)


def attention_backward(grad, saved, weights, context, window):
    gain, w_qkv, w_out = weights
    cosine, sine = context[3], context[4]
    state, flat, queries, keys, values, log_total, mixed = saved
    rows = flat.shape[0]
    kv_here = keys.shape[1]
    span = kv_here * HEAD_DIM
    grad_low = ring_gather(grad.astype(BF16))
    grad_mixed = jnp.einsum("rd,qd->rq", grad_low, w_out, preferred_element_type=F32)
    grad_mixed = grad_mixed.astype(BF16).reshape(queries.shape)
    scores, allowed = masked_scores(queries, keys, context, window)
    probs = jnp.where(allowed, jnp.exp(jnp.where(allowed, scores - log_total, NEGATIVE)), 0.0)
    grad_probs = jnp.einsum("qkgd,pkd->kgqp", grad_mixed, values, preferred_element_type=F32)
    inner = jnp.sum(grad_probs * probs, axis=-1, keepdims=True)
    grad_raw = (probs * (grad_probs - inner) * HEAD_DIM ** (-0.5)).astype(BF16)
    grad_keys = jnp.einsum("kgqp,qkgd->pkd", grad_raw, queries, preferred_element_type=F32)
    grad_values = jnp.einsum(
        "kgqp,qkgd->pkd", probs.astype(BF16), grad_mixed, preferred_element_type=F32
    )
    both = jnp.concatenate(
        [grad_keys.reshape(2 * rows, span), grad_values.reshape(2 * rows, span)], axis=1
    )
    other = lax.ppermute(both[rows:].astype(BF16), "core", SWAP)
    grad_query = jnp.einsum("kgqp,pkd->qkgd", grad_raw, keys, preferred_element_type=F32)
    query_low = turn(grad_query.reshape(rows, 2 * kv_here, HEAD_DIM), cosine, -sine)
    query_low = query_low.reshape(rows, 2 * span).astype(BF16)
    both = both[:rows] + other.astype(F32)
    keys_low = turn(both[:, :span].reshape(rows, kv_here, HEAD_DIM), cosine, -sine)
    low = jnp.concatenate(
        [query_low, keys_low.reshape(rows, span).astype(BF16), both[:, span:].astype(BF16)], axis=1
    )
    partial = jnp.einsum("rq,dq->rd", low, w_qkv, preferred_element_type=F32)
    own_normed = ring_scatter(partial)
    grad_wout = jnp.einsum("rq,rd->qd", mixed, grad_low, preferred_element_type=F32)
    grad_wqkv = jnp.einsum("rd,rq->dq", flat, low, preferred_element_type=F32)
    grad_state, grad_gain = jax.vjp(rms_norm, state, gain)[1](own_normed)
    return grad + grad_state, grad_gain, grad_wqkv.astype(BF16), grad_wout.astype(BF16)


def feed_forward(state, weights):
    gain, w_pair, w_down = weights
    hidden_here = w_down.shape[0]
    normed = rms_norm(state, gain).astype(BF16)
    flat = ring_gather(normed)
    gate = jnp.dot(flat, w_pair[:, :hidden_here], preferred_element_type=F32)
    lifted = jnp.dot(flat, w_pair[:, hidden_here:], preferred_element_type=F32)
    hidden = (jax.nn.silu(gate) * lifted).astype(BF16)
    partial = jnp.dot(hidden, w_down, preferred_element_type=F32)
    return state + ring_scatter(partial), (state, flat, gate, lifted, hidden)


def feed_backward(grad, saved, weights):
    gain, w_pair, w_down = weights
    state, flat, gate, lifted, hidden = saved
    grad_low = ring_gather(grad.astype(BF16))
    grad_hidden = jnp.einsum("rd,fd->rf", grad_low, w_down, preferred_element_type=F32)
    sigma = jax.nn.sigmoid(gate)
    grad_gate = (grad_hidden * lifted * sigma * (1.0 + gate * (1.0 - sigma))).astype(BF16)
    grad_lift = (grad_hidden * gate * sigma).astype(BF16)
    low = jnp.concatenate([grad_gate, grad_lift], axis=1)
    partial = jnp.einsum("rf,df->rd", low, w_pair, preferred_element_type=F32)
    own_normed = ring_scatter(partial)
    grad_pair = jnp.einsum("rd,rf->df", flat, low, preferred_element_type=F32)
    grad_down = jnp.einsum("rf,rd->fd", hidden, grad_low, preferred_element_type=F32)
    grad_state, grad_gain = jax.vjp(rms_norm, state, gain)[1](own_normed)
    return grad + grad_state, grad_gain, grad_pair.astype(BF16), grad_down.astype(BF16)


def spread_sum(parts):
    sums = lax.psum_scatter(parts, SPREAD, scatter_dimension=0, tiled=True)
    return tuple(
        (item.astype(F32) + lax.ppermute(item, "ylo", SWAP).astype(F32)).astype(BF16)
        for item in sums
    )


def home_columns(pieces, widths):
    every = lax.all_gather(pieces, ("x", "core"), axis=0, tiled=False)
    out = []
    start = 0
    for width in widths:
        part = every[:, :, start : start + width]
        rows = part.shape[1]
        part = part.reshape(4, 2, rows, width).transpose(1, 2, 0, 3)
        out.append(part.reshape(2 * rows, 4 * width).astype(F32))
        start += width
    return out


def home_rows(piece):
    piece = lax.ppermute(piece, AXES, inverse(ROWS))
    return lax.all_gather(piece, ("x", "core"), axis=0, tiled=True).astype(F32)


def body(tokens, lengths, grad_output, *weights):
    slots, stretch, width = tokens.shape
    x = lax.axis_index("x")
    core = lax.axis_index("core")
    z = lax.axis_index("z")
    yhi = lax.axis_index("yhi")
    piece = 2 * x + core
    here = (2 * z + yhi) * stretch + jnp.arange(stretch, dtype=jnp.int32)
    valid = (here < lengths[0])[:, None]
    grad_start = jnp.where(valid, grad_output[0], 0).astype(BF16)

    def rows_piece(weight):
        part = weight.shape[0] // 8
        return lax.dynamic_slice_in_dim(weight, piece * part, part, axis=0)

    def columns_piece(weight):
        rows, columns = weight.shape
        return lax.dynamic_slice(
            weight, (core * (rows // 2), x * (columns // 4)), (rows // 2, columns // 4)
        )

    layers = []
    gains = jnp.stack([weights[0], weights[5], weights[9], weights[14]])
    gains = lax.dynamic_slice_in_dim(gains, core * 96, 96, axis=1)[None]
    gathered_gains = None
    for index, base in enumerate((0, 9)):
        w_q, w_k, w_v, w_out = weights[base + 1 : base + 5]
        w_gate, w_up, w_down = weights[base + 6 : base + 9]
        w_qkv = jnp.concatenate([columns_piece(w) for w in (w_q, w_k, w_v)], axis=1)
        pair = jnp.concatenate([columns_piece(w_gate), columns_piece(w_up)], axis=1)
        out_piece = lax.ppermute(rows_piece(w_out), AXES, ROWS)
        down_piece = lax.ppermute(rows_piece(w_down), AXES, ROWS)
        attn = (w_qkv, out_piece) + ((gains,) if index == 0 else ())
        attn = lax.all_gather(attn, SPREAD, axis=0, tiled=True)
        feed = lax.all_gather((pair, down_piece), SPREAD, axis=0, tiled=True)
        if index == 0:
            gathered_gains = attn[2].transpose(1, 0, 2).reshape(4, width).astype(F32)
        layers.append((attn[0], attn[1], feed[0], feed[1]))

    state = to_lines(tokens[0], z).astype(F32)
    length = lax.ppermute(lengths, AXES, LINES_LENGTH)[0]
    grad = to_lines(grad_start, z).astype(F32)

    part = stretch // 4

    def member_places(member, side):
        block = jnp.arange(4, dtype=jnp.int32)
        inner = jnp.arange(part, dtype=jnp.int32)
        home = (member - block + 4) % 4
        return (
            home[:, None] * (2 * stretch) + side * stretch + member * part + inner[None, :]
        ).reshape(-1)

    def line_places(side):
        return jnp.concatenate(
            [member_places((x + step) % 4, side) for step in (0, 3, 1, 2)]
        )

    places = line_places(core)
    key_places = jnp.concatenate([places, line_places(1 - core)])
    half = HEAD_DIM // 2
    freq = ROPE_BASE ** (-jnp.arange(half, dtype=F32) * (2.0 / HEAD_DIM))
    angle = places.astype(F32)[:, None] * freq[None, :]
    context = (places, key_places, length, jnp.cos(angle)[:, None, :], jnp.sin(angle)[:, None, :])
    span = 8 * stretch

    records = []
    for index, window in enumerate((WINDOW, span)):
        w_qkv, w_out, pair, down = layers[index]
        attn = (gathered_gains[2 * index], w_qkv, w_out)
        feed = (gathered_gains[2 * index + 1], pair, down)
        state, attn_saved = attention_forward(state, attn, context, window)
        state, feed_saved = feed_forward(state, feed)
        records.append((attn, feed, attn_saved, feed_saved, window))
    output = from_lines(state.astype(BF16), z)[None]

    results = [None] * 18
    gain_grads = [None] * 4
    for index in (1, 0):
        attn, feed, attn_saved, feed_saved, window = records[index]
        base = 9 * index
        grad, gain_grads[2 * index + 1], g_pair, g_down = feed_backward(grad, feed_saved, feed)
        g_pair, g_down = spread_sum((g_pair, g_down))
        results[base + 6], results[base + 7] = home_columns(g_pair, (1024, 1024))
        results[base + 8] = home_rows(g_down)
        grad, gain_grads[2 * index], g_qkv, g_out = attention_backward(
            grad, attn_saved, attn, context, window
        )
        if index:
            g_qkv, g_out = spread_sum((g_qkv, g_out))
        else:
            g_gain = jnp.stack(gain_grads).astype(BF16).reshape(4, 16, 96).transpose(1, 0, 2)
            g_qkv, g_out, g_gain = spread_sum((g_qkv, g_out, g_gain))
            g_gain = lax.all_gather(g_gain[0], ("x", "core"), axis=0, tiled=False).astype(F32)
            g_gain = g_gain.reshape(4, 2, 4, 96).sum(axis=0).transpose(1, 0, 2).reshape(4, 192)
        results[base + 1 : base + 4] = home_columns(g_qkv, (384, 192, 192))
        results[base + 4] = home_rows(g_out)
    for index, slot in enumerate((0, 5, 9, 14)):
        results[slot] = g_gain[index]
    input_grad = from_lines(grad.astype(BF16), z).astype(F32)[None]
    return (output, input_grad, *results)


LINES_LENGTH = permutation(lambda x, c, z, h: (z, h, x, c))


def solution(mesh):
    fine = Mesh(mesh.devices.reshape(SIZES), AXES)
    token = P(REP, SHARD, None)
    vector = P(SHARD)
    matrix = P(SHARD, None)
    layer = (vector, matrix, matrix, matrix, matrix, vector, matrix, matrix, matrix)
    return jax.shard_map(
        body,
        mesh=fine,
        in_specs=(token, P(REP), token) + layer + layer,
        out_specs=(token, token) + layer + layer,
        check_vma=False,
    )
```

```python
import jax
import jax.numpy as jnp
from jax import lax
from jax.sharding import Mesh
from jax.sharding import PartitionSpec as P

HEAD_DIM = 96
WINDOW = 512
EPSILON = 1e-05
ROPE_BASE = 100000.0
NEGATIVE = -1e30

F32 = jnp.float32
BF16 = jnp.bfloat16

AXES = ("ylo", "x", "core", "z", "yhi")
SIZES = (2, 4, 2, 4, 2)
REP = ("ylo", "x", "core")
SHARD = ("z", "yhi")
SPREAD = ("z", "yhi", "core")

ATTN_UNIT, ATTN_SPLIT = 256, 288
FEED_UNIT, FEED_SPLIT = 512, 384

RIGHT = [(i, (i + 1) % 4) for i in range(4)]
LEFT = [(i, (i - 1) % 4) for i in range(4)]
SWAP = [(0, 1), (1, 0)]


def number(ylo, x, core, z, yhi):
    return (((ylo * 4 + x) * 2 + core) * 4 + z) * 2 + yhi


def permutation(place):
    pairs = []
    for ylo in range(2):
        for x in range(4):
            for core in range(2):
                for z in range(4):
                    for yhi in range(2):
                        pairs.append(
                            (number(ylo, x, core, z, yhi), number(ylo, *place(x, core, z, yhi)))
                        )
    return pairs


def inverse(pairs):
    return [(there, here) for here, there in pairs]


LINES = [permutation(lambda x, c, z, h, k=k: ((z + k) % 4, h, x, c)) for k in range(4)]
ROWS = permutation(lambda x, c, z, h: (z, c, 2 * h + x // 2, x % 2))


def to_lines(block, z):
    part = block.shape[0] // 4
    out = []
    for k in range(4):
        piece = lax.dynamic_slice_in_dim(block, ((z + k) % 4) * part, part, axis=0)
        out.append(lax.ppermute(piece, AXES, LINES[k]))
    return jnp.concatenate(out, axis=0)


def from_lines(block, z):
    part = block.shape[0] // 4
    out = jnp.zeros_like(block)
    for k in range(4):
        piece = lax.ppermute(block[part * k : part * (k + 1)], AXES, inverse(LINES[k]))
        out = lax.dynamic_update_slice_in_dim(out, piece, ((z + k) % 4) * part, axis=0)
    return out


def ring_gather(block):
    half = block.shape[0] // 2
    from_left = lax.ppermute(block, "x", RIGHT)
    from_right = lax.ppermute(block, "x", LEFT)
    far_first = lax.ppermute(from_left[:half], "x", RIGHT)
    far_second = lax.ppermute(from_right[half:], "x", LEFT)
    return jnp.concatenate([block, from_left, from_right, far_first, far_second], axis=0)


def ring_scatter(partial):
    rows = partial.shape[0] // 4
    half = rows // 2
    own = partial[:rows]
    left = partial[rows : 2 * rows]
    right = partial[2 * rows : 3 * rows]
    far = partial[3 * rows :].astype(BF16)
    first = lax.ppermute(far[:half], "x", RIGHT).astype(F32)
    second = lax.ppermute(far[half:], "x", LEFT).astype(F32)
    right = jnp.concatenate([right[:half] + first, right[half:]], axis=0).astype(BF16)
    left = jnp.concatenate([left[:half], left[half:] + second], axis=0).astype(BF16)
    from_left = lax.ppermute(right, "x", RIGHT).astype(F32)
    from_right = lax.ppermute(left, "x", LEFT).astype(F32)
    return own + from_left + from_right


def rms_norm(values, gain):
    return values * lax.rsqrt(jnp.mean(values * values, axis=-1, keepdims=True) + EPSILON) * gain


def turn(tensor, cosine, sine):
    half = tensor.shape[-1] // 2
    first = tensor[..., :half]
    second = tensor[..., half:]
    return jnp.concatenate(
        [first * cosine - second * sine, second * cosine + first * sine], axis=-1
    )


def masked_scores(queries, keys, context, window):
    places, key_places, length = context[0], context[1], context[2]
    raw = jnp.einsum("qkgd,pkd->kgqp", queries, keys, preferred_element_type=F32)
    gap = places[:, None] - key_places[None, :]
    allowed = ((key_places[None, :] < length) & (gap >= 0) & (gap < window)) | (gap == 0)
    return raw * HEAD_DIM ** (-0.5), allowed[None, None]


def attention_forward(state, weights, context, window):
    gain, w_qkv, w_out = weights
    cosine, sine = context[3], context[4]
    normed = rms_norm(state, gain).astype(BF16)
    flat = ring_gather(normed)
    rows = flat.shape[0]
    raw = jnp.dot(flat, w_qkv, preferred_element_type=F32)
    kv_here = w_qkv.shape[1] // (4 * HEAD_DIM)
    span = kv_here * HEAD_DIM
    queries = turn(raw[:, : 2 * span].reshape(rows, 2 * kv_here, HEAD_DIM), cosine, sine)
    queries = queries.astype(BF16).reshape(rows, kv_here, 2, HEAD_DIM)
    keys = turn(raw[:, 2 * span : 3 * span].reshape(rows, kv_here, HEAD_DIM), cosine, sine)
    both = jnp.concatenate([keys.reshape(rows, span), raw[:, 3 * span :]], axis=1).astype(BF16)
    both = jnp.concatenate([both, lax.ppermute(both, "core", SWAP)], axis=0)
    keys = both[:, :span].reshape(2 * rows, kv_here, HEAD_DIM)
    values = both[:, span:].reshape(2 * rows, kv_here, HEAD_DIM)
    scores, allowed = masked_scores(queries, keys, context, window)
    masked = jnp.where(allowed, scores, NEGATIVE)
    peak = jnp.max(masked, axis=-1, keepdims=True)
    shifted = jnp.where(allowed, jnp.exp(masked - peak), 0.0)
    totals = jnp.sum(shifted, axis=-1, keepdims=True)
    probs = (shifted / totals).astype(BF16)
    mixed = jnp.einsum("kgqp,pkd->qkgd", probs, values, preferred_element_type=F32)
    mixed = mixed.reshape(rows, 2 * span).astype(BF16)
    partial = jnp.dot(mixed, w_out, preferred_element_type=F32)
    result = state + ring_scatter(partial)
    return result, (state, flat, queries, keys, values, peak + jnp.log(totals), mixed)


def attention_backward(grad, saved, weights, context, window):
    gain, w_qkv, w_out = weights
    cosine, sine = context[3], context[4]
    state, flat, queries, keys, values, log_total, mixed = saved
    rows = flat.shape[0]
    kv_here = keys.shape[1]
    span = kv_here * HEAD_DIM
    grad_low = ring_gather(grad.astype(BF16))
    grad_mixed = jnp.einsum("rd,qd->rq", grad_low, w_out, preferred_element_type=F32)
    grad_mixed = grad_mixed.astype(BF16).reshape(queries.shape)
    scores, allowed = masked_scores(queries, keys, context, window)
    probs = jnp.where(allowed, jnp.exp(jnp.where(allowed, scores - log_total, NEGATIVE)), 0.0)
    grad_probs = jnp.einsum("qkgd,pkd->kgqp", grad_mixed, values, preferred_element_type=F32)
    inner = jnp.sum(grad_probs * probs, axis=-1, keepdims=True)
    grad_raw = (probs * (grad_probs - inner) * HEAD_DIM ** (-0.5)).astype(BF16)
    grad_keys = jnp.einsum("kgqp,qkgd->pkd", grad_raw, queries, preferred_element_type=F32)
    grad_values = jnp.einsum(
        "kgqp,qkgd->pkd", probs.astype(BF16), grad_mixed, preferred_element_type=F32
    )
    both = jnp.concatenate(
        [grad_keys.reshape(2 * rows, span), grad_values.reshape(2 * rows, span)], axis=1
    )
    other = lax.ppermute(both[rows:].astype(BF16), "core", SWAP)
    grad_query = jnp.einsum("kgqp,pkd->qkgd", grad_raw, keys, preferred_element_type=F32)
    query_low = turn(grad_query.reshape(rows, 2 * kv_here, HEAD_DIM), cosine, -sine)
    query_low = query_low.reshape(rows, 2 * span).astype(BF16)
    both = both[:rows] + other.astype(F32)
    keys_low = turn(both[:, :span].reshape(rows, kv_here, HEAD_DIM), cosine, -sine)
    low = jnp.concatenate(
        [query_low, keys_low.reshape(rows, span).astype(BF16), both[:, span:].astype(BF16)], axis=1
    )
    partial = jnp.einsum("rq,dq->rd", low, w_qkv, preferred_element_type=F32)
    own_normed = ring_scatter(partial)
    grad_wout = jnp.einsum("rq,rd->qd", mixed, grad_low, preferred_element_type=F32)
    grad_wqkv = jnp.einsum("rd,rq->dq", flat, low, preferred_element_type=F32)
    grad_state, grad_gain = jax.vjp(rms_norm, state, gain)[1](own_normed)
    return grad + grad_state, grad_gain, grad_wqkv.astype(BF16), grad_wout.astype(BF16)


def feed_forward(state, weights):
    gain, w_pair, w_down = weights
    hidden_here = w_down.shape[0]
    normed = rms_norm(state, gain).astype(BF16)
    flat = ring_gather(normed)
    gate = jnp.dot(flat, w_pair[:, :hidden_here], preferred_element_type=F32)
    lifted = jnp.dot(flat, w_pair[:, hidden_here:], preferred_element_type=F32)
    hidden = (jax.nn.silu(gate) * lifted).astype(BF16)
    partial = jnp.dot(hidden, w_down, preferred_element_type=F32)
    return state + ring_scatter(partial), (state, flat, gate, lifted, hidden)


def feed_backward(grad, saved, weights):
    gain, w_pair, w_down = weights
    state, flat, gate, lifted, hidden = saved
    grad_low = ring_gather(grad.astype(BF16))
    grad_hidden = jnp.einsum("rd,fd->rf", grad_low, w_down, preferred_element_type=F32)
    sigma = jax.nn.sigmoid(gate)
    grad_gate = (grad_hidden * lifted * sigma * (1.0 + gate * (1.0 - sigma))).astype(BF16)
    grad_lift = (grad_hidden * gate * sigma).astype(BF16)
    low = jnp.concatenate([grad_gate, grad_lift], axis=1)
    partial = jnp.einsum("rf,df->rd", low, w_pair, preferred_element_type=F32)
    own_normed = ring_scatter(partial)
    grad_pair = jnp.einsum("rd,rf->df", flat, low, preferred_element_type=F32)
    grad_down = jnp.einsum("rf,rd->fd", hidden, grad_low, preferred_element_type=F32)
    grad_state, grad_gain = jax.vjp(rms_norm, state, gain)[1](own_normed)
    return grad + grad_state, grad_gain, grad_pair.astype(BF16), grad_down.astype(BF16)


def fold(block, unit):
    rows, columns = block.shape
    return block.reshape(rows, columns // unit, unit).transpose(1, 0, 2).reshape(-1, unit)


def unfold(block, rows):
    lead, (height, unit) = block.shape[:-2], block.shape[-2:]
    order = tuple(range(len(lead))) + tuple(len(lead) + i for i in (1, 0, 2))
    block = block.reshape(lead + (height // rows, rows, unit)).transpose(order)
    return block.reshape(lead + (rows, height // rows * unit))


def pack(columns, rows, unit):
    def each(block):
        return fold_pieces(block.reshape((16, -1) + block.shape[1:]), unit)

    return jnp.concatenate([each(columns), each(rows)], axis=1)


def fold_pieces(block, unit):
    pieces, rows, columns = block.shape
    block = block.reshape(pieces, rows, columns // unit, unit).transpose(0, 2, 1, 3)
    return block.reshape(pieces, -1, unit)


def either(index, first, second):
    return jnp.where(index == 0, first, second)


def roll_home(relative, index):
    twice = jnp.concatenate([relative, relative], axis=0)
    return lax.dynamic_slice_in_dim(twice, (4 - index) % 4, 4, axis=0)


def ring_stack(block, axis):
    half = block.shape[0] // 2
    before = lax.ppermute(block, axis, RIGHT)
    after = lax.ppermute(block, axis, LEFT)
    first = lax.ppermute(before[:half], axis, RIGHT)
    second = lax.ppermute(after[half:], axis, LEFT)
    far = jnp.concatenate([first, second], axis=0)
    return jnp.stack([block, after, far, before])


def spread_gather(piece, where):
    other = lax.ppermute(piece, "yhi", SWAP)
    pair = either(where["yhi"], jnp.stack([piece, other]), jnp.stack([other, piece]))
    line = ring_stack(pair, "z")
    other = lax.ppermute(line, "core", SWAP)
    line = either(
        where["core"], jnp.stack([line, other], axis=2), jnp.stack([other, line], axis=2)
    )
    return roll_home(line, where["z"]).reshape((16,) + piece.shape)


def spread_scatter(pieces, where):
    tall = pieces.reshape((4, 2, 2) + pieces.shape[1:])
    mine = lax.dynamic_index_in_dim(tall, where["core"], axis=2, keepdims=False)
    theirs = lax.dynamic_index_in_dim(tall, 1 - where["core"], axis=2, keepdims=False)
    line = (mine.astype(F32) + lax.ppermute(theirs, "core", SWAP).astype(F32)).astype(BF16)

    def step(r):
        return lax.dynamic_index_in_dim(line, (where["z"] + r) % 4, axis=0, keepdims=False)

    own, after, far, before = step(0), step(1), step(2), step(3)
    first = lax.ppermute(far[:1], "z", RIGHT).astype(F32)
    second = lax.ppermute(far[1:], "z", LEFT).astype(F32)
    after = jnp.concatenate([(after[:1].astype(F32) + first).astype(BF16), after[1:]])
    before = jnp.concatenate([before[:1], (before[1:].astype(F32) + second).astype(BF16)])
    from_before = lax.ppermute(after, "z", RIGHT).astype(F32)
    from_after = lax.ppermute(before, "z", LEFT).astype(F32)
    pair = (own.astype(F32) + from_before + from_after).astype(BF16)
    mine = lax.dynamic_index_in_dim(pair, where["yhi"], axis=0, keepdims=False)
    theirs = lax.dynamic_index_in_dim(pair, 1 - where["yhi"], axis=0, keepdims=False)
    return (mine.astype(F32) + lax.ppermute(theirs, "yhi", SWAP).astype(F32)).astype(BF16)


def go_home(piece, split, where, offload):
    piece = (piece.astype(F32) + lax.ppermute(piece, "ylo", SWAP).astype(F32)).astype(BF16)
    moved = lax.ppermute(piece[split:], AXES, inverse(ROWS))
    piece = jnp.concatenate([piece[:split], moved], axis=0)
    if offload:
        return lax.all_gather(piece, ("x", "core"), axis=0, tiled=False).reshape(
            (4, 2) + piece.shape
        )
    line = ring_stack(piece, "x")
    other = lax.ppermute(line, "core", SWAP)
    line = either(
        where["core"], jnp.stack([line, other], axis=1), jnp.stack([other, line], axis=1)
    )
    return roll_home(line, where["x"])


def home_weights(every, split, part, widths):
    columns = unfold(every[:, :, :split], 96)
    out = []
    start = 0
    for width in widths:
        block = columns[..., start : start + width].transpose(1, 2, 0, 3)
        out.append(block.reshape(192, 4 * width).astype(F32))
        start += width
    rows = unfold(every[:, :, split:], part)
    out.append(rows.reshape(8 * part, -1).astype(F32))
    return out


def butterfly(values):
    for axis, size in (("core", 2), ("x", 4), ("z", 4), ("yhi", 2), ("ylo", 2)):
        step = 1
        while step < size:
            pairs = [(i, i ^ step) for i in range(size)]
            values = values + lax.ppermute(values, axis, pairs)
            step *= 2
    return values


def body(tokens, lengths, grad_output, *weights):
    slots, stretch, width = tokens.shape
    x = lax.axis_index("x")
    core = lax.axis_index("core")
    z = lax.axis_index("z")
    yhi = lax.axis_index("yhi")
    piece = 2 * x + core
    here = (2 * z + yhi) * stretch + jnp.arange(stretch, dtype=jnp.int32)
    valid = (here < lengths[0])[:, None]
    grad_start = jnp.where(valid, grad_output[0], 0).astype(BF16)

    def rows_piece(weight):
        part = weight.shape[0] // 8
        return lax.dynamic_slice_in_dim(weight, piece * part, part, axis=0)

    def columns_piece(weight):
        rows, columns = weight.shape
        return lax.dynamic_slice(
            weight, (core * (rows // 2), x * (columns // 4)), (rows // 2, columns // 4)
        )

    where = {"x": x, "core": core, "z": z, "yhi": yhi}
    layers = []
    for base in (0, 9):
        w_q, w_k, w_v, w_out = weights[base + 1 : base + 5]
        w_gate, w_up, w_down = weights[base + 6 : base + 9]
        gains = jnp.stack([weights[base], weights[base + 5]])
        gains = lax.dynamic_slice_in_dim(gains, core * 96, 96, axis=1)
        gains = jnp.pad(gains, ((0, 14), (0, ATTN_UNIT - 96)))
        out_piece = lax.ppermute(rows_piece(w_out), AXES, ROWS)
        down_piece = lax.ppermute(rows_piece(w_down), AXES, ROWS)
        w_qkv = jnp.concatenate([columns_piece(w) for w in (w_q, w_k, w_v)], axis=1)
        attn = [fold(w_qkv, ATTN_UNIT), fold(out_piece, ATTN_UNIT), gains]
        attn = spread_gather(jnp.concatenate(attn, axis=0), where)
        pair = jnp.concatenate([columns_piece(w_gate), columns_piece(w_up)], axis=1)
        feed = jnp.concatenate([fold(pair, FEED_UNIT), fold(down_piece, FEED_UNIT)], axis=0)
        feed = lax.all_gather(feed, SPREAD, axis=0, tiled=False)
        layers.append(
            (
                unfold(attn[:, :ATTN_SPLIT], 96).reshape(width, -1),
                unfold(attn[:, ATTN_SPLIT:-16], 24).reshape(-1, width),
                attn[:, -16:-14, :96].transpose(1, 0, 2).reshape(2, width).astype(F32),
                unfold(feed[:, :FEED_SPLIT], 96).reshape(width, -1),
                unfold(feed[:, FEED_SPLIT:], 64).reshape(-1, width),
            )
        )

    state = to_lines(tokens[0], z).astype(F32)
    length = lax.ppermute(lengths, AXES, LINES_LENGTH)[0]
    grad = to_lines(grad_start, z).astype(F32)

    part = stretch // 4

    def member_places(member, side):
        block = jnp.arange(4, dtype=jnp.int32)
        inner = jnp.arange(part, dtype=jnp.int32)
        home = (member - block + 4) % 4
        return (
            home[:, None] * (2 * stretch) + side * stretch + member * part + inner[None, :]
        ).reshape(-1)

    def line_places(side):
        return jnp.concatenate(
            [member_places((x + step) % 4, side) for step in (0, 3, 1, 2)]
        )

    places = line_places(core)
    key_places = jnp.concatenate([places, line_places(1 - core)])
    half = HEAD_DIM // 2
    freq = ROPE_BASE ** (-jnp.arange(half, dtype=F32) * (2.0 / HEAD_DIM))
    angle = places.astype(F32)[:, None] * freq[None, :]
    context = (places, key_places, length, jnp.cos(angle)[:, None, :], jnp.sin(angle)[:, None, :])
    span = 8 * stretch

    records = []
    for index, window in enumerate((WINDOW, span)):
        w_qkv, w_out, gains, pair, down = layers[index]
        attn = (gains[0], w_qkv, w_out)
        feed = (gains[1], pair, down)
        state, attn_saved = attention_forward(state, attn, context, window)
        state, feed_saved = feed_forward(state, feed)
        records.append((attn, feed, attn_saved, feed_saved, window))
    output = from_lines(state.astype(BF16), z)[None]

    results = [None] * 18
    gain_grads = [None] * 4
    for index in (1, 0):
        attn, feed, attn_saved, feed_saved, window = records[index]
        base = 9 * index
        grad, gain_grads[2 * index + 1], g_pair, g_down = feed_backward(grad, feed_saved, feed)
        packed = pack(g_pair, g_down, FEED_UNIT)
        if index:
            piece = lax.psum_scatter(packed, SPREAD, scatter_dimension=0, tiled=True)[0]
        else:
            piece = spread_scatter(packed, where)
        every = go_home(piece, FEED_SPLIT, where, index)
        results[base + 6 : base + 9] = home_weights(every, FEED_SPLIT, 64, (1024, 1024))
        grad, gain_grads[2 * index], g_qkv, g_out = attention_backward(
            grad, attn_saved, attn, context, window
        )
        piece = spread_scatter(pack(g_qkv, g_out, ATTN_UNIT), where)
        every = go_home(piece, ATTN_SPLIT, where, 0)
        results[base + 1 : base + 5] = home_weights(every, ATTN_SPLIT, 24, (384, 192, 192))
    gain_sums = butterfly(jnp.stack(gain_grads))
    gain_sums = lax.dynamic_slice_in_dim(gain_sums, (2 * z + yhi) * 192, 192, axis=1)
    for index, slot in enumerate((0, 5, 9, 14)):
        results[slot] = gain_sums[index]
    input_grad = from_lines(grad.astype(BF16), z).astype(F32)[None]
    return (output, input_grad, *results)


LINES_LENGTH = permutation(lambda x, c, z, h: (z, h, x, c))


def solution(mesh):
    fine = Mesh(mesh.devices.reshape(SIZES), AXES)
    token = P(REP, SHARD, None)
    vector = P(SHARD)
    matrix = P(SHARD, None)
    layer = (vector, matrix, matrix, matrix, matrix, vector, matrix, matrix, matrix)
    return jax.shard_map(
        body,
        mesh=fine,
        in_specs=(token, P(REP), token) + layer + layer,
        out_specs=(token, token) + layer + layer,
        check_vma=False,
    )
```

```python
import functools
import jax
import jax.numpy as jnp
from jax import lax
from jax.experimental import pallas as pl
from jax.experimental.pallas import tpu as pltpu
from jax.sharding import Mesh
from jax.sharding import PartitionSpec as P

F32 = jnp.float32
BF16 = jnp.bfloat16
HEAD_DIM = 96
NEGATIVE = -1e30
MIB = 1 << 20

OFFSETS = (0, 128, 256, 384, 448)
SIZES_OF = (128, 128, 128, 64, 64)


def params(mib, semantics=None):
    return pltpu.CompilerParams(vmem_limit_bytes=mib * MIB, dimension_semantics=semantics)


def cost(flops, nbytes, transcendentals=0):
    return pl.CostEstimate(
        flops=int(flops), bytes_accessed=int(nbytes), transcendentals=int(transcendentals)
    )


def fill(target, refs):
    start = 0
    for ref in refs:
        rows = ref.shape[0]
        target[start : start + rows, :] = ref[...]
        start += rows


def nn(a, b):
    return lax.dot_general(a, b, (((1,), (0,)), ((), ())), preferred_element_type=F32)


def nt(a, b):
    return lax.dot_general(a, b, (((1,), (1,)), ((), ())), preferred_element_type=F32)


def tn(a, b):
    return lax.dot_general(a, b, (((0,), (0,)), ((), ())), preferred_element_type=F32)


def whole(shape):
    return pl.BlockSpec(shape, lambda *_: (0,) * len(shape))


PIECES = [whole((rows, 1536)) for rows in SIZES_OF]
PARTIAL_SHAPES = [
    jax.ShapeDtypeStruct((128, 1536), F32),
    jax.ShapeDtypeStruct((128, 1536), F32),
    jax.ShapeDtypeStruct((128, 1536), F32),
    jax.ShapeDtypeStruct((128, 1536), BF16),
]
PARTIALS = [whole((128, 1536))] * 4


def emit(total, outs):
    for place, out in enumerate(outs):
        out[...] = total[128 * place : 128 * (place + 1), :].astype(out.dtype)


def down_parts(block):
    left = block[:, 0:64, :].reshape(256, 1024)
    right = jnp.concatenate([block[:, 64:96, 0:512], block[:, 64:96, 512:1024]], axis=1)
    return left, right.reshape(256, 512)


def feed_forward_kernel(*refs):
    pieces, (wg, wu, wd), outs = refs[:5], refs[5:8], refs[8:12]
    gate, up, hidden, flat, total = refs[12:]
    step = pl.program_id(0)

    @pl.when(step == 0)
    def _():
        fill(flat, pieces)

    rows = flat[...]
    g = nn(rows, wg[...])
    u = nn(rows, wu[...])
    gate[...] = g
    up[...] = u
    h = (g * jax.nn.sigmoid(g) * u).astype(BF16)
    hidden[...] = h
    left, right = down_parts(wd[...])
    left, right = nn(h, left), nn(h, right)

    @pl.when(step == 0)
    def _():
        total[:, :1024] = left
        total[:, 1024:] = right

    @pl.when(step > 0)
    def _():
        total[:, :1024] += left
        total[:, 1024:] += right

    @pl.when(step == 3)
    def _():
        emit(total, outs)


def feed_specs():
    return [
        pl.BlockSpec((1536, 256), lambda b: (0, b)),
        pl.BlockSpec((1536, 256), lambda b: (0, 4 + b)),
        pl.BlockSpec((4, 96, 1024), lambda b: (b, 0, 2)),
    ]


def column_block(rows):
    return pl.BlockSpec((rows, 256), lambda b: (0, b))


def feed_forward_call(pieces, packed):
    flat_packed = packed.reshape(1536, 3072)
    return pl.pallas_call(
        feed_forward_kernel,
        grid=(4,),
        in_specs=PIECES + feed_specs(),
        out_specs=PARTIALS + [column_block(512)] * 3,
        out_shape=PARTIAL_SHAPES
        + [
            jax.ShapeDtypeStruct((512, 1024), F32),
            jax.ShapeDtypeStruct((512, 1024), F32),
            jax.ShapeDtypeStruct((512, 1024), BF16),
        ],
        scratch_shapes=[pltpu.VMEM((512, 1536), BF16), pltpu.VMEM((512, 1536), F32)],
        compiler_params=params(40),
        cost_estimate=cost(4.9e9, 18e6),
        name="feed_forward",
    )(*pieces, flat_packed, flat_packed, packed)


def feed_backward_kernel(*refs):
    pieces, (wg, wu, wd, gate, up), outs = refs[:5], refs[5:10], refs[10:14]
    low_gate, low_up, flat, total = refs[14:]
    step = pl.program_id(0)

    @pl.when(step == 0)
    def _():
        fill(flat, pieces)

    rows = flat[...]
    left, right = down_parts(wd[...])
    grad = nt(rows[:, :1024], left) + nt(rows[:, 1024:], right)
    g = gate[...]
    s = jax.nn.sigmoid(g)
    a = (grad * up[...] * s * (1.0 + g * (1.0 - s))).astype(BF16)
    b = (grad * (g * s)).astype(BF16)
    low_gate[...] = a
    low_up[...] = b
    part = nt(a, wg[...]) + nt(b, wu[...])

    @pl.when(step == 0)
    def _():
        total[...] = part

    @pl.when(step > 0)
    def _():
        total[...] += part

    @pl.when(step == 3)
    def _():
        emit(total, outs)


def feed_backward_call(pieces, packed, gate, up):
    flat_packed = packed.reshape(1536, 3072)
    return pl.pallas_call(
        feed_backward_kernel,
        grid=(4,),
        in_specs=PIECES + feed_specs() + [column_block(512)] * 2,
        out_specs=PARTIALS + [column_block(512)] * 2,
        out_shape=PARTIAL_SHAPES + [jax.ShapeDtypeStruct((512, 1024), BF16)] * 2,
        scratch_shapes=[pltpu.VMEM((512, 1536), BF16), pltpu.VMEM((512, 1536), F32)],
        compiler_params=params(40),
        cost_estimate=cost(4.9e9, 20e6),
        name="feed_backward",
    )(*pieces, flat_packed, flat_packed, packed, gate, up)


def store_halves(side, mine, theirs, even, odd, rows, columns):
    @pl.when(side == 0)
    def _():
        mine[:, rows, columns] = even
        theirs[:, rows, columns] = odd

    @pl.when(side != 0)
    def _():
        mine[:, rows, columns] = odd
        theirs[:, rows, columns] = even


def feed_weights_kernel(side_ref, *refs):
    flats, grads = refs[:5], refs[5:10]
    low_gate, low_up, hidden, mine, theirs, flat_t, hidden_t, grad = refs[10:]
    step = pl.program_id(0)
    side = side_ref[0]

    @pl.when(step == 0)
    def _():
        start = 0
        for ref in flats:
            n = ref.shape[0]
            flat_t[:, start : start + n] = ref[...].T
            start += n

    @pl.when(step == 4)
    def _():
        hidden_t[...] = hidden[...].T
        fill(grad, grads)

    def columns(block):
        out = nn(flat_t[...], block).astype(BF16).reshape(8, 192, 256)
        store_halves(
            side, mine, theirs, out[:, :96], out[:, 96:], slice(0, 96), slice(0, 256)
        )

    @pl.when(step < 4)
    def _():
        columns(low_gate[...])

    @pl.when((step >= 4) & (step < 8))
    def _():
        columns(low_up[...])

    for q in range(4):

        @pl.when(step == 8 + q)
        def _():
            top = nn(hidden_t[...], grad[:, 256 * q : 256 * (q + 1)]).astype(BF16)
            top = top.reshape(8, 128, 256)
            store_halves(
                side, mine, theirs, top[:, :64], top[:, 64:], slice(0, 64), slice(0, 256)
            )
            half = 32 * (q // 2)
            some = hidden_t[...].reshape(16, 64, 512)[:, half : half + 32].reshape(512, 512)
            start = 1024 + 256 * (q % 2)
            low = nn(some, grad[:, start : start + 256]).astype(BF16).reshape(8, 64, 256)
            store_halves(
                side, mine, theirs, low[:, :32], low[:, 32:], slice(64, 96), slice(0, 256)
            )


def feed_weights_call(side, flats, grads, low_gate, low_up, hidden):
    block = pl.BlockSpec((8, 96, 256), lambda b, s: (0, 0, b))
    shape = jax.ShapeDtypeStruct((8, 96, 3072), BF16)
    spec = pltpu.PrefetchScalarGridSpec(
        num_scalar_prefetch=1,
        grid=(12,),
        in_specs=PIECES
        + PIECES
        + [
            pl.BlockSpec((512, 256), lambda b, s: (0, jnp.minimum(b, 3))),
            pl.BlockSpec((512, 256), lambda b, s: (0, jnp.clip(b - 4, 0, 3))),
            whole((512, 1024)),
        ],
        out_specs=[block, block],
        scratch_shapes=[
            pltpu.VMEM((1536, 512), BF16),
            pltpu.VMEM((1024, 512), BF16),
            pltpu.VMEM((512, 1536), BF16),
        ],
    )
    return pl.pallas_call(
        feed_weights_kernel,
        grid_spec=spec,
        out_shape=[shape, shape],
        compiler_params=params(40),
        cost_estimate=cost(4.9e9, 18e6),
        name="feed_weights",
    )(side, *flats, *grads, low_gate, low_up, hidden)


def piece_specs(pieces):
    return [whole(item.shape) for item in pieces]


def turn_columns(block, cosine, sine):
    out = []
    for start in range(0, block.shape[1], HEAD_DIM):
        a = block[:, start : start + 48]
        b = block[:, start + 48 : start + HEAD_DIM]
        out.append(a * cosine - b * sine)
        out.append(b * cosine + a * sine)
    return jnp.concatenate(out, axis=1)


def project_kernel(raw, count, *refs):
    pieces, (gain, weight, cosine, sine, queries, pair) = refs[:count], refs[count : count + 6]
    if raw:
        flat = refs[-1]
        start = 0
        for ref in pieces:
            n = ref.shape[0]
            rows = ref[...].astype(F32)
            scale = lax.rsqrt(jnp.mean(rows * rows, axis=-1, keepdims=True) + 1e-05)
            flat[start : start + n, :] = (rows * scale * gain[...]).astype(BF16)
            start += n
    else:
        flat = refs[-1]
        fill(flat, pieces)
    both = nn(flat[...], weight[...])
    cos, sin = cosine[...], sine[...]
    queries[...] = turn_columns(both[:, :384], cos, sin).astype(BF16)
    keys = turn_columns(both[:, 384:576], cos, sin)
    pair[...] = jnp.concatenate([keys, both[:, 576:768]], axis=1).astype(BF16)


def project_call(raw, pieces, gain, packed, cosine, sine):
    wide = packed.shape[-1]
    shape = jax.ShapeDtypeStruct((512, 384), BF16)
    flat_shape = jax.ShapeDtypeStruct((512, 1536), BF16)
    return pl.pallas_call(
        functools.partial(project_kernel, raw, len(pieces)),
        grid=(1,),
        in_specs=piece_specs(pieces)
        + [whole((1, 1536)), whole((1536, 768)), whole((512, 48)), whole((512, 48))],
        out_specs=[whole((512, 384))] * 2 + ([whole((512, 1536))] if raw else []),
        out_shape=[shape, shape] + ([flat_shape] if raw else []),
        scratch_shapes=[] if raw else [pltpu.VMEM((512, 1536), BF16)],
        compiler_params=params(40),
        cost_estimate=cost(1.3e9, 6e6),
        name="project",
    )(*pieces, gain.reshape(1, 1536), packed.reshape(1536, wide), cosine, sine)


def fill_bias(bias, length, places, key_places, window):
    gap = places[...] - key_places[...]
    inside = (key_places[...] < length) & (gap >= 0) & (gap < window)
    bias[...] = jnp.where(inside | (gap == 0), 0.0, NEGATIVE)


def both_rows(own, other, start):
    return jnp.concatenate(
        [own[:, start : start + HEAD_DIM], other[:, start : start + HEAD_DIM]], axis=0
    )


def attend_kernel(window, length, queries, own, other, places, key_places, w_out, *refs):
    outs, (mixed, log_total, total, bias) = refs[:4], refs[4:]
    fill_bias(bias, length[0], places, key_places, window)
    sums = []
    stats = []
    for head in range(4):
        if head % 2 == 0:
            keys = both_rows(own[...], other[...], HEAD_DIM * (head // 2))
            values = both_rows(own[...], other[...], 192 + HEAD_DIM * (head // 2)).T
        query = queries[:, HEAD_DIM * head : HEAD_DIM * (head + 1)]
        scores = nt(keys, query) * HEAD_DIM ** (-0.5) + bias[...]
        peak = jnp.max(scores, axis=0, keepdims=True)
        probs = jnp.exp(scores - peak)
        totals = jnp.sum(probs, axis=0, keepdims=True)
        part = nn(values, probs.astype(BF16)) / totals
        sums.append(part.astype(BF16).astype(F32).T.astype(BF16))
        stats.append(peak + jnp.log(totals))
        for block in range(4):
            cols = slice(384 * block, 384 * (block + 1))
            value = nn(sums[-1], w_out[4 * head + block])
            if head == 0:
                total[:, cols] = value
            else:
                total[:, cols] += value
    mixed[...] = jnp.concatenate(sums, axis=1)
    log_total[...] = jnp.concatenate(stats + stats, axis=0)
    emit(total, outs)


def line_specs():
    return [whole((512, 384))] * 3 + [whole((1, 512)), whole((1024, 1))]


def out_spec():
    return pl.BlockSpec((16, 96, 384), lambda *_: (0, 0, 2))


def attend_call(window, length, queries, own, other, places, key_places, packed):
    return pl.pallas_call(
        functools.partial(attend_kernel, window),
        grid=(1,),
        in_specs=[pl.BlockSpec(memory_space=pltpu.SMEM)] + line_specs() + [out_spec()],
        out_specs=PARTIALS + [whole((512, 384)), whole((8, 512))],
        out_shape=PARTIAL_SHAPES
        + [jax.ShapeDtypeStruct((512, 384), BF16), jax.ShapeDtypeStruct((8, 512), F32)],
        scratch_shapes=[pltpu.VMEM((512, 1536), F32), pltpu.VMEM((1024, 512), F32)],
        compiler_params=params(48),
        cost_estimate=cost(3e9, 6e6, 2e6),
        name="attend",
    )(length, queries, own, other, places, key_places, packed)


def attend_backward_kernel(window, length, *refs):
    pieces, refs = refs[:5], refs[5:]
    queries, own, other, places, key_places, w_out, log_total, cosine, sine = refs[:9]
    low_queries, pair_own, pair_other, grad, bias = refs[9:]
    fill(grad, pieces)
    fill_bias(bias, length[0], places, key_places, window)
    cos, sin = cosine[...], sine[...]
    lows = []
    key_sums = []
    value_sums = []
    for head in range(4):
        if head % 2 == 0:
            keys = both_rows(own[...], other[...], HEAD_DIM * (head // 2))
            values = both_rows(own[...], other[...], 192 + HEAD_DIM * (head // 2))
            keys_t = keys.T
        query = queries[:, HEAD_DIM * head : HEAD_DIM * (head + 1)]
        mixed = nt(grad[:, :384], w_out[4 * head])
        for block in range(1, 4):
            mixed += nt(grad[:, 384 * block : 384 * (block + 1)], w_out[4 * head + block])
        mixed = mixed.astype(BF16)
        scores = nt(keys, query) * HEAD_DIM ** (-0.5) + bias[...]
        probs = jnp.exp(scores - log_total[head : head + 1, :])
        slopes = nt(values, mixed)
        inner = jnp.sum(probs * slopes, axis=0, keepdims=True)
        raw = (probs * (slopes - inner) * HEAD_DIM ** (-0.5)).astype(BF16)
        key_part = nn(raw, query)
        value_part = nn(probs.astype(BF16), mixed)
        if head % 2 == 0:
            key_sums.append(key_part)
            value_sums.append(value_part)
        else:
            key_sums[-1] += key_part
            value_sums[-1] += value_part
        turned = nn(keys_t, raw)
        a, b = turned[:48], turned[48:]
        turned = jnp.concatenate([a * cos + b * sin, b * cos - a * sin], axis=0)
        lows.append(turned.T.astype(BF16))
    low_queries[...] = jnp.concatenate(lows, axis=1)
    both = jnp.concatenate(key_sums + value_sums, axis=1)
    pair_own[...] = both[:512]
    pair_other[...] = both[512:].astype(BF16)


def attend_backward_call(
    window, length, pieces, queries, own, other, places, key_places, packed, log_total, cosine, sine
):
    return pl.pallas_call(
        functools.partial(attend_backward_kernel, window),
        grid=(1,),
        in_specs=[pl.BlockSpec(memory_space=pltpu.SMEM)]
        + PIECES
        + line_specs()
        + [out_spec(), whole((8, 512)), whole((48, 512)), whole((48, 512))],
        out_specs=[whole((512, 384))] * 3,
        out_shape=[
            jax.ShapeDtypeStruct((512, 384), BF16),
            jax.ShapeDtypeStruct((512, 384), F32),
            jax.ShapeDtypeStruct((512, 384), BF16),
        ],
        scratch_shapes=[pltpu.VMEM((512, 1536), BF16), pltpu.VMEM((1024, 512), F32)],
        compiler_params=params(52),
        cost_estimate=cost(6e9, 6e6, 2e6),
        name="attend_backward",
    )(
        length,
        *pieces,
        queries,
        own,
        other,
        places,
        key_places,
        packed,
        log_total,
        cosine,
        sine,
    )


def unproject_kernel(low_queries, pair_own, pair_came, cosine, sine, weight, *refs):
    outs, low = refs[:4], refs[4]
    both = pair_own[...] + pair_came[...].astype(F32)
    keys = turn_columns(both[:, :192], cosine[...], -sine[...])
    rows = jnp.concatenate(
        [low_queries[...], keys.astype(BF16), both[:, 192:].astype(BF16)], axis=1
    )
    low[...] = rows
    emit(nt(rows, weight[...]), outs)


def unproject_call(low_queries, pair_own, pair_came, cosine, sine, packed):
    wide = packed.shape[-1]
    return pl.pallas_call(
        unproject_kernel,
        grid=(1,),
        in_specs=[whole((512, 384))] * 3 + [whole((512, 48))] * 2 + [whole((1536, 768))],
        out_specs=PARTIALS + [whole((512, 768))],
        out_shape=PARTIAL_SHAPES + [jax.ShapeDtypeStruct((512, 768), BF16)],
        compiler_params=params(40),
        cost_estimate=cost(1.3e9, 7e6),
        name="unproject",
    )(low_queries, pair_own, pair_came, cosine, sine, packed.reshape(1536, wide))


def attend_weights_kernel(count, side_ref, *refs):
    flats, grads, (low, mixed) = refs[:count], refs[count : count + 5], refs[count + 5 : count + 7]
    mine, theirs, flat_t, grad = refs[count + 7 :]
    side = side_ref[0]
    start = 0
    for ref in flats:
        n = ref.shape[0]
        flat_t[:, start : start + n] = ref[...].T
        start += n
    fill(grad, grads)
    for block in range(3):
        cols = slice(256 * block, 256 * (block + 1))
        out = nn(flat_t[...], low[:, cols]).astype(BF16).reshape(8, 192, 256)
        store_halves(side, mine, theirs, out[:, :96], out[:, 96:], slice(0, 96), cols)
    mixed_t = mixed[...].T
    for half in range(2):
        out = [
            nn(mixed_t, grad[:, 384 * q : 384 * (q + 1)]).astype(BF16).reshape(4, 96, 384)
            for q in (2 * half, 2 * half + 1)
        ]
        for head in range(4):
            place = slice(2 * head + half, 2 * head + half + 1)
            store_at(side, mine, theirs, out[0][head : head + 1], out[1][head : head + 1], place)


def store_at(side, mine, theirs, even, odd, place):
    cols = slice(768, 1152)

    @pl.when(side == 0)
    def _():
        mine[place, :, cols] = even
        theirs[place, :, cols] = odd

    @pl.when(side != 0)
    def _():
        mine[place, :, cols] = odd
        theirs[place, :, cols] = even


def attend_weights_call(side, flats, grads, low, mixed):
    shape = jax.ShapeDtypeStruct((8, 96, 1152), BF16)
    return pl.pallas_call(
        functools.partial(attend_weights_kernel, len(flats)),
        grid=(1,),
        in_specs=[pl.BlockSpec(memory_space=pltpu.SMEM)]
        + piece_specs(flats)
        + PIECES
        + [whole((512, 768)), whole((512, 384))],
        out_specs=[whole((8, 96, 1152))] * 2,
        out_shape=[shape, shape],
        scratch_shapes=[pltpu.VMEM((1536, 512), BF16), pltpu.VMEM((512, 1536), BF16)],
        compiler_params=params(40),
        cost_estimate=cost(1.9e9, 10e6),
        name="attend_weights",
    )(side, *flats, *grads, low, mixed)


def unpack_attention(side, blocks, refs):
    wq, wk, wv, wo = refs
    for x, block in enumerate(blocks):
        wq[:, 384 * x : 384 * (x + 1)] = block[:, :384].astype(F32)
    wk[...] = jnp.concatenate([block[:, 384:576].astype(F32) for block in blocks], axis=1)
    wv[...] = jnp.concatenate([block[:, 576:768].astype(F32) for block in blocks], axis=1)
    for x, block in enumerate(blocks):
        rows = slice(96 * (x // 2), 96 * (x // 2) + 96)
        for core in range(2):
            start = 384 * (2 * (x % 2) + core)

            @pl.when(side == core)
            def _(rows=rows, start=start, block=block):
                wo[rows, start : start + 384] = block[:, 768:1152].astype(F32)


def unpack_feed(blocks, refs):
    gate, up, down = refs
    for x, block in enumerate(blocks):
        for s in range(8):
            cols = slice(512 * s + 128 * x, 512 * s + 128 * (x + 1))
            gate[:, cols] = block[:, 128 * s : 128 * (s + 1)].astype(F32)
            up[:, cols] = block[:, 1024 + 128 * s : 1024 + 128 * (s + 1)].astype(F32)
        down[x, 0, :, :1024] = block[0:64, 2048:3072].astype(F32)
        down[x, 0, 0:32, 1024:] = block[64:96, 2048:2560].astype(F32)
        down[x, 0, 32:64, 1024:] = block[64:96, 2560:3072].astype(F32)


ATTENTION_SPECS = [
    pl.BlockSpec((96, 1536), lambda b, s: (b, 0)),
    pl.BlockSpec((96, 768), lambda b, s: (b, 0)),
    pl.BlockSpec((96, 768), lambda b, s: (b, 0)),
    pl.BlockSpec((192, 1536), lambda b, s: (0, 0)),
]
ATTENTION_SHAPES = [
    jax.ShapeDtypeStruct((192, 1536), F32),
    jax.ShapeDtypeStruct((192, 768), F32),
    jax.ShapeDtypeStruct((192, 768), F32),
    jax.ShapeDtypeStruct((192, 1536), F32),
]
FEED_OUT_SPECS = [
    pl.BlockSpec((96, 4096), lambda b, s: (b, 0)),
    pl.BlockSpec((96, 4096), lambda b, s: (b, 0)),
    pl.BlockSpec((4, 1, 64, 1536), lambda b, s: (0, b, 0, 0)),
]
FEED_SHAPES = [
    jax.ShapeDtypeStruct((192, 4096), F32),
    jax.ShapeDtypeStruct((192, 4096), F32),
    jax.ShapeDtypeStruct((4, 2, 64, 1536), F32),
]


def unpack_kernel(attention, feed, me, *refs):
    side = pl.program_id(0)
    blocks = [ref[0, 0] for ref in refs[:4]]
    refs = refs[4:]
    if attention:
        unpack_attention(side, [block[:, :1152] for block in blocks], refs[:4])
        refs = refs[4:]
    if feed:
        start = 1152 if attention else 0
        unpack_feed([block[:, start : start + 3072] for block in blocks], refs)


def unpack_call(attention, feed, me, every):
    wide = every.shape[-1]
    specs = [
        pl.BlockSpec((1, 1, 96, wide), lambda b, s, x=x: (lax.rem(x - s[0] + 4, 4), b, 0, 0))
        for x in range(4)
    ]
    out_specs = (ATTENTION_SPECS if attention else []) + (FEED_OUT_SPECS if feed else [])
    shapes = (ATTENTION_SHAPES if attention else []) + (FEED_SHAPES if feed else [])
    out = pl.pallas_call(
        functools.partial(unpack_kernel, attention, feed),
        grid_spec=pltpu.PrefetchScalarGridSpec(
            num_scalar_prefetch=1, grid=(2,), in_specs=specs, out_specs=out_specs
        ),
        out_shape=shapes,
        compiler_params=params(48),
        cost_estimate=cost(1e6, 30e6),
        name="unpack",
    )(me, every, every, every, every)
    if feed:
        out = list(out[:-1]) + [out[-1].reshape(512, 1536)]
    return out


def pack_feed_kernel(where, w_gate, w_up, w_down, out):
    x = where[0]
    for s in range(8):
        cols = pl.ds(pl.multiple_of(512 * s + 128 * x, 128), 128)
        out[:, 128 * s : 128 * (s + 1)] = w_gate[:, cols]
        out[:, 1024 + 128 * s : 1024 + 128 * (s + 1)] = w_up[:, cols]
    out[0:64, 2048:3072] = w_down[:, 0:1024]
    out[64:96, 2048:2560] = w_down[0:32, 1024:1536]
    out[64:96, 2560:3072] = w_down[32:64, 1024:1536]


def pack_feed_call(where, w_gate, w_up, w_down):
    return pl.pallas_call(
        pack_feed_kernel,
        grid_spec=pltpu.PrefetchScalarGridSpec(
            num_scalar_prefetch=1,
            grid=(1,),
            in_specs=[
                pl.BlockSpec((96, 4096), lambda b, w: (w[1], 0)),
                pl.BlockSpec((96, 4096), lambda b, w: (w[1], 0)),
                pl.BlockSpec((64, 1536), lambda b, w: (2 * w[0] + w[1], 0)),
            ],
            out_specs=pl.BlockSpec((96, 3072), lambda b, w: (0, 0)),
        ),
        out_shape=jax.ShapeDtypeStruct((96, 3072), BF16),
        compiler_params=params(24),
        cost_estimate=cost(1e3, 24e5),
        name="pack_feed",
    )(where, w_gate, w_up, w_down)


WINDOW = 512
EPSILON = 1e-05
ROPE_BASE = 100000.0

AXES = ("ylo", "x", "core", "z", "yhi")
SIZES = (2, 4, 2, 4, 2)
REP = ("ylo", "x", "core")
SHARD = ("z", "yhi")
SPREAD = ("z", "yhi", "core")

RIGHT = [(i, (i + 1) % 4) for i in range(4)]
LEFT = [(i, (i - 1) % 4) for i in range(4)]
SWAP = [(0, 1), (1, 0)]


def number(ylo, x, core, z, yhi):
    return (((ylo * 4 + x) * 2 + core) * 4 + z) * 2 + yhi


def permutation(place):
    pairs = []
    for ylo in range(2):
        for x in range(4):
            for core in range(2):
                for z in range(4):
                    for yhi in range(2):
                        pairs.append(
                            (number(ylo, x, core, z, yhi), number(ylo, *place(x, core, z, yhi)))
                        )
    return pairs


def inverse(pairs):
    return [(there, here) for here, there in pairs]


LINES = [permutation(lambda x, c, z, h, k=k: ((z + k) % 4, h, x, c)) for k in range(4)]
LINES_LENGTH = permutation(lambda x, c, z, h: (z, h, x, c))
ROWS = permutation(lambda x, c, z, h: (z, c, 2 * h + x // 2, x % 2))


def to_lines(block, z):
    part = block.shape[0] // 4
    out = []
    for k in range(4):
        piece = lax.dynamic_slice_in_dim(block, ((z + k) % 4) * part, part, axis=0)
        out.append(lax.ppermute(piece, AXES, LINES[k]))
    return jnp.concatenate(out, axis=0)


def from_lines(block, z):
    part = block.shape[0] // 4
    out = jnp.zeros_like(block)
    for k in range(4):
        piece = lax.ppermute(block[part * k : part * (k + 1)], AXES, inverse(LINES[k]))
        out = lax.dynamic_update_slice_in_dim(out, piece, ((z + k) % 4) * part, axis=0)
    return out


def ring_gather(block):
    half = block.shape[0] // 2
    from_left = lax.ppermute(block, "x", RIGHT)
    from_right = lax.ppermute(block, "x", LEFT)
    far_first = lax.ppermute(from_left[:half], "x", RIGHT)
    far_second = lax.ppermute(from_right[half:], "x", LEFT)
    return block, from_left, from_right, far_first, far_second


def ring_scatter(own, left, right, far):
    half = far.shape[0] // 2
    first = lax.ppermute(far[:half], "x", RIGHT).astype(F32)
    second = lax.ppermute(far[half:], "x", LEFT).astype(F32)
    right = jnp.concatenate([right[:half] + first, right[half:]], axis=0).astype(BF16)
    left = jnp.concatenate([left[:half], left[half:] + second], axis=0).astype(BF16)
    from_left = lax.ppermute(right, "x", RIGHT).astype(F32)
    from_right = lax.ppermute(left, "x", LEFT).astype(F32)
    return own + from_left + from_right


def rms_norm(values, gain):
    return values * lax.rsqrt(jnp.mean(values * values, axis=-1, keepdims=True) + EPSILON) * gain


def either(index, first, second):
    return jnp.where(index == 0, first, second)


def add_low(mine, came):
    return (mine.astype(F32) + came.astype(F32)).astype(BF16)


def ring_stack(block, axis):
    half = block.shape[0] // 2
    before = lax.ppermute(block, axis, RIGHT)
    after = lax.ppermute(block, axis, LEFT)
    first = lax.ppermute(before[:half], axis, RIGHT)
    second = lax.ppermute(after[half:], axis, LEFT)
    far = jnp.concatenate([first, second], axis=0)
    return jnp.stack([block, after, far, before])


def core_sum(mine, theirs):
    return add_low(mine, lax.ppermute(theirs, "core", SWAP))


def z_sum(line, where, offload):
    if offload:
        return lax.psum_scatter(line, "z", scatter_dimension=0, tiled=True)
    tall = line.reshape((4, 2) + line.shape[1:])

    def step(r):
        return lax.dynamic_index_in_dim(tall, (where["z"] + r) % 4, axis=0, keepdims=False)

    own, after, far, before = step(0), step(1), step(2), step(3)
    first = lax.ppermute(far[:1], "z", RIGHT)
    second = lax.ppermute(far[1:], "z", LEFT)
    after = jnp.concatenate([add_low(after[:1], first), after[1:]])
    before = jnp.concatenate([before[:1], add_low(before[1:], second)])
    from_before = lax.ppermute(after, "z", RIGHT).astype(F32)
    from_after = lax.ppermute(before, "z", LEFT).astype(F32)
    return (own.astype(F32) + from_before + from_after).astype(BF16)


def y_sum(pair, where):
    mine = lax.dynamic_index_in_dim(pair, where["yhi"], axis=0, keepdims=False)
    theirs = lax.dynamic_index_in_dim(pair, 1 - where["yhi"], axis=0, keepdims=False)
    piece = add_low(mine, lax.ppermute(theirs, "yhi", SWAP))
    return add_low(piece, lax.ppermute(piece, "ylo", SWAP))


def out_home(piece):
    moved = lax.ppermute(piece[:, 768:1152], AXES, inverse(ROWS))
    return jnp.concatenate([piece[:, :768], moved, piece[:, 1152:]], axis=1)


def butterfly(values):
    for axis, size in (("core", 2), ("x", 4), ("z", 4), ("yhi", 2), ("ylo", 2)):
        step = 1
        while step < size:
            pairs = [(i, i ^ step) for i in range(size)]
            values = values + lax.ppermute(values, axis, pairs)
            step *= 2
    return values


def norm_back(grad, own_normed, state, gain):
    grad_state, grad_gain = jax.vjp(rms_norm, state, gain)[1](own_normed)
    return grad + grad_state, grad_gain


def body(tokens, lengths, grad_output, *weights):
    stretch, width = tokens.shape[1:]
    x = lax.axis_index("x")
    core = lax.axis_index("core")
    z = lax.axis_index("z")
    yhi = lax.axis_index("yhi")
    where = {"x": x, "core": core, "z": z, "yhi": yhi}
    pair_index = jnp.stack([x, core]).astype(jnp.int32)
    side = core.astype(jnp.int32).reshape(1)

    gains = jnp.stack([weights[0], weights[5], weights[9], weights[14]])
    gains = lax.dynamic_slice_in_dim(gains, core * 96, 96, axis=1).T
    gains = jnp.pad(gains, ((0, 0), (0, 124)))
    packed = []
    for index, base in enumerate((0, 9)):
        w_q, w_k, w_v, w_out = weights[base + 1 : base + 5]
        out_block = lax.dynamic_slice(
            w_out, (96 * (x // 2), 384 * (2 * (x % 2) + core)), (96, 384)
        )
        out_block = lax.ppermute(out_block, AXES, ROWS)
        parts = [
            lax.dynamic_slice(w, (core * 96, x * (w.shape[1] // 4)), (96, w.shape[1] // 4))
            for w in (w_q, w_k, w_v)
        ]
        parts += [out_block] + ([] if index else [gains])
        attn = lax.all_gather(jnp.concatenate(parts, axis=1), SPREAD, axis=0, tiled=False)
        feed = pack_feed_call(pair_index, *weights[base + 6 : base + 9])
        feed = lax.all_gather(feed, SPREAD, axis=0, tiled=False)
        packed.append((attn, feed))
    gains = packed[0][0][:, :, 1152:1156].transpose(2, 0, 1).reshape(4, width).astype(F32)

    here = (2 * z + yhi) * stretch + jnp.arange(stretch, dtype=jnp.int32)
    valid = (here < lengths[0])[:, None]
    length = lax.ppermute(lengths, AXES, LINES_LENGTH)
    rows = to_lines(tokens[0], z)
    pieces = ring_gather(rows)
    state = rows.astype(F32)
    grad_rows = to_lines(jnp.where(valid, grad_output[0], 0).astype(BF16), z)
    grad_pieces = ring_gather(grad_rows)
    grad = grad_rows.astype(F32)

    part = stretch // 4

    def member_places(member, side_index):
        block = jnp.arange(4, dtype=jnp.int32)
        inner = jnp.arange(part, dtype=jnp.int32)
        home = (member - block + 4) % 4
        return (
            home[:, None] * (2 * stretch) + side_index * stretch + member * part + inner[None, :]
        ).reshape(-1)

    def line_places(side_index):
        return jnp.concatenate([member_places((x + step) % 4, side_index) for step in (0, 3, 1, 2)])

    places = line_places(core)
    key_places = jnp.concatenate([places, line_places(1 - core)]).reshape(1024, 1)
    half = HEAD_DIM // 2
    freq = ROPE_BASE ** (-jnp.arange(half, dtype=F32) * (2.0 / HEAD_DIM))
    angle = places.astype(F32)[:, None] * freq[None, :]
    cosine, sine = jnp.cos(angle), jnp.sin(angle)
    cosine_t, sine_t = cosine.T, sine.T
    places = places.reshape(1, 512)

    records = []
    for index, window in enumerate((WINDOW, 8 * stretch)):
        attn, feed = packed[index]
        gain_attn, gain_feed = gains[2 * index], gains[2 * index + 1]
        if index == 0:
            queries, own, flat = project_call(True, pieces, gain_attn, attn, cosine, sine)
            flats = (flat,)
        else:
            flats = ring_gather(rms_norm(state, gain_attn).astype(BF16))
            queries, own = project_call(False, flats, gain_attn, attn, cosine, sine)
        other = lax.ppermute(own, "core", SWAP)
        line = (queries, own, other, places, key_places)
        *partial, mixed, log_total = attend_call(window, length, *line, attn)
        saved_attn = (state, flats, line, mixed, log_total)
        state = state + ring_scatter(*partial)
        flats = ring_gather(rms_norm(state, gain_feed).astype(BF16))
        *partial, gate, up, hidden = feed_forward_call(flats, feed)
        saved_feed = (state, flats, gate, up, hidden)
        state = state + ring_scatter(*partial)
        records.append((saved_attn, saved_feed, window))
    output = from_lines(state.astype(BF16), z)[None]

    results = [None] * 18
    gain_grads = [None] * 4
    zero = jnp.zeros((1,), jnp.int32)
    for index in (1, 0):
        attn, feed = packed[index]
        gain_attn, gain_feed = gains[2 * index], gains[2 * index + 1]
        saved_attn, saved_feed, window = records[index]
        base = 9 * index

        state, flats, gate, up, hidden = saved_feed
        if index == 0:
            grad_pieces = ring_gather(grad.astype(BF16))
        *partial, low_gate, low_up = feed_backward_call(grad_pieces, feed, gate, up)
        grad, gain_grads[2 * index + 1] = norm_back(grad, ring_scatter(*partial), state, gain_feed)
        halves = feed_weights_call(side, flats, grad_pieces, low_gate, low_up, hidden)
        feed_pair = z_sum(core_sum(*halves), where, True)

        state, flats, line, mixed, log_total = saved_attn
        grad_pieces = ring_gather(grad.astype(BF16))
        low_queries, pair_own, pair_other = attend_backward_call(
            window, length, grad_pieces, *line, attn, log_total, cosine_t, sine_t
        )
        came = lax.ppermute(pair_other, "core", SWAP)
        *partial, low = unproject_call(low_queries, pair_own, came, cosine, sine, attn)
        grad, gain_grads[2 * index] = norm_back(grad, ring_scatter(*partial), state, gain_attn)
        halves = attend_weights_call(side, flats, grad_pieces, low, mixed)
        line_sum = core_sum(*halves)
        if index:
            attn_pair = z_sum(line_sum, where, True)
            piece = y_sum(jnp.concatenate([attn_pair, feed_pair], axis=2), where)
            every = lax.all_gather(out_home(piece), ("x", "core"), axis=0, tiled=False)
            out = unpack_call(True, True, zero, every.reshape(4, 2, 96, -1))
            results[base + 1 : base + 5] = out[:4]
            results[base + 6 : base + 9] = out[4:]
        else:
            every = lax.all_gather(y_sum(feed_pair, where), ("x", "core"), axis=0, tiled=False)
            results[base + 6 : base + 9] = unpack_call(
                False, True, zero, every.reshape(4, 2, 96, -1)
            )
            piece = out_home(y_sum(z_sum(line_sum, where, False), where))
            ring = ring_stack(piece, "x")
            came = lax.ppermute(ring, "core", SWAP)
            every = either(core, jnp.stack([ring, came], axis=1), jnp.stack([came, ring], axis=1))
            results[base + 1 : base + 5] = unpack_call(
                True, False, x.astype(jnp.int32).reshape(1), every
            )
    gain_sums = butterfly(jnp.stack(gain_grads))
    gain_sums = lax.dynamic_slice_in_dim(gain_sums, (2 * z + yhi) * 192, 192, axis=1)
    for index, slot in enumerate((0, 5, 9, 14)):
        results[slot] = gain_sums[index]
    input_grad = from_lines(grad.astype(BF16), z).astype(F32)[None]
    return (output, input_grad, *results)


def solution(mesh):
    fine = Mesh(mesh.devices.reshape(SIZES), AXES)
    token = P(REP, SHARD, None)
    vector = P(SHARD)
    matrix = P(SHARD, None)
    layer = (vector, matrix, matrix, matrix, matrix, vector, matrix, matrix, matrix)
    return jax.shard_map(
        body,
        mesh=fine,
        in_specs=(token, P(REP), token) + layer + layer,
        out_specs=(token, token) + layer + layer,
        check_vma=False,
    )
```

```python
import functools
import jax
import jax.numpy as jnp
from jax import lax
from jax.experimental import pallas as pl
from jax.experimental.pallas import tpu as pltpu
from jax.sharding import Mesh
from jax.sharding import PartitionSpec as P

F32 = jnp.float32
BF16 = jnp.bfloat16
HEAD_DIM = 96
NEGATIVE = -1e30
MIB = 1 << 20

OFFSETS = (0, 128, 256, 384, 448)
SIZES_OF = (128, 128, 128, 64, 64)


def params(mib, semantics=None):
    return pltpu.CompilerParams(vmem_limit_bytes=mib * MIB, dimension_semantics=semantics)


def cost(flops, nbytes, transcendentals=0):
    return pl.CostEstimate(
        flops=int(flops), bytes_accessed=int(nbytes), transcendentals=int(transcendentals)
    )


def fill(target, refs):
    start = 0
    for ref in refs:
        rows = ref.shape[0]
        target[start : start + rows, :] = ref[...]
        start += rows


def nn(a, b):
    return lax.dot_general(a, b, (((1,), (0,)), ((), ())), preferred_element_type=F32)


def nt(a, b):
    return lax.dot_general(a, b, (((1,), (1,)), ((), ())), preferred_element_type=F32)


def tn(a, b):
    return lax.dot_general(a, b, (((0,), (0,)), ((), ())), preferred_element_type=F32)


def later(kernel, count, lead=0):
    if not count:
        return kernel

    def wrapped(*refs):
        return kernel(*refs[:lead], *refs[lead + count :])

    return wrapped


def anywhere(after):
    return [pl.BlockSpec(memory_space=pl.ANY)] * len(after)


def whole(shape):
    return pl.BlockSpec(shape, lambda *_: (0,) * len(shape))


PIECES = [whole((rows, 1536)) for rows in SIZES_OF]
PARTIAL_SHAPES = [
    jax.ShapeDtypeStruct((128, 1536), F32),
    jax.ShapeDtypeStruct((128, 1536), F32),
    jax.ShapeDtypeStruct((128, 1536), F32),
    jax.ShapeDtypeStruct((128, 1536), BF16),
]
PARTIALS = [whole((128, 1536))] * 4


def emit(total, outs):
    for place, out in enumerate(outs):
        out[...] = total[128 * place : 128 * (place + 1), :].astype(out.dtype)


def down_parts(block):
    left = block[:, 0:64, :].reshape(256, 1024)
    right = jnp.concatenate([block[:, 64:96, 0:512], block[:, 64:96, 512:1024]], axis=1)
    return left, right.reshape(256, 512)


def feed_forward_kernel(*refs):
    pieces, (wg, wu, wd), outs = refs[:5], refs[5:8], refs[8:12]
    gate, up, hidden, flat, total = refs[12:]
    step = pl.program_id(0)

    @pl.when(step == 0)
    def _():
        fill(flat, pieces)

    rows = flat[...]
    g = nn(rows, wg[...])
    u = nn(rows, wu[...])
    gate[...] = g
    up[...] = u
    h = (g * jax.nn.sigmoid(g) * u).astype(BF16)
    hidden[...] = h
    left, right = down_parts(wd[...])
    left, right = nn(h, left), nn(h, right)

    @pl.when(step == 0)
    def _():
        total[:, :1024] = left
        total[:, 1024:] = right

    @pl.when(step > 0)
    def _():
        total[:, :1024] += left
        total[:, 1024:] += right

    @pl.when(step == 3)
    def _():
        emit(total, outs)


def feed_specs():
    return [
        pl.BlockSpec((1536, 256), lambda b: (0, b)),
        pl.BlockSpec((1536, 256), lambda b: (0, 4 + b)),
        pl.BlockSpec((4, 96, 1024), lambda b: (b, 0, 2)),
    ]


def column_block(rows):
    return pl.BlockSpec((rows, 256), lambda b: (0, b))


def feed_forward_call(pieces, packed, after=()):
    flat_packed = packed.reshape(1536, 3072)
    return pl.pallas_call(
        later(feed_forward_kernel, len(after)),
        grid=(4,),
        in_specs=anywhere(after) + PIECES + feed_specs(),
        out_specs=PARTIALS + [column_block(512)] * 3,
        out_shape=PARTIAL_SHAPES
        + [
            jax.ShapeDtypeStruct((512, 1024), F32),
            jax.ShapeDtypeStruct((512, 1024), F32),
            jax.ShapeDtypeStruct((512, 1024), BF16),
        ],
        scratch_shapes=[pltpu.VMEM((512, 1536), BF16), pltpu.VMEM((512, 1536), F32)],
        compiler_params=params(40),
        cost_estimate=cost(4.9e9, 18e6),
        name="feed_forward",
    )(*after, *pieces, flat_packed, flat_packed, packed)


def feed_backward_kernel(*refs):
    pieces, (wg, wu, wd, gate, up), outs = refs[:5], refs[5:10], refs[10:14]
    low_gate, low_up, flat, total = refs[14:]
    step = pl.program_id(0)

    @pl.when(step == 0)
    def _():
        fill(flat, pieces)

    rows = flat[...]
    left, right = down_parts(wd[...])
    grad = nt(rows[:, :1024], left) + nt(rows[:, 1024:], right)
    g = gate[...]
    s = jax.nn.sigmoid(g)
    a = (grad * up[...] * s * (1.0 + g * (1.0 - s))).astype(BF16)
    b = (grad * (g * s)).astype(BF16)
    low_gate[...] = a
    low_up[...] = b
    part = nt(a, wg[...]) + nt(b, wu[...])

    @pl.when(step == 0)
    def _():
        total[...] = part

    @pl.when(step > 0)
    def _():
        total[...] += part

    @pl.when(step == 3)
    def _():
        emit(total, outs)


def feed_backward_call(pieces, packed, gate, up, after=()):
    flat_packed = packed.reshape(1536, 3072)
    return pl.pallas_call(
        later(feed_backward_kernel, len(after)),
        grid=(4,),
        in_specs=anywhere(after) + PIECES + feed_specs() + [column_block(512)] * 2,
        out_specs=PARTIALS + [column_block(512)] * 2,
        out_shape=PARTIAL_SHAPES + [jax.ShapeDtypeStruct((512, 1024), BF16)] * 2,
        scratch_shapes=[pltpu.VMEM((512, 1536), BF16), pltpu.VMEM((512, 1536), F32)],
        compiler_params=params(40),
        cost_estimate=cost(4.9e9, 20e6),
        name="feed_backward",
    )(*after, *pieces, flat_packed, flat_packed, packed, gate, up)


def store_halves(side, mine, theirs, even, odd, rows, columns):
    @pl.when(side == 0)
    def _():
        mine[:, rows, columns] = even
        theirs[:, rows, columns] = odd

    @pl.when(side != 0)
    def _():
        mine[:, rows, columns] = odd
        theirs[:, rows, columns] = even


def feed_weights_kernel(side_ref, *refs):
    flats, grads = refs[:5], refs[5:10]
    low_gate, low_up, hidden, mine, theirs, flat_t, hidden_t, grad = refs[10:]
    step = pl.program_id(0)
    side = side_ref[0]

    @pl.when(step == 0)
    def _():
        start = 0
        for ref in flats:
            n = ref.shape[0]
            flat_t[:, start : start + n] = ref[...].T
            start += n

    @pl.when(step == 4)
    def _():
        hidden_t[...] = hidden[...].T
        fill(grad, grads)

    def columns(block):
        out = nn(flat_t[...], block).astype(BF16).reshape(8, 192, 256)
        store_halves(
            side, mine, theirs, out[:, :96], out[:, 96:], slice(0, 96), slice(0, 256)
        )

    @pl.when(step < 4)
    def _():
        columns(low_gate[...])

    @pl.when((step >= 4) & (step < 8))
    def _():
        columns(low_up[...])

    for q in range(4):

        @pl.when(step == 8 + q)
        def _():
            top = nn(hidden_t[...], grad[:, 256 * q : 256 * (q + 1)]).astype(BF16)
            top = top.reshape(8, 128, 256)
            store_halves(
                side, mine, theirs, top[:, :64], top[:, 64:], slice(0, 64), slice(0, 256)
            )
            half = 32 * (q // 2)
            some = hidden_t[...].reshape(16, 64, 512)[:, half : half + 32].reshape(512, 512)
            start = 1024 + 256 * (q % 2)
            low = nn(some, grad[:, start : start + 256]).astype(BF16).reshape(8, 64, 256)
            store_halves(
                side, mine, theirs, low[:, :32], low[:, 32:], slice(64, 96), slice(0, 256)
            )


def feed_weights_call(side, flats, grads, low_gate, low_up, hidden):
    block = pl.BlockSpec((8, 96, 256), lambda b, s: (0, 0, b))
    shape = jax.ShapeDtypeStruct((8, 96, 3072), BF16)
    spec = pltpu.PrefetchScalarGridSpec(
        num_scalar_prefetch=1,
        grid=(12,),
        in_specs=PIECES
        + PIECES
        + [
            pl.BlockSpec((512, 256), lambda b, s: (0, jnp.minimum(b, 3))),
            pl.BlockSpec((512, 256), lambda b, s: (0, jnp.clip(b - 4, 0, 3))),
            whole((512, 1024)),
        ],
        out_specs=[block, block],
        scratch_shapes=[
            pltpu.VMEM((1536, 512), BF16),
            pltpu.VMEM((1024, 512), BF16),
            pltpu.VMEM((512, 1536), BF16),
        ],
    )
    return pl.pallas_call(
        feed_weights_kernel,
        grid_spec=spec,
        out_shape=[shape, shape],
        compiler_params=params(40),
        cost_estimate=cost(4.9e9, 18e6),
        name="feed_weights",
    )(side, *flats, *grads, low_gate, low_up, hidden)


def piece_specs(pieces):
    return [whole(item.shape) for item in pieces]


def turn_columns(block, cosine, sine):
    out = []
    for start in range(0, block.shape[1], HEAD_DIM):
        a = block[:, start : start + 48]
        b = block[:, start + 48 : start + HEAD_DIM]
        out.append(a * cosine - b * sine)
        out.append(b * cosine + a * sine)
    return jnp.concatenate(out, axis=1)


def project_kernel(raw, count, *refs):
    pieces, (gain, weight, cosine, sine, queries, pair) = refs[:count], refs[count : count + 6]
    if raw:
        flat = refs[-1]
        start = 0
        for ref in pieces:
            n = ref.shape[0]
            rows = ref[...].astype(F32)
            scale = lax.rsqrt(jnp.mean(rows * rows, axis=-1, keepdims=True) + 1e-05)
            flat[start : start + n, :] = (rows * scale * gain[...]).astype(BF16)
            start += n
    else:
        flat = refs[-1]
        fill(flat, pieces)
    both = nn(flat[...], weight[...])
    cos, sin = cosine[...], sine[...]
    queries[...] = turn_columns(both[:, :384], cos, sin).astype(BF16)
    keys = turn_columns(both[:, 384:576], cos, sin)
    pair[...] = jnp.concatenate([keys, both[:, 576:768]], axis=1).astype(BF16)


def project_call(raw, pieces, gain, packed, cosine, sine, after=()):
    wide = packed.shape[-1]
    shape = jax.ShapeDtypeStruct((512, 384), BF16)
    flat_shape = jax.ShapeDtypeStruct((512, 1536), BF16)
    return pl.pallas_call(
        later(functools.partial(project_kernel, raw, len(pieces)), len(after)),
        grid=(1,),
        in_specs=anywhere(after)
        + piece_specs(pieces)
        + [whole((1, 1536)), whole((1536, 768)), whole((512, 48)), whole((512, 48))],
        out_specs=[whole((512, 384))] * 2 + ([whole((512, 1536))] if raw else []),
        out_shape=[shape, shape] + ([flat_shape] if raw else []),
        scratch_shapes=[] if raw else [pltpu.VMEM((512, 1536), BF16)],
        compiler_params=params(40),
        cost_estimate=cost(1.3e9, 6e6),
        name="project",
    )(*after, *pieces, gain.reshape(1, 1536), packed.reshape(1536, wide), cosine, sine)


def fill_bias(bias, length, places, key_places, window):
    gap = places[...] - key_places[...]
    inside = (key_places[...] < length) & (gap >= 0) & (gap < window)
    bias[...] = jnp.where(inside | (gap == 0), 0.0, NEGATIVE)


def both_rows(own, other, start):
    return jnp.concatenate(
        [own[:, start : start + HEAD_DIM], other[:, start : start + HEAD_DIM]], axis=0
    )


def attend_kernel(window, length, queries, own, other, places, key_places, w_out, *refs):
    outs, (mixed, log_total, total, bias) = refs[:4], refs[4:]
    fill_bias(bias, length[0], places, key_places, window)
    sums = []
    stats = []
    for head in range(4):
        if head % 2 == 0:
            keys = both_rows(own[...], other[...], HEAD_DIM * (head // 2))
            values = both_rows(own[...], other[...], 192 + HEAD_DIM * (head // 2)).T
        query = queries[:, HEAD_DIM * head : HEAD_DIM * (head + 1)]
        scores = nt(keys, query) * HEAD_DIM ** (-0.5) + bias[...]
        peak = jnp.max(scores, axis=0, keepdims=True)
        probs = jnp.exp(scores - peak)
        totals = jnp.sum(probs, axis=0, keepdims=True)
        part = nn(values, probs.astype(BF16)) / totals
        sums.append(part.astype(BF16).astype(F32).T.astype(BF16))
        stats.append(peak + jnp.log(totals))
        for block in range(4):
            cols = slice(384 * block, 384 * (block + 1))
            value = nn(sums[-1], w_out[4 * head + block])
            if head == 0:
                total[:, cols] = value
            else:
                total[:, cols] += value
    mixed[...] = jnp.concatenate(sums, axis=1)
    log_total[...] = jnp.concatenate(stats + stats, axis=0)
    emit(total, outs)


def line_specs():
    return [whole((512, 384))] * 3 + [whole((1, 512)), whole((1024, 1))]


def out_spec():
    return pl.BlockSpec((16, 96, 384), lambda *_: (0, 0, 2))


def attend_call(window, length, queries, own, other, places, key_places, packed, after=()):
    return pl.pallas_call(
        later(functools.partial(attend_kernel, window), len(after)),
        grid=(1,),
        in_specs=anywhere(after)
        + [pl.BlockSpec(memory_space=pltpu.SMEM)] + line_specs() + [out_spec()],
        out_specs=PARTIALS + [whole((512, 384)), whole((8, 512))],
        out_shape=PARTIAL_SHAPES
        + [jax.ShapeDtypeStruct((512, 384), BF16), jax.ShapeDtypeStruct((8, 512), F32)],
        scratch_shapes=[pltpu.VMEM((512, 1536), F32), pltpu.VMEM((1024, 512), F32)],
        compiler_params=params(48),
        cost_estimate=cost(3e9, 6e6, 2e6),
        name="attend",
    )(*after, length, queries, own, other, places, key_places, packed)


def attend_backward_kernel(window, length, *refs):
    pieces, refs = refs[:5], refs[5:]
    queries, own, other, places, key_places, w_out, log_total, cosine, sine = refs[:9]
    low_queries, pair_own, pair_other, grad, bias = refs[9:]
    fill(grad, pieces)
    fill_bias(bias, length[0], places, key_places, window)
    cos, sin = cosine[...], sine[...]
    lows = []
    key_sums = []
    value_sums = []
    for head in range(4):
        if head % 2 == 0:
            keys = both_rows(own[...], other[...], HEAD_DIM * (head // 2))
            values = both_rows(own[...], other[...], 192 + HEAD_DIM * (head // 2))
            keys_t = keys.T
        query = queries[:, HEAD_DIM * head : HEAD_DIM * (head + 1)]
        mixed = nt(grad[:, :384], w_out[4 * head])
        for block in range(1, 4):
            mixed += nt(grad[:, 384 * block : 384 * (block + 1)], w_out[4 * head + block])
        mixed = mixed.astype(BF16)
        scores = nt(keys, query) * HEAD_DIM ** (-0.5) + bias[...]
        probs = jnp.exp(scores - log_total[head : head + 1, :])
        slopes = nt(values, mixed)
        inner = jnp.sum(probs * slopes, axis=0, keepdims=True)
        raw = (probs * (slopes - inner) * HEAD_DIM ** (-0.5)).astype(BF16)
        key_part = nn(raw, query)
        value_part = nn(probs.astype(BF16), mixed)
        if head % 2 == 0:
            key_sums.append(key_part)
            value_sums.append(value_part)
        else:
            key_sums[-1] += key_part
            value_sums[-1] += value_part
        turned = nn(keys_t, raw)
        a, b = turned[:48], turned[48:]
        turned = jnp.concatenate([a * cos + b * sin, b * cos - a * sin], axis=0)
        lows.append(turned.T.astype(BF16))
    low_queries[...] = jnp.concatenate(lows, axis=1)
    both = jnp.concatenate(key_sums + value_sums, axis=1)
    pair_own[...] = both[:512]
    pair_other[...] = both[512:].astype(BF16)


def attend_backward_call(
    window,
    length,
    pieces,
    queries,
    own,
    other,
    places,
    key_places,
    packed,
    log_total,
    cosine,
    sine,
    after=(),
):
    return pl.pallas_call(
        later(functools.partial(attend_backward_kernel, window), len(after)),
        grid=(1,),
        in_specs=anywhere(after)
        + [pl.BlockSpec(memory_space=pltpu.SMEM)]
        + PIECES
        + line_specs()
        + [out_spec(), whole((8, 512)), whole((48, 512)), whole((48, 512))],
        out_specs=[whole((512, 384))] * 3,
        out_shape=[
            jax.ShapeDtypeStruct((512, 384), BF16),
            jax.ShapeDtypeStruct((512, 384), F32),
            jax.ShapeDtypeStruct((512, 384), BF16),
        ],
        scratch_shapes=[pltpu.VMEM((512, 1536), BF16), pltpu.VMEM((1024, 512), F32)],
        compiler_params=params(52),
        cost_estimate=cost(6e9, 6e6, 2e6),
        name="attend_backward",
    )(
        *after,
        length,
        *pieces,
        queries,
        own,
        other,
        places,
        key_places,
        packed,
        log_total,
        cosine,
        sine,
    )


def unproject_kernel(low_queries, pair_own, pair_came, cosine, sine, weight, *refs):
    outs, low = refs[:4], refs[4]
    both = pair_own[...] + pair_came[...].astype(F32)
    keys = turn_columns(both[:, :192], cosine[...], -sine[...])
    rows = jnp.concatenate(
        [low_queries[...], keys.astype(BF16), both[:, 192:].astype(BF16)], axis=1
    )
    low[...] = rows
    emit(nt(rows, weight[...]), outs)


def unproject_call(low_queries, pair_own, pair_came, cosine, sine, packed):
    wide = packed.shape[-1]
    return pl.pallas_call(
        unproject_kernel,
        grid=(1,),
        in_specs=[whole((512, 384))] * 3 + [whole((512, 48))] * 2 + [whole((1536, 768))],
        out_specs=PARTIALS + [whole((512, 768))],
        out_shape=PARTIAL_SHAPES + [jax.ShapeDtypeStruct((512, 768), BF16)],
        compiler_params=params(40),
        cost_estimate=cost(1.3e9, 7e6),
        name="unproject",
    )(low_queries, pair_own, pair_came, cosine, sine, packed.reshape(1536, wide))


def attend_weights_kernel(count, side_ref, *refs):
    flats, grads, (low, mixed) = refs[:count], refs[count : count + 5], refs[count + 5 : count + 7]
    mine, theirs, flat_t, grad = refs[count + 7 :]
    side = side_ref[0]
    start = 0
    for ref in flats:
        n = ref.shape[0]
        flat_t[:, start : start + n] = ref[...].T
        start += n
    fill(grad, grads)
    for block in range(3):
        cols = slice(256 * block, 256 * (block + 1))
        out = nn(flat_t[...], low[:, cols]).astype(BF16).reshape(8, 192, 256)
        store_halves(side, mine, theirs, out[:, :96], out[:, 96:], slice(0, 96), cols)
    mixed_t = mixed[...].T
    for half in range(2):
        out = [
            nn(mixed_t, grad[:, 384 * q : 384 * (q + 1)]).astype(BF16).reshape(4, 96, 384)
            for q in (2 * half, 2 * half + 1)
        ]
        for head in range(4):
            place = slice(2 * head + half, 2 * head + half + 1)
            store_at(side, mine, theirs, out[0][head : head + 1], out[1][head : head + 1], place)


def store_at(side, mine, theirs, even, odd, place):
    cols = slice(768, 1152)

    @pl.when(side == 0)
    def _():
        mine[place, :, cols] = even
        theirs[place, :, cols] = odd

    @pl.when(side != 0)
    def _():
        mine[place, :, cols] = odd
        theirs[place, :, cols] = even


def attend_weights_call(side, flats, grads, low, mixed, after=()):
    shape = jax.ShapeDtypeStruct((8, 96, 1152), BF16)
    return pl.pallas_call(
        later(functools.partial(attend_weights_kernel, len(flats)), len(after)),
        grid=(1,),
        in_specs=anywhere(after)
        + [pl.BlockSpec(memory_space=pltpu.SMEM)]
        + piece_specs(flats)
        + PIECES
        + [whole((512, 768)), whole((512, 384))],
        out_specs=[whole((8, 96, 1152))] * 2,
        out_shape=[shape, shape],
        scratch_shapes=[pltpu.VMEM((1536, 512), BF16), pltpu.VMEM((512, 1536), BF16)],
        compiler_params=params(40),
        cost_estimate=cost(1.9e9, 10e6),
        name="attend_weights",
    )(*after, side, *flats, *grads, low, mixed)


def unpack_attention(side, blocks, refs):
    wq, wk, wv, wo = refs
    for x, block in enumerate(blocks):
        wq[:, 384 * x : 384 * (x + 1)] = block[:, :384].astype(F32)
    wk[...] = jnp.concatenate([block[:, 384:576].astype(F32) for block in blocks], axis=1)
    wv[...] = jnp.concatenate([block[:, 576:768].astype(F32) for block in blocks], axis=1)
    for x, block in enumerate(blocks):
        rows = slice(96 * (x // 2), 96 * (x // 2) + 96)
        for core in range(2):
            start = 384 * (2 * (x % 2) + core)

            @pl.when(side == core)
            def _(rows=rows, start=start, block=block):
                wo[rows, start : start + 384] = block[:, 768:1152].astype(F32)


def unpack_feed(blocks, refs):
    gate, up, down = refs
    for x, block in enumerate(blocks):
        for s in range(8):
            cols = slice(512 * s + 128 * x, 512 * s + 128 * (x + 1))
            gate[:, cols] = block[:, 128 * s : 128 * (s + 1)].astype(F32)
            up[:, cols] = block[:, 1024 + 128 * s : 1024 + 128 * (s + 1)].astype(F32)
        down[x, 0, :, :1024] = block[0:64, 2048:3072].astype(F32)
        down[x, 0, 0:32, 1024:] = block[64:96, 2048:2560].astype(F32)
        down[x, 0, 32:64, 1024:] = block[64:96, 2560:3072].astype(F32)


ATTENTION_SPECS = [
    pl.BlockSpec((96, 1536), lambda b, s: (b, 0)),
    pl.BlockSpec((96, 768), lambda b, s: (b, 0)),
    pl.BlockSpec((96, 768), lambda b, s: (b, 0)),
    pl.BlockSpec((192, 1536), lambda b, s: (0, 0)),
]
ATTENTION_SHAPES = [
    jax.ShapeDtypeStruct((192, 1536), F32),
    jax.ShapeDtypeStruct((192, 768), F32),
    jax.ShapeDtypeStruct((192, 768), F32),
    jax.ShapeDtypeStruct((192, 1536), F32),
]
FEED_OUT_SPECS = [
    pl.BlockSpec((96, 4096), lambda b, s: (b, 0)),
    pl.BlockSpec((96, 4096), lambda b, s: (b, 0)),
    pl.BlockSpec((4, 1, 64, 1536), lambda b, s: (0, b, 0, 0)),
]
FEED_SHAPES = [
    jax.ShapeDtypeStruct((192, 4096), F32),
    jax.ShapeDtypeStruct((192, 4096), F32),
    jax.ShapeDtypeStruct((4, 2, 64, 1536), F32),
]


def unpack_kernel(attention, feed, me, *refs):
    side = pl.program_id(0)
    blocks = [ref[0, 0] for ref in refs[:4]]
    refs = refs[4:]
    if attention:
        unpack_attention(side, [block[:, :1152] for block in blocks], refs[:4])
        refs = refs[4:]
    if feed:
        start = 1152 if attention else 0
        unpack_feed([block[:, start : start + 3072] for block in blocks], refs)


def unpack_call(attention, feed, me, every):
    wide = every.shape[-1]
    specs = [
        pl.BlockSpec((1, 1, 96, wide), lambda b, s, x=x: (lax.rem(x - s[0] + 4, 4), b, 0, 0))
        for x in range(4)
    ]
    out_specs = (ATTENTION_SPECS if attention else []) + (FEED_OUT_SPECS if feed else [])
    shapes = (ATTENTION_SHAPES if attention else []) + (FEED_SHAPES if feed else [])
    out = pl.pallas_call(
        functools.partial(unpack_kernel, attention, feed),
        grid_spec=pltpu.PrefetchScalarGridSpec(
            num_scalar_prefetch=1, grid=(2,), in_specs=specs, out_specs=out_specs
        ),
        out_shape=shapes,
        compiler_params=params(48),
        cost_estimate=cost(1e6, 30e6),
        name="unpack",
    )(me, every, every, every, every)
    if feed:
        out = list(out[:-1]) + [out[-1].reshape(512, 1536)]
    return out


def pack_feed_kernel(where, w_gate, w_up, w_down, out):
    x = where[0]
    for s in range(8):
        cols = pl.ds(pl.multiple_of(512 * s + 128 * x, 128), 128)
        out[:, 128 * s : 128 * (s + 1)] = w_gate[:, cols]
        out[:, 1024 + 128 * s : 1024 + 128 * (s + 1)] = w_up[:, cols]
    out[0:64, 2048:3072] = w_down[:, 0:1024]
    out[64:96, 2048:2560] = w_down[0:32, 1024:1536]
    out[64:96, 2560:3072] = w_down[32:64, 1024:1536]


def pack_feed_call(where, w_gate, w_up, w_down, after=()):
    return pl.pallas_call(
        later(pack_feed_kernel, len(after), 1),
        grid_spec=pltpu.PrefetchScalarGridSpec(
            num_scalar_prefetch=1,
            grid=(1,),
            in_specs=anywhere(after)
            + [
                pl.BlockSpec((96, 4096), lambda b, w: (w[1], 0)),
                pl.BlockSpec((96, 4096), lambda b, w: (w[1], 0)),
                pl.BlockSpec((64, 1536), lambda b, w: (2 * w[0] + w[1], 0)),
            ],
            out_specs=pl.BlockSpec((96, 3072), lambda b, w: (0, 0)),
        ),
        out_shape=jax.ShapeDtypeStruct((96, 3072), BF16),
        compiler_params=params(24),
        cost_estimate=cost(1e3, 24e5),
        name="pack_feed",
    )(where, *after, w_gate, w_up, w_down)


def assemble_kernel(where, *refs):
    pieces, out, sems = refs[:10], refs[10], refs[11]
    z, yhi, core = where[0], where[1], where[2]
    handles = []
    for turn in range(2):
        side = core if turn == 0 else 1 - core
        pair, after, before, first, second = pieces[5 * turn : 5 * turn + 5]
        for step, parts in (
            (0, (pair.at[0], pair.at[1])),
            (1, (after.at[0], after.at[1])),
            (3, (before.at[0], before.at[1])),
            (2, (first.at[0], second.at[0])),
        ):
            for other, part in enumerate(parts):
                high = yhi if other == 0 else 1 - yhi
                place = 4 * lax.rem(z + step, 4) + 2 * high + side
                handles.append(pltpu.make_async_copy(part, out.at[place], sems.at[len(handles)]))
    for handle in handles:
        handle.start()
    for handle in handles:
        handle.wait()


def assemble_call(where, pieces, width):
    return pl.pallas_call(
        assemble_kernel,
        in_specs=[pl.BlockSpec(memory_space=pltpu.SMEM)] + anywhere(pieces),
        out_specs=pl.BlockSpec(memory_space=pl.ANY),
        out_shape=jax.ShapeDtypeStruct((16, 96, width), BF16),
        scratch_shapes=[pltpu.SemaphoreType.DMA((16,))],
        cost_estimate=cost(1e3, 2 * 16 * 96 * width * 2),
        name="assemble",
    )(where, *pieces)


WINDOW = 512
EPSILON = 1e-05
ROPE_BASE = 100000.0

AXES = ("ylo", "x", "core", "z", "yhi")
SIZES = (2, 4, 2, 4, 2)
REP = ("ylo", "x", "core")
SHARD = ("z", "yhi")
SPREAD = ("z", "yhi", "core")

RIGHT = [(i, (i + 1) % 4) for i in range(4)]
LEFT = [(i, (i - 1) % 4) for i in range(4)]
SWAP = [(0, 1), (1, 0)]


def number(ylo, x, core, z, yhi):
    return (((ylo * 4 + x) * 2 + core) * 4 + z) * 2 + yhi


def permutation(place):
    pairs = []
    for ylo in range(2):
        for x in range(4):
            for core in range(2):
                for z in range(4):
                    for yhi in range(2):
                        pairs.append(
                            (number(ylo, x, core, z, yhi), number(ylo, *place(x, core, z, yhi)))
                        )
    return pairs


def inverse(pairs):
    return [(there, here) for here, there in pairs]


LINES = [permutation(lambda x, c, z, h, k=k: ((z + k) % 4, h, x, c)) for k in range(4)]
LINES_LENGTH = permutation(lambda x, c, z, h: (z, h, x, c))
ROWS = permutation(lambda x, c, z, h: (z, c, 2 * h + x // 2, x % 2))


def to_lines(block, z):
    part = block.shape[0] // 4
    out = []
    for k in range(4):
        piece = lax.dynamic_slice_in_dim(block, ((z + k) % 4) * part, part, axis=0)
        out.append(lax.ppermute(piece, AXES, LINES[k]))
    return jnp.concatenate(out, axis=0)


def from_lines(block, z):
    part = block.shape[0] // 4
    out = jnp.zeros_like(block)
    for k in range(4):
        piece = lax.ppermute(block[part * k : part * (k + 1)], AXES, inverse(LINES[k]))
        out = lax.dynamic_update_slice_in_dim(out, piece, ((z + k) % 4) * part, axis=0)
    return out


def ring_gather(block):
    half = block.shape[0] // 2
    from_left = lax.ppermute(block, "x", RIGHT)
    from_right = lax.ppermute(block, "x", LEFT)
    far_first = lax.ppermute(from_left[:half], "x", RIGHT)
    far_second = lax.ppermute(from_right[half:], "x", LEFT)
    return block, from_left, from_right, far_first, far_second


def ring_scatter(own, left, right, far):
    half = far.shape[0] // 2
    first = lax.ppermute(far[:half], "x", RIGHT).astype(F32)
    second = lax.ppermute(far[half:], "x", LEFT).astype(F32)
    right = jnp.concatenate([right[:half] + first, right[half:]], axis=0).astype(BF16)
    left = jnp.concatenate([left[:half], left[half:] + second], axis=0).astype(BF16)
    from_left = lax.ppermute(right, "x", RIGHT).astype(F32)
    from_right = lax.ppermute(left, "x", LEFT).astype(F32)
    return own + from_left + from_right


def rms_norm(values, gain):
    return values * lax.rsqrt(jnp.mean(values * values, axis=-1, keepdims=True) + EPSILON) * gain


def either(index, first, second):
    return jnp.where(index == 0, first, second)


def add_low(mine, came):
    return (mine.astype(F32) + came.astype(F32)).astype(BF16)


def ring_stack(block, axis):
    half = block.shape[0] // 2
    before = lax.ppermute(block, axis, RIGHT)
    after = lax.ppermute(block, axis, LEFT)
    first = lax.ppermute(before[:half], axis, RIGHT)
    second = lax.ppermute(after[half:], axis, LEFT)
    far = jnp.concatenate([first, second], axis=0)
    return jnp.stack([block, after, far, before])


def line_gather(piece, core):
    ring = ring_stack(piece, "x")
    came = lax.ppermute(ring, "core", SWAP)
    return either(core, jnp.stack([ring, came], axis=1), jnp.stack([came, ring], axis=1))


def core_sum(mine, theirs):
    return add_low(mine, lax.ppermute(theirs, "core", SWAP))


def z_sum(line, where, offload):
    if offload:
        return lax.psum_scatter(line, "z", scatter_dimension=0, tiled=True)
    tall = line.reshape((4, 2) + line.shape[1:])

    def step(r):
        return lax.dynamic_index_in_dim(tall, (where["z"] + r) % 4, axis=0, keepdims=False)

    own, after, far, before = step(0), step(1), step(2), step(3)
    first = lax.ppermute(far[:1], "z", RIGHT)
    second = lax.ppermute(far[1:], "z", LEFT)
    after = jnp.concatenate([add_low(after[:1], first), after[1:]])
    before = jnp.concatenate([before[:1], add_low(before[1:], second)])
    from_before = lax.ppermute(after, "z", RIGHT).astype(F32)
    from_after = lax.ppermute(before, "z", LEFT).astype(F32)
    return (own.astype(F32) + from_before + from_after).astype(BF16)


def y_sum(pair, where):
    mine = lax.dynamic_index_in_dim(pair, where["yhi"], axis=0, keepdims=False)
    theirs = lax.dynamic_index_in_dim(pair, 1 - where["yhi"], axis=0, keepdims=False)
    piece = add_low(mine, lax.ppermute(theirs, "yhi", SWAP))
    return add_low(piece, lax.ppermute(piece, "ylo", SWAP))


def out_home(piece):
    moved = lax.ppermute(piece[:, 768:1152], AXES, inverse(ROWS))
    return jnp.concatenate([piece[:, :768], moved, piece[:, 1152:]], axis=1)


def butterfly(values):
    for axis, size in (("core", 2), ("x", 4), ("z", 4), ("yhi", 2), ("ylo", 2)):
        step = 1
        while step < size:
            pairs = [(i, i ^ step) for i in range(size)]
            values = values + lax.ppermute(values, axis, pairs)
            step *= 2
    return values


def norm_back(grad, own_normed, state, gain):
    grad_state, grad_gain = jax.vjp(rms_norm, state, gain)[1](own_normed)
    return grad + grad_state, grad_gain


def body(tokens, lengths, grad_output, *weights):
    stretch, width = tokens.shape[1:]
    x = lax.axis_index("x")
    core = lax.axis_index("core")
    z = lax.axis_index("z")
    yhi = lax.axis_index("yhi")
    where = {"x": x, "core": core, "z": z, "yhi": yhi}
    pair_index = jnp.stack([x, core]).astype(jnp.int32)
    side = core.astype(jnp.int32).reshape(1)

    gains = jnp.stack([weights[0], weights[5], weights[9], weights[14]])
    gains = lax.dynamic_slice_in_dim(gains, core * 96, 96, axis=1).T
    gains = jnp.pad(gains, ((0, 0), (0, 124)))
    def attention_piece(base, extra):
        w_q, w_k, w_v, w_out = weights[base + 1 : base + 5]
        out_block = lax.dynamic_slice(
            w_out, (96 * (x // 2), 384 * (2 * (x % 2) + core)), (96, 384)
        )
        out_block = lax.ppermute(out_block, AXES, ROWS)
        parts = [
            lax.dynamic_slice(w, (core * 96, x * (w.shape[1] // 4)), (96, w.shape[1] // 4))
            for w in (w_q, w_k, w_v)
        ]
        return jnp.concatenate(parts + [out_block] + extra, axis=1)

    attn_one = lax.all_gather(attention_piece(0, [gains]), SPREAD, axis=0, tiled=False)
    gains = attn_one[:, :, 1152:1156].transpose(2, 0, 1).reshape(4, width).astype(F32)

    length = lax.ppermute(lengths, AXES, LINES_LENGTH)
    rows = to_lines(tokens[0], z)
    pieces = ring_gather(rows)
    state = rows.astype(F32)

    feed_one = pack_feed_call(pair_index, *weights[6:9], after=(rows,))
    across = lax.ppermute(feed_one, "yhi", SWAP)
    pair = jnp.stack([feed_one, across])
    before = lax.ppermute(pair, "z", RIGHT)
    ahead = lax.ppermute(pair, "z", LEFT)
    first = lax.ppermute(before[:1], "z", RIGHT)
    second = lax.ppermute(ahead[1:], "z", LEFT)
    feed_parts = [pair, ahead, before, first, second]
    feed_parts += [lax.ppermute(item, "core", SWAP) for item in feed_parts]
    feed_one = assemble_call(jnp.stack([z, yhi, core]).astype(jnp.int32), feed_parts, 3072)

    attn_two = lax.all_gather(attention_piece(9, []), SPREAD, axis=0, tiled=False)
    feed_two = pack_feed_call(pair_index, *weights[15:18], after=(rows,))
    feed_two = lax.all_gather(feed_two, SPREAD, axis=0, tiled=False)
    packed = ((attn_one, feed_one), (attn_two, feed_two))

    here = (2 * z + yhi) * stretch + jnp.arange(stretch, dtype=jnp.int32)
    valid = (here < lengths[0])[:, None]
    grad_rows = to_lines(jnp.where(valid, grad_output[0], 0).astype(BF16), z)
    grad_pieces = ring_gather(grad_rows)
    grad = grad_rows.astype(F32)

    part = stretch // 4

    def member_places(member, side_index):
        block = jnp.arange(4, dtype=jnp.int32)
        inner = jnp.arange(part, dtype=jnp.int32)
        home = (member - block + 4) % 4
        return (
            home[:, None] * (2 * stretch) + side_index * stretch + member * part + inner[None, :]
        ).reshape(-1)

    def line_places(side_index):
        return jnp.concatenate([member_places((x + step) % 4, side_index) for step in (0, 3, 1, 2)])

    places = line_places(core)
    key_places = jnp.concatenate([places, line_places(1 - core)]).reshape(1024, 1)
    half = HEAD_DIM // 2
    freq = ROPE_BASE ** (-jnp.arange(half, dtype=F32) * (2.0 / HEAD_DIM))
    angle = places.astype(F32)[:, None] * freq[None, :]
    cosine, sine = jnp.cos(angle), jnp.sin(angle)
    cosine_t, sine_t = cosine.T, sine.T
    places = places.reshape(1, 512)

    records = []
    for index, window in enumerate((WINDOW, 8 * stretch)):
        attn, feed = packed[index]
        gain_attn, gain_feed = gains[2 * index], gains[2 * index + 1]
        if index == 0:
            queries, own, flat = project_call(
                True, pieces, gain_attn, attn, cosine, sine, after=(across,)
            )
            flats = (flat,)
        else:
            flats = ring_gather(rms_norm(state, gain_attn).astype(BF16))
            queries, own = project_call(False, flats, gain_attn, attn, cosine, sine)
        other = lax.ppermute(own, "core", SWAP)
        line = (queries, own, other, places, key_places)
        after = grad_pieces[3:] if index else (ahead,)
        *partial, mixed, log_total = attend_call(window, length, *line, attn, after=after)
        saved_attn = (state, flats, line, mixed, log_total)
        state = state + ring_scatter(*partial)
        flats = ring_gather(rms_norm(state, gain_feed).astype(BF16))
        after = () if index else (grad_rows,)
        *partial, gate, up, hidden = feed_forward_call(flats, feed, after=after)
        saved_feed = (state, flats, gate, up, hidden)
        state = state + ring_scatter(*partial)
        records.append((saved_attn, saved_feed, window))
    output = from_lines(state.astype(BF16), z)[None]

    results = [None] * 18
    gain_grads = [None] * 4
    zero = jnp.zeros((1,), jnp.int32)
    for index in (1, 0):
        attn, feed = packed[index]
        gain_attn, gain_feed = gains[2 * index], gains[2 * index + 1]
        saved_attn, saved_feed, window = records[index]
        base = 9 * index

        state, flats, gate, up, hidden = saved_feed
        if index == 0:
            grad_pieces = ring_gather(grad.astype(BF16))
        after = () if index else (attn_sum,)
        *partial, low_gate, low_up = feed_backward_call(grad_pieces, feed, gate, up, after=after)
        grad, gain_grads[2 * index + 1] = norm_back(grad, ring_scatter(*partial), state, gain_feed)
        halves = feed_weights_call(side, flats, grad_pieces, low_gate, low_up, hidden)
        feed_sum = core_sum(*halves)

        state, flats, line, mixed, log_total = saved_attn
        grad_pieces = ring_gather(grad.astype(BF16))
        low_queries, pair_own, pair_other = attend_backward_call(
            window,
            length,
            grad_pieces,
            *line,
            attn,
            log_total,
            cosine_t,
            sine_t,
            after=(feed_sum,) if index else (feed_sum, output),
        )
        came = lax.ppermute(pair_other, "core", SWAP)
        *partial, low = unproject_call(low_queries, pair_own, came, cosine, sine, attn)
        grad, gain_grads[2 * index] = norm_back(grad, ring_scatter(*partial), state, gain_attn)
        after = () if index else (second_piece,)
        halves = attend_weights_call(side, flats, grad_pieces, low, mixed, after=after)
        attn_sum = core_sum(*halves)
        feed_pair = z_sum(feed_sum, where, index)
        attn_pair = z_sum(attn_sum, where, index)
        if index:
            piece = y_sum(jnp.concatenate([attn_pair, feed_pair], axis=2), where)
            second_piece = out_home(piece)
            every = lax.all_gather(second_piece, ("x", "core"), axis=0, tiled=False)
            out = unpack_call(True, True, zero, every.reshape(4, 2, 96, -1))
            results[base + 1 : base + 5] = out[:4]
            results[base + 6 : base + 9] = out[4:]
        else:
            every = line_gather(y_sum(feed_pair, where), core)
            place = x.astype(jnp.int32).reshape(1)
            results[base + 6 : base + 9] = unpack_call(False, True, place, every)
            every = line_gather(out_home(y_sum(attn_pair, where)), core)
            results[base + 1 : base + 5] = unpack_call(True, False, place, every)
    gain_sums = butterfly(jnp.stack(gain_grads))
    gain_sums = lax.dynamic_slice_in_dim(gain_sums, (2 * z + yhi) * 192, 192, axis=1)
    for index, slot in enumerate((0, 5, 9, 14)):
        results[slot] = gain_sums[index]
    input_grad = from_lines(grad.astype(BF16), z).astype(F32)[None]
    return (output, input_grad, *results)


def solution(mesh):
    fine = Mesh(mesh.devices.reshape(SIZES), AXES)
    token = P(REP, SHARD, None)
    vector = P(SHARD)
    matrix = P(SHARD, None)
    layer = (vector, matrix, matrix, matrix, matrix, vector, matrix, matrix, matrix)
    return jax.shard_map(
        body,
        mesh=fine,
        in_specs=(token, P(REP), token) + layer + layer,
        out_specs=(token, token) + layer + layer,
        check_vma=False,
    )
```

```python
import functools
import jax
import jax.numpy as jnp
from jax import lax
from jax.experimental import pallas as pl
from jax.experimental.pallas import tpu as pltpu
from jax.sharding import Mesh
from jax.sharding import PartitionSpec as P

F32 = jnp.float32
BF16 = jnp.bfloat16
HEAD_DIM = 96
NEGATIVE = -1e30
MIB = 1 << 20

OFFSETS = (0, 128, 256, 384, 448)
SIZES_OF = (128, 128, 128, 64, 64)


def params(mib, semantics=None):
    return pltpu.CompilerParams(vmem_limit_bytes=mib * MIB, dimension_semantics=semantics)


def cost(flops, nbytes, transcendentals=0):
    return pl.CostEstimate(
        flops=int(flops), bytes_accessed=int(nbytes), transcendentals=int(transcendentals)
    )


def fill(target, refs):
    start = 0
    for ref in refs:
        rows = ref.shape[0]
        target[start : start + rows, :] = ref[...]
        start += rows


def nn(a, b):
    return lax.dot_general(a, b, (((1,), (0,)), ((), ())), preferred_element_type=F32)


def nt(a, b):
    return lax.dot_general(a, b, (((1,), (1,)), ((), ())), preferred_element_type=F32)


def tn(a, b):
    return lax.dot_general(a, b, (((0,), (0,)), ((), ())), preferred_element_type=F32)


def later(kernel, count, lead=0):
    if not count:
        return kernel

    def wrapped(*refs):
        return kernel(*refs[:lead], *refs[lead + count :])

    return wrapped


def anywhere(after):
    return [pl.BlockSpec(memory_space=pl.ANY)] * len(after)


def whole(shape):
    return pl.BlockSpec(shape, lambda *_: (0,) * len(shape))


PIECES = [whole((rows, 1536)) for rows in SIZES_OF]
PARTIAL_SHAPES = [
    jax.ShapeDtypeStruct((128, 1536), F32),
    jax.ShapeDtypeStruct((128, 1536), F32),
    jax.ShapeDtypeStruct((128, 1536), F32),
    jax.ShapeDtypeStruct((128, 1536), BF16),
]
LOW_PARTIAL_SHAPES = PARTIAL_SHAPES[:1] + [jax.ShapeDtypeStruct((128, 1536), BF16)] * 3
PARTIALS = [whole((128, 1536))] * 4


def emit(total, outs):
    for place, out in enumerate(outs):
        out[...] = total[128 * place : 128 * (place + 1), :].astype(out.dtype)


def down_parts(block):
    left = block[:, 0:64, :].reshape(256, 1024)
    right = jnp.concatenate([block[:, 64:96, 0:512], block[:, 64:96, 512:1024]], axis=1)
    return left, right.reshape(256, 512)


def feed_forward_kernel(*refs):
    pieces, (wg, wu, wd), outs = refs[:5], refs[5:8], refs[8:12]
    gate, up, hidden, flat, total = refs[12:]
    step = pl.program_id(0)

    @pl.when(step == 0)
    def _():
        fill(flat, pieces)

    rows = flat[...]
    g = nn(rows, wg[...])
    u = nn(rows, wu[...])
    gate[...] = g
    up[...] = u
    h = (g * jax.nn.sigmoid(g) * u).astype(BF16)
    hidden[...] = h
    left, right = down_parts(wd[...])
    left, right = nn(h, left), nn(h, right)

    @pl.when(step == 0)
    def _():
        total[:, :1024] = left
        total[:, 1024:] = right

    @pl.when(step > 0)
    def _():
        total[:, :1024] += left
        total[:, 1024:] += right

    @pl.when(step == 3)
    def _():
        emit(total, outs)


def feed_specs():
    return [
        pl.BlockSpec((1536, 256), lambda b: (0, b)),
        pl.BlockSpec((1536, 256), lambda b: (0, 4 + b)),
        pl.BlockSpec((4, 96, 1024), lambda b: (b, 0, 2)),
    ]


def column_block(rows):
    return pl.BlockSpec((rows, 256), lambda b: (0, b))


def feed_forward_call(pieces, packed, after=()):
    flat_packed = packed.reshape(1536, -1)
    return pl.pallas_call(
        later(feed_forward_kernel, len(after)),
        grid=(4,),
        in_specs=anywhere(after) + PIECES + feed_specs(),
        out_specs=PARTIALS + [column_block(512)] * 3,
        out_shape=PARTIAL_SHAPES
        + [
            jax.ShapeDtypeStruct((512, 1024), F32),
            jax.ShapeDtypeStruct((512, 1024), F32),
            jax.ShapeDtypeStruct((512, 1024), BF16),
        ],
        scratch_shapes=[pltpu.VMEM((512, 1536), BF16), pltpu.VMEM((512, 1536), F32)],
        compiler_params=params(40),
        cost_estimate=cost(4.9e9, 18e6),
        name="feed_forward",
    )(*after, *pieces, flat_packed, flat_packed, packed)


def feed_backward_kernel(*refs):
    pieces, (wg, wu, wd, gate, up), outs = refs[:5], refs[5:10], refs[10:14]
    low_gate, low_up, flat, total = refs[14:]
    step = pl.program_id(0)

    @pl.when(step == 0)
    def _():
        fill(flat, pieces)

    rows = flat[...]
    left, right = down_parts(wd[...])
    grad = nt(rows[:, :1024], left) + nt(rows[:, 1024:], right)
    g = gate[...]
    s = jax.nn.sigmoid(g)
    a = (grad * up[...] * s * (1.0 + g * (1.0 - s))).astype(BF16)
    b = (grad * (g * s)).astype(BF16)
    low_gate[...] = a
    low_up[...] = b
    part = nt(a, wg[...]) + nt(b, wu[...])

    @pl.when(step == 0)
    def _():
        total[...] = part

    @pl.when(step > 0)
    def _():
        total[...] += part

    @pl.when(step == 3)
    def _():
        emit(total, outs)


def feed_backward_call(pieces, packed, gate, up, after=()):
    flat_packed = packed.reshape(1536, -1)
    return pl.pallas_call(
        later(feed_backward_kernel, len(after)),
        grid=(4,),
        in_specs=anywhere(after) + PIECES + feed_specs() + [column_block(512)] * 2,
        out_specs=PARTIALS + [column_block(512)] * 2,
        out_shape=LOW_PARTIAL_SHAPES + [jax.ShapeDtypeStruct((512, 1024), BF16)] * 2,
        scratch_shapes=[pltpu.VMEM((512, 1536), BF16), pltpu.VMEM((512, 1536), F32)],
        compiler_params=params(40),
        cost_estimate=cost(4.9e9, 20e6),
        name="feed_backward",
    )(*after, *pieces, flat_packed, flat_packed, packed, gate, up)


def store_halves(side, mine, theirs, even, odd, rows, columns):
    @pl.when(side == 0)
    def _():
        mine[:, rows, columns] = even
        theirs[:, rows, columns] = odd

    @pl.when(side != 0)
    def _():
        mine[:, rows, columns] = odd
        theirs[:, rows, columns] = even


def feed_weights_kernel(side_ref, *refs):
    flats, grads = refs[:5], refs[5:10]
    low_gate, low_up, hidden, mine, theirs, flat_t, hidden_t, grad = refs[10:]
    step = pl.program_id(0)
    side = side_ref[0]

    @pl.when(step == 0)
    def _():
        start = 0
        for ref in flats:
            n = ref.shape[0]
            flat_t[:, start : start + n] = ref[...].T
            start += n

    @pl.when(step == 4)
    def _():
        hidden_t[...] = hidden[...].T
        fill(grad, grads)

    def columns(block):
        out = nn(flat_t[...], block).astype(BF16).reshape(8, 192, 256)
        store_halves(
            side, mine, theirs, out[:, :96], out[:, 96:], slice(0, 96), slice(0, 256)
        )

    @pl.when(step < 4)
    def _():
        columns(low_gate[...])

    @pl.when((step >= 4) & (step < 8))
    def _():
        columns(low_up[...])

    for q in range(4):

        @pl.when(step == 8 + q)
        def _():
            top = nn(hidden_t[...], grad[:, 256 * q : 256 * (q + 1)]).astype(BF16)
            top = top.reshape(8, 128, 256)
            store_halves(
                side, mine, theirs, top[:, :64], top[:, 64:], slice(0, 64), slice(0, 256)
            )
            half = 32 * (q // 2)
            some = hidden_t[...].reshape(16, 64, 512)[:, half : half + 32].reshape(512, 512)
            start = 1024 + 256 * (q % 2)
            low = nn(some, grad[:, start : start + 256]).astype(BF16).reshape(8, 64, 256)
            store_halves(
                side, mine, theirs, low[:, :32], low[:, 32:], slice(64, 96), slice(0, 256)
            )


def feed_weights_call(side, flats, grads, low_gate, low_up, hidden):
    block = pl.BlockSpec((8, 96, 256), lambda b, s: (0, 0, b))
    shape = jax.ShapeDtypeStruct((8, 96, 3072), BF16)
    spec = pltpu.PrefetchScalarGridSpec(
        num_scalar_prefetch=1,
        grid=(12,),
        in_specs=PIECES
        + PIECES
        + [
            pl.BlockSpec((512, 256), lambda b, s: (0, jnp.minimum(b, 3))),
            pl.BlockSpec((512, 256), lambda b, s: (0, jnp.clip(b - 4, 0, 3))),
            whole((512, 1024)),
        ],
        out_specs=[block, block],
        scratch_shapes=[
            pltpu.VMEM((1536, 512), BF16),
            pltpu.VMEM((1024, 512), BF16),
            pltpu.VMEM((512, 1536), BF16),
        ],
    )
    return pl.pallas_call(
        feed_weights_kernel,
        grid_spec=spec,
        out_shape=[shape, shape],
        compiler_params=params(40),
        cost_estimate=cost(4.9e9, 18e6),
        name="feed_weights",
    )(side, *flats, *grads, low_gate, low_up, hidden)


def piece_specs(pieces):
    return [whole(item.shape) for item in pieces]


def turn_columns(block, cosine, sine):
    out = []
    for start in range(0, block.shape[1], HEAD_DIM):
        a = block[:, start : start + 48]
        b = block[:, start + 48 : start + HEAD_DIM]
        out.append(a * cosine - b * sine)
        out.append(b * cosine + a * sine)
    return jnp.concatenate(out, axis=1)


def project_kernel(raw, count, *refs):
    pieces, (gain, weight, cosine, sine, queries, pair) = refs[:count], refs[count : count + 6]
    if raw:
        flat = refs[-1]
        start = 0
        for ref in pieces:
            n = ref.shape[0]
            rows = ref[...].astype(F32)
            scale = lax.rsqrt(jnp.mean(rows * rows, axis=-1, keepdims=True) + 1e-05)
            flat[start : start + n, :] = (rows * scale * gain[...]).astype(BF16)
            start += n
    else:
        flat = refs[-1]
        fill(flat, pieces)
    both = nn(flat[...], weight[...])
    cos, sin = cosine[...], sine[...]
    queries[...] = turn_columns(both[:, :384], cos, sin).astype(BF16)
    keys = turn_columns(both[:, 384:576], cos, sin)
    pair[...] = jnp.concatenate([keys, both[:, 576:768]], axis=1).astype(BF16)


def project_call(raw, pieces, gain, packed, cosine, sine, after=()):
    wide = packed.shape[-1]
    shape = jax.ShapeDtypeStruct((512, 384), BF16)
    flat_shape = jax.ShapeDtypeStruct((512, 1536), BF16)
    return pl.pallas_call(
        later(functools.partial(project_kernel, raw, len(pieces)), len(after)),
        grid=(1,),
        in_specs=anywhere(after)
        + piece_specs(pieces)
        + [whole((1, 1536)), projection_spec(), whole((512, 48)), whole((512, 48))],
        out_specs=[whole((512, 384))] * 2 + ([whole((512, 1536))] if raw else []),
        out_shape=[shape, shape] + ([flat_shape] if raw else []),
        scratch_shapes=[] if raw else [pltpu.VMEM((512, 1536), BF16)],
        compiler_params=params(40),
        cost_estimate=cost(1.3e9, 6e6),
        name="project",
    )(*after, *pieces, gain.reshape(1, 1536), packed.reshape(1536, wide), cosine, sine)


def fill_bias(bias, length, places, key_places, window):
    gap = places[...] - key_places[...]
    inside = (key_places[...] < length) & (gap >= 0) & (gap < window)
    bias[...] = jnp.where(inside | (gap == 0), 0.0, NEGATIVE)


def both_rows(own, other, start):
    return jnp.concatenate(
        [own[:, start : start + HEAD_DIM], other[:, start : start + HEAD_DIM]], axis=0
    )


def attend_kernel(window, length, queries, own, other, places, key_places, w_out, *refs):
    outs, (mixed, log_total, total, bias) = refs[:4], refs[4:]
    fill_bias(bias, length[0], places, key_places, window)
    sums = []
    stats = []
    for head in range(4):
        if head % 2 == 0:
            keys = both_rows(own[...], other[...], HEAD_DIM * (head // 2))
            values = both_rows(own[...], other[...], 192 + HEAD_DIM * (head // 2)).T
        query = queries[:, HEAD_DIM * head : HEAD_DIM * (head + 1)]
        scores = nt(keys, query) * HEAD_DIM ** (-0.5) + bias[...]
        peak = jnp.max(scores, axis=0, keepdims=True)
        probs = jnp.exp(scores - peak)
        totals = jnp.sum(probs, axis=0, keepdims=True)
        part = nn(values, probs.astype(BF16)) / totals
        sums.append(part.astype(BF16).astype(F32).T.astype(BF16))
        stats.append(peak + jnp.log(totals))
        for block in range(4):
            cols = slice(384 * block, 384 * (block + 1))
            value = nn(sums[-1], w_out[4 * head + block])
            if head == 0:
                total[:, cols] = value
            else:
                total[:, cols] += value
    mixed[...] = jnp.concatenate(sums, axis=1)
    log_total[...] = jnp.concatenate(stats + stats, axis=0)
    emit(total, outs)


def line_specs():
    return [whole((512, 384))] * 3 + [whole((1, 512)), whole((1024, 1))]


def out_spec():
    return pl.BlockSpec((16, 96, 384), lambda *_: (0, 0, 10))


def projection_spec():
    return pl.BlockSpec((1536, 768), lambda *_: (0, 4))


def attend_call(window, length, queries, own, other, places, key_places, packed, after=()):
    return pl.pallas_call(
        later(functools.partial(attend_kernel, window), len(after)),
        grid=(1,),
        in_specs=anywhere(after)
        + [pl.BlockSpec(memory_space=pltpu.SMEM)] + line_specs() + [out_spec()],
        out_specs=PARTIALS + [whole((512, 384)), whole((8, 512))],
        out_shape=PARTIAL_SHAPES
        + [jax.ShapeDtypeStruct((512, 384), BF16), jax.ShapeDtypeStruct((8, 512), F32)],
        scratch_shapes=[pltpu.VMEM((512, 1536), F32), pltpu.VMEM((1024, 512), F32)],
        compiler_params=params(48),
        cost_estimate=cost(3e9, 6e6, 2e6),
        name="attend",
    )(*after, length, queries, own, other, places, key_places, packed)


def attend_backward_kernel(window, length, *refs):
    pieces, refs = refs[:5], refs[5:]
    queries, own, other, places, key_places, w_out, log_total, cosine, sine = refs[:9]
    low_queries, pair_own, pair_other, grad, bias = refs[9:]
    fill(grad, pieces)
    fill_bias(bias, length[0], places, key_places, window)
    cos, sin = cosine[...], sine[...]
    lows = []
    key_sums = []
    value_sums = []
    for head in range(4):
        if head % 2 == 0:
            keys = both_rows(own[...], other[...], HEAD_DIM * (head // 2))
            values = both_rows(own[...], other[...], 192 + HEAD_DIM * (head // 2))
            keys_t = keys.T
        query = queries[:, HEAD_DIM * head : HEAD_DIM * (head + 1)]
        mixed = nt(grad[:, :384], w_out[4 * head])
        for block in range(1, 4):
            mixed += nt(grad[:, 384 * block : 384 * (block + 1)], w_out[4 * head + block])
        mixed = mixed.astype(BF16)
        scores = nt(keys, query) * HEAD_DIM ** (-0.5) + bias[...]
        probs = jnp.exp(scores - log_total[head : head + 1, :])
        slopes = nt(values, mixed)
        inner = jnp.sum(probs * slopes, axis=0, keepdims=True)
        raw = (probs * (slopes - inner) * HEAD_DIM ** (-0.5)).astype(BF16)
        key_part = nn(raw, query)
        value_part = nn(probs.astype(BF16), mixed)
        if head % 2 == 0:
            key_sums.append(key_part)
            value_sums.append(value_part)
        else:
            key_sums[-1] += key_part
            value_sums[-1] += value_part
        turned = nn(keys_t, raw)
        a, b = turned[:48], turned[48:]
        turned = jnp.concatenate([a * cos + b * sin, b * cos - a * sin], axis=0)
        lows.append(turned.T.astype(BF16))
    low_queries[...] = jnp.concatenate(lows, axis=1)
    both = jnp.concatenate(key_sums + value_sums, axis=1)
    pair_own[...] = both[:512]
    pair_other[...] = both[512:].astype(BF16)


def attend_backward_call(
    window,
    length,
    pieces,
    queries,
    own,
    other,
    places,
    key_places,
    packed,
    log_total,
    cosine,
    sine,
    after=(),
):
    return pl.pallas_call(
        later(functools.partial(attend_backward_kernel, window), len(after)),
        grid=(1,),
        in_specs=anywhere(after)
        + [pl.BlockSpec(memory_space=pltpu.SMEM)]
        + PIECES
        + line_specs()
        + [out_spec(), whole((8, 512)), whole((48, 512)), whole((48, 512))],
        out_specs=[whole((512, 384))] * 3,
        out_shape=[
            jax.ShapeDtypeStruct((512, 384), BF16),
            jax.ShapeDtypeStruct((512, 384), F32),
            jax.ShapeDtypeStruct((512, 384), BF16),
        ],
        scratch_shapes=[pltpu.VMEM((512, 1536), BF16), pltpu.VMEM((1024, 512), F32)],
        compiler_params=params(52),
        cost_estimate=cost(6e9, 6e6, 2e6),
        name="attend_backward",
    )(
        *after,
        length,
        *pieces,
        queries,
        own,
        other,
        places,
        key_places,
        packed,
        log_total,
        cosine,
        sine,
    )


def unproject_kernel(low_queries, pair_own, pair_came, cosine, sine, weight, *refs):
    outs, low = refs[:4], refs[4]
    both = pair_own[...] + pair_came[...].astype(F32)
    keys = turn_columns(both[:, :192], cosine[...], -sine[...])
    rows = jnp.concatenate(
        [low_queries[...], keys.astype(BF16), both[:, 192:].astype(BF16)], axis=1
    )
    low[...] = rows
    emit(nt(rows, weight[...]), outs)


def unproject_call(low_queries, pair_own, pair_came, cosine, sine, packed, after=()):
    wide = packed.shape[-1]
    return pl.pallas_call(
        later(unproject_kernel, len(after)),
        grid=(1,),
        in_specs=anywhere(after)
        + [whole((512, 384))] * 3
        + [whole((512, 48))] * 2
        + [projection_spec()],
        out_specs=PARTIALS + [whole((512, 768))],
        out_shape=LOW_PARTIAL_SHAPES + [jax.ShapeDtypeStruct((512, 768), BF16)],
        compiler_params=params(40),
        cost_estimate=cost(1.3e9, 7e6),
        name="unproject",
    )(*after, low_queries, pair_own, pair_came, cosine, sine, packed.reshape(1536, wide))


def attend_weights_kernel(count, side_ref, *refs):
    flats, grads, (low, mixed) = refs[:count], refs[count : count + 5], refs[count + 5 : count + 7]
    mine, theirs, flat_t, grad = refs[count + 7 :]
    side = side_ref[0]
    start = 0
    for ref in flats:
        n = ref.shape[0]
        flat_t[:, start : start + n] = ref[...].T
        start += n
    fill(grad, grads)
    for block in range(3):
        cols = slice(256 * block, 256 * (block + 1))
        out = nn(flat_t[...], low[:, cols]).astype(BF16).reshape(8, 192, 256)
        store_halves(side, mine, theirs, out[:, :96], out[:, 96:], slice(0, 96), cols)
    mixed_t = mixed[...].T
    for half in range(2):
        out = [
            nn(mixed_t, grad[:, 384 * q : 384 * (q + 1)]).astype(BF16).reshape(4, 96, 384)
            for q in (2 * half, 2 * half + 1)
        ]
        for head in range(4):
            place = slice(2 * head + half, 2 * head + half + 1)
            store_at(side, mine, theirs, out[0][head : head + 1], out[1][head : head + 1], place)


def store_at(side, mine, theirs, even, odd, place):
    cols = slice(768, 1152)

    @pl.when(side == 0)
    def _():
        mine[place, :, cols] = even
        theirs[place, :, cols] = odd

    @pl.when(side != 0)
    def _():
        mine[place, :, cols] = odd
        theirs[place, :, cols] = even


def attend_weights_call(side, flats, grads, low, mixed, after=()):
    shape = jax.ShapeDtypeStruct((8, 96, 1152), BF16)
    return pl.pallas_call(
        later(functools.partial(attend_weights_kernel, len(flats)), len(after)),
        grid=(1,),
        in_specs=anywhere(after)
        + [pl.BlockSpec(memory_space=pltpu.SMEM)]
        + piece_specs(flats)
        + PIECES
        + [whole((512, 768)), whole((512, 384))],
        out_specs=[whole((8, 96, 1152))] * 2,
        out_shape=[shape, shape],
        scratch_shapes=[pltpu.VMEM((1536, 512), BF16), pltpu.VMEM((512, 1536), BF16)],
        compiler_params=params(40),
        cost_estimate=cost(1.9e9, 10e6),
        name="attend_weights",
    )(*after, side, *flats, *grads, low, mixed)


def unpack_attention(side, blocks, refs):
    wq, wk, wv, wo = refs
    for x, block in enumerate(blocks):
        wq[:, 384 * x : 384 * (x + 1)] = block[:, :384].astype(F32)
    wk[...] = jnp.concatenate([block[:, 384:576].astype(F32) for block in blocks], axis=1)
    wv[...] = jnp.concatenate([block[:, 576:768].astype(F32) for block in blocks], axis=1)
    for x, block in enumerate(blocks):
        rows = slice(96 * (x // 2), 96 * (x // 2) + 96)
        for core in range(2):
            start = 384 * (2 * (x % 2) + core)

            @pl.when(side == core)
            def _(rows=rows, start=start, block=block):
                wo[rows, start : start + 384] = block[:, 768:1152].astype(F32)


def unpack_feed(blocks, refs):
    gate, up, down = refs
    for x, block in enumerate(blocks):
        for s in range(8):
            cols = slice(512 * s + 128 * x, 512 * s + 128 * (x + 1))
            gate[:, cols] = block[:, 128 * s : 128 * (s + 1)].astype(F32)
            up[:, cols] = block[:, 1024 + 128 * s : 1024 + 128 * (s + 1)].astype(F32)
        down[x, 0, :, :1024] = block[0:64, 2048:3072].astype(F32)
        down[x, 0, 0:32, 1024:] = block[64:96, 2048:2560].astype(F32)
        down[x, 0, 32:64, 1024:] = block[64:96, 2560:3072].astype(F32)


ATTENTION_SPECS = [
    pl.BlockSpec((96, 1536), lambda b, s: (b, 0)),
    pl.BlockSpec((96, 768), lambda b, s: (b, 0)),
    pl.BlockSpec((96, 768), lambda b, s: (b, 0)),
    pl.BlockSpec((192, 1536), lambda b, s: (0, 0)),
]
ATTENTION_SHAPES = [
    jax.ShapeDtypeStruct((192, 1536), F32),
    jax.ShapeDtypeStruct((192, 768), F32),
    jax.ShapeDtypeStruct((192, 768), F32),
    jax.ShapeDtypeStruct((192, 1536), F32),
]
FEED_OUT_SPECS = [
    pl.BlockSpec((96, 4096), lambda b, s: (b, 0)),
    pl.BlockSpec((96, 4096), lambda b, s: (b, 0)),
    pl.BlockSpec((4, 1, 64, 1536), lambda b, s: (0, b, 0, 0)),
]
FEED_SHAPES = [
    jax.ShapeDtypeStruct((192, 4096), F32),
    jax.ShapeDtypeStruct((192, 4096), F32),
    jax.ShapeDtypeStruct((4, 2, 64, 1536), F32),
]


def unpack_kernel(attention, feed, me, *refs):
    side = pl.program_id(0)
    blocks = [ref[0, 0] for ref in refs[:4]]
    refs = refs[4:]
    if attention:
        start = 3072 if feed else 0
        unpack_attention(side, [block[:, start : start + 1152] for block in blocks], refs[:4])
        refs = refs[4:]
    if feed:
        unpack_feed([block[:, :3072] for block in blocks], refs)


def unpack_call(attention, feed, me, every):
    wide = every.shape[-1]
    specs = [
        pl.BlockSpec((1, 1, 96, wide), lambda b, s, x=x: (lax.rem(x - s[0] + 4, 4), b, 0, 0))
        for x in range(4)
    ]
    out_specs = (ATTENTION_SPECS if attention else []) + (FEED_OUT_SPECS if feed else [])
    shapes = (ATTENTION_SHAPES if attention else []) + (FEED_SHAPES if feed else [])
    out = pl.pallas_call(
        functools.partial(unpack_kernel, attention, feed),
        grid_spec=pltpu.PrefetchScalarGridSpec(
            num_scalar_prefetch=1, grid=(2,), in_specs=specs, out_specs=out_specs
        ),
        out_shape=shapes,
        compiler_params=params(48),
        cost_estimate=cost(1e6, 30e6),
        name="unpack",
    )(me, every, every, every, every)
    if feed:
        out = list(out[:-1]) + [out[-1].reshape(512, 1536)]
    return out


def pack_feed_kernel(where, w_gate, w_up, w_down, out):
    x = where[0]
    for s in range(8):
        cols = pl.ds(pl.multiple_of(512 * s + 128 * x, 128), 128)
        out[:, 128 * s : 128 * (s + 1)] = w_gate[:, cols]
        out[:, 1024 + 128 * s : 1024 + 128 * (s + 1)] = w_up[:, cols]
    out[0:64, 2048:3072] = w_down[:, 0:1024]
    out[64:96, 2048:2560] = w_down[0:32, 1024:1536]
    out[64:96, 2560:3072] = w_down[32:64, 1024:1536]


def pack_feed_call(where, w_gate, w_up, w_down, after=()):
    return pl.pallas_call(
        later(pack_feed_kernel, len(after), 1),
        grid_spec=pltpu.PrefetchScalarGridSpec(
            num_scalar_prefetch=1,
            grid=(1,),
            in_specs=anywhere(after)
            + [
                pl.BlockSpec((96, 4096), lambda b, w: (w[1], 0)),
                pl.BlockSpec((96, 4096), lambda b, w: (w[1], 0)),
                pl.BlockSpec((64, 1536), lambda b, w: (2 * w[0] + w[1], 0)),
            ],
            out_specs=pl.BlockSpec((96, 3072), lambda b, w: (0, 0)),
        ),
        out_shape=jax.ShapeDtypeStruct((96, 3072), BF16),
        compiler_params=params(24),
        cost_estimate=cost(1e3, 24e5),
        name="pack_feed",
    )(where, *after, w_gate, w_up, w_down)


WINDOW = 512
EPSILON = 1e-05
ROPE_BASE = 100000.0

AXES = ("ylo", "x", "core", "z", "yhi")
SIZES = (2, 4, 2, 4, 2)
REP = ("ylo", "x", "core")
SHARD = ("z", "yhi")
SPREAD = ("z", "yhi", "core")

RIGHT = [(i, (i + 1) % 4) for i in range(4)]
LEFT = [(i, (i - 1) % 4) for i in range(4)]
ACROSS = [(i, (i + 2) % 4) for i in range(4)]
SWAP = [(0, 1), (1, 0)]


def number(ylo, x, core, z, yhi):
    return (((ylo * 4 + x) * 2 + core) * 4 + z) * 2 + yhi


def permutation(place):
    pairs = []
    for ylo in range(2):
        for x in range(4):
            for core in range(2):
                for z in range(4):
                    for yhi in range(2):
                        pairs.append(
                            (number(ylo, x, core, z, yhi), number(ylo, *place(x, core, z, yhi)))
                        )
    return pairs


def inverse(pairs):
    return [(there, here) for here, there in pairs]


LINES = [permutation(lambda x, c, z, h, k=k: ((z + k) % 4, h, x, c)) for k in range(4)]
LINES_LENGTH = permutation(lambda x, c, z, h: (z, h, x, c))
ROWS = permutation(lambda x, c, z, h: (z, c, 2 * h + x // 2, x % 2))


def to_lines(block, z):
    part = block.shape[0] // 4
    out = []
    for k in range(4):
        piece = lax.dynamic_slice_in_dim(block, ((z + k) % 4) * part, part, axis=0)
        out.append(lax.ppermute(piece, AXES, LINES[k]))
    return jnp.concatenate(out, axis=0)


def from_lines(block, z):
    part = block.shape[0] // 4
    out = jnp.zeros_like(block)
    for k in range(4):
        piece = lax.ppermute(block[part * k : part * (k + 1)], AXES, inverse(LINES[k]))
        out = lax.dynamic_update_slice_in_dim(out, piece, ((z + k) % 4) * part, axis=0)
    return out


def ring_gather(block):
    half = block.shape[0] // 2
    from_left = lax.ppermute(block, "x", RIGHT)
    from_right = lax.ppermute(block, "x", LEFT)
    far_first = lax.ppermute(from_left[:half], "x", RIGHT)
    far_second = lax.ppermute(from_right[half:], "x", LEFT)
    return block, from_left, from_right, far_first, far_second


def ring_scatter(own, left, right, far):
    half = far.shape[0] // 2
    first = lax.ppermute(far[:half], "x", RIGHT).astype(F32)
    second = lax.ppermute(far[half:], "x", LEFT).astype(F32)
    right = jnp.concatenate([right[:half] + first, right[half:]], axis=0).astype(BF16)
    left = jnp.concatenate([left[:half], left[half:] + second], axis=0).astype(BF16)
    from_left = lax.ppermute(right, "x", RIGHT).astype(F32)
    from_right = lax.ppermute(left, "x", LEFT).astype(F32)
    return own + from_left + from_right


def ring_scatter_direct(own, left, right, far):
    from_left = lax.ppermute(right, "x", RIGHT).astype(F32)
    from_right = lax.ppermute(left, "x", LEFT).astype(F32)
    from_far = lax.ppermute(far, "x", ACROSS).astype(F32)
    return own + from_left + from_right + from_far


def tie(value, *others):
    return lax.optimization_barrier((value, *others))[0]


def rms_norm(values, gain):
    return values * lax.rsqrt(jnp.mean(values * values, axis=-1, keepdims=True) + EPSILON) * gain


def either(index, first, second):
    return jnp.where(index == 0, first, second)


def add_low(mine, came):
    return (mine.astype(F32) + came.astype(F32)).astype(BF16)


def ring_stack(block, axis):
    half = block.shape[0] // 2
    before = lax.ppermute(block, axis, RIGHT)
    after = lax.ppermute(block, axis, LEFT)
    first = lax.ppermute(before[:half], axis, RIGHT)
    second = lax.ppermute(after[half:], axis, LEFT)
    far = jnp.concatenate([first, second], axis=0)
    return jnp.stack([block, after, far, before])


def line_gather(piece, core):
    ring = ring_stack(piece, "x")
    came = lax.ppermute(ring, "core", SWAP)
    return either(core, jnp.stack([ring, came], axis=1), jnp.stack([came, ring], axis=1))


def core_sum(mine, theirs):
    return add_low(mine, lax.ppermute(theirs, "core", SWAP))


def z_sum(line, where, offload):
    if offload:
        return lax.psum_scatter(line, "z", scatter_dimension=0, tiled=True)
    tall = line.reshape((4, 2) + line.shape[1:])

    def step(r):
        return lax.dynamic_index_in_dim(tall, (where["z"] + r) % 4, axis=0, keepdims=False)

    own, after, far, before = step(0), step(1), step(2), step(3)
    first = lax.ppermute(far[:1], "z", RIGHT)
    second = lax.ppermute(far[1:], "z", LEFT)
    after = jnp.concatenate([add_low(after[:1], first), after[1:]])
    before = jnp.concatenate([before[:1], add_low(before[1:], second)])
    from_before = lax.ppermute(after, "z", RIGHT).astype(F32)
    from_after = lax.ppermute(before, "z", LEFT).astype(F32)
    return (own.astype(F32) + from_before + from_after).astype(BF16)


def y_sum(pair, where):
    mine = lax.dynamic_index_in_dim(pair, where["yhi"], axis=0, keepdims=False)
    theirs = lax.dynamic_index_in_dim(pair, 1 - where["yhi"], axis=0, keepdims=False)
    piece = add_low(mine, lax.ppermute(theirs, "yhi", SWAP))
    return add_low(piece, lax.ppermute(piece, "ylo", SWAP))


def out_home(piece, start):
    first, last = start + 768, start + 1152
    moved = lax.ppermute(piece[:, first:last], AXES, inverse(ROWS))
    return jnp.concatenate([piece[:, :first], moved], axis=1)


def butterfly(values):
    for axis, size in (("core", 2), ("x", 4), ("z", 4), ("yhi", 2), ("ylo", 2)):
        step = 1
        while step < size:
            pairs = [(i, i ^ step) for i in range(size)]
            values = values + lax.ppermute(values, axis, pairs)
            step *= 2
    return values


def norm_back(grad, own_normed, state, gain):
    grad_state, grad_gain = jax.vjp(rms_norm, state, gain)[1](own_normed)
    return grad + grad_state, grad_gain


def body(tokens, lengths, grad_output, *weights):
    stretch, width = tokens.shape[1:]
    x = lax.axis_index("x")
    core = lax.axis_index("core")
    z = lax.axis_index("z")
    yhi = lax.axis_index("yhi")
    where = {"x": x, "core": core, "z": z, "yhi": yhi}
    pair_index = jnp.stack([x, core]).astype(jnp.int32)
    side = core.astype(jnp.int32).reshape(1)

    gains = jnp.stack([weights[0], weights[5], weights[9], weights[14]])
    gains = lax.dynamic_slice_in_dim(gains, core * 96, 96, axis=1).T
    gains = jnp.pad(gains, ((0, 0), (0, 124)))
    def line_weights(base, extra, after):
        w_q, w_k, w_v, w_out = weights[base + 1 : base + 5]
        out_block = lax.dynamic_slice(
            w_out, (96 * (x // 2), 384 * (2 * (x % 2) + core)), (96, 384)
        )
        out_block = lax.ppermute(out_block, AXES, ROWS)
        parts = [pack_feed_call(pair_index, *weights[base + 6 : base + 9], after=after)]
        parts += [
            lax.dynamic_slice(w, (core * 96, x * (w.shape[1] // 4)), (96, w.shape[1] // 4))
            for w in (w_q, w_k, w_v)
        ]
        piece = jnp.concatenate(parts + [out_block] + extra, axis=1)
        return lax.all_gather(piece, SPREAD, axis=0, tiled=False)

    first_weights = line_weights(0, [gains], ())
    gains = first_weights[:, :, 4224:4228].transpose(2, 0, 1).reshape(4, width).astype(F32)

    length = lax.ppermute(lengths, AXES, LINES_LENGTH)
    rows = to_lines(tokens[0], z)
    pieces = ring_gather(rows)
    state = rows.astype(F32)
    packed = (first_weights, line_weights(9, [], (rows,)))

    here = (2 * z + yhi) * stretch + jnp.arange(stretch, dtype=jnp.int32)
    valid = (here < lengths[0])[:, None]
    grad_rows = to_lines(jnp.where(valid, grad_output[0], 0).astype(BF16), z)
    grad_pieces = ring_gather(grad_rows)
    grad = grad_rows.astype(F32)

    part = stretch // 4

    def member_places(member, side_index):
        block = jnp.arange(4, dtype=jnp.int32)
        inner = jnp.arange(part, dtype=jnp.int32)
        home = (member - block + 4) % 4
        return (
            home[:, None] * (2 * stretch) + side_index * stretch + member * part + inner[None, :]
        ).reshape(-1)

    def line_places(side_index):
        return jnp.concatenate([member_places((x + step) % 4, side_index) for step in (0, 3, 1, 2)])

    places = line_places(core)
    key_places = jnp.concatenate([places, line_places(1 - core)]).reshape(1024, 1)
    half = HEAD_DIM // 2
    freq = ROPE_BASE ** (-jnp.arange(half, dtype=F32) * (2.0 / HEAD_DIM))
    angle = places.astype(F32)[:, None] * freq[None, :]
    cosine, sine = jnp.cos(angle), jnp.sin(angle)
    cosine_t, sine_t = cosine.T, sine.T
    places = places.reshape(1, 512)

    records = []
    for index, window in enumerate((WINDOW, 8 * stretch)):
        attn = feed = packed[index]
        gain_attn, gain_feed = gains[2 * index], gains[2 * index + 1]
        if index == 0:
            queries, own, flat = project_call(True, pieces, gain_attn, attn, cosine, sine)
            flats = (flat,)
        else:
            flats = ring_gather(rms_norm(state, gain_attn).astype(BF16))
            queries, own = project_call(False, flats, gain_attn, attn, cosine, sine)
        other = lax.ppermute(own, "core", SWAP)
        line = (queries, own, other, places, key_places)
        after = grad_pieces[3:] if index else ()
        *partial, mixed, log_total = attend_call(window, length, *line, attn, after=after)
        saved_attn = (state, flats, line, mixed, log_total)
        state = state + ring_scatter(*partial)
        flats = ring_gather(rms_norm(state, gain_feed).astype(BF16))
        after = () if index else (grad_rows,)
        *partial, gate, up, hidden = feed_forward_call(flats, feed, after=after)
        saved_feed = (state, flats, gate, up, hidden)
        state = state + ring_scatter(*partial)
        records.append((saved_attn, saved_feed, window))
    output = from_lines(state.astype(BF16), z)[None]

    results = [None] * 18
    gain_grads = [None] * 4
    zero = jnp.zeros((1,), jnp.int32)
    for index in (1, 0):
        line_packed = packed[index]
        gain_attn, gain_feed = gains[2 * index], gains[2 * index + 1]
        saved_attn, saved_feed, window = records[index]
        base = 9 * index

        state, flats, gate, up, hidden = saved_feed
        if index == 0:
            grad_pieces = ring_gather(tie(grad.astype(BF16), output))
        after = () if index else (second_feed, second_sum)
        *partial, low_gate, low_up = feed_backward_call(
            grad_pieces, line_packed, gate, up, after=after
        )
        own_normed = ring_scatter_direct(*partial)
        grad, gain_grads[2 * index + 1] = norm_back(grad, own_normed, state, gain_feed)
        halves = feed_weights_call(side, flats, grad_pieces, low_gate, low_up, hidden)
        feed_sum = core_sum(*halves)

        state, flats, line, mixed, log_total = saved_attn
        grad_pieces = ring_gather(grad.astype(BF16))
        low_queries, pair_own, pair_other = attend_backward_call(
            window,
            length,
            grad_pieces,
            *line,
            line_packed,
            log_total,
            cosine_t,
            sine_t,
            after=(feed_sum,) if index else (feed_sum, second_attn),
        )
        came = lax.ppermute(pair_other, "core", SWAP)
        *partial, low = unproject_call(
            low_queries,
            pair_own,
            came,
            cosine,
            sine,
            line_packed,
            after=() if index else (second_piece,),
        )
        own_normed = ring_scatter_direct(*partial)
        grad, gain_grads[2 * index] = norm_back(grad, own_normed, state, gain_attn)
        halves = attend_weights_call(side, flats, grad_pieces, low, mixed)
        attn_sum = core_sum(*halves)
        if index:
            second_sum = attn_sum
            second_feed = z_sum(feed_sum, where, True)
            second_attn = z_sum(attn_sum, where, True)
            piece = y_sum(jnp.concatenate([second_feed, second_attn], axis=2), where)
            second_piece = out_home(piece, 3072)
            every = lax.all_gather(second_piece, ("x", "core"), axis=0, tiled=False)
            out = unpack_call(True, True, zero, every.reshape(4, 2, 96, -1))
            results[base + 1 : base + 5] = out[:4]
            results[base + 6 : base + 9] = out[4:]
        else:
            place = x.astype(jnp.int32).reshape(1)
            every = line_gather(y_sum(z_sum(feed_sum, where, False), where), core)
            results[base + 6 : base + 9] = unpack_call(False, True, place, every)
            piece = y_sum(z_sum(attn_sum, where, False), where)
            every = line_gather(out_home(piece, 0), core)
            results[base + 1 : base + 5] = unpack_call(True, False, place, every)
    gain_sums = butterfly(jnp.stack(gain_grads))
    gain_sums = lax.dynamic_slice_in_dim(gain_sums, (2 * z + yhi) * 192, 192, axis=1)
    for index, slot in enumerate((0, 5, 9, 14)):
        results[slot] = gain_sums[index]
    input_grad = from_lines(grad.astype(BF16), z).astype(F32)[None]
    return (output, input_grad, *results)


def solution(mesh):
    fine = Mesh(mesh.devices.reshape(SIZES), AXES)
    token = P(REP, SHARD, None)
    vector = P(SHARD)
    matrix = P(SHARD, None)
    layer = (vector, matrix, matrix, matrix, matrix, vector, matrix, matrix, matrix)
    return jax.shard_map(
        body,
        mesh=fine,
        in_specs=(token, P(REP), token) + layer + layer,
        out_specs=(token, token) + layer + layer,
        check_vma=False,
    )
```

```python
import functools
import jax
import jax.numpy as jnp
from jax import lax
from jax.experimental import pallas as pl
from jax.experimental.pallas import tpu as pltpu
from jax.sharding import Mesh
from jax.sharding import PartitionSpec as P

F32 = jnp.float32
BF16 = jnp.bfloat16
HEAD_DIM = 96
NEGATIVE = -1e30
MIB = 1 << 20

OFFSETS = (0, 128, 256, 384, 448)
SIZES_OF = (128, 128, 128, 64, 64)


def params(mib, semantics=None):
    return pltpu.CompilerParams(vmem_limit_bytes=mib * MIB, dimension_semantics=semantics)


def cost(flops, nbytes, transcendentals=0):
    return pl.CostEstimate(
        flops=int(flops), bytes_accessed=int(nbytes), transcendentals=int(transcendentals)
    )


def fill(target, refs):
    start = 0
    for ref in refs:
        rows = ref.shape[0]
        target[start : start + rows, :] = ref[...]
        start += rows


def nn(a, b):
    return lax.dot_general(a, b, (((1,), (0,)), ((), ())), preferred_element_type=F32)


def nt(a, b):
    return lax.dot_general(a, b, (((1,), (1,)), ((), ())), preferred_element_type=F32)


def tn(a, b):
    return lax.dot_general(a, b, (((0,), (0,)), ((), ())), preferred_element_type=F32)


def later(kernel, count, lead=0):
    if not count:
        return kernel

    def wrapped(*refs):
        return kernel(*refs[:lead], *refs[lead + count :])

    return wrapped


def anywhere(after):
    return [pl.BlockSpec(memory_space=pl.ANY)] * len(after)


def whole(shape):
    return pl.BlockSpec(shape, lambda *_: (0,) * len(shape))


PIECES = [whole((rows, 1536)) for rows in SIZES_OF]
PARTIAL_SHAPES = [
    jax.ShapeDtypeStruct((128, 1536), F32),
    jax.ShapeDtypeStruct((128, 1536), F32),
    jax.ShapeDtypeStruct((128, 1536), F32),
    jax.ShapeDtypeStruct((128, 1536), BF16),
]
LOW_PARTIAL_SHAPES = PARTIAL_SHAPES[:1] + [jax.ShapeDtypeStruct((128, 1536), BF16)] * 3
PARTIALS = [whole((128, 1536))] * 4


def emit(total, outs):
    for place, out in enumerate(outs):
        out[...] = total[128 * place : 128 * (place + 1), :].astype(out.dtype)


def down_parts(block):
    left = block[:, 0:64, :].reshape(256, 1024)
    right = jnp.concatenate([block[:, 64:96, 0:512], block[:, 64:96, 512:1024]], axis=1)
    return left, right.reshape(256, 512)


def feed_forward_kernel(*refs):
    pieces, (wg, wu, wd), outs = refs[:5], refs[5:8], refs[8:12]
    gate, up, hidden, flat, total = refs[12:]
    step = pl.program_id(0)

    @pl.when(step == 0)
    def _():
        fill(flat, pieces)

    rows = flat[...]
    g = nn(rows, wg[...])
    u = nn(rows, wu[...])
    gate[...] = g
    up[...] = u
    h = (g * jax.nn.sigmoid(g) * u).astype(BF16)
    hidden[...] = h
    left, right = down_parts(wd[...])
    left, right = nn(h, left), nn(h, right)

    @pl.when(step == 0)
    def _():
        total[:, :1024] = left
        total[:, 1024:] = right

    @pl.when(step > 0)
    def _():
        total[:, :1024] += left
        total[:, 1024:] += right

    @pl.when(step == 3)
    def _():
        emit(total, outs)


def feed_specs():
    return [
        pl.BlockSpec((1536, 256), lambda b: (0, b)),
        pl.BlockSpec((1536, 256), lambda b: (0, 4 + b)),
        pl.BlockSpec((4, 96, 1024), lambda b: (b, 0, 2)),
    ]


def column_block(rows):
    return pl.BlockSpec((rows, 256), lambda b: (0, b))


def feed_forward_call(pieces, packed, after=()):
    flat_packed = packed.reshape(1536, -1)
    return pl.pallas_call(
        later(feed_forward_kernel, len(after)),
        grid=(4,),
        in_specs=anywhere(after) + PIECES + feed_specs(),
        out_specs=PARTIALS + [column_block(512)] * 3,
        out_shape=PARTIAL_SHAPES
        + [
            jax.ShapeDtypeStruct((512, 1024), F32),
            jax.ShapeDtypeStruct((512, 1024), F32),
            jax.ShapeDtypeStruct((512, 1024), BF16),
        ],
        scratch_shapes=[pltpu.VMEM((512, 1536), BF16), pltpu.VMEM((512, 1536), F32)],
        compiler_params=params(40),
        cost_estimate=cost(4.9e9, 18e6),
        name="feed_forward",
    )(*after, *pieces, flat_packed, flat_packed, packed)


def feed_backward_kernel(*refs):
    pieces, (wg, wu, wd, gate, up), outs = refs[:5], refs[5:10], refs[10:14]
    low_gate, low_up, flat, total = refs[14:]
    step = pl.program_id(0)

    @pl.when(step == 0)
    def _():
        fill(flat, pieces)

    rows = flat[...]
    left, right = down_parts(wd[...])
    grad = nt(rows[:, :1024], left) + nt(rows[:, 1024:], right)
    g = gate[...]
    s = jax.nn.sigmoid(g)
    a = (grad * up[...] * s * (1.0 + g * (1.0 - s))).astype(BF16)
    b = (grad * (g * s)).astype(BF16)
    low_gate[...] = a
    low_up[...] = b
    part = nt(a, wg[...]) + nt(b, wu[...])

    @pl.when(step == 0)
    def _():
        total[...] = part

    @pl.when(step > 0)
    def _():
        total[...] += part

    @pl.when(step == 3)
    def _():
        emit(total, outs)


def feed_backward_call(pieces, packed, gate, up, after=()):
    flat_packed = packed.reshape(1536, -1)
    return pl.pallas_call(
        later(feed_backward_kernel, len(after)),
        grid=(4,),
        in_specs=anywhere(after) + PIECES + feed_specs() + [column_block(512)] * 2,
        out_specs=PARTIALS + [column_block(512)] * 2,
        out_shape=LOW_PARTIAL_SHAPES + [jax.ShapeDtypeStruct((512, 1024), BF16)] * 2,
        scratch_shapes=[pltpu.VMEM((512, 1536), BF16), pltpu.VMEM((512, 1536), F32)],
        compiler_params=params(40),
        cost_estimate=cost(4.9e9, 20e6),
        name="feed_backward",
    )(*after, *pieces, flat_packed, flat_packed, packed, gate, up)


def store_halves(side, mine, theirs, even, odd, rows, columns):
    @pl.when(side == 0)
    def _():
        mine[:, rows, columns] = even
        theirs[:, rows, columns] = odd

    @pl.when(side != 0)
    def _():
        mine[:, rows, columns] = odd
        theirs[:, rows, columns] = even


def feed_weights_kernel(side_ref, *refs):
    flats, grads = refs[:5], refs[5:10]
    low_gate, low_up, hidden, mine, theirs, flat_t, hidden_t, grad = refs[10:]
    step = pl.program_id(0)
    side = side_ref[0]

    @pl.when(step == 0)
    def _():
        start = 0
        for ref in flats:
            n = ref.shape[0]
            flat_t[:, start : start + n] = ref[...].T
            start += n

    @pl.when(step == 4)
    def _():
        hidden_t[...] = hidden[...].T
        fill(grad, grads)

    def columns(block):
        out = nn(flat_t[...], block).astype(BF16).reshape(8, 192, 256)
        store_halves(
            side, mine, theirs, out[:, :96], out[:, 96:], slice(0, 96), slice(0, 256)
        )

    @pl.when(step < 4)
    def _():
        columns(low_gate[...])

    @pl.when((step >= 4) & (step < 8))
    def _():
        columns(low_up[...])

    for q in range(4):

        @pl.when(step == 8 + q)
        def _():
            top = nn(hidden_t[...], grad[:, 256 * q : 256 * (q + 1)]).astype(BF16)
            top = top.reshape(8, 128, 256)
            store_halves(
                side, mine, theirs, top[:, :64], top[:, 64:], slice(0, 64), slice(0, 256)
            )
            half = 32 * (q // 2)
            some = hidden_t[...].reshape(16, 64, 512)[:, half : half + 32].reshape(512, 512)
            start = 1024 + 256 * (q % 2)
            low = nn(some, grad[:, start : start + 256]).astype(BF16).reshape(8, 64, 256)
            store_halves(
                side, mine, theirs, low[:, :32], low[:, 32:], slice(64, 96), slice(0, 256)
            )


def feed_weights_call(side, flats, grads, low_gate, low_up, hidden):
    block = pl.BlockSpec((8, 96, 256), lambda b, s: (0, 0, b))
    shape = jax.ShapeDtypeStruct((8, 96, 3072), BF16)
    spec = pltpu.PrefetchScalarGridSpec(
        num_scalar_prefetch=1,
        grid=(12,),
        in_specs=PIECES
        + PIECES
        + [
            pl.BlockSpec((512, 256), lambda b, s: (0, jnp.minimum(b, 3))),
            pl.BlockSpec((512, 256), lambda b, s: (0, jnp.clip(b - 4, 0, 3))),
            whole((512, 1024)),
        ],
        out_specs=[block, block],
        scratch_shapes=[
            pltpu.VMEM((1536, 512), BF16),
            pltpu.VMEM((1024, 512), BF16),
            pltpu.VMEM((512, 1536), BF16),
        ],
    )
    return pl.pallas_call(
        feed_weights_kernel,
        grid_spec=spec,
        out_shape=[shape, shape],
        compiler_params=params(40),
        cost_estimate=cost(4.9e9, 18e6),
        name="feed_weights",
    )(side, *flats, *grads, low_gate, low_up, hidden)


def piece_specs(pieces):
    return [whole(item.shape) for item in pieces]


def turn_columns(block, cosine, sine):
    out = []
    for start in range(0, block.shape[1], HEAD_DIM):
        a = block[:, start : start + 48]
        b = block[:, start + 48 : start + HEAD_DIM]
        out.append(a * cosine - b * sine)
        out.append(b * cosine + a * sine)
    return jnp.concatenate(out, axis=1)


def project_kernel(raw, count, *refs):
    pieces, (gain, weight, cosine, sine, queries, pair) = refs[:count], refs[count : count + 6]
    if raw:
        flat = refs[-1]
        start = 0
        for ref in pieces:
            n = ref.shape[0]
            rows = ref[...].astype(F32)
            scale = lax.rsqrt(jnp.mean(rows * rows, axis=-1, keepdims=True) + 1e-05)
            flat[start : start + n, :] = (rows * scale * gain[...]).astype(BF16)
            start += n
    else:
        flat = refs[-1]
        fill(flat, pieces)
    both = nn(flat[...], weight[...])
    cos, sin = cosine[...], sine[...]
    queries[...] = turn_columns(both[:, :384], cos, sin).astype(BF16)
    keys = turn_columns(both[:, 384:576], cos, sin)
    pair[...] = jnp.concatenate([keys, both[:, 576:768]], axis=1).astype(BF16)


def project_call(raw, pieces, gain, packed, cosine, sine, after=()):
    wide = packed.shape[-1]
    shape = jax.ShapeDtypeStruct((512, 384), BF16)
    flat_shape = jax.ShapeDtypeStruct((512, 1536), BF16)
    return pl.pallas_call(
        later(functools.partial(project_kernel, raw, len(pieces)), len(after)),
        grid=(1,),
        in_specs=anywhere(after)
        + piece_specs(pieces)
        + [whole((1, 1536)), projection_spec(), whole((512, 48)), whole((512, 48))],
        out_specs=[whole((512, 384))] * 2 + ([whole((512, 1536))] if raw else []),
        out_shape=[shape, shape] + ([flat_shape] if raw else []),
        scratch_shapes=[] if raw else [pltpu.VMEM((512, 1536), BF16)],
        compiler_params=params(40),
        cost_estimate=cost(1.3e9, 6e6),
        name="project",
    )(*after, *pieces, gain.reshape(1, 1536), packed.reshape(1536, wide), cosine, sine)


def fill_bias(bias, length, places, key_places, window):
    gap = places[...] - key_places[...]
    inside = (key_places[...] < length) & (gap >= 0) & (gap < window)
    bias[...] = jnp.where(inside | (gap == 0), 0.0, NEGATIVE)


def both_rows(own, other, start):
    return jnp.concatenate(
        [own[:, start : start + HEAD_DIM], other[:, start : start + HEAD_DIM]], axis=0
    )


def attend_kernel(window, length, queries, own, other, places, key_places, w_out, *refs):
    outs, (mixed, log_total, total, bias) = refs[:4], refs[4:]
    fill_bias(bias, length[0], places, key_places, window)
    sums = []
    stats = []
    for head in range(4):
        if head % 2 == 0:
            keys = both_rows(own[...], other[...], HEAD_DIM * (head // 2))
            values = both_rows(own[...], other[...], 192 + HEAD_DIM * (head // 2)).T
        query = queries[:, HEAD_DIM * head : HEAD_DIM * (head + 1)]
        scores = nt(keys, query) * HEAD_DIM ** (-0.5) + bias[...]
        peak = jnp.max(scores, axis=0, keepdims=True)
        probs = jnp.exp(scores - peak)
        totals = jnp.sum(probs, axis=0, keepdims=True)
        part = nn(values, probs.astype(BF16)) / totals
        sums.append(part.astype(BF16).astype(F32).T.astype(BF16))
        stats.append(peak + jnp.log(totals))
        for block in range(4):
            cols = slice(384 * block, 384 * (block + 1))
            value = nn(sums[-1], w_out[4 * head + block])
            if head == 0:
                total[:, cols] = value
            else:
                total[:, cols] += value
    mixed[...] = jnp.concatenate(sums, axis=1)
    log_total[...] = jnp.concatenate(stats + stats, axis=0)
    emit(total, outs)


def line_specs():
    return [whole((512, 384))] * 3 + [whole((1, 512)), whole((1024, 1))]


def out_spec():
    return pl.BlockSpec((16, 96, 384), lambda *_: (0, 0, 10))


def projection_spec():
    return pl.BlockSpec((1536, 768), lambda *_: (0, 4))


def attend_call(window, length, queries, own, other, places, key_places, packed, after=()):
    return pl.pallas_call(
        later(functools.partial(attend_kernel, window), len(after)),
        grid=(1,),
        in_specs=anywhere(after)
        + [pl.BlockSpec(memory_space=pltpu.SMEM)] + line_specs() + [out_spec()],
        out_specs=PARTIALS + [whole((512, 384)), whole((8, 512))],
        out_shape=PARTIAL_SHAPES
        + [jax.ShapeDtypeStruct((512, 384), BF16), jax.ShapeDtypeStruct((8, 512), F32)],
        scratch_shapes=[pltpu.VMEM((512, 1536), F32), pltpu.VMEM((1024, 512), F32)],
        compiler_params=params(48),
        cost_estimate=cost(3e9, 6e6, 2e6),
        name="attend",
    )(*after, length, queries, own, other, places, key_places, packed)


def attend_backward_kernel(window, length, *refs):
    pieces, refs = refs[:5], refs[5:]
    queries, own, other, places, key_places, w_out, log_total, cosine, sine = refs[:9]
    low_queries, pair_own, pair_other, grad, bias = refs[9:]
    fill(grad, pieces)
    fill_bias(bias, length[0], places, key_places, window)
    cos, sin = cosine[...], sine[...]
    lows = []
    key_sums = []
    value_sums = []
    for head in range(4):
        if head % 2 == 0:
            keys = both_rows(own[...], other[...], HEAD_DIM * (head // 2))
            values = both_rows(own[...], other[...], 192 + HEAD_DIM * (head // 2))
            keys_t = keys.T
        query = queries[:, HEAD_DIM * head : HEAD_DIM * (head + 1)]
        mixed = nt(grad[:, :384], w_out[4 * head])
        for block in range(1, 4):
            mixed += nt(grad[:, 384 * block : 384 * (block + 1)], w_out[4 * head + block])
        mixed = mixed.astype(BF16)
        scores = nt(keys, query) * HEAD_DIM ** (-0.5) + bias[...]
        probs = jnp.exp(scores - log_total[head : head + 1, :])
        slopes = nt(values, mixed)
        inner = jnp.sum(probs * slopes, axis=0, keepdims=True)
        raw = (probs * (slopes - inner) * HEAD_DIM ** (-0.5)).astype(BF16)
        key_part = nn(raw, query)
        value_part = nn(probs.astype(BF16), mixed)
        if head % 2 == 0:
            key_sums.append(key_part)
            value_sums.append(value_part)
        else:
            key_sums[-1] += key_part
            value_sums[-1] += value_part
        turned = nn(keys_t, raw)
        a, b = turned[:48], turned[48:]
        turned = jnp.concatenate([a * cos + b * sin, b * cos - a * sin], axis=0)
        lows.append(turned.T.astype(BF16))
    low_queries[...] = jnp.concatenate(lows, axis=1)
    both = jnp.concatenate(key_sums + value_sums, axis=1)
    pair_own[...] = both[:512]
    pair_other[...] = both[512:].astype(BF16)


def attend_backward_call(
    window,
    length,
    pieces,
    queries,
    own,
    other,
    places,
    key_places,
    packed,
    log_total,
    cosine,
    sine,
    after=(),
):
    return pl.pallas_call(
        later(functools.partial(attend_backward_kernel, window), len(after)),
        grid=(1,),
        in_specs=anywhere(after)
        + [pl.BlockSpec(memory_space=pltpu.SMEM)]
        + PIECES
        + line_specs()
        + [out_spec(), whole((8, 512)), whole((48, 512)), whole((48, 512))],
        out_specs=[whole((512, 384))] * 3,
        out_shape=[
            jax.ShapeDtypeStruct((512, 384), BF16),
            jax.ShapeDtypeStruct((512, 384), F32),
            jax.ShapeDtypeStruct((512, 384), BF16),
        ],
        scratch_shapes=[pltpu.VMEM((512, 1536), BF16), pltpu.VMEM((1024, 512), F32)],
        compiler_params=params(52),
        cost_estimate=cost(6e9, 6e6, 2e6),
        name="attend_backward",
    )(
        *after,
        length,
        *pieces,
        queries,
        own,
        other,
        places,
        key_places,
        packed,
        log_total,
        cosine,
        sine,
    )


def unproject_kernel(low_queries, pair_own, pair_came, cosine, sine, weight, *refs):
    outs, low = refs[:4], refs[4]
    both = pair_own[...] + pair_came[...].astype(F32)
    keys = turn_columns(both[:, :192], cosine[...], -sine[...])
    rows = jnp.concatenate(
        [low_queries[...], keys.astype(BF16), both[:, 192:].astype(BF16)], axis=1
    )
    low[...] = rows
    emit(nt(rows, weight[...]), outs)


def unproject_call(low_queries, pair_own, pair_came, cosine, sine, packed, after=()):
    wide = packed.shape[-1]
    return pl.pallas_call(
        later(unproject_kernel, len(after)),
        grid=(1,),
        in_specs=anywhere(after)
        + [whole((512, 384))] * 3
        + [whole((512, 48))] * 2
        + [projection_spec()],
        out_specs=PARTIALS + [whole((512, 768))],
        out_shape=LOW_PARTIAL_SHAPES + [jax.ShapeDtypeStruct((512, 768), BF16)],
        compiler_params=params(40),
        cost_estimate=cost(1.3e9, 7e6),
        name="unproject",
    )(*after, low_queries, pair_own, pair_came, cosine, sine, packed.reshape(1536, wide))


def attend_weights_kernel(count, side_ref, *refs):
    flats, grads, (low, mixed) = refs[:count], refs[count : count + 5], refs[count + 5 : count + 7]
    mine, theirs, flat_t, grad = refs[count + 7 :]
    side = side_ref[0]
    start = 0
    for ref in flats:
        n = ref.shape[0]
        flat_t[:, start : start + n] = ref[...].T
        start += n
    fill(grad, grads)
    for block in range(3):
        cols = slice(256 * block, 256 * (block + 1))
        out = nn(flat_t[...], low[:, cols]).astype(BF16).reshape(8, 192, 256)
        store_halves(side, mine, theirs, out[:, :96], out[:, 96:], slice(0, 96), cols)
    mixed_t = mixed[...].T
    for half in range(2):
        out = [
            nn(mixed_t, grad[:, 384 * q : 384 * (q + 1)]).astype(BF16).reshape(4, 96, 384)
            for q in (2 * half, 2 * half + 1)
        ]
        for head in range(4):
            place = slice(2 * head + half, 2 * head + half + 1)
            store_at(side, mine, theirs, out[0][head : head + 1], out[1][head : head + 1], place)


def store_at(side, mine, theirs, even, odd, place):
    cols = slice(768, 1152)

    @pl.when(side == 0)
    def _():
        mine[place, :, cols] = even
        theirs[place, :, cols] = odd

    @pl.when(side != 0)
    def _():
        mine[place, :, cols] = odd
        theirs[place, :, cols] = even


def attend_weights_call(side, flats, grads, low, mixed, after=()):
    shape = jax.ShapeDtypeStruct((8, 96, 1152), BF16)
    return pl.pallas_call(
        later(functools.partial(attend_weights_kernel, len(flats)), len(after)),
        grid=(1,),
        in_specs=anywhere(after)
        + [pl.BlockSpec(memory_space=pltpu.SMEM)]
        + piece_specs(flats)
        + PIECES
        + [whole((512, 768)), whole((512, 384))],
        out_specs=[whole((8, 96, 1152))] * 2,
        out_shape=[shape, shape],
        scratch_shapes=[pltpu.VMEM((1536, 512), BF16), pltpu.VMEM((512, 1536), BF16)],
        compiler_params=params(40),
        cost_estimate=cost(1.9e9, 10e6),
        name="attend_weights",
    )(*after, side, *flats, *grads, low, mixed)


def unpack_attention(side, blocks, refs):
    wq, wk, wv, wo = refs
    for x, block in enumerate(blocks):
        wq[:, 384 * x : 384 * (x + 1)] = block[:, :384].astype(F32)
    wk[...] = jnp.concatenate([block[:, 384:576].astype(F32) for block in blocks], axis=1)
    wv[...] = jnp.concatenate([block[:, 576:768].astype(F32) for block in blocks], axis=1)
    for x, block in enumerate(blocks):
        rows = slice(96 * (x // 2), 96 * (x // 2) + 96)
        for core in range(2):
            start = 384 * (2 * (x % 2) + core)

            @pl.when(side == core)
            def _(rows=rows, start=start, block=block):
                wo[rows, start : start + 384] = block[:, 768:1152].astype(F32)


def unpack_feed(blocks, refs):
    gate, up, down = refs
    for x, block in enumerate(blocks):
        for s in range(8):
            cols = slice(512 * s + 128 * x, 512 * s + 128 * (x + 1))
            gate[:, cols] = block[:, 128 * s : 128 * (s + 1)].astype(F32)
            up[:, cols] = block[:, 1024 + 128 * s : 1024 + 128 * (s + 1)].astype(F32)
        down[x, 0, :, :1024] = block[0:64, 2048:3072].astype(F32)
        down[x, 0, 0:32, 1024:] = block[64:96, 2048:2560].astype(F32)
        down[x, 0, 32:64, 1024:] = block[64:96, 2560:3072].astype(F32)


ATTENTION_SPECS = [
    pl.BlockSpec((96, 1536), lambda b, s: (b, 0)),
    pl.BlockSpec((96, 768), lambda b, s: (b, 0)),
    pl.BlockSpec((96, 768), lambda b, s: (b, 0)),
    pl.BlockSpec((192, 1536), lambda b, s: (0, 0)),
]
ATTENTION_SHAPES = [
    jax.ShapeDtypeStruct((192, 1536), F32),
    jax.ShapeDtypeStruct((192, 768), F32),
    jax.ShapeDtypeStruct((192, 768), F32),
    jax.ShapeDtypeStruct((192, 1536), F32),
]
FEED_OUT_SPECS = [
    pl.BlockSpec((96, 4096), lambda b, s: (b, 0)),
    pl.BlockSpec((96, 4096), lambda b, s: (b, 0)),
    pl.BlockSpec((4, 1, 64, 1536), lambda b, s: (0, b, 0, 0)),
]
FEED_SHAPES = [
    jax.ShapeDtypeStruct((192, 4096), F32),
    jax.ShapeDtypeStruct((192, 4096), F32),
    jax.ShapeDtypeStruct((4, 2, 64, 1536), F32),
]


def unpack_kernel(attention, feed, me, *refs):
    side = pl.program_id(0)
    blocks = [ref[0, 0] for ref in refs[:4]]
    refs = refs[4:]
    if attention:
        start = 3072 if feed else 0
        unpack_attention(side, [block[:, start : start + 1152] for block in blocks], refs[:4])
        refs = refs[4:]
    if feed:
        unpack_feed([block[:, :3072] for block in blocks], refs)


def unpack_call(attention, feed, me, every):
    wide = every.shape[-1]
    specs = [
        pl.BlockSpec((1, 1, 96, wide), lambda b, s, x=x: (lax.rem(x - s[0] + 4, 4), b, 0, 0))
        for x in range(4)
    ]
    out_specs = (ATTENTION_SPECS if attention else []) + (FEED_OUT_SPECS if feed else [])
    shapes = (ATTENTION_SHAPES if attention else []) + (FEED_SHAPES if feed else [])
    out = pl.pallas_call(
        functools.partial(unpack_kernel, attention, feed),
        grid_spec=pltpu.PrefetchScalarGridSpec(
            num_scalar_prefetch=1, grid=(2,), in_specs=specs, out_specs=out_specs
        ),
        out_shape=shapes,
        compiler_params=params(48),
        cost_estimate=cost(1e6, 30e6),
        name="unpack",
    )(me, every, every, every, every)
    if feed:
        out = list(out[:-1]) + [out[-1].reshape(512, 1536)]
    return out


def pack_feed_kernel(where, w_gate, w_up, w_down, out):
    x = where[0]
    for s in range(8):
        cols = pl.ds(pl.multiple_of(512 * s + 128 * x, 128), 128)
        out[:, 128 * s : 128 * (s + 1)] = w_gate[:, cols]
        out[:, 1024 + 128 * s : 1024 + 128 * (s + 1)] = w_up[:, cols]
    out[0:64, 2048:3072] = w_down[:, 0:1024]
    out[64:96, 2048:2560] = w_down[0:32, 1024:1536]
    out[64:96, 2560:3072] = w_down[32:64, 1024:1536]


def pack_feed_call(where, w_gate, w_up, w_down, after=()):
    return pl.pallas_call(
        later(pack_feed_kernel, len(after), 1),
        grid_spec=pltpu.PrefetchScalarGridSpec(
            num_scalar_prefetch=1,
            grid=(1,),
            in_specs=anywhere(after)
            + [
                pl.BlockSpec((96, 4096), lambda b, w: (w[1], 0)),
                pl.BlockSpec((96, 4096), lambda b, w: (w[1], 0)),
                pl.BlockSpec((64, 1536), lambda b, w: (2 * w[0] + w[1], 0)),
            ],
            out_specs=pl.BlockSpec((96, 3072), lambda b, w: (0, 0)),
        ),
        out_shape=jax.ShapeDtypeStruct((96, 3072), BF16),
        compiler_params=params(24),
        cost_estimate=cost(1e3, 24e5),
        name="pack_feed",
    )(where, *after, w_gate, w_up, w_down)


WINDOW = 512
EPSILON = 1e-05
ROPE_BASE = 100000.0

AXES = ("ylo", "x", "core", "z", "yhi")
SIZES = (2, 4, 2, 4, 2)
REP = ("ylo", "x", "core")
SHARD = ("z", "yhi")
SPREAD = ("z", "yhi", "core")

RIGHT = [(i, (i + 1) % 4) for i in range(4)]
LEFT = [(i, (i - 1) % 4) for i in range(4)]
ACROSS = [(i, (i + 2) % 4) for i in range(4)]
SWAP = [(0, 1), (1, 0)]


def number(ylo, x, core, z, yhi):
    return (((ylo * 4 + x) * 2 + core) * 4 + z) * 2 + yhi


def permutation(place):
    pairs = []
    for ylo in range(2):
        for x in range(4):
            for core in range(2):
                for z in range(4):
                    for yhi in range(2):
                        pairs.append(
                            (number(ylo, x, core, z, yhi), number(ylo, *place(x, core, z, yhi)))
                        )
    return pairs


def inverse(pairs):
    return [(there, here) for here, there in pairs]


LINES = [permutation(lambda x, c, z, h, k=k: ((z + k) % 4, h, x, c)) for k in range(4)]
LINES_LENGTH = permutation(lambda x, c, z, h: (z, h, x, c))
ROWS = permutation(lambda x, c, z, h: (z, c, 2 * h + x // 2, x % 2))


def to_lines(block, z):
    part = block.shape[0] // 4
    out = []
    for k in range(4):
        piece = lax.dynamic_slice_in_dim(block, ((z + k) % 4) * part, part, axis=0)
        out.append(lax.ppermute(piece, AXES, LINES[k]))
    return jnp.concatenate(out, axis=0)


def from_lines(block, z):
    part = block.shape[0] // 4
    out = jnp.zeros_like(block)
    for k in range(4):
        piece = lax.ppermute(block[part * k : part * (k + 1)], AXES, inverse(LINES[k]))
        out = lax.dynamic_update_slice_in_dim(out, piece, ((z + k) % 4) * part, axis=0)
    return out


def ring_gather(block):
    half = block.shape[0] // 2
    from_left = lax.ppermute(block, "x", RIGHT)
    from_right = lax.ppermute(block, "x", LEFT)
    far_first = lax.ppermute(from_left[:half], "x", RIGHT)
    far_second = lax.ppermute(from_right[half:], "x", LEFT)
    return block, from_left, from_right, far_first, far_second


def ring_scatter(own, left, right, far):
    half = far.shape[0] // 2
    first = lax.ppermute(far[:half], "x", RIGHT).astype(F32)
    second = lax.ppermute(far[half:], "x", LEFT).astype(F32)
    right = jnp.concatenate([right[:half] + first, right[half:]], axis=0).astype(BF16)
    left = jnp.concatenate([left[:half], left[half:] + second], axis=0).astype(BF16)
    from_left = lax.ppermute(right, "x", RIGHT).astype(F32)
    from_right = lax.ppermute(left, "x", LEFT).astype(F32)
    return own + from_left + from_right


def ring_scatter_direct(own, left, right, far):
    from_left = lax.ppermute(right, "x", RIGHT).astype(F32)
    from_right = lax.ppermute(left, "x", LEFT).astype(F32)
    from_far = lax.ppermute(far, "x", ACROSS).astype(F32)
    return own + from_left + from_right + from_far


def tie(value, *others):
    return lax.optimization_barrier((value, *others))[0]


def rms_norm(values, gain):
    return values * lax.rsqrt(jnp.mean(values * values, axis=-1, keepdims=True) + EPSILON) * gain


def either(index, first, second):
    return jnp.where(index == 0, first, second)


def add_low(mine, came):
    return (mine.astype(F32) + came.astype(F32)).astype(BF16)


def ring_stack(block, axis):
    half = block.shape[0] // 2
    before = lax.ppermute(block, axis, RIGHT)
    after = lax.ppermute(block, axis, LEFT)
    first = lax.ppermute(before[:half], axis, RIGHT)
    second = lax.ppermute(after[half:], axis, LEFT)
    far = jnp.concatenate([first, second], axis=0)
    return jnp.stack([block, after, far, before])


def line_gather(piece, core):
    ring = ring_stack(piece, "x")
    came = lax.ppermute(ring, "core", SWAP)
    return either(core, jnp.stack([ring, came], axis=1), jnp.stack([came, ring], axis=1))


def core_sum(mine, theirs):
    return add_low(mine, lax.ppermute(theirs, "core", SWAP))


def z_sum(line, where, offload):
    if offload:
        return lax.psum_scatter(line, "z", scatter_dimension=0, tiled=True)
    tall = line.reshape((4, 2) + line.shape[1:])

    def step(r):
        return lax.dynamic_index_in_dim(tall, (where["z"] + r) % 4, axis=0, keepdims=False)

    own, after, far, before = step(0), step(1), step(2), step(3)
    first = lax.ppermute(far[:1], "z", RIGHT)
    second = lax.ppermute(far[1:], "z", LEFT)
    after = jnp.concatenate([add_low(after[:1], first), after[1:]])
    before = jnp.concatenate([before[:1], add_low(before[1:], second)])
    from_before = lax.ppermute(after, "z", RIGHT).astype(F32)
    from_after = lax.ppermute(before, "z", LEFT).astype(F32)
    return (own.astype(F32) + from_before + from_after).astype(BF16)


def yhi_sum(pair, where):
    mine = lax.dynamic_index_in_dim(pair, where["yhi"], axis=0, keepdims=False)
    theirs = lax.dynamic_index_in_dim(pair, 1 - where["yhi"], axis=0, keepdims=False)
    return add_low(mine, lax.ppermute(theirs, "yhi", SWAP))


def ylo_sum(piece):
    return add_low(piece, lax.ppermute(piece, "ylo", SWAP))


def y_sum(pair, where):
    return ylo_sum(yhi_sum(pair, where))


def out_home(piece, start):
    first, last = start + 768, start + 1152
    moved = lax.ppermute(piece[:, first:last], AXES, inverse(ROWS))
    return jnp.concatenate([piece[:, :first], moved, piece[:, last:]], axis=1)


def gain_halves(grads, core):
    tall = grads.astype(BF16).T.reshape(8, 2, 96, 4)
    tall = jnp.pad(tall, ((0, 0), (0, 0), (0, 0), (0, 124)))
    return either(core, tall[:, 0], tall[:, 1]), either(core, tall[:, 1], tall[:, 0])


def norm_back(grad, own_normed, state, gain):
    grad_state, grad_gain = jax.vjp(rms_norm, state, gain)[1](own_normed)
    return grad + grad_state, grad_gain


def body(tokens, lengths, grad_output, *weights):
    stretch, width = tokens.shape[1:]
    x = lax.axis_index("x")
    core = lax.axis_index("core")
    z = lax.axis_index("z")
    yhi = lax.axis_index("yhi")
    where = {"x": x, "core": core, "z": z, "yhi": yhi}
    pair_index = jnp.stack([x, core]).astype(jnp.int32)
    side = core.astype(jnp.int32).reshape(1)

    gains = jnp.stack([weights[0], weights[5], weights[9], weights[14]])
    gains = lax.dynamic_slice_in_dim(gains, core * 96, 96, axis=1).T
    gains = jnp.pad(gains, ((0, 0), (0, 124)))
    def line_weights(base, extra, after):
        w_q, w_k, w_v, w_out = weights[base + 1 : base + 5]
        out_block = lax.dynamic_slice(
            w_out, (96 * (x // 2), 384 * (2 * (x % 2) + core)), (96, 384)
        )
        out_block = lax.ppermute(out_block, AXES, ROWS)
        parts = [pack_feed_call(pair_index, *weights[base + 6 : base + 9], after=after)]
        parts += [
            lax.dynamic_slice(w, (core * 96, x * (w.shape[1] // 4)), (96, w.shape[1] // 4))
            for w in (w_q, w_k, w_v)
        ]
        piece = jnp.concatenate(parts + [out_block] + extra, axis=1)
        return lax.all_gather(piece, SPREAD, axis=0, tiled=False)

    first_weights = line_weights(0, [gains], ())
    gains = first_weights[:, :, 4224:4228].transpose(2, 0, 1).reshape(4, width).astype(F32)

    length = lax.ppermute(lengths, AXES, LINES_LENGTH)
    rows = to_lines(tokens[0], z)
    pieces = ring_gather(rows)
    state = rows.astype(F32)
    packed = (first_weights, line_weights(9, [], (rows,)))

    here = (2 * z + yhi) * stretch + jnp.arange(stretch, dtype=jnp.int32)
    valid = (here < lengths[0])[:, None]
    grad_rows = to_lines(jnp.where(valid, grad_output[0], 0).astype(BF16), z)
    grad_pieces = ring_gather(grad_rows)
    grad = grad_rows.astype(F32)

    part = stretch // 4

    def member_places(member, side_index):
        block = jnp.arange(4, dtype=jnp.int32)
        inner = jnp.arange(part, dtype=jnp.int32)
        home = (member - block + 4) % 4
        return (
            home[:, None] * (2 * stretch) + side_index * stretch + member * part + inner[None, :]
        ).reshape(-1)

    def line_places(side_index):
        return jnp.concatenate([member_places((x + step) % 4, side_index) for step in (0, 3, 1, 2)])

    places = line_places(core)
    key_places = jnp.concatenate([places, line_places(1 - core)]).reshape(1024, 1)
    half = HEAD_DIM // 2
    freq = ROPE_BASE ** (-jnp.arange(half, dtype=F32) * (2.0 / HEAD_DIM))
    angle = places.astype(F32)[:, None] * freq[None, :]
    cosine, sine = jnp.cos(angle), jnp.sin(angle)
    cosine_t, sine_t = cosine.T, sine.T
    places = places.reshape(1, 512)

    records = []
    for index, window in enumerate((WINDOW, 8 * stretch)):
        attn = feed = packed[index]
        gain_attn, gain_feed = gains[2 * index], gains[2 * index + 1]
        if index == 0:
            queries, own, flat = project_call(True, pieces, gain_attn, attn, cosine, sine)
            flats = (flat,)
        else:
            flats = ring_gather(rms_norm(state, gain_attn).astype(BF16))
            queries, own = project_call(False, flats, gain_attn, attn, cosine, sine)
        other = lax.ppermute(own, "core", SWAP)
        line = (queries, own, other, places, key_places)
        after = grad_pieces[3:] if index else ()
        *partial, mixed, log_total = attend_call(window, length, *line, attn, after=after)
        saved_attn = (state, flats, line, mixed, log_total)
        state = state + ring_scatter(*partial)
        flats = ring_gather(rms_norm(state, gain_feed).astype(BF16))
        after = () if index else (grad_rows,)
        *partial, gate, up, hidden = feed_forward_call(flats, feed, after=after)
        saved_feed = (state, flats, gate, up, hidden)
        state = state + ring_scatter(*partial)
        records.append((saved_attn, saved_feed, window))
    last_rows = state.astype(BF16)

    results = [None] * 18
    gain_grads = [None] * 4
    zero = jnp.zeros((1,), jnp.int32)
    place = x.astype(jnp.int32).reshape(1)

    def feed_back(index, grad, pieces, after):
        state, flats, gate, up, hidden = records[index][1]
        *partial, low_gate, low_up = feed_backward_call(
            pieces, packed[index], gate, up, after=after
        )
        own_normed = ring_scatter_direct(*partial)
        grad, gain_grads[2 * index + 1] = norm_back(
            grad, own_normed, state, gains[2 * index + 1]
        )
        return grad, feed_weights_call(side, flats, pieces, low_gate, low_up, hidden)

    def attention_back(index, grad, pieces, after):
        state, flats, line, mixed, log_total = records[index][0]
        window = records[index][2]
        low_queries, pair_own, pair_other = attend_backward_call(
            window, length, pieces, *line, packed[index], log_total, cosine_t, sine_t, after=after
        )
        came = lax.ppermute(pair_other, "core", SWAP)
        *partial, low = unproject_call(low_queries, pair_own, came, cosine, sine, packed[index])
        own_normed = ring_scatter_direct(*partial)
        grad, gain_grads[2 * index] = norm_back(grad, own_normed, state, gains[2 * index])
        return grad, attend_weights_call(side, flats, pieces, low, mixed)

    def swap_after(halves, *others):
        return halves[0], tie(halves[1], *others)

    grad, halves = feed_back(1, grad, grad_pieces, ())
    low = grad.astype(BF16)
    feed_sum = core_sum(*swap_after(halves, low))
    grad, halves = attention_back(1, grad, ring_gather(low), (feed_sum, last_rows))
    low = grad.astype(BF16)
    attn_sum = core_sum(*swap_after(halves, low))
    both_sum = jnp.concatenate([feed_sum, attn_sum], axis=2)

    grad, halves = feed_back(0, grad, ring_gather(low), (both_sum,))
    second_pair = z_sum(both_sum, where, True)
    low = grad.astype(BF16)
    feed_sum = core_sum(*swap_after(halves, low))
    grad, halves = attention_back(0, grad, ring_gather(low), (feed_sum,))
    attn_sum = core_sum(*halves)
    gain_sum = core_sum(*gain_halves(jnp.stack(gain_grads), core))
    feed_pair = z_sum(feed_sum, where, False)
    output = from_lines(tie(last_rows, feed_pair), z)[None]

    second_piece = out_home(y_sum(tie(second_pair, halves[0]), where), 3072)
    every = lax.all_gather(second_piece, ("x", "core"), axis=0, tiled=False)
    out = unpack_call(True, True, zero, every.reshape(4, 2, 96, -1))
    results[10:14] = out[:4]
    results[15:18] = out[4:]

    every = line_gather(y_sum(feed_pair, where), core)
    results[6:9] = unpack_call(False, True, place, every)
    attn_sum = jnp.concatenate([attn_sum, gain_sum], axis=2)
    piece = y_sum(z_sum(attn_sum, where, False), where)
    every = line_gather(out_home(piece, 0), core)
    results[1:5] = unpack_call(True, False, place, every)
    gain_sums = every[..., 1152:1156].astype(F32).sum(axis=0).reshape(192, 4).T
    input_grad = from_lines(grad.astype(BF16), z).astype(F32)[None]
    for index, slot in enumerate((0, 5, 9, 14)):
        results[slot] = gain_sums[index]
    return (output, input_grad, *results)


def solution(mesh):
    fine = Mesh(mesh.devices.reshape(SIZES), AXES)
    token = P(REP, SHARD, None)
    vector = P(SHARD)
    matrix = P(SHARD, None)
    layer = (vector, matrix, matrix, matrix, matrix, vector, matrix, matrix, matrix)
    return jax.shard_map(
        body,
        mesh=fine,
        in_specs=(token, P(REP), token) + layer + layer,
        out_specs=(token, token) + layer + layer,
        check_vma=False,
    )
```

```python
import functools
import jax
import jax.numpy as jnp
from jax import lax
from jax.experimental import pallas as pl
from jax.experimental.pallas import tpu as pltpu
from jax.sharding import Mesh
from jax.sharding import PartitionSpec as P

F32 = jnp.float32
BF16 = jnp.bfloat16
HEAD_DIM = 96
NEGATIVE = -1e30
MIB = 1 << 20

OFFSETS = (0, 128, 256, 384, 448)
SIZES_OF = (128, 128, 128, 64, 64)


def params(mib, semantics=None):
    return pltpu.CompilerParams(vmem_limit_bytes=mib * MIB, dimension_semantics=semantics)


def cost(flops, nbytes, transcendentals=0):
    return pl.CostEstimate(
        flops=int(flops), bytes_accessed=int(nbytes), transcendentals=int(transcendentals)
    )


def fill(target, refs):
    start = 0
    for ref in refs:
        rows = ref.shape[0]
        target[start : start + rows, :] = ref[...]
        start += rows


def nn(a, b):
    return lax.dot_general(a, b, (((1,), (0,)), ((), ())), preferred_element_type=F32)


def nt(a, b):
    return lax.dot_general(a, b, (((1,), (1,)), ((), ())), preferred_element_type=F32)


def tn(a, b):
    return lax.dot_general(a, b, (((0,), (0,)), ((), ())), preferred_element_type=F32)


def later(kernel, count, lead=0):
    if not count:
        return kernel

    def wrapped(*refs):
        return kernel(*refs[:lead], *refs[lead + count :])

    return wrapped


def anywhere(after):
    return [pl.BlockSpec(memory_space=pl.ANY)] * len(after)


def whole(shape):
    return pl.BlockSpec(shape, lambda *_: (0,) * len(shape))


PIECES = [whole((rows, 1536)) for rows in SIZES_OF]
PARTIAL_SHAPES = [
    jax.ShapeDtypeStruct((128, 1536), F32),
    jax.ShapeDtypeStruct((128, 1536), F32),
    jax.ShapeDtypeStruct((128, 1536), F32),
    jax.ShapeDtypeStruct((128, 1536), BF16),
]
LOW_PARTIAL_SHAPES = PARTIAL_SHAPES[:1] + [jax.ShapeDtypeStruct((128, 1536), BF16)] * 3
PARTIALS = [whole((128, 1536))] * 4


def emit(total, outs):
    for place, out in enumerate(outs):
        out[...] = total[128 * place : 128 * (place + 1), :].astype(out.dtype)


def down_parts(block):
    left = block[:, 0:128, :].reshape(256, 1024)
    right = jnp.concatenate([block[:, 128:192, 0:512], block[:, 128:192, 512:1024]], axis=1)
    return left, right.reshape(256, 512)


def feed_forward_kernel(*refs):
    pieces, (wg, wu, wd), outs = refs[:5], refs[5:8], refs[8:12]
    gate, up, hidden, flat, total = refs[12:]
    step = pl.program_id(0)

    @pl.when(step == 0)
    def _():
        fill(flat, pieces)

    rows = flat[...]
    g = nn(rows, wg[...])
    u = nn(rows, wu[...])
    gate[...] = g
    up[...] = u
    h = (g * jax.nn.sigmoid(g) * u).astype(BF16)
    hidden[...] = h
    left, right = down_parts(wd[...])
    left, right = nn(h, left), nn(h, right)

    @pl.when(step == 0)
    def _():
        total[:, :1024] = left
        total[:, 1024:] = right

    @pl.when(step > 0)
    def _():
        total[:, :1024] += left
        total[:, 1024:] += right

    @pl.when(step == 3)
    def _():
        emit(total, outs)


def feed_specs():
    return [
        pl.BlockSpec((1536, 256), lambda b: (0, b)),
        pl.BlockSpec((1536, 256), lambda b: (0, 4 + b)),
        pl.BlockSpec((2, 192, 1024), lambda b: (b, 0, 2)),
    ]


def column_block(rows):
    return pl.BlockSpec((rows, 256), lambda b: (0, b))


def feed_forward_call(pieces, packed, after=()):
    flat_packed = packed.reshape(1536, -1)
    return pl.pallas_call(
        later(feed_forward_kernel, len(after)),
        grid=(4,),
        in_specs=anywhere(after) + PIECES + feed_specs(),
        out_specs=PARTIALS + [column_block(512)] * 3,
        out_shape=PARTIAL_SHAPES
        + [
            jax.ShapeDtypeStruct((512, 1024), F32),
            jax.ShapeDtypeStruct((512, 1024), F32),
            jax.ShapeDtypeStruct((512, 1024), BF16),
        ],
        scratch_shapes=[pltpu.VMEM((512, 1536), BF16), pltpu.VMEM((512, 1536), F32)],
        compiler_params=params(40),
        cost_estimate=cost(4.9e9, 18e6),
        name="feed_forward",
    )(*after, *pieces, flat_packed, flat_packed, packed)


def feed_backward_kernel(*refs):
    pieces, (wg, wu, wd, gate, up), outs = refs[:5], refs[5:10], refs[10:14]
    low_gate, low_up, flat, total = refs[14:]
    step = pl.program_id(0)

    @pl.when(step == 0)
    def _():
        fill(flat, pieces)

    rows = flat[...]
    left, right = down_parts(wd[...])
    grad = nt(rows[:, :1024], left) + nt(rows[:, 1024:], right)
    g = gate[...]
    s = jax.nn.sigmoid(g)
    a = (grad * up[...] * s * (1.0 + g * (1.0 - s))).astype(BF16)
    b = (grad * (g * s)).astype(BF16)
    low_gate[...] = a
    low_up[...] = b
    part = nt(a, wg[...]) + nt(b, wu[...])

    @pl.when(step == 0)
    def _():
        total[...] = part

    @pl.when(step > 0)
    def _():
        total[...] += part

    @pl.when(step == 3)
    def _():
        emit(total, outs)


def feed_backward_call(pieces, packed, gate, up, after=()):
    flat_packed = packed.reshape(1536, -1)
    return pl.pallas_call(
        later(feed_backward_kernel, len(after)),
        grid=(4,),
        in_specs=anywhere(after) + PIECES + feed_specs() + [column_block(512)] * 2,
        out_specs=PARTIALS + [column_block(512)] * 2,
        out_shape=LOW_PARTIAL_SHAPES + [jax.ShapeDtypeStruct((512, 1024), BF16)] * 2,
        scratch_shapes=[pltpu.VMEM((512, 1536), BF16), pltpu.VMEM((512, 1536), F32)],
        compiler_params=params(40),
        cost_estimate=cost(4.9e9, 20e6),
        name="feed_backward",
    )(*after, *pieces, flat_packed, flat_packed, packed, gate, up)


def feed_weights_kernel(*refs):
    flats, grads = refs[:5], refs[5:10]
    low_gate, low_up, hidden, out, flat_t, hidden_t, grad = refs[10:]
    step = pl.program_id(0)

    @pl.when(step == 0)
    def _():
        start = 0
        for ref in flats:
            n = ref.shape[0]
            flat_t[:, start : start + n] = ref[...].T
            start += n

    @pl.when(step == 4)
    def _():
        hidden_t[...] = hidden[...].T
        fill(grad, grads)

    @pl.when(step < 4)
    def _():
        out[...] = nn(flat_t[...], low_gate[...]).astype(BF16).reshape(8, 192, 256)

    @pl.when((step >= 4) & (step < 8))
    def _():
        out[...] = nn(flat_t[...], low_up[...]).astype(BF16).reshape(8, 192, 256)

    for q in range(4):

        @pl.when(step == 8 + q)
        def _():
            top = nn(hidden_t[...], grad[:, 256 * q : 256 * (q + 1)]).astype(BF16)
            out[:, 0:128, :] = top.reshape(8, 128, 256)
            half = 64 * (q // 2)
            some = hidden_t[...].reshape(8, 128, 512)[:, half : half + 64].reshape(512, 512)
            start = 1024 + 256 * (q % 2)
            low = nn(some, grad[:, start : start + 256]).astype(BF16)
            out[:, 128:192, :] = low.reshape(8, 64, 256)


def feed_weights_call(flats, grads, low_gate, low_up, hidden):
    return pl.pallas_call(
        feed_weights_kernel,
        grid=(12,),
        in_specs=PIECES
        + PIECES
        + [
            pl.BlockSpec((512, 256), lambda b: (0, jnp.minimum(b, 3))),
            pl.BlockSpec((512, 256), lambda b: (0, jnp.clip(b - 4, 0, 3))),
            whole((512, 1024)),
        ],
        out_specs=pl.BlockSpec((8, 192, 256), lambda b: (0, 0, b)),
        out_shape=jax.ShapeDtypeStruct((8, 192, 3072), BF16),
        scratch_shapes=[
            pltpu.VMEM((1536, 512), BF16),
            pltpu.VMEM((1024, 512), BF16),
            pltpu.VMEM((512, 1536), BF16),
        ],
        compiler_params=params(40),
        cost_estimate=cost(4.9e9, 18e6),
        name="feed_weights",
    )(*flats, *grads, low_gate, low_up, hidden)


def piece_specs(pieces):
    return [whole(item.shape) for item in pieces]


def turn_columns(block, cosine, sine):
    out = []
    for start in range(0, block.shape[1], HEAD_DIM):
        a = block[:, start : start + 48]
        b = block[:, start + 48 : start + HEAD_DIM]
        out.append(a * cosine - b * sine)
        out.append(b * cosine + a * sine)
    return jnp.concatenate(out, axis=1)


def project_kernel(raw, count, *refs):
    pieces, (gain, weight, cosine, sine, queries, pair) = refs[:count], refs[count : count + 6]
    if raw:
        flat = refs[-1]
        start = 0
        for ref in pieces:
            n = ref.shape[0]
            rows = ref[...].astype(F32)
            scale = lax.rsqrt(jnp.mean(rows * rows, axis=-1, keepdims=True) + 1e-05)
            flat[start : start + n, :] = (rows * scale * gain[...]).astype(BF16)
            start += n
    else:
        flat = refs[-1]
        fill(flat, pieces)
    both = nn(flat[...], weight[...])
    cos, sin = cosine[...], sine[...]
    queries[...] = turn_columns(both[:, :384], cos, sin).astype(BF16)
    keys = turn_columns(both[:, 384:576], cos, sin)
    pair[...] = jnp.concatenate([keys, both[:, 576:768]], axis=1).astype(BF16)


def project_call(raw, pieces, gain, packed, cosine, sine, after=()):
    wide = packed.shape[-1]
    shape = jax.ShapeDtypeStruct((512, 384), BF16)
    flat_shape = jax.ShapeDtypeStruct((512, 1536), BF16)
    return pl.pallas_call(
        later(functools.partial(project_kernel, raw, len(pieces)), len(after)),
        grid=(1,),
        in_specs=anywhere(after)
        + piece_specs(pieces)
        + [whole((1, 1536)), projection_spec(), whole((512, 48)), whole((512, 48))],
        out_specs=[whole((512, 384))] * 2 + ([whole((512, 1536))] if raw else []),
        out_shape=[shape, shape] + ([flat_shape] if raw else []),
        scratch_shapes=[] if raw else [pltpu.VMEM((512, 1536), BF16)],
        compiler_params=params(40),
        cost_estimate=cost(1.3e9, 6e6),
        name="project",
    )(*after, *pieces, gain.reshape(1, 1536), packed.reshape(1536, wide), cosine, sine)


def fill_bias(bias, length, places, key_places, window):
    gap = places[...] - key_places[...]
    inside = (key_places[...] < length) & (gap >= 0) & (gap < window)
    bias[...] = jnp.where(inside | (gap == 0), 0.0, NEGATIVE)


def both_rows(own, other, start):
    return jnp.concatenate(
        [own[:, start : start + HEAD_DIM], other[:, start : start + HEAD_DIM]], axis=0
    )


def attend_kernel(window, length, queries, own, other, places, key_places, w_out, *refs):
    outs, (mixed, log_total, total, bias) = refs[:4], refs[4:]
    fill_bias(bias, length[0], places, key_places, window)
    sums = []
    stats = []
    for head in range(4):
        if head % 2 == 0:
            keys = both_rows(own[...], other[...], HEAD_DIM * (head // 2))
            values = both_rows(own[...], other[...], 192 + HEAD_DIM * (head // 2)).T
        query = queries[:, HEAD_DIM * head : HEAD_DIM * (head + 1)]
        scores = nt(keys, query) * HEAD_DIM ** (-0.5) + bias[...]
        peak = jnp.max(scores, axis=0, keepdims=True)
        probs = jnp.exp(scores - peak)
        totals = jnp.sum(probs, axis=0, keepdims=True)
        part = nn(values, probs.astype(BF16)) / totals
        sums.append(part.astype(BF16).astype(F32).T.astype(BF16))
        stats.append(peak + jnp.log(totals))
        for block in range(4):
            cols = slice(384 * block, 384 * (block + 1))
            value = nn(sums[-1], out_block(w_out, head, block))
            if head == 0:
                total[:, cols] = value
            else:
                total[:, cols] += value
    mixed[...] = jnp.concatenate(sums, axis=1)
    log_total[...] = jnp.concatenate(stats + stats, axis=0)
    emit(total, outs)


def line_specs():
    return [whole((512, 384))] * 3 + [whole((1, 512)), whole((1024, 1))]


def out_spec():
    return pl.BlockSpec((8, 192, 384), lambda *_: (0, 0, 2))


def out_block(w_out, head, block):
    start = 96 * (head % 2)
    return w_out[2 * block + head // 2, start : start + 96, :]


def projection_spec():
    return pl.BlockSpec((1536, 768), lambda *_: (0, 0))


def attend_call(window, length, queries, own, other, places, key_places, packed, after=()):
    return pl.pallas_call(
        later(functools.partial(attend_kernel, window), len(after)),
        grid=(1,),
        in_specs=anywhere(after)
        + [pl.BlockSpec(memory_space=pltpu.SMEM)] + line_specs() + [out_spec()],
        out_specs=PARTIALS + [whole((512, 384)), whole((8, 512))],
        out_shape=PARTIAL_SHAPES
        + [jax.ShapeDtypeStruct((512, 384), BF16), jax.ShapeDtypeStruct((8, 512), F32)],
        scratch_shapes=[pltpu.VMEM((512, 1536), F32), pltpu.VMEM((1024, 512), F32)],
        compiler_params=params(48),
        cost_estimate=cost(3e9, 6e6, 2e6),
        name="attend",
    )(*after, length, queries, own, other, places, key_places, packed)


def attend_backward_kernel(window, length, *refs):
    pieces, refs = refs[:5], refs[5:]
    queries, own, other, places, key_places, w_out, log_total, cosine, sine = refs[:9]
    low_queries, pair_own, pair_other, grad, bias = refs[9:]
    fill(grad, pieces)
    fill_bias(bias, length[0], places, key_places, window)
    cos, sin = cosine[...], sine[...]
    lows = []
    key_sums = []
    value_sums = []
    for head in range(4):
        if head % 2 == 0:
            keys = both_rows(own[...], other[...], HEAD_DIM * (head // 2))
            values = both_rows(own[...], other[...], 192 + HEAD_DIM * (head // 2))
            keys_t = keys.T
        query = queries[:, HEAD_DIM * head : HEAD_DIM * (head + 1)]
        mixed = nt(grad[:, :384], out_block(w_out, head, 0))
        for block in range(1, 4):
            mixed += nt(
                grad[:, 384 * block : 384 * (block + 1)], out_block(w_out, head, block)
            )
        mixed = mixed.astype(BF16)
        scores = nt(keys, query) * HEAD_DIM ** (-0.5) + bias[...]
        probs = jnp.exp(scores - log_total[head : head + 1, :])
        slopes = nt(values, mixed)
        inner = jnp.sum(probs * slopes, axis=0, keepdims=True)
        raw = (probs * (slopes - inner) * HEAD_DIM ** (-0.5)).astype(BF16)
        key_part = nn(raw, query)
        value_part = nn(probs.astype(BF16), mixed)
        if head % 2 == 0:
            key_sums.append(key_part)
            value_sums.append(value_part)
        else:
            key_sums[-1] += key_part
            value_sums[-1] += value_part
        turned = nn(keys_t, raw)
        a, b = turned[:48], turned[48:]
        turned = jnp.concatenate([a * cos + b * sin, b * cos - a * sin], axis=0)
        lows.append(turned.T.astype(BF16))
    low_queries[...] = jnp.concatenate(lows, axis=1)
    both = jnp.concatenate(key_sums + value_sums, axis=1)
    pair_own[...] = both[:512]
    pair_other[...] = both[512:].astype(BF16)


def attend_backward_call(
    window,
    length,
    pieces,
    queries,
    own,
    other,
    places,
    key_places,
    packed,
    log_total,
    cosine,
    sine,
    after=(),
):
    return pl.pallas_call(
        later(functools.partial(attend_backward_kernel, window), len(after)),
        grid=(1,),
        in_specs=anywhere(after)
        + [pl.BlockSpec(memory_space=pltpu.SMEM)]
        + PIECES
        + line_specs()
        + [out_spec(), whole((8, 512)), whole((48, 512)), whole((48, 512))],
        out_specs=[whole((512, 384))] * 3,
        out_shape=[
            jax.ShapeDtypeStruct((512, 384), BF16),
            jax.ShapeDtypeStruct((512, 384), F32),
            jax.ShapeDtypeStruct((512, 384), BF16),
        ],
        scratch_shapes=[pltpu.VMEM((512, 1536), BF16), pltpu.VMEM((1024, 512), F32)],
        compiler_params=params(52),
        cost_estimate=cost(6e9, 6e6, 2e6),
        name="attend_backward",
    )(
        *after,
        length,
        *pieces,
        queries,
        own,
        other,
        places,
        key_places,
        packed,
        log_total,
        cosine,
        sine,
    )


def unproject_kernel(low_queries, pair_own, pair_came, cosine, sine, weight, *refs):
    outs, low = refs[:4], refs[4]
    both = pair_own[...] + pair_came[...].astype(F32)
    keys = turn_columns(both[:, :192], cosine[...], -sine[...])
    rows = jnp.concatenate(
        [low_queries[...], keys.astype(BF16), both[:, 192:].astype(BF16)], axis=1
    )
    low[...] = rows
    emit(nt(rows, weight[...]), outs)


def unproject_call(low_queries, pair_own, pair_came, cosine, sine, packed, after=()):
    wide = packed.shape[-1]
    return pl.pallas_call(
        later(unproject_kernel, len(after)),
        grid=(1,),
        in_specs=anywhere(after)
        + [whole((512, 384))] * 3
        + [whole((512, 48))] * 2
        + [projection_spec()],
        out_specs=PARTIALS + [whole((512, 768))],
        out_shape=LOW_PARTIAL_SHAPES + [jax.ShapeDtypeStruct((512, 768), BF16)],
        compiler_params=params(40),
        cost_estimate=cost(1.3e9, 7e6),
        name="unproject",
    )(*after, low_queries, pair_own, pair_came, cosine, sine, packed.reshape(1536, wide))


def attend_weights_kernel(count, *refs):
    flats, grads, (low, mixed) = refs[:count], refs[count : count + 5], refs[count + 5 : count + 7]
    out, flat_t, grad = refs[count + 7 :]
    start = 0
    for ref in flats:
        n = ref.shape[0]
        flat_t[:, start : start + n] = ref[...].T
        start += n
    fill(grad, grads)
    for block in range(3):
        cols = slice(256 * block, 256 * (block + 1))
        out[:, :, cols] = nn(flat_t[...], low[:, cols]).astype(BF16).reshape(8, 192, 256)
    mixed_t = mixed[...].T
    for block in range(4):
        part = nn(mixed_t, grad[:, 384 * block : 384 * (block + 1)]).astype(BF16)
        out[2 * block : 2 * block + 2, :, 768:1152] = part.reshape(2, 192, 384)


def attend_weights_call(flats, grads, low, mixed):
    return pl.pallas_call(
        functools.partial(attend_weights_kernel, len(flats)),
        grid=(1,),
        in_specs=piece_specs(flats) + PIECES + [whole((512, 768)), whole((512, 384))],
        out_specs=whole((8, 192, 1152)),
        out_shape=jax.ShapeDtypeStruct((8, 192, 1152), BF16),
        scratch_shapes=[pltpu.VMEM((1536, 512), BF16), pltpu.VMEM((512, 1536), BF16)],
        compiler_params=params(40),
        cost_estimate=cost(1.9e9, 10e6),
        name="attend_weights",
    )(*flats, *grads, low, mixed)


def unpack_kernel(*refs):
    every, wq, wk, wv, wo, gate, up, down = refs
    side = pl.program_id(0)
    blocks = [every[x, 0] for x in range(4)]
    for x, block in enumerate(blocks):
        wq[:, 384 * x : 384 * (x + 1)] = block[:, 3072:3456].astype(F32)
        wo[:, 384 * x : 384 * (x + 1)] = block[:, 3840:4224].astype(F32)
        for s in range(8):
            cols = slice(512 * s + 128 * x, 512 * s + 128 * (x + 1))
            gate[:, cols] = block[:, 128 * s : 128 * (s + 1)].astype(F32)
            up[:, cols] = block[:, 1024 + 128 * s : 1024 + 128 * (s + 1)].astype(F32)

        @pl.when(side == 0)
        def _(x=x, block=block):
            down[x, 0:96, :1024] = block[:, 2048:3072].astype(F32)

        @pl.when(side == 1)
        def _(x=x, block=block):
            down[x, 96:128, :1024] = block[0:32, 2048:3072].astype(F32)
            down[x, 0:64, 1024:] = block[32:96, 2048:2560].astype(F32)
            down[x, 64:128, 1024:] = block[32:96, 2560:3072].astype(F32)

    wk[...] = jnp.concatenate([block[:, 3456:3648].astype(F32) for block in blocks], axis=1)
    wv[...] = jnp.concatenate([block[:, 3648:3840].astype(F32) for block in blocks], axis=1)


def unpack_call(every):
    widths = (1536, 768, 768, 1536, 4096, 4096)
    out = pl.pallas_call(
        unpack_kernel,
        grid=(2,),
        in_specs=[pl.BlockSpec((4, 1, 96, 4224), lambda b: (0, b, 0, 0))],
        out_specs=[pl.BlockSpec((96, width), lambda b: (b, 0)) for width in widths]
        + [whole((4, 128, 1536))],
        out_shape=[jax.ShapeDtypeStruct((192, width), F32) for width in widths]
        + [jax.ShapeDtypeStruct((4, 128, 1536), F32)],
        compiler_params=params(48),
        cost_estimate=cost(1e6, 30e6),
        name="unpack",
    )(every)
    return out[:4], (out[4], out[5], out[6].reshape(512, 1536))


def pack_feed_kernel(where, w_gate, w_up, w_down, out):
    x = where[0]
    for s in range(8):
        cols = pl.ds(pl.multiple_of(512 * s + 128 * x, 128), 128)
        out[:, 128 * s : 128 * (s + 1)] = w_gate[:, cols]
        out[:, 1024 + 128 * s : 1024 + 128 * (s + 1)] = w_up[:, cols]
    out[0:128, 2048:3072] = w_down[:, 0:1024]
    out[128:192, 2048:2560] = w_down[0:64, 1024:1536]
    out[128:192, 2560:3072] = w_down[64:128, 1024:1536]


def pack_feed_call(where, w_gate, w_up, w_down, after=()):
    return pl.pallas_call(
        later(pack_feed_kernel, len(after), 1),
        grid_spec=pltpu.PrefetchScalarGridSpec(
            num_scalar_prefetch=1,
            grid=(1,),
            in_specs=anywhere(after)
            + [
                pl.BlockSpec((192, 4096), lambda b, w: (0, 0)),
                pl.BlockSpec((192, 4096), lambda b, w: (0, 0)),
                pl.BlockSpec((128, 1536), lambda b, w: (w[0], 0)),
            ],
            out_specs=pl.BlockSpec((192, 3072), lambda b, w: (0, 0)),
        ),
        out_shape=jax.ShapeDtypeStruct((192, 3072), BF16),
        compiler_params=params(24),
        cost_estimate=cost(1e3, 5e6),
        name="pack_feed",
    )(where, *after, w_gate, w_up, w_down)


WINDOW = 512
EPSILON = 1e-05
ROPE_BASE = 100000.0

AXES = ("ylo", "x", "core", "z", "yhi")
SIZES = (2, 4, 2, 4, 2)
REP = ("ylo", "x", "core")
SHARD = ("z", "yhi")
SPREAD = ("z", "core")

RIGHT = [(i, (i + 1) % 4) for i in range(4)]
LEFT = [(i, (i - 1) % 4) for i in range(4)]
ACROSS = [(i, (i + 2) % 4) for i in range(4)]
SWAP = [(0, 1), (1, 0)]


def number(ylo, x, core, z, yhi):
    return (((ylo * 4 + x) * 2 + core) * 4 + z) * 2 + yhi


def permutation(place, taken=None):
    pairs = []
    for ylo in range(2):
        for x in range(4):
            for core in range(2):
                for z in range(4):
                    for yhi in range(2):
                        here = (ylo, x, core, z, yhi)
                        if taken is None or taken(*here):
                            pairs.append((number(*here), number(*place(*here))))
    return pairs


def inverse(pairs):
    return [(there, here) for here, there in pairs]


def at_home(ylo, x, core, z, yhi):
    return core == yhi


def not_home(*place):
    return not at_home(*place)


LINES = [
    permutation(lambda l, x, c, z, h, k=k: (l, (z + k) % 4, h, x, c)) for k in range(4)
]
TURN = permutation(lambda l, x, c, z, h: (l, z, h, x, c))
SHARE = permutation(lambda l, x, c, z, h: (l, x, c, z, 1 - h), at_home)
COLLECT = permutation(lambda l, x, c, z, h: (l, x, c, z, 1 - h), not_home)
BESIDE = permutation(lambda l, x, c, z, h: (1 - l, x, c, z, h), at_home)
CROSS = permutation(lambda l, x, c, z, h: (l, z, c, x, h), at_home)


def to_lines(block, z):
    part = block.shape[0] // 4
    out = []
    for k in range(4):
        piece = lax.dynamic_slice_in_dim(block, ((z + k) % 4) * part, part, axis=0)
        out.append(lax.ppermute(piece, AXES, LINES[k]))
    return jnp.concatenate(out, axis=0)


def from_lines(block, z):
    part = block.shape[0] // 4
    out = jnp.zeros_like(block)
    for k in range(4):
        piece = lax.ppermute(block[part * k : part * (k + 1)], AXES, inverse(LINES[k]))
        out = lax.dynamic_update_slice_in_dim(out, piece, ((z + k) % 4) * part, axis=0)
    return out


def ring_gather(block):
    half = block.shape[0] // 2
    from_left = lax.ppermute(block, "x", RIGHT)
    from_right = lax.ppermute(block, "x", LEFT)
    far_first = lax.ppermute(from_left[:half], "x", RIGHT)
    far_second = lax.ppermute(from_right[half:], "x", LEFT)
    return block, from_left, from_right, far_first, far_second


def ring_scatter(own, left, right, far):
    half = far.shape[0] // 2
    first = lax.ppermute(far[:half], "x", RIGHT).astype(F32)
    second = lax.ppermute(far[half:], "x", LEFT).astype(F32)
    right = jnp.concatenate([right[:half] + first, right[half:]], axis=0).astype(BF16)
    left = jnp.concatenate([left[:half], left[half:] + second], axis=0).astype(BF16)
    from_left = lax.ppermute(right, "x", RIGHT).astype(F32)
    from_right = lax.ppermute(left, "x", LEFT).astype(F32)
    return own + from_left + from_right


def ring_scatter_direct(own, left, right, far):
    from_left = lax.ppermute(right, "x", RIGHT).astype(F32)
    from_right = lax.ppermute(left, "x", LEFT).astype(F32)
    from_far = lax.ppermute(far, "x", ACROSS).astype(F32)
    return own + from_left + from_right + from_far


def tie(value, *others):
    return lax.optimization_barrier((value, *others))[0]


def rms_norm(values, gain):
    return values * lax.rsqrt(jnp.mean(values * values, axis=-1, keepdims=True) + EPSILON) * gain


def add_low(mine, came):
    return (mine.astype(F32) + came.astype(F32)).astype(BF16)


def home_sum(rows):
    return add_low(rows, lax.ppermute(rows, AXES, COLLECT))


def home_piece(rows, core, yhi):
    rows = add_low(rows, lax.ppermute(rows, AXES, BESIDE))
    moved = lax.ppermute(rows[:, 3840:], AXES, CROSS)
    rows = jnp.concatenate([rows[:, :3840], moved], axis=1)
    theirs = lax.dynamic_slice_in_dim(rows, 96 * (1 - core), 96, axis=0)
    mine = lax.dynamic_slice_in_dim(rows, 96 * core, 96, axis=0)
    return jnp.where(core == yhi, mine, lax.ppermute(theirs, "core", SWAP))


def butterfly(values):
    for axis, size in (("core", 2), ("x", 4), ("z", 4), ("yhi", 2), ("ylo", 2)):
        step = 1
        while step < size:
            pairs = [(i, i ^ step) for i in range(size)]
            values = values + lax.ppermute(values, axis, pairs)
            step *= 2
    return values


def norm_back(grad, own_normed, state, gain):
    grad_state, grad_gain = jax.vjp(rms_norm, state, gain)[1](own_normed)
    return grad + grad_state, grad_gain


def body(tokens, lengths, grad_output, *weights):
    stretch, width = tokens.shape[1:]
    x = lax.axis_index("x")
    core = lax.axis_index("core")
    z = lax.axis_index("z")
    yhi = lax.axis_index("yhi")
    member = x.astype(jnp.int32).reshape(1)
    home = core == yhi

    gains = jnp.stack([weights[0], weights[5], weights[9], weights[14]]).T
    gains = jnp.pad(gains, ((0, 0), (0, 124)))

    def shared(block):
        return jnp.where(home, block, lax.ppermute(block, AXES, SHARE))

    def attention_weights(base, extra):
        w_out = weights[base + 4]
        block = lax.dynamic_slice(w_out, (0, 384 * x), (192, 384))
        block = lax.ppermute(block, AXES, TURN)
        parts = [
            lax.dynamic_slice(w, (0, x * (w.shape[1] // 4)), (192, w.shape[1] // 4))
            for w in weights[base + 1 : base + 4]
        ]
        parts = shared(jnp.concatenate(parts + extra, axis=1))
        piece = jnp.concatenate([parts[:, :768], block, parts[:, 768:]], axis=1)
        return lax.all_gather(piece, SPREAD, axis=0, tiled=False)

    def feed_weights(base, after):
        piece = shared(pack_feed_call(member, *weights[base + 6 : base + 9], after=after))
        return lax.all_gather(piece, SPREAD, axis=0, tiled=False)

    attn_one = attention_weights(0, [gains])
    gains = attn_one[:, :, 1152:1156].transpose(2, 0, 1).reshape(4, width).astype(F32)

    length = lax.ppermute(lengths, AXES, TURN)
    rows = to_lines(tokens[0], z)
    pieces = ring_gather(rows)
    state = rows.astype(F32)
    feed_one = feed_weights(0, ())
    attn_two = attention_weights(9, [])
    feed_two = feed_weights(9, (rows,))
    packed = ((attn_one, feed_one), (attn_two, feed_two))

    here = (2 * z + yhi) * stretch + jnp.arange(stretch, dtype=jnp.int32)
    valid = (here < lengths[0])[:, None]
    grad_rows = to_lines(jnp.where(valid, grad_output[0], 0).astype(BF16), z)
    grad_pieces = ring_gather(grad_rows)
    grad = grad_rows.astype(F32)

    part = stretch // 4

    def member_places(member, side_index):
        block = jnp.arange(4, dtype=jnp.int32)
        inner = jnp.arange(part, dtype=jnp.int32)
        home = (member - block + 4) % 4
        return (
            home[:, None] * (2 * stretch) + side_index * stretch + member * part + inner[None, :]
        ).reshape(-1)

    def line_places(side_index):
        return jnp.concatenate([member_places((x + step) % 4, side_index) for step in (0, 3, 1, 2)])

    places = line_places(core)
    key_places = jnp.concatenate([places, line_places(1 - core)]).reshape(1024, 1)
    half = HEAD_DIM // 2
    freq = ROPE_BASE ** (-jnp.arange(half, dtype=F32) * (2.0 / HEAD_DIM))
    angle = places.astype(F32)[:, None] * freq[None, :]
    cosine, sine = jnp.cos(angle), jnp.sin(angle)
    cosine_t, sine_t = cosine.T, sine.T
    places = places.reshape(1, 512)

    records = []
    for index, window in enumerate((WINDOW, 8 * stretch)):
        attn, feed = packed[index]
        gain_attn, gain_feed = gains[2 * index], gains[2 * index + 1]
        if index == 0:
            queries, own, flat = project_call(True, pieces, gain_attn, attn, cosine, sine)
            flats = (flat,)
        else:
            flats = ring_gather(rms_norm(state, gain_attn).astype(BF16))
            queries, own = project_call(False, flats, gain_attn, attn, cosine, sine)
        other = lax.ppermute(own, "core", SWAP)
        line = (queries, own, other, places, key_places)
        after = grad_pieces[3:] if index else ()
        *partial, mixed, log_total = attend_call(window, length, *line, attn, after=after)
        saved_attn = (state, flats, line, mixed, log_total)
        state = state + ring_scatter(*partial)
        flats = ring_gather(rms_norm(state, gain_feed).astype(BF16))
        after = () if index else (grad_rows,)
        *partial, gate, up, hidden = feed_forward_call(flats, feed, after=after)
        saved_feed = (state, flats, gate, up, hidden)
        state = state + ring_scatter(*partial)
        records.append((saved_attn, saved_feed, window))
    last_rows = state.astype(BF16)

    results = [None] * 18
    gain_grads = [None] * 4

    def feed_back(index, grad, pieces, after):
        state, flats, gate, up, hidden = records[index][1]
        *partial, low_gate, low_up = feed_backward_call(
            pieces, packed[index][1], gate, up, after=after
        )
        own_normed = ring_scatter_direct(*partial)
        grad, gain_grads[2 * index + 1] = norm_back(
            grad, own_normed, state, gains[2 * index + 1]
        )
        return grad, feed_weights_call(flats, pieces, low_gate, low_up, hidden)

    def attention_back(index, grad, pieces, after, late):
        state, flats, line, mixed, log_total = records[index][0]
        window = records[index][2]
        attn = packed[index][0]
        low_queries, pair_own, pair_other = attend_backward_call(
            window, length, pieces, *line, attn, log_total, cosine_t, sine_t, after=after
        )
        came = lax.ppermute(pair_other, "core", SWAP)
        *partial, low = unproject_call(
            low_queries, pair_own, came, cosine, sine, attn, after=late
        )
        own_normed = ring_scatter_direct(*partial)
        grad, gain_grads[2 * index] = norm_back(grad, own_normed, state, gains[2 * index])
        return grad, attend_weights_call(flats, pieces, low, mixed)

    def scatter(block, *others):
        return lax.psum_scatter(
            tie(block, *others), SPREAD, scatter_dimension=0, tiled=True
        )[0]

    grad, feed_grad = feed_back(1, grad, grad_pieces, ())
    low = grad.astype(BF16)
    second_feed = scatter(feed_grad, low)
    grad, attn_grad = attention_back(1, grad, ring_gather(low), (feed_grad, last_rows), ())
    low = grad.astype(BF16)
    second_attn = scatter(attn_grad, low)

    grad, feed_grad = feed_back(0, grad, ring_gather(low), (attn_grad, second_feed))
    second = home_sum(jnp.concatenate([second_feed, second_attn], axis=1))
    low = grad.astype(BF16)
    first_feed = scatter(feed_grad, low)
    second_piece = home_piece(second, core, yhi)
    grad, attn_grad = attention_back(
        0, grad, ring_gather(low), (feed_grad, second), (second_piece,)
    )
    first_attn = scatter(attn_grad)
    gain_sums = butterfly(jnp.stack(gain_grads))
    gain_sums = lax.dynamic_slice_in_dim(gain_sums, (2 * z + yhi) * 192, 192, axis=1)

    every = lax.all_gather(tie(second_piece, first_attn), ("x", "core"), axis=0, tiled=False)
    results[10:14], results[15:18] = unpack_call(every.reshape(4, 2, 96, -1))
    first = home_sum(jnp.concatenate([first_feed, first_attn], axis=1))
    first_piece = home_piece(first, core, yhi)
    every = lax.all_gather(first_piece, ("x", "core"), axis=0, tiled=False)
    results[1:5], results[6:9] = unpack_call(every.reshape(4, 2, 96, -1))

    both = jnp.stack([last_rows, grad.astype(BF16)]).reshape(2, 4, 32, width)
    both = both.transpose(1, 0, 2, 3).reshape(2 * stretch, width)
    both = from_lines(both, z).reshape(4, 2, 32, width).transpose(1, 0, 2, 3)
    both = both.reshape(2, stretch, width)
    output, input_grad = both[:1], both[1:].astype(F32)
    for index, slot in enumerate((0, 5, 9, 14)):
        results[slot] = gain_sums[index]
    return (output, input_grad, *results)


def solution(mesh):
    fine = Mesh(mesh.devices.reshape(SIZES), AXES)
    token = P(REP, SHARD, None)
    vector = P(SHARD)
    matrix = P(SHARD, None)
    layer = (vector, matrix, matrix, matrix, matrix, vector, matrix, matrix, matrix)
    return jax.shard_map(
        body,
        mesh=fine,
        in_specs=(token, P(REP), token) + layer + layer,
        out_specs=(token, token) + layer + layer,
        check_vma=False,
    )
```

```python
import functools
import jax
import jax.numpy as jnp
from jax import lax
from jax.experimental import pallas as pl
from jax.experimental.pallas import tpu as pltpu
from jax.sharding import Mesh
from jax.sharding import PartitionSpec as P

F32 = jnp.float32
BF16 = jnp.bfloat16
HEAD_DIM = 96
NEGATIVE = -1e30
MIB = 1 << 20

OFFSETS = (0, 128, 256, 384, 448)
SIZES_OF = (128, 128, 128, 64, 64)


def params(mib, semantics=None):
    return pltpu.CompilerParams(vmem_limit_bytes=mib * MIB, dimension_semantics=semantics)


def cost(flops, nbytes, transcendentals=0):
    return pl.CostEstimate(
        flops=int(flops), bytes_accessed=int(nbytes), transcendentals=int(transcendentals)
    )


def fill(target, refs):
    start = 0
    for ref in refs:
        rows = ref.shape[0]
        target[start : start + rows, :] = ref[...]
        start += rows


def nn(a, b):
    return lax.dot_general(a, b, (((1,), (0,)), ((), ())), preferred_element_type=F32)


def nt(a, b):
    return lax.dot_general(a, b, (((1,), (1,)), ((), ())), preferred_element_type=F32)


def tn(a, b):
    return lax.dot_general(a, b, (((0,), (0,)), ((), ())), preferred_element_type=F32)


def later(kernel, count, lead=0):
    if not count:
        return kernel

    def wrapped(*refs):
        return kernel(*refs[:lead], *refs[lead + count :])

    return wrapped


def anywhere(after):
    return [pl.BlockSpec(memory_space=pl.ANY)] * len(after)


def whole(shape):
    return pl.BlockSpec(shape, lambda *_: (0,) * len(shape))


PIECES = [whole((rows, 1536)) for rows in SIZES_OF]
PARTIAL_SHAPES = [
    jax.ShapeDtypeStruct((128, 1536), F32),
    jax.ShapeDtypeStruct((128, 1536), F32),
    jax.ShapeDtypeStruct((128, 1536), F32),
    jax.ShapeDtypeStruct((128, 1536), BF16),
]
LOW_PARTIAL_SHAPES = PARTIAL_SHAPES[:1] + [jax.ShapeDtypeStruct((128, 1536), BF16)] * 3
PARTIALS = [whole((128, 1536))] * 4


def emit(total, outs):
    for place, out in enumerate(outs):
        out[...] = total[128 * place : 128 * (place + 1), :].astype(out.dtype)


def down_parts(block):
    left = block[:, 0:128, :].reshape(256, 1024)
    right = jnp.concatenate([block[:, 128:192, 0:512], block[:, 128:192, 512:1024]], axis=1)
    return left, right.reshape(256, 512)


def feed_forward_kernel(*refs):
    pieces, (wg, wu, wd), outs = refs[:5], refs[5:8], refs[8:12]
    gate, up, hidden, flat, total = refs[12:]
    step = pl.program_id(0)

    @pl.when(step == 0)
    def _():
        fill(flat, pieces)

    rows = flat[...]
    g = nn(rows, wg[...])
    u = nn(rows, wu[...])
    gate[...] = g
    up[...] = u
    h = (g * jax.nn.sigmoid(g) * u).astype(BF16)
    hidden[...] = h
    left, right = down_parts(wd[...])
    left, right = nn(h, left), nn(h, right)

    @pl.when(step == 0)
    def _():
        total[:, :1024] = left
        total[:, 1024:] = right

    @pl.when(step > 0)
    def _():
        total[:, :1024] += left
        total[:, 1024:] += right

    @pl.when(step == 3)
    def _():
        emit(total, outs)


def feed_specs():
    return [
        pl.BlockSpec((1536, 256), lambda b: (0, b)),
        pl.BlockSpec((1536, 256), lambda b: (0, 4 + b)),
        pl.BlockSpec((2, 192, 1024), lambda b: (b, 0, 2)),
    ]


def column_block(rows):
    return pl.BlockSpec((rows, 256), lambda b: (0, b))


def feed_forward_call(pieces, packed, after=()):
    flat_packed = packed.reshape(1536, -1)
    return pl.pallas_call(
        later(feed_forward_kernel, len(after)),
        grid=(4,),
        in_specs=anywhere(after) + PIECES + feed_specs(),
        out_specs=PARTIALS + [column_block(512)] * 3,
        out_shape=PARTIAL_SHAPES
        + [
            jax.ShapeDtypeStruct((512, 1024), F32),
            jax.ShapeDtypeStruct((512, 1024), F32),
            jax.ShapeDtypeStruct((512, 1024), BF16),
        ],
        scratch_shapes=[pltpu.VMEM((512, 1536), BF16), pltpu.VMEM((512, 1536), F32)],
        compiler_params=params(40),
        cost_estimate=cost(4.9e9, 18e6),
        name="feed_forward",
    )(*after, *pieces, flat_packed, flat_packed, packed)


def feed_backward_kernel(*refs):
    pieces, (wg, wu, wd, gate, up), outs = refs[:5], refs[5:10], refs[10:14]
    low_gate, low_up, flat, total = refs[14:]
    step = pl.program_id(0)

    @pl.when(step == 0)
    def _():
        fill(flat, pieces)

    rows = flat[...]
    left, right = down_parts(wd[...])
    grad = nt(rows[:, :1024], left) + nt(rows[:, 1024:], right)
    g = gate[...]
    s = jax.nn.sigmoid(g)
    a = (grad * up[...] * s * (1.0 + g * (1.0 - s))).astype(BF16)
    b = (grad * (g * s)).astype(BF16)
    low_gate[...] = a
    low_up[...] = b
    part = nt(a, wg[...]) + nt(b, wu[...])

    @pl.when(step == 0)
    def _():
        total[...] = part

    @pl.when(step > 0)
    def _():
        total[...] += part

    @pl.when(step == 3)
    def _():
        emit(total, outs)


def feed_backward_call(pieces, packed, gate, up, after=()):
    flat_packed = packed.reshape(1536, -1)
    return pl.pallas_call(
        later(feed_backward_kernel, len(after)),
        grid=(4,),
        in_specs=anywhere(after) + PIECES + feed_specs() + [column_block(512)] * 2,
        out_specs=PARTIALS + [column_block(512)] * 2,
        out_shape=LOW_PARTIAL_SHAPES + [jax.ShapeDtypeStruct((512, 1024), BF16)] * 2,
        scratch_shapes=[pltpu.VMEM((512, 1536), BF16), pltpu.VMEM((512, 1536), F32)],
        compiler_params=params(40),
        cost_estimate=cost(4.9e9, 20e6),
        name="feed_backward",
    )(*after, *pieces, flat_packed, flat_packed, packed, gate, up)


def feed_weights_kernel(*refs):
    flats, grads = refs[:5], refs[5:10]
    low_gate, low_up, hidden, out, flat_t, hidden_t, grad = refs[10:]
    step = pl.program_id(0)

    @pl.when(step == 0)
    def _():
        start = 0
        for ref in flats:
            n = ref.shape[0]
            flat_t[:, start : start + n] = ref[...].T
            start += n

    @pl.when(step == 4)
    def _():
        hidden_t[...] = hidden[...].T
        fill(grad, grads)

    @pl.when(step < 4)
    def _():
        out[...] = nn(flat_t[...], low_gate[...]).astype(BF16).reshape(8, 192, 256)

    @pl.when((step >= 4) & (step < 8))
    def _():
        out[...] = nn(flat_t[...], low_up[...]).astype(BF16).reshape(8, 192, 256)

    for q in range(4):

        @pl.when(step == 8 + q)
        def _():
            top = nn(hidden_t[...], grad[:, 256 * q : 256 * (q + 1)]).astype(BF16)
            out[:, 0:128, :] = top.reshape(8, 128, 256)
            half = 64 * (q // 2)
            some = hidden_t[...].reshape(8, 128, 512)[:, half : half + 64].reshape(512, 512)
            start = 1024 + 256 * (q % 2)
            low = nn(some, grad[:, start : start + 256]).astype(BF16)
            out[:, 128:192, :] = low.reshape(8, 64, 256)


def feed_weights_call(flats, grads, low_gate, low_up, hidden):
    return pl.pallas_call(
        feed_weights_kernel,
        grid=(12,),
        in_specs=PIECES
        + PIECES
        + [
            pl.BlockSpec((512, 256), lambda b: (0, jnp.minimum(b, 3))),
            pl.BlockSpec((512, 256), lambda b: (0, jnp.clip(b - 4, 0, 3))),
            whole((512, 1024)),
        ],
        out_specs=pl.BlockSpec((8, 192, 256), lambda b: (0, 0, b)),
        out_shape=jax.ShapeDtypeStruct((8, 192, 3072), BF16),
        scratch_shapes=[
            pltpu.VMEM((1536, 512), BF16),
            pltpu.VMEM((1024, 512), BF16),
            pltpu.VMEM((512, 1536), BF16),
        ],
        compiler_params=params(40),
        cost_estimate=cost(4.9e9, 18e6),
        name="feed_weights",
    )(*flats, *grads, low_gate, low_up, hidden)


def piece_specs(pieces):
    return [whole(item.shape) for item in pieces]


def turn_columns(block, cosine, sine):
    out = []
    for start in range(0, block.shape[1], HEAD_DIM):
        a = block[:, start : start + 48]
        b = block[:, start + 48 : start + HEAD_DIM]
        out.append(a * cosine - b * sine)
        out.append(b * cosine + a * sine)
    return jnp.concatenate(out, axis=1)


def project_kernel(raw, count, *refs):
    pieces, (gain, weight, cosine, sine, queries, pair) = refs[:count], refs[count : count + 6]
    if raw:
        flat = refs[-1]
        start = 0
        for ref in pieces:
            n = ref.shape[0]
            rows = ref[...].astype(F32)
            scale = lax.rsqrt(jnp.mean(rows * rows, axis=-1, keepdims=True) + 1e-05)
            flat[start : start + n, :] = (rows * scale * gain[...]).astype(BF16)
            start += n
    else:
        flat = refs[-1]
        fill(flat, pieces)
    both = nn(flat[...], weight[...])
    cos, sin = cosine[...], sine[...]
    queries[...] = turn_columns(both[:, :384], cos, sin).astype(BF16)
    keys = turn_columns(both[:, 384:576], cos, sin)
    pair[...] = jnp.concatenate([keys, both[:, 576:768]], axis=1).astype(BF16)


def project_call(raw, pieces, gain, packed, cosine, sine, after=()):
    wide = packed.shape[-1]
    shape = jax.ShapeDtypeStruct((512, 384), BF16)
    flat_shape = jax.ShapeDtypeStruct((512, 1536), BF16)
    return pl.pallas_call(
        later(functools.partial(project_kernel, raw, len(pieces)), len(after)),
        grid=(1,),
        in_specs=anywhere(after)
        + piece_specs(pieces)
        + [whole((1, 1536)), projection_spec(), whole((512, 48)), whole((512, 48))],
        out_specs=[whole((512, 384))] * 2 + ([whole((512, 1536))] if raw else []),
        out_shape=[shape, shape] + ([flat_shape] if raw else []),
        scratch_shapes=[] if raw else [pltpu.VMEM((512, 1536), BF16)],
        compiler_params=params(40),
        cost_estimate=cost(1.3e9, 6e6),
        name="project",
    )(*after, *pieces, gain.reshape(1, 1536), packed.reshape(1536, wide), cosine, sine)


def fill_bias(bias, length, places, key_places, window):
    gap = places[...] - key_places[...]
    inside = (key_places[...] < length) & (gap >= 0) & (gap < window)
    bias[...] = jnp.where(inside | (gap == 0), 0.0, NEGATIVE)


def both_rows(own, other, start):
    return jnp.concatenate(
        [own[:, start : start + HEAD_DIM], other[:, start : start + HEAD_DIM]], axis=0
    )


def attend_kernel(window, length, queries, own, other, places, key_places, w_out, *refs):
    outs, (mixed, log_total, total, bias) = refs[:4], refs[4:]
    fill_bias(bias, length[0], places, key_places, window)
    sums = []
    stats = []
    for head in range(4):
        if head % 2 == 0:
            keys = both_rows(own[...], other[...], HEAD_DIM * (head // 2))
            values = both_rows(own[...], other[...], 192 + HEAD_DIM * (head // 2)).T
        query = queries[:, HEAD_DIM * head : HEAD_DIM * (head + 1)]
        scores = nt(keys, query) * HEAD_DIM ** (-0.5) + bias[...]
        peak = jnp.max(scores, axis=0, keepdims=True)
        probs = jnp.exp(scores - peak)
        totals = jnp.sum(probs, axis=0, keepdims=True)
        part = nn(values, probs.astype(BF16)) / totals
        sums.append(part.astype(BF16).astype(F32).T.astype(BF16))
        stats.append(peak + jnp.log(totals))
        for block in range(4):
            cols = slice(384 * block, 384 * (block + 1))
            value = nn(sums[-1], out_block(w_out, head, block))
            if head == 0:
                total[:, cols] = value
            else:
                total[:, cols] += value
    mixed[...] = jnp.concatenate(sums, axis=1)
    log_total[...] = jnp.concatenate(stats + stats, axis=0)
    emit(total, outs)


def line_specs():
    return [whole((512, 384))] * 3 + [whole((1, 512)), whole((1024, 1))]


def out_spec():
    return pl.BlockSpec((8, 192, 384), lambda *_: (0, 0, 2))


def out_block(w_out, head, block):
    start = 96 * (head % 2)
    return w_out[2 * block + head // 2, start : start + 96, :]


def projection_spec():
    return pl.BlockSpec((1536, 768), lambda *_: (0, 0))


def attend_call(window, length, queries, own, other, places, key_places, packed, after=()):
    return pl.pallas_call(
        later(functools.partial(attend_kernel, window), len(after)),
        grid=(1,),
        in_specs=anywhere(after)
        + [pl.BlockSpec(memory_space=pltpu.SMEM)] + line_specs() + [out_spec()],
        out_specs=PARTIALS + [whole((512, 384)), whole((8, 512))],
        out_shape=PARTIAL_SHAPES
        + [jax.ShapeDtypeStruct((512, 384), BF16), jax.ShapeDtypeStruct((8, 512), F32)],
        scratch_shapes=[pltpu.VMEM((512, 1536), F32), pltpu.VMEM((1024, 512), F32)],
        compiler_params=params(48),
        cost_estimate=cost(3e9, 6e6, 2e6),
        name="attend",
    )(*after, length, queries, own, other, places, key_places, packed)


def attend_backward_kernel(window, length, *refs):
    pieces, refs = refs[:5], refs[5:]
    queries, own, other, places, key_places, w_out, log_total, cosine, sine = refs[:9]
    low_queries, pair_own, pair_other, grad, bias = refs[9:]
    fill(grad, pieces)
    fill_bias(bias, length[0], places, key_places, window)
    cos, sin = cosine[...], sine[...]
    lows = []
    key_sums = []
    value_sums = []
    for head in range(4):
        if head % 2 == 0:
            keys = both_rows(own[...], other[...], HEAD_DIM * (head // 2))
            values = both_rows(own[...], other[...], 192 + HEAD_DIM * (head // 2))
            keys_t = keys.T
        query = queries[:, HEAD_DIM * head : HEAD_DIM * (head + 1)]
        mixed = nt(grad[:, :384], out_block(w_out, head, 0))
        for block in range(1, 4):
            mixed += nt(
                grad[:, 384 * block : 384 * (block + 1)], out_block(w_out, head, block)
            )
        mixed = mixed.astype(BF16)
        scores = nt(keys, query) * HEAD_DIM ** (-0.5) + bias[...]
        probs = jnp.exp(scores - log_total[head : head + 1, :])
        slopes = nt(values, mixed)
        inner = jnp.sum(probs * slopes, axis=0, keepdims=True)
        raw = (probs * (slopes - inner) * HEAD_DIM ** (-0.5)).astype(BF16)
        key_part = nn(raw, query)
        value_part = nn(probs.astype(BF16), mixed)
        if head % 2 == 0:
            key_sums.append(key_part)
            value_sums.append(value_part)
        else:
            key_sums[-1] += key_part
            value_sums[-1] += value_part
        turned = nn(keys_t, raw)
        a, b = turned[:48], turned[48:]
        turned = jnp.concatenate([a * cos + b * sin, b * cos - a * sin], axis=0)
        lows.append(turned.T.astype(BF16))
    low_queries[...] = jnp.concatenate(lows, axis=1)
    both = jnp.concatenate(key_sums + value_sums, axis=1)
    pair_own[...] = both[:512]
    pair_other[...] = both[512:].astype(BF16)


def attend_backward_call(
    window,
    length,
    pieces,
    queries,
    own,
    other,
    places,
    key_places,
    packed,
    log_total,
    cosine,
    sine,
    after=(),
):
    return pl.pallas_call(
        later(functools.partial(attend_backward_kernel, window), len(after)),
        grid=(1,),
        in_specs=anywhere(after)
        + [pl.BlockSpec(memory_space=pltpu.SMEM)]
        + PIECES
        + line_specs()
        + [out_spec(), whole((8, 512)), whole((48, 512)), whole((48, 512))],
        out_specs=[whole((512, 384))] * 3,
        out_shape=[
            jax.ShapeDtypeStruct((512, 384), BF16),
            jax.ShapeDtypeStruct((512, 384), F32),
            jax.ShapeDtypeStruct((512, 384), BF16),
        ],
        scratch_shapes=[pltpu.VMEM((512, 1536), BF16), pltpu.VMEM((1024, 512), F32)],
        compiler_params=params(52),
        cost_estimate=cost(6e9, 6e6, 2e6),
        name="attend_backward",
    )(
        *after,
        length,
        *pieces,
        queries,
        own,
        other,
        places,
        key_places,
        packed,
        log_total,
        cosine,
        sine,
    )


def unproject_kernel(low_queries, pair_own, pair_came, cosine, sine, weight, *refs):
    outs, low = refs[:4], refs[4]
    both = pair_own[...] + pair_came[...].astype(F32)
    keys = turn_columns(both[:, :192], cosine[...], -sine[...])
    rows = jnp.concatenate(
        [low_queries[...], keys.astype(BF16), both[:, 192:].astype(BF16)], axis=1
    )
    low[...] = rows
    emit(nt(rows, weight[...]), outs)


def unproject_call(low_queries, pair_own, pair_came, cosine, sine, packed, after=()):
    wide = packed.shape[-1]
    return pl.pallas_call(
        later(unproject_kernel, len(after)),
        grid=(1,),
        in_specs=anywhere(after)
        + [whole((512, 384))] * 3
        + [whole((512, 48))] * 2
        + [projection_spec()],
        out_specs=PARTIALS + [whole((512, 768))],
        out_shape=LOW_PARTIAL_SHAPES + [jax.ShapeDtypeStruct((512, 768), BF16)],
        compiler_params=params(40),
        cost_estimate=cost(1.3e9, 7e6),
        name="unproject",
    )(*after, low_queries, pair_own, pair_came, cosine, sine, packed.reshape(1536, wide))


def attend_weights_kernel(count, *refs):
    flats, grads, (low, mixed) = refs[:count], refs[count : count + 5], refs[count + 5 : count + 7]
    out, flat_t, grad = refs[count + 7 :]
    start = 0
    for ref in flats:
        n = ref.shape[0]
        flat_t[:, start : start + n] = ref[...].T
        start += n
    fill(grad, grads)
    for block in range(3):
        cols = slice(256 * block, 256 * (block + 1))
        out[:, :, cols] = nn(flat_t[...], low[:, cols]).astype(BF16).reshape(8, 192, 256)
    mixed_t = mixed[...].T
    for block in range(4):
        part = nn(mixed_t, grad[:, 384 * block : 384 * (block + 1)]).astype(BF16)
        out[2 * block : 2 * block + 2, :, 768:1152] = part.reshape(2, 192, 384)


def attend_weights_call(flats, grads, low, mixed):
    return pl.pallas_call(
        functools.partial(attend_weights_kernel, len(flats)),
        grid=(1,),
        in_specs=piece_specs(flats) + PIECES + [whole((512, 768)), whole((512, 384))],
        out_specs=whole((8, 192, 1152)),
        out_shape=jax.ShapeDtypeStruct((8, 192, 1152), BF16),
        scratch_shapes=[pltpu.VMEM((1536, 512), BF16), pltpu.VMEM((512, 1536), BF16)],
        compiler_params=params(40),
        cost_estimate=cost(1.9e9, 10e6),
        name="attend_weights",
    )(*flats, *grads, low, mixed)


def unpack_kernel(*refs):
    every, wq, wk, wv, wo, gate, up, down = refs
    side = pl.program_id(0)
    blocks = [every[x, 0] for x in range(4)]
    for x, block in enumerate(blocks):
        wq[:, 384 * x : 384 * (x + 1)] = block[:, 3072:3456].astype(F32)
        wo[:, 384 * x : 384 * (x + 1)] = block[:, 3840:4224].astype(F32)
        for s in range(8):
            cols = slice(512 * s + 128 * x, 512 * s + 128 * (x + 1))
            gate[:, cols] = block[:, 128 * s : 128 * (s + 1)].astype(F32)
            up[:, cols] = block[:, 1024 + 128 * s : 1024 + 128 * (s + 1)].astype(F32)

        @pl.when(side == 0)
        def _(x=x, block=block):
            down[x, 0:96, :1024] = block[:, 2048:3072].astype(F32)

        @pl.when(side == 1)
        def _(x=x, block=block):
            down[x, 96:128, :1024] = block[0:32, 2048:3072].astype(F32)
            down[x, 0:64, 1024:] = block[32:96, 2048:2560].astype(F32)
            down[x, 64:128, 1024:] = block[32:96, 2560:3072].astype(F32)

    wk[...] = jnp.concatenate([block[:, 3456:3648].astype(F32) for block in blocks], axis=1)
    wv[...] = jnp.concatenate([block[:, 3648:3840].astype(F32) for block in blocks], axis=1)


def unpack_call(every):
    widths = (1536, 768, 768, 1536, 4096, 4096)
    out = pl.pallas_call(
        unpack_kernel,
        grid=(2,),
        in_specs=[pl.BlockSpec((4, 1, 96, 4224), lambda b: (0, b, 0, 0))],
        out_specs=[pl.BlockSpec((96, width), lambda b: (b, 0)) for width in widths]
        + [whole((4, 128, 1536))],
        out_shape=[jax.ShapeDtypeStruct((192, width), F32) for width in widths]
        + [jax.ShapeDtypeStruct((4, 128, 1536), F32)],
        compiler_params=params(48),
        cost_estimate=cost(1e6, 30e6),
        name="unpack",
    )(every)
    return out[:4], (out[4], out[5], out[6].reshape(512, 1536))


def pack_feed_kernel(where, w_gate, w_up, w_down, out):
    x = where[0]
    for s in range(8):
        cols = pl.ds(pl.multiple_of(512 * s + 128 * x, 128), 128)
        out[:, 128 * s : 128 * (s + 1)] = w_gate[:, cols]
        out[:, 1024 + 128 * s : 1024 + 128 * (s + 1)] = w_up[:, cols]
    out[0:128, 2048:3072] = w_down[:, 0:1024]
    out[128:192, 2048:2560] = w_down[0:64, 1024:1536]
    out[128:192, 2560:3072] = w_down[64:128, 1024:1536]


def pack_feed_call(where, w_gate, w_up, w_down, after=()):
    return pl.pallas_call(
        later(pack_feed_kernel, len(after), 1),
        grid_spec=pltpu.PrefetchScalarGridSpec(
            num_scalar_prefetch=1,
            grid=(1,),
            in_specs=anywhere(after)
            + [
                pl.BlockSpec((192, 4096), lambda b, w: (0, 0)),
                pl.BlockSpec((192, 4096), lambda b, w: (0, 0)),
                pl.BlockSpec((128, 1536), lambda b, w: (w[0], 0)),
            ],
            out_specs=pl.BlockSpec((192, 3072), lambda b, w: (0, 0)),
        ),
        out_shape=jax.ShapeDtypeStruct((192, 3072), BF16),
        compiler_params=params(24),
        cost_estimate=cost(1e3, 5e6),
        name="pack_feed",
    )(where, *after, w_gate, w_up, w_down)


WINDOW = 512
EPSILON = 1e-05
ROPE_BASE = 100000.0

AXES = ("ylo", "x", "core", "z", "yhi")
SIZES = (2, 4, 2, 4, 2)
REP = ("ylo", "x", "core")
SHARD = ("z", "yhi")
SPREAD = ("z", "core")

RIGHT = [(i, (i + 1) % 4) for i in range(4)]
LEFT = [(i, (i - 1) % 4) for i in range(4)]
ACROSS = [(i, (i + 2) % 4) for i in range(4)]
SWAP = [(0, 1), (1, 0)]


def number(ylo, x, core, z, yhi):
    return (((ylo * 4 + x) * 2 + core) * 4 + z) * 2 + yhi


def permutation(place, taken=None):
    pairs = []
    for ylo in range(2):
        for x in range(4):
            for core in range(2):
                for z in range(4):
                    for yhi in range(2):
                        here = (ylo, x, core, z, yhi)
                        if taken is None or taken(*here):
                            pairs.append((number(*here), number(*place(*here))))
    return pairs


def inverse(pairs):
    return [(there, here) for here, there in pairs]


def at_home(ylo, x, core, z, yhi):
    return core == yhi


def not_home(*place):
    return not at_home(*place)


LINES = [
    permutation(lambda l, x, c, z, h, k=k: (l, (z + k) % 4, h, x, c)) for k in range(4)
]
TURN = permutation(lambda l, x, c, z, h: (l, z, h, x, c))
SHARE = permutation(lambda l, x, c, z, h: (l, x, c, z, 1 - h), at_home)
COLLECT = permutation(lambda l, x, c, z, h: (l, x, c, z, 1 - h), not_home)
BESIDE = permutation(lambda l, x, c, z, h: (1 - l, x, c, z, h), at_home)
CROSS = permutation(lambda l, x, c, z, h: (l, z, c, x, h), at_home)


def to_lines(block, z):
    part = block.shape[0] // 4
    out = []
    for k in range(4):
        piece = lax.dynamic_slice_in_dim(block, ((z + k) % 4) * part, part, axis=0)
        out.append(lax.ppermute(piece, AXES, LINES[k]))
    return jnp.concatenate(out, axis=0)


def from_lines(block, z):
    part = block.shape[0] // 4
    out = jnp.zeros_like(block)
    for k in range(4):
        piece = lax.ppermute(block[part * k : part * (k + 1)], AXES, inverse(LINES[k]))
        out = lax.dynamic_update_slice_in_dim(out, piece, ((z + k) % 4) * part, axis=0)
    return out


def ring_gather(block):
    half = block.shape[0] // 2
    from_left = lax.ppermute(block, "x", RIGHT)
    from_right = lax.ppermute(block, "x", LEFT)
    far_first = lax.ppermute(from_left[:half], "x", RIGHT)
    far_second = lax.ppermute(from_right[half:], "x", LEFT)
    return block, from_left, from_right, far_first, far_second


def ring_scatter(own, left, right, far):
    half = far.shape[0] // 2
    first = lax.ppermute(far[:half], "x", RIGHT).astype(F32)
    second = lax.ppermute(far[half:], "x", LEFT).astype(F32)
    right = jnp.concatenate([right[:half] + first, right[half:]], axis=0).astype(BF16)
    left = jnp.concatenate([left[:half], left[half:] + second], axis=0).astype(BF16)
    from_left = lax.ppermute(right, "x", RIGHT).astype(F32)
    from_right = lax.ppermute(left, "x", LEFT).astype(F32)
    return own + from_left + from_right


def ring_scatter_direct(own, left, right, far):
    from_left = lax.ppermute(right, "x", RIGHT).astype(F32)
    from_right = lax.ppermute(left, "x", LEFT).astype(F32)
    from_far = lax.ppermute(far, "x", ACROSS).astype(F32)
    return own + from_left + from_right + from_far


def tie(value, *others):
    return lax.optimization_barrier((value, *others))[0]


def rms_norm(values, gain):
    return values * lax.rsqrt(jnp.mean(values * values, axis=-1, keepdims=True) + EPSILON) * gain


def add_low(mine, came):
    return (mine.astype(F32) + came.astype(F32)).astype(BF16)


def home_sum(rows):
    return add_low(rows, lax.ppermute(rows, AXES, COLLECT))


def home_piece(rows, core, yhi):
    rows = add_low(rows, lax.ppermute(rows, AXES, BESIDE))
    moved = lax.ppermute(rows[:, 3840:], AXES, CROSS)
    rows = jnp.concatenate([rows[:, :3840], moved], axis=1)
    theirs = lax.dynamic_slice_in_dim(rows, 96 * (1 - core), 96, axis=0)
    mine = lax.dynamic_slice_in_dim(rows, 96 * core, 96, axis=0)
    return jnp.where(core == yhi, mine, lax.ppermute(theirs, "core", SWAP))


def butterfly(values):
    for axis, size in (("core", 2), ("x", 4), ("z", 4), ("yhi", 2), ("ylo", 2)):
        step = 1
        while step < size:
            pairs = [(i, i ^ step) for i in range(size)]
            values = values + lax.ppermute(values, axis, pairs)
            step *= 2
    return values


def norm_back(grad, own_normed, state, gain):
    grad_state, grad_gain = jax.vjp(rms_norm, state, gain)[1](own_normed)
    return grad + grad_state, grad_gain


def body(tokens, lengths, grad_output, *weights):
    stretch, width = tokens.shape[1:]
    x = lax.axis_index("x")
    core = lax.axis_index("core")
    z = lax.axis_index("z")
    yhi = lax.axis_index("yhi")
    member = x.astype(jnp.int32).reshape(1)
    home = core == yhi

    gains = jnp.stack([weights[0], weights[5], weights[9], weights[14]]).T
    gains = jnp.pad(gains, ((0, 0), (0, 124)))

    def shared(block):
        return jnp.where(home, block, lax.ppermute(block, AXES, SHARE))

    def attention_weights(base, extra, after):
        w_out = weights[base + 4]
        block = lax.dynamic_slice(w_out, (0, 384 * x), (192, 384))
        block = lax.ppermute(block, AXES, TURN)
        parts = [
            lax.dynamic_slice(w, (0, x * (w.shape[1] // 4)), (192, w.shape[1] // 4))
            for w in weights[base + 1 : base + 4]
        ]
        parts = shared(tie(jnp.concatenate(parts + extra, axis=1), *after))
        piece = jnp.concatenate([parts[:, :768], block, parts[:, 768:]], axis=1)
        return lax.all_gather(piece, SPREAD, axis=0, tiled=False)

    def feed_weights(base, after):
        piece = shared(pack_feed_call(member, *weights[base + 6 : base + 9], after=after))
        return lax.all_gather(piece, SPREAD, axis=0, tiled=False)

    attn_one = attention_weights(0, [gains], ())
    gains = attn_one[:, :, 1152:1156].transpose(2, 0, 1).reshape(4, width).astype(F32)

    length = lax.ppermute(lengths, AXES, TURN)
    rows = to_lines(tokens[0], z)
    pieces = ring_gather(rows)
    state = rows.astype(F32)
    feed_one = feed_weights(0, (rows,))
    attn_two = attention_weights(9, [], pieces[3:])
    feed_two = feed_weights(9, pieces[3:])
    packed = ((attn_one, feed_one), (attn_two, feed_two))

    here = (2 * z + yhi) * stretch + jnp.arange(stretch, dtype=jnp.int32)
    valid = (here < lengths[0])[:, None]
    grad_rows = to_lines(tie(jnp.where(valid, grad_output[0], 0).astype(BF16), *pieces[3:]), z)
    grad_pieces = ring_gather(grad_rows)
    grad = grad_rows.astype(F32)

    part = stretch // 4

    def member_places(member, side_index):
        block = jnp.arange(4, dtype=jnp.int32)
        inner = jnp.arange(part, dtype=jnp.int32)
        home = (member - block + 4) % 4
        return (
            home[:, None] * (2 * stretch) + side_index * stretch + member * part + inner[None, :]
        ).reshape(-1)

    def line_places(side_index):
        return jnp.concatenate([member_places((x + step) % 4, side_index) for step in (0, 3, 1, 2)])

    places = line_places(core)
    key_places = jnp.concatenate([places, line_places(1 - core)]).reshape(1024, 1)
    half = HEAD_DIM // 2
    freq = ROPE_BASE ** (-jnp.arange(half, dtype=F32) * (2.0 / HEAD_DIM))
    angle = places.astype(F32)[:, None] * freq[None, :]
    cosine, sine = jnp.cos(angle), jnp.sin(angle)
    cosine_t, sine_t = cosine.T, sine.T
    places = places.reshape(1, 512)

    records = []
    for index, window in enumerate((WINDOW, 8 * stretch)):
        attn, feed = packed[index]
        gain_attn, gain_feed = gains[2 * index], gains[2 * index + 1]
        if index == 0:
            queries, own, flat = project_call(True, pieces, gain_attn, attn, cosine, sine)
            flats = (flat,)
        else:
            flats = ring_gather(rms_norm(state, gain_attn).astype(BF16))
            queries, own = project_call(False, flats, gain_attn, attn, cosine, sine)
        other = lax.ppermute(own, "core", SWAP)
        line = (queries, own, other, places, key_places)
        after = grad_pieces[3:] if index else ()
        *partial, mixed, log_total = attend_call(window, length, *line, attn, after=after)
        saved_attn = (state, flats, line, mixed, log_total)
        state = state + ring_scatter(*partial)
        flats = ring_gather(rms_norm(state, gain_feed).astype(BF16))
        after = () if index else (grad_rows,)
        *partial, gate, up, hidden = feed_forward_call(flats, feed, after=after)
        saved_feed = (state, flats, gate, up, hidden)
        state = state + ring_scatter(*partial)
        records.append((saved_attn, saved_feed, window))
    last_rows = state.astype(BF16)

    results = [None] * 18
    gain_grads = [None] * 4

    def feed_back(index, grad, pieces, after):
        state, flats, gate, up, hidden = records[index][1]
        *partial, low_gate, low_up = feed_backward_call(
            pieces, packed[index][1], gate, up, after=after
        )
        own_normed = ring_scatter_direct(*partial)
        grad, gain_grads[2 * index + 1] = norm_back(
            grad, own_normed, state, gains[2 * index + 1]
        )
        return grad, feed_weights_call(flats, pieces, low_gate, low_up, hidden)

    def attention_back(index, grad, pieces, after, late):
        state, flats, line, mixed, log_total = records[index][0]
        window = records[index][2]
        attn = packed[index][0]
        low_queries, pair_own, pair_other = attend_backward_call(
            window, length, pieces, *line, attn, log_total, cosine_t, sine_t, after=after
        )
        came = lax.ppermute(pair_other, "core", SWAP)
        *partial, low = unproject_call(
            low_queries, pair_own, came, cosine, sine, attn, after=late
        )
        own_normed = ring_scatter_direct(*partial)
        grad, gain_grads[2 * index] = norm_back(grad, own_normed, state, gains[2 * index])
        return grad, attend_weights_call(flats, pieces, low, mixed)

    def scatter(block, *others):
        return lax.psum_scatter(
            tie(block, *others), SPREAD, scatter_dimension=0, tiled=True
        )[0]

    grad, feed_grad = feed_back(1, grad, grad_pieces, ())
    low = tie(grad.astype(BF16), feed_grad)
    second_feed = scatter(feed_grad, low)
    grad, attn_grad = attention_back(1, grad, ring_gather(low), (last_rows,), ())
    low = tie(grad.astype(BF16), attn_grad)
    second_attn = scatter(attn_grad, low, second_feed)

    grad, feed_grad = feed_back(0, grad, ring_gather(low), (second_feed,))
    low = tie(grad.astype(BF16), feed_grad)
    first_feed = scatter(feed_grad, low, second_attn)
    second = home_sum(jnp.concatenate([second_feed, second_attn], axis=1))
    grad, attn_grad = attention_back(0, grad, ring_gather(low), (), (second,))
    first_attn = scatter(attn_grad, first_feed)
    second_piece = home_piece(second, core, yhi)
    gain_sums = butterfly(jnp.stack(gain_grads))

    every = lax.all_gather(tie(second_piece, first_attn), ("x", "core"), axis=0, tiled=False)
    results[10:14], results[15:18] = unpack_call(every.reshape(4, 2, 96, -1))
    first = jnp.concatenate([first_feed, first_attn], axis=1)
    first_piece = home_piece(home_sum(tie(first, gain_sums)), core, yhi)
    every = lax.all_gather(first_piece, ("x", "core"), axis=0, tiled=False)
    results[1:5], results[6:9] = unpack_call(every.reshape(4, 2, 96, -1))
    gain_sums = lax.dynamic_slice_in_dim(gain_sums, (2 * z + yhi) * 192, 192, axis=1)

    both = jnp.stack([last_rows, grad.astype(BF16)]).reshape(2, 4, 32, width)
    both = both.transpose(1, 0, 2, 3).reshape(2 * stretch, width)
    both = from_lines(both, z).reshape(4, 2, 32, width).transpose(1, 0, 2, 3)
    both = both.reshape(2, stretch, width)
    output, input_grad = both[:1], both[1:].astype(F32)
    for index, slot in enumerate((0, 5, 9, 14)):
        results[slot] = gain_sums[index]
    return (output, input_grad, *results)


def solution(mesh):
    fine = Mesh(mesh.devices.reshape(SIZES), AXES)
    token = P(REP, SHARD, None)
    vector = P(SHARD)
    matrix = P(SHARD, None)
    layer = (vector, matrix, matrix, matrix, matrix, vector, matrix, matrix, matrix)
    return jax.shard_map(
        body,
        mesh=fine,
        in_specs=(token, P(REP), token) + layer + layer,
        out_specs=(token, token) + layer + layer,
        check_vma=False,
    )
```

```python
import functools
import jax
import jax.numpy as jnp
from jax import lax
from jax.experimental import pallas as pl
from jax.experimental.pallas import tpu as pltpu
from jax.sharding import Mesh
from jax.sharding import PartitionSpec as P

F32 = jnp.float32
BF16 = jnp.bfloat16
HEAD_DIM = 96
NEGATIVE = -1e30
MIB = 1 << 20

OFFSETS = (0, 128, 256, 384, 448)
SIZES_OF = (128, 128, 128, 64, 64)


def params(mib, semantics=None):
    return pltpu.CompilerParams(vmem_limit_bytes=mib * MIB, dimension_semantics=semantics)


def cost(flops, nbytes, transcendentals=0):
    return pl.CostEstimate(
        flops=int(flops), bytes_accessed=int(nbytes), transcendentals=int(transcendentals)
    )


def fill(target, refs):
    start = 0
    for ref in refs:
        rows = ref.shape[0]
        target[start : start + rows, :] = ref[...]
        start += rows


def nn(a, b):
    return lax.dot_general(a, b, (((1,), (0,)), ((), ())), preferred_element_type=F32)


def nt(a, b):
    return lax.dot_general(a, b, (((1,), (1,)), ((), ())), preferred_element_type=F32)


def tn(a, b):
    return lax.dot_general(a, b, (((0,), (0,)), ((), ())), preferred_element_type=F32)


def later(kernel, count, lead=0):
    if not count:
        return kernel

    def wrapped(*refs):
        return kernel(*refs[:lead], *refs[lead + count :])

    return wrapped


def anywhere(after):
    return [pl.BlockSpec(memory_space=pl.ANY)] * len(after)


def whole(shape):
    return pl.BlockSpec(shape, lambda *_: (0,) * len(shape))


PIECES = [whole((rows, 1536)) for rows in SIZES_OF]
PARTIAL_SHAPES = [
    jax.ShapeDtypeStruct((128, 1536), F32),
    jax.ShapeDtypeStruct((128, 1536), F32),
    jax.ShapeDtypeStruct((128, 1536), F32),
    jax.ShapeDtypeStruct((128, 1536), BF16),
]
LOW_PARTIAL_SHAPES = PARTIAL_SHAPES[:1] + [jax.ShapeDtypeStruct((128, 1536), BF16)] * 3
PARTIALS = [whole((128, 1536))] * 4


def emit(total, outs):
    for place, out in enumerate(outs):
        out[...] = total[128 * place : 128 * (place + 1), :].astype(out.dtype)


def down_parts(block):
    left = block[:, 0:128, :].reshape(256, 1024)
    right = jnp.concatenate([block[:, 128:192, 0:512], block[:, 128:192, 512:1024]], axis=1)
    return left, right.reshape(256, 512)


def feed_forward_kernel(*refs):
    pieces, (wg, wu, wd), outs = refs[:5], refs[5:8], refs[8:12]
    gate, up, hidden, flat, total = refs[12:]
    step = pl.program_id(0)

    @pl.when(step == 0)
    def _():
        fill(flat, pieces)

    rows = flat[...]
    g = nn(rows, wg[...])
    u = nn(rows, wu[...])
    gate[...] = g
    up[...] = u
    h = (g * jax.nn.sigmoid(g) * u).astype(BF16)
    hidden[...] = h
    left, right = down_parts(wd[...])
    left, right = nn(h, left), nn(h, right)

    @pl.when(step == 0)
    def _():
        total[:, :1024] = left
        total[:, 1024:] = right

    @pl.when(step > 0)
    def _():
        total[:, :1024] += left
        total[:, 1024:] += right

    @pl.when(step == 3)
    def _():
        emit(total, outs)


def feed_specs():
    return [
        pl.BlockSpec((1536, 256), lambda b: (0, b)),
        pl.BlockSpec((1536, 256), lambda b: (0, 4 + b)),
        pl.BlockSpec((2, 192, 1024), lambda b: (b, 0, 2)),
    ]


def column_block(rows):
    return pl.BlockSpec((rows, 256), lambda b: (0, b))


def feed_forward_call(pieces, packed, after=()):
    flat_packed = packed.reshape(1536, -1)
    return pl.pallas_call(
        later(feed_forward_kernel, len(after)),
        grid=(4,),
        in_specs=anywhere(after) + PIECES + feed_specs(),
        out_specs=PARTIALS + [column_block(512)] * 3,
        out_shape=PARTIAL_SHAPES
        + [
            jax.ShapeDtypeStruct((512, 1024), F32),
            jax.ShapeDtypeStruct((512, 1024), F32),
            jax.ShapeDtypeStruct((512, 1024), BF16),
        ],
        scratch_shapes=[pltpu.VMEM((512, 1536), BF16), pltpu.VMEM((512, 1536), F32)],
        compiler_params=params(40),
        cost_estimate=cost(4.9e9, 18e6),
        name="feed_forward",
    )(*after, *pieces, flat_packed, flat_packed, packed)


def feed_backward_kernel(*refs):
    pieces, (wg, wu, wd, gate, up), outs = refs[:5], refs[5:10], refs[10:14]
    low_gate, low_up, flat, total = refs[14:]
    step = pl.program_id(0)

    @pl.when(step == 0)
    def _():
        fill(flat, pieces)

    rows = flat[...]
    left, right = down_parts(wd[...])
    grad = nt(rows[:, :1024], left) + nt(rows[:, 1024:], right)
    g = gate[...]
    s = jax.nn.sigmoid(g)
    a = (grad * up[...] * s * (1.0 + g * (1.0 - s))).astype(BF16)
    b = (grad * (g * s)).astype(BF16)
    low_gate[...] = a
    low_up[...] = b
    part = nt(a, wg[...]) + nt(b, wu[...])

    @pl.when(step == 0)
    def _():
        total[...] = part

    @pl.when(step > 0)
    def _():
        total[...] += part

    @pl.when(step == 3)
    def _():
        emit(total, outs)


def feed_backward_call(pieces, packed, gate, up, after=()):
    flat_packed = packed.reshape(1536, -1)
    return pl.pallas_call(
        later(feed_backward_kernel, len(after)),
        grid=(4,),
        in_specs=anywhere(after) + PIECES + feed_specs() + [column_block(512)] * 2,
        out_specs=PARTIALS + [column_block(512)] * 2,
        out_shape=LOW_PARTIAL_SHAPES + [jax.ShapeDtypeStruct((512, 1024), BF16)] * 2,
        scratch_shapes=[pltpu.VMEM((512, 1536), BF16), pltpu.VMEM((512, 1536), F32)],
        compiler_params=params(40),
        cost_estimate=cost(4.9e9, 20e6),
        name="feed_backward",
    )(*after, *pieces, flat_packed, flat_packed, packed, gate, up)


def feed_weights_kernel(*refs):
    flats, grads = refs[:5], refs[5:10]
    low_gate, low_up, hidden, out, flat_t, hidden_t, grad = refs[10:]
    step = pl.program_id(0)

    @pl.when(step == 0)
    def _():
        start = 0
        for ref in flats:
            n = ref.shape[0]
            flat_t[:, start : start + n] = ref[...].T
            start += n

    @pl.when(step == 4)
    def _():
        hidden_t[...] = hidden[...].T
        fill(grad, grads)

    @pl.when(step < 4)
    def _():
        out[...] = nn(flat_t[...], low_gate[...]).astype(BF16).reshape(8, 192, 256)

    @pl.when((step >= 4) & (step < 8))
    def _():
        out[...] = nn(flat_t[...], low_up[...]).astype(BF16).reshape(8, 192, 256)

    for q in range(4):

        @pl.when(step == 8 + q)
        def _():
            top = nn(hidden_t[...], grad[:, 256 * q : 256 * (q + 1)]).astype(BF16)
            out[:, 0:128, :] = top.reshape(8, 128, 256)
            half = 64 * (q // 2)
            some = hidden_t[...].reshape(8, 128, 512)[:, half : half + 64].reshape(512, 512)
            start = 1024 + 256 * (q % 2)
            low = nn(some, grad[:, start : start + 256]).astype(BF16)
            out[:, 128:192, :] = low.reshape(8, 64, 256)


def feed_weights_call(flats, grads, low_gate, low_up, hidden):
    return pl.pallas_call(
        feed_weights_kernel,
        grid=(12,),
        in_specs=PIECES
        + PIECES
        + [
            pl.BlockSpec((512, 256), lambda b: (0, jnp.minimum(b, 3))),
            pl.BlockSpec((512, 256), lambda b: (0, jnp.clip(b - 4, 0, 3))),
            whole((512, 1024)),
        ],
        out_specs=pl.BlockSpec((8, 192, 256), lambda b: (0, 0, b)),
        out_shape=jax.ShapeDtypeStruct((8, 192, 3072), BF16),
        scratch_shapes=[
            pltpu.VMEM((1536, 512), BF16),
            pltpu.VMEM((1024, 512), BF16),
            pltpu.VMEM((512, 1536), BF16),
        ],
        compiler_params=params(40),
        cost_estimate=cost(4.9e9, 18e6),
        name="feed_weights",
    )(*flats, *grads, low_gate, low_up, hidden)


def piece_specs(pieces):
    return [whole(item.shape) for item in pieces]


def turn_columns(block, cosine, sine):
    out = []
    for start in range(0, block.shape[1], HEAD_DIM):
        a = block[:, start : start + 48]
        b = block[:, start + 48 : start + HEAD_DIM]
        out.append(a * cosine - b * sine)
        out.append(b * cosine + a * sine)
    return jnp.concatenate(out, axis=1)


def project_kernel(raw, count, *refs):
    pieces, (gain, weight, cosine, sine, queries, pair) = refs[:count], refs[count : count + 6]
    if raw:
        flat = refs[-1]
        start = 0
        for ref in pieces:
            n = ref.shape[0]
            rows = ref[...].astype(F32)
            scale = lax.rsqrt(jnp.mean(rows * rows, axis=-1, keepdims=True) + 1e-05)
            flat[start : start + n, :] = (rows * scale * gain[...]).astype(BF16)
            start += n
    else:
        flat = refs[-1]
        fill(flat, pieces)
    both = nn(flat[...], weight[...])
    cos, sin = cosine[...], sine[...]
    queries[...] = turn_columns(both[:, :384], cos, sin).astype(BF16)
    keys = turn_columns(both[:, 384:576], cos, sin)
    pair[...] = jnp.concatenate([keys, both[:, 576:768]], axis=1).astype(BF16)


def project_call(raw, pieces, gain, packed, cosine, sine, after=()):
    wide = packed.shape[-1]
    shape = jax.ShapeDtypeStruct((512, 384), BF16)
    flat_shape = jax.ShapeDtypeStruct((512, 1536), BF16)
    return pl.pallas_call(
        later(functools.partial(project_kernel, raw, len(pieces)), len(after)),
        grid=(1,),
        in_specs=anywhere(after)
        + piece_specs(pieces)
        + [whole((1, 1536)), projection_spec(), whole((512, 48)), whole((512, 48))],
        out_specs=[whole((512, 384))] * 2 + ([whole((512, 1536))] if raw else []),
        out_shape=[shape, shape] + ([flat_shape] if raw else []),
        scratch_shapes=[] if raw else [pltpu.VMEM((512, 1536), BF16)],
        compiler_params=params(40),
        cost_estimate=cost(1.3e9, 6e6),
        name="project",
    )(*after, *pieces, gain.reshape(1, 1536), packed.reshape(1536, wide), cosine, sine)


def fill_bias(bias, length, places, key_places, window):
    gap = places[...] - key_places[...]
    inside = (key_places[...] < length) & (gap >= 0) & (gap < window)
    bias[...] = jnp.where(inside | (gap == 0), 0.0, NEGATIVE)


def both_rows(own, other, start):
    return jnp.concatenate(
        [own[:, start : start + HEAD_DIM], other[:, start : start + HEAD_DIM]], axis=0
    )


def attend_kernel(window, length, queries, own, other, places, key_places, w_out, *refs):
    outs, (mixed, log_total, total, bias) = refs[:4], refs[4:]
    fill_bias(bias, length[0], places, key_places, window)
    sums = []
    stats = []
    for head in range(4):
        if head % 2 == 0:
            keys = both_rows(own[...], other[...], HEAD_DIM * (head // 2))
            values = both_rows(own[...], other[...], 192 + HEAD_DIM * (head // 2)).T
        query = queries[:, HEAD_DIM * head : HEAD_DIM * (head + 1)]
        scores = nt(keys, query) * HEAD_DIM ** (-0.5) + bias[...]
        peak = jnp.max(scores, axis=0, keepdims=True)
        probs = jnp.exp(scores - peak)
        totals = jnp.sum(probs, axis=0, keepdims=True)
        part = nn(values, probs.astype(BF16)) / totals
        sums.append(part.astype(BF16).astype(F32).T.astype(BF16))
        stats.append(peak + jnp.log(totals))
        for block in range(4):
            cols = slice(384 * block, 384 * (block + 1))
            value = nn(sums[-1], out_block(w_out, head, block))
            if head == 0:
                total[:, cols] = value
            else:
                total[:, cols] += value
    mixed[...] = jnp.concatenate(sums, axis=1)
    log_total[...] = jnp.concatenate(stats + stats, axis=0)
    emit(total, outs)


def line_specs():
    return [whole((512, 384))] * 3 + [whole((1, 512)), whole((1024, 1))]


def out_spec():
    return pl.BlockSpec((8, 192, 384), lambda *_: (0, 0, 2))


def out_block(w_out, head, block):
    start = 96 * (head % 2)
    return w_out[2 * block + head // 2, start : start + 96, :]


def projection_spec():
    return pl.BlockSpec((1536, 768), lambda *_: (0, 0))


def attend_call(window, length, queries, own, other, places, key_places, packed, after=()):
    return pl.pallas_call(
        later(functools.partial(attend_kernel, window), len(after)),
        grid=(1,),
        in_specs=anywhere(after)
        + [pl.BlockSpec(memory_space=pltpu.SMEM)] + line_specs() + [out_spec()],
        out_specs=PARTIALS + [whole((512, 384)), whole((8, 512))],
        out_shape=PARTIAL_SHAPES
        + [jax.ShapeDtypeStruct((512, 384), BF16), jax.ShapeDtypeStruct((8, 512), F32)],
        scratch_shapes=[pltpu.VMEM((512, 1536), F32), pltpu.VMEM((1024, 512), F32)],
        compiler_params=params(48),
        cost_estimate=cost(3e9, 6e6, 2e6),
        name="attend",
    )(*after, length, queries, own, other, places, key_places, packed)


def attend_backward_kernel(window, length, *refs):
    pieces, refs = refs[:5], refs[5:]
    queries, own, other, places, key_places, w_out, log_total, cosine, sine = refs[:9]
    low_queries, pair_own, pair_other, grad, bias = refs[9:]
    fill(grad, pieces)
    fill_bias(bias, length[0], places, key_places, window)
    cos, sin = cosine[...], sine[...]
    lows = []
    key_sums = []
    value_sums = []
    for head in range(4):
        if head % 2 == 0:
            keys = both_rows(own[...], other[...], HEAD_DIM * (head // 2))
            values = both_rows(own[...], other[...], 192 + HEAD_DIM * (head // 2))
            keys_t = keys.T
        query = queries[:, HEAD_DIM * head : HEAD_DIM * (head + 1)]
        mixed = nt(grad[:, :384], out_block(w_out, head, 0))
        for block in range(1, 4):
            mixed += nt(
                grad[:, 384 * block : 384 * (block + 1)], out_block(w_out, head, block)
            )
        mixed = mixed.astype(BF16)
        scores = nt(keys, query) * HEAD_DIM ** (-0.5) + bias[...]
        probs = jnp.exp(scores - log_total[head : head + 1, :])
        slopes = nt(values, mixed)
        inner = jnp.sum(probs * slopes, axis=0, keepdims=True)
        raw = (probs * (slopes - inner) * HEAD_DIM ** (-0.5)).astype(BF16)
        key_part = nn(raw, query)
        value_part = nn(probs.astype(BF16), mixed)
        if head % 2 == 0:
            key_sums.append(key_part)
            value_sums.append(value_part)
        else:
            key_sums[-1] += key_part
            value_sums[-1] += value_part
        turned = nn(keys_t, raw)
        a, b = turned[:48], turned[48:]
        turned = jnp.concatenate([a * cos + b * sin, b * cos - a * sin], axis=0)
        lows.append(turned.T.astype(BF16))
    low_queries[...] = jnp.concatenate(lows, axis=1)
    both = jnp.concatenate(key_sums + value_sums, axis=1)
    pair_own[...] = both[:512]
    pair_other[...] = both[512:].astype(BF16)


def attend_backward_call(
    window,
    length,
    pieces,
    queries,
    own,
    other,
    places,
    key_places,
    packed,
    log_total,
    cosine,
    sine,
    after=(),
):
    return pl.pallas_call(
        later(functools.partial(attend_backward_kernel, window), len(after)),
        grid=(1,),
        in_specs=anywhere(after)
        + [pl.BlockSpec(memory_space=pltpu.SMEM)]
        + PIECES
        + line_specs()
        + [out_spec(), whole((8, 512)), whole((48, 512)), whole((48, 512))],
        out_specs=[whole((512, 384))] * 3,
        out_shape=[
            jax.ShapeDtypeStruct((512, 384), BF16),
            jax.ShapeDtypeStruct((512, 384), F32),
            jax.ShapeDtypeStruct((512, 384), BF16),
        ],
        scratch_shapes=[pltpu.VMEM((512, 1536), BF16), pltpu.VMEM((1024, 512), F32)],
        compiler_params=params(52),
        cost_estimate=cost(6e9, 6e6, 2e6),
        name="attend_backward",
    )(
        *after,
        length,
        *pieces,
        queries,
        own,
        other,
        places,
        key_places,
        packed,
        log_total,
        cosine,
        sine,
    )


def unproject_kernel(low_queries, pair_own, pair_came, cosine, sine, weight, *refs):
    outs, low = refs[:4], refs[4]
    both = pair_own[...] + pair_came[...].astype(F32)
    keys = turn_columns(both[:, :192], cosine[...], -sine[...])
    rows = jnp.concatenate(
        [low_queries[...], keys.astype(BF16), both[:, 192:].astype(BF16)], axis=1
    )
    low[...] = rows
    emit(nt(rows, weight[...]), outs)


def unproject_call(low_queries, pair_own, pair_came, cosine, sine, packed, after=()):
    wide = packed.shape[-1]
    return pl.pallas_call(
        later(unproject_kernel, len(after)),
        grid=(1,),
        in_specs=anywhere(after)
        + [whole((512, 384))] * 3
        + [whole((512, 48))] * 2
        + [projection_spec()],
        out_specs=PARTIALS + [whole((512, 768))],
        out_shape=LOW_PARTIAL_SHAPES + [jax.ShapeDtypeStruct((512, 768), BF16)],
        compiler_params=params(40),
        cost_estimate=cost(1.3e9, 7e6),
        name="unproject",
    )(*after, low_queries, pair_own, pair_came, cosine, sine, packed.reshape(1536, wide))


def attend_weights_kernel(count, *refs):
    flats, grads, (low, mixed) = refs[:count], refs[count : count + 5], refs[count + 5 : count + 7]
    out, flat_t, grad = refs[count + 7 :]
    start = 0
    for ref in flats:
        n = ref.shape[0]
        flat_t[:, start : start + n] = ref[...].T
        start += n
    fill(grad, grads)
    for block in range(3):
        cols = slice(256 * block, 256 * (block + 1))
        out[:, :, cols] = nn(flat_t[...], low[:, cols]).astype(BF16).reshape(8, 192, 256)
    mixed_t = mixed[...].T
    for block in range(4):
        part = nn(mixed_t, grad[:, 384 * block : 384 * (block + 1)]).astype(BF16)
        out[2 * block : 2 * block + 2, :, 768:1152] = part.reshape(2, 192, 384)


def attend_weights_call(flats, grads, low, mixed):
    return pl.pallas_call(
        functools.partial(attend_weights_kernel, len(flats)),
        grid=(1,),
        in_specs=piece_specs(flats) + PIECES + [whole((512, 768)), whole((512, 384))],
        out_specs=whole((8, 192, 1152)),
        out_shape=jax.ShapeDtypeStruct((8, 192, 1152), BF16),
        scratch_shapes=[pltpu.VMEM((1536, 512), BF16), pltpu.VMEM((512, 1536), BF16)],
        compiler_params=params(40),
        cost_estimate=cost(1.9e9, 10e6),
        name="attend_weights",
    )(*flats, *grads, low, mixed)


def unpack_kernel(*refs):
    every, wq, wk, wv, wo, gate, up, down = refs
    side = pl.program_id(0)
    blocks = [every[x, 0] for x in range(4)]
    for x, block in enumerate(blocks):
        wq[:, 384 * x : 384 * (x + 1)] = block[:, 3072:3456].astype(F32)
        wo[:, 384 * x : 384 * (x + 1)] = block[:, 3840:4224].astype(F32)
        for s in range(8):
            cols = slice(512 * s + 128 * x, 512 * s + 128 * (x + 1))
            gate[:, cols] = block[:, 128 * s : 128 * (s + 1)].astype(F32)
            up[:, cols] = block[:, 1024 + 128 * s : 1024 + 128 * (s + 1)].astype(F32)

        @pl.when(side == 0)
        def _(x=x, block=block):
            down[x, 0:96, :1024] = block[:, 2048:3072].astype(F32)

        @pl.when(side == 1)
        def _(x=x, block=block):
            down[x, 96:128, :1024] = block[0:32, 2048:3072].astype(F32)
            down[x, 0:64, 1024:] = block[32:96, 2048:2560].astype(F32)
            down[x, 64:128, 1024:] = block[32:96, 2560:3072].astype(F32)

    wk[...] = jnp.concatenate([block[:, 3456:3648].astype(F32) for block in blocks], axis=1)
    wv[...] = jnp.concatenate([block[:, 3648:3840].astype(F32) for block in blocks], axis=1)


def unpack_call(every):
    widths = (1536, 768, 768, 1536, 4096, 4096)
    out = pl.pallas_call(
        unpack_kernel,
        grid=(2,),
        in_specs=[pl.BlockSpec((4, 1, 96, 4224), lambda b: (0, b, 0, 0))],
        out_specs=[pl.BlockSpec((96, width), lambda b: (b, 0)) for width in widths]
        + [whole((4, 128, 1536))],
        out_shape=[jax.ShapeDtypeStruct((192, width), F32) for width in widths]
        + [jax.ShapeDtypeStruct((4, 128, 1536), F32)],
        compiler_params=params(48),
        cost_estimate=cost(1e6, 30e6),
        name="unpack",
    )(every)
    return out[:4], (out[4], out[5], out[6].reshape(512, 1536))


def pack_feed_kernel(where, w_gate, w_up, w_down, out):
    x = where[0]
    for s in range(8):
        cols = pl.ds(pl.multiple_of(512 * s + 128 * x, 128), 128)
        out[:, 128 * s : 128 * (s + 1)] = w_gate[:, cols]
        out[:, 1024 + 128 * s : 1024 + 128 * (s + 1)] = w_up[:, cols]
    out[0:128, 2048:3072] = w_down[:, 0:1024]
    out[128:192, 2048:2560] = w_down[0:64, 1024:1536]
    out[128:192, 2560:3072] = w_down[64:128, 1024:1536]


def pack_feed_call(where, w_gate, w_up, w_down, after=()):
    return pl.pallas_call(
        later(pack_feed_kernel, len(after), 1),
        grid_spec=pltpu.PrefetchScalarGridSpec(
            num_scalar_prefetch=1,
            grid=(1,),
            in_specs=anywhere(after)
            + [
                pl.BlockSpec((192, 4096), lambda b, w: (0, 0)),
                pl.BlockSpec((192, 4096), lambda b, w: (0, 0)),
                pl.BlockSpec((128, 1536), lambda b, w: (w[0], 0)),
            ],
            out_specs=pl.BlockSpec((192, 3072), lambda b, w: (0, 0)),
        ),
        out_shape=jax.ShapeDtypeStruct((192, 3072), BF16),
        compiler_params=params(24),
        cost_estimate=cost(1e3, 5e6),
        name="pack_feed",
    )(where, *after, w_gate, w_up, w_down)


WINDOW = 512
EPSILON = 1e-05
ROPE_BASE = 100000.0

AXES = ("ylo", "x", "core", "z", "yhi")
SIZES = (2, 4, 2, 4, 2)
REP = ("ylo", "x", "core")
SHARD = ("z", "yhi")
SPREAD = ("z", "core")

RIGHT = [(i, (i + 1) % 4) for i in range(4)]
LEFT = [(i, (i - 1) % 4) for i in range(4)]
ACROSS = [(i, (i + 2) % 4) for i in range(4)]
SWAP = [(0, 1), (1, 0)]


def number(ylo, x, core, z, yhi):
    return (((ylo * 4 + x) * 2 + core) * 4 + z) * 2 + yhi


def permutation(place, taken=None):
    pairs = []
    for ylo in range(2):
        for x in range(4):
            for core in range(2):
                for z in range(4):
                    for yhi in range(2):
                        here = (ylo, x, core, z, yhi)
                        if taken is None or taken(*here):
                            pairs.append((number(*here), number(*place(*here))))
    return pairs


def inverse(pairs):
    return [(there, here) for here, there in pairs]


def at_home(ylo, x, core, z, yhi):
    return core == yhi


def not_home(*place):
    return not at_home(*place)


LINES = [
    permutation(lambda l, x, c, z, h, k=k: (l, (z + k) % 4, h, x, c)) for k in range(4)
]
TURN = permutation(lambda l, x, c, z, h: (l, z, h, x, c))
SHARE = permutation(lambda l, x, c, z, h: (l, x, c, z, 1 - h), at_home)
COLLECT = permutation(lambda l, x, c, z, h: (l, x, c, z, 1 - h), not_home)
BESIDE = permutation(lambda l, x, c, z, h: (1 - l, x, c, z, h), at_home)
CROSS = permutation(lambda l, x, c, z, h: (l, z, c, x, h), at_home)


def to_lines(block, z):
    part = block.shape[0] // 4
    out = []
    for k in range(4):
        piece = lax.dynamic_slice_in_dim(block, ((z + k) % 4) * part, part, axis=0)
        out.append(lax.ppermute(piece, AXES, LINES[k]))
    return out


def from_lines(block, z):
    part = block.shape[0] // 4
    out = jnp.zeros_like(block)
    for k in range(4):
        piece = lax.ppermute(block[part * k : part * (k + 1)], AXES, inverse(LINES[k]))
        out = lax.dynamic_update_slice_in_dim(out, piece, ((z + k) % 4) * part, axis=0)
    return out


def interleave(first, second):
    parts = [item[32 * k : 32 * (k + 1)] for k in range(4) for item in (first, second)]
    return jnp.concatenate(parts, axis=0)


def separate(block):
    parts = [block[32 * k : 32 * (k + 1)] for k in range(8)]
    return jnp.concatenate(parts[::2], axis=0), jnp.concatenate(parts[1::2], axis=0)


def ring_gather(block):
    half = block.shape[0] // 2
    from_left = lax.ppermute(block, "x", RIGHT)
    from_right = lax.ppermute(block, "x", LEFT)
    far_first = lax.ppermute(from_left[:half], "x", RIGHT)
    far_second = lax.ppermute(from_right[half:], "x", LEFT)
    return block, from_left, from_right, far_first, far_second


def ring_scatter(own, left, right, far):
    half = far.shape[0] // 2
    first = lax.ppermute(far[:half], "x", RIGHT).astype(F32)
    second = lax.ppermute(far[half:], "x", LEFT).astype(F32)
    right = jnp.concatenate([right[:half] + first, right[half:]], axis=0).astype(BF16)
    left = jnp.concatenate([left[:half], left[half:] + second], axis=0).astype(BF16)
    from_left = lax.ppermute(right, "x", RIGHT).astype(F32)
    from_right = lax.ppermute(left, "x", LEFT).astype(F32)
    return own + from_left + from_right


def ring_scatter_direct(own, left, right, far):
    from_left = lax.ppermute(right, "x", RIGHT).astype(F32)
    from_right = lax.ppermute(left, "x", LEFT).astype(F32)
    from_far = lax.ppermute(far, "x", ACROSS).astype(F32)
    return own + from_left + from_right + from_far


def tie(value, *others):
    return lax.optimization_barrier((value, *others))[0]


def rms_norm(values, gain):
    return values * lax.rsqrt(jnp.mean(values * values, axis=-1, keepdims=True) + EPSILON) * gain


def add_low(mine, came):
    return (mine.astype(F32) + came.astype(F32)).astype(BF16)


def home_sum(rows):
    return add_low(rows, lax.ppermute(rows, AXES, COLLECT))


def home_piece(rows, core, yhi):
    rows = add_low(rows, lax.ppermute(rows, AXES, BESIDE))
    moved = lax.ppermute(rows[:, 3840:], AXES, CROSS)
    rows = jnp.concatenate([rows[:, :3840], moved], axis=1)
    theirs = lax.dynamic_slice_in_dim(rows, 96 * (1 - core), 96, axis=0)
    mine = lax.dynamic_slice_in_dim(rows, 96 * core, 96, axis=0)
    return jnp.where(core == yhi, mine, lax.ppermute(theirs, "core", SWAP))


def butterfly(values):
    for axis, size in (("core", 2), ("x", 4), ("z", 4), ("yhi", 2), ("ylo", 2)):
        step = 1
        while step < size:
            pairs = [(i, i ^ step) for i in range(size)]
            values = values + lax.ppermute(values, axis, pairs)
            step *= 2
    return values


def norm_back(grad, own_normed, state, gain):
    grad_state, grad_gain = jax.vjp(rms_norm, state, gain)[1](own_normed)
    return grad + grad_state, grad_gain


def body(tokens, lengths, grad_output, *weights):
    stretch, width = tokens.shape[1:]
    x = lax.axis_index("x")
    core = lax.axis_index("core")
    z = lax.axis_index("z")
    yhi = lax.axis_index("yhi")
    member = x.astype(jnp.int32).reshape(1)
    home = core == yhi

    gains = jnp.stack([weights[0], weights[5], weights[9], weights[14]]).T
    gains = jnp.pad(gains, ((0, 0), (0, 124)))

    def weight_parts(base, extra, after, joined):
        block = lax.dynamic_slice(tie(weights[base + 4], *after), (0, 384 * x), (192, 384))
        block = lax.ppermute(block, AXES, TURN)
        parts = [
            lax.dynamic_slice(w, (0, x * (w.shape[1] // 4)), (192, w.shape[1] // 4))
            for w in weights[base + 1 : base + 4]
        ]
        parts += [pack_feed_call(member, *weights[base + 6 : base + 9], after=after)]
        parts = jnp.concatenate(parts + extra, axis=1)
        came = tie(lax.ppermute(parts, AXES, SHARE), *joined)
        parts = jnp.where(home, parts, came)
        attn = jnp.concatenate([parts[:, :768], block, parts[:, 3840:]], axis=1)
        return attn, parts[:, 768:3840]

    def line_weights(piece, *after):
        return lax.all_gather(tie(piece, *after), SPREAD, axis=0, tiled=False)

    here = (2 * z + yhi) * stretch + jnp.arange(stretch, dtype=jnp.int32)
    valid = (here < lengths[0])[:, None]
    grad_start = jnp.where(valid, grad_output[0], 0).astype(BF16)
    length = lax.ppermute(lengths, AXES, TURN)
    moved = to_lines(interleave(tokens[0], grad_start), z)
    rows, grad_rows = separate(jnp.concatenate(moved, axis=0))

    attn_one, feed_one = weight_parts(0, [gains], (), moved)
    attn_one = line_weights(attn_one)
    gains = attn_one[:, :, 1152:1156].transpose(2, 0, 1).reshape(4, width).astype(F32)
    pieces = ring_gather(rows)
    state = rows.astype(F32)
    feed_one = line_weights(feed_one, *pieces[3:])
    grad_pieces = ring_gather(grad_rows)
    grad = grad_rows.astype(F32)

    part = stretch // 4

    def member_places(member, side_index):
        block = jnp.arange(4, dtype=jnp.int32)
        inner = jnp.arange(part, dtype=jnp.int32)
        home = (member - block + 4) % 4
        return (
            home[:, None] * (2 * stretch) + side_index * stretch + member * part + inner[None, :]
        ).reshape(-1)

    def line_places(side_index):
        return jnp.concatenate([member_places((x + step) % 4, side_index) for step in (0, 3, 1, 2)])

    places = line_places(core)
    key_places = jnp.concatenate([places, line_places(1 - core)]).reshape(1024, 1)
    half = HEAD_DIM // 2
    freq = ROPE_BASE ** (-jnp.arange(half, dtype=F32) * (2.0 / HEAD_DIM))
    angle = places.astype(F32)[:, None] * freq[None, :]
    cosine, sine = jnp.cos(angle), jnp.sin(angle)
    cosine_t, sine_t = cosine.T, sine.T
    places = places.reshape(1, 512)

    records = []
    for index, window in enumerate((WINDOW, 8 * stretch)):
        if index == 0:
            attn, feed = attn_one, feed_one
        else:
            attn, feed = attn_two, feed_two
        gain_attn, gain_feed = gains[2 * index], gains[2 * index + 1]
        if index == 0:
            queries, own, flat = project_call(True, pieces, gain_attn, attn, cosine, sine)
            flats = (flat,)
        else:
            flats = ring_gather(rms_norm(state, gain_attn).astype(BF16))
            feed_two = feed = line_weights(feed_two, *flats[3:])
            queries, own = project_call(False, flats, gain_attn, attn, cosine, sine)
        other = lax.ppermute(own, "core", SWAP)
        line = (queries, own, other, places, key_places)
        after = grad_pieces[3:] if index else ()
        *partial, mixed, log_total = attend_call(window, length, *line, attn, after=after)
        saved_attn = (state, flats, line, mixed, log_total)
        state = state + ring_scatter(*partial)
        if index == 0:
            attn_two, feed_two = weight_parts(9, [], (mixed,), ())
        flats = ring_gather(rms_norm(state, gain_feed).astype(BF16))
        if index == 0:
            attn_two = line_weights(attn_two, *flats[3:])
        *partial, gate, up, hidden = feed_forward_call(flats, feed)
        saved_feed = (state, flats, gate, up, hidden)
        state = state + ring_scatter(*partial)
        records.append((saved_attn, saved_feed, window))
    last_rows = state.astype(BF16)
    packed = ((attn_one, feed_one), (attn_two, feed_two))

    results = [None] * 18
    gain_grads = [None] * 4

    def feed_back(index, grad, pieces, after):
        state, flats, gate, up, hidden = records[index][1]
        *partial, low_gate, low_up = feed_backward_call(
            pieces, packed[index][1], gate, up, after=after
        )
        own_normed = ring_scatter_direct(*partial)
        grad, gain_grads[2 * index + 1] = norm_back(
            grad, own_normed, state, gains[2 * index + 1]
        )
        return grad, feed_weights_call(flats, pieces, low_gate, low_up, hidden)

    def attention_back(index, grad, pieces, after, late):
        state, flats, line, mixed, log_total = records[index][0]
        window = records[index][2]
        attn = packed[index][0]
        low_queries, pair_own, pair_other = attend_backward_call(
            window, length, pieces, *line, attn, log_total, cosine_t, sine_t, after=after
        )
        came = lax.ppermute(pair_other, "core", SWAP)
        *partial, low = unproject_call(
            low_queries, pair_own, came, cosine, sine, attn, after=late
        )
        own_normed = ring_scatter_direct(*partial)
        grad, gain_grads[2 * index] = norm_back(grad, own_normed, state, gains[2 * index])
        return grad, attend_weights_call(flats, pieces, low, mixed)

    def scatter(block, *others):
        return lax.psum_scatter(
            tie(block, *others), SPREAD, scatter_dimension=0, tiled=True
        )[0]

    grad, feed_grad = feed_back(1, grad, grad_pieces, ())
    low = tie(grad.astype(BF16), feed_grad)
    second_feed = scatter(feed_grad, low)
    grad, attn_grad = attention_back(1, grad, ring_gather(low), (last_rows,), ())
    low = tie(grad.astype(BF16), attn_grad)
    second_attn = scatter(attn_grad, low, second_feed)

    grad, feed_grad = feed_back(0, grad, ring_gather(low), (second_feed,))
    low = tie(grad.astype(BF16), feed_grad)
    first_feed = scatter(feed_grad, low, second_attn)
    second = home_sum(jnp.concatenate([second_feed, second_attn], axis=1))
    grad, attn_grad = attention_back(0, grad, ring_gather(low), (), (second,))
    low = grad.astype(BF16)
    first_attn = scatter(attn_grad, first_feed, low)
    second_piece = home_piece(second, core, yhi)
    gain_sums = butterfly(jnp.stack(gain_grads))
    back = from_lines(interleave(last_rows, low), z)
    output, input_grad = separate(back)
    output, input_grad = output[None], input_grad.astype(F32)[None]

    every = lax.all_gather(tie(second_piece, first_attn), ("x", "core"), axis=0, tiled=False)
    results[10:14], results[15:18] = unpack_call(every.reshape(4, 2, 96, -1))
    first = jnp.concatenate([first_feed, first_attn], axis=1)
    first_piece = home_piece(home_sum(tie(first, gain_sums, back)), core, yhi)
    every = lax.all_gather(first_piece, ("x", "core"), axis=0, tiled=False)
    results[1:5], results[6:9] = unpack_call(every.reshape(4, 2, 96, -1))
    gain_sums = lax.dynamic_slice_in_dim(gain_sums, (2 * z + yhi) * 192, 192, axis=1)
    for index, slot in enumerate((0, 5, 9, 14)):
        results[slot] = gain_sums[index]
    return (output, input_grad, *results)


def solution(mesh):
    fine = Mesh(mesh.devices.reshape(SIZES), AXES)
    token = P(REP, SHARD, None)
    vector = P(SHARD)
    matrix = P(SHARD, None)
    layer = (vector, matrix, matrix, matrix, matrix, vector, matrix, matrix, matrix)
    return jax.shard_map(
        body,
        mesh=fine,
        in_specs=(token, P(REP), token) + layer + layer,
        out_specs=(token, token) + layer + layer,
        check_vma=False,
    )
```

```python
import functools
import jax
import jax.numpy as jnp
from jax import lax
from jax.experimental import pallas as pl
from jax.experimental.pallas import tpu as pltpu
from jax.sharding import Mesh
from jax.sharding import PartitionSpec as P

F32 = jnp.float32
BF16 = jnp.bfloat16
HEAD_DIM = 96
NEGATIVE = -1e30
MIB = 1 << 20

OFFSETS = (0, 128, 256, 384, 448)
SIZES_OF = (128, 128, 128, 64, 64)


def params(mib, semantics=None):
    return pltpu.CompilerParams(vmem_limit_bytes=mib * MIB, dimension_semantics=semantics)


def cost(flops, nbytes, transcendentals=0):
    return pl.CostEstimate(
        flops=int(flops), bytes_accessed=int(nbytes), transcendentals=int(transcendentals)
    )


def fill(target, refs):
    start = 0
    for ref in refs:
        rows = ref.shape[0]
        target[start : start + rows, :] = ref[...]
        start += rows


def nn(a, b):
    return lax.dot_general(a, b, (((1,), (0,)), ((), ())), preferred_element_type=F32)


def nt(a, b):
    return lax.dot_general(a, b, (((1,), (1,)), ((), ())), preferred_element_type=F32)


def tn(a, b):
    return lax.dot_general(a, b, (((0,), (0,)), ((), ())), preferred_element_type=F32)


def later(kernel, count, lead=0):
    if not count:
        return kernel

    def wrapped(*refs):
        return kernel(*refs[:lead], *refs[lead + count :])

    return wrapped


def anywhere(after):
    return [pl.BlockSpec(memory_space=pl.ANY)] * len(after)


def whole(shape):
    return pl.BlockSpec(shape, lambda *_: (0,) * len(shape))


PIECES = [whole((rows, 1536)) for rows in SIZES_OF]
PARTIAL_SHAPES = [
    jax.ShapeDtypeStruct((128, 1536), F32),
    jax.ShapeDtypeStruct((128, 1536), F32),
    jax.ShapeDtypeStruct((128, 1536), F32),
    jax.ShapeDtypeStruct((128, 1536), BF16),
]
LOW_PARTIAL_SHAPES = PARTIAL_SHAPES[:1] + [jax.ShapeDtypeStruct((128, 1536), BF16)] * 3
PARTIALS = [whole((128, 1536))] * 4


def emit(total, outs):
    for place, out in enumerate(outs):
        out[...] = total[128 * place : 128 * (place + 1), :].astype(out.dtype)


def down_parts(block):
    left = block[:, 0:128, :].reshape(256, 1024)
    right = jnp.concatenate([block[:, 128:192, 0:512], block[:, 128:192, 512:1024]], axis=1)
    return left, right.reshape(256, 512)


def feed_forward_kernel(*refs):
    pieces, (wg, wu, wd), outs = refs[:5], refs[5:8], refs[8:12]
    gate, up, hidden, flat, total = refs[12:]
    step = pl.program_id(0)

    @pl.when(step == 0)
    def _():
        fill(flat, pieces)

    rows = flat[...]
    g = nn(rows, wg[...])
    u = nn(rows, wu[...])
    gate[...] = g
    up[...] = u
    h = (g * jax.nn.sigmoid(g) * u).astype(BF16)
    hidden[...] = h
    left, right = down_parts(wd[...])
    left, right = nn(h, left), nn(h, right)

    @pl.when(step == 0)
    def _():
        total[:, :1024] = left
        total[:, 1024:] = right

    @pl.when(step > 0)
    def _():
        total[:, :1024] += left
        total[:, 1024:] += right

    @pl.when(step == 3)
    def _():
        emit(total, outs)


def feed_specs():
    return [
        pl.BlockSpec((1536, 256), lambda b: (0, b)),
        pl.BlockSpec((1536, 256), lambda b: (0, 4 + b)),
        pl.BlockSpec((2, 192, 1024), lambda b: (b, 0, 2)),
    ]


def column_block(rows):
    return pl.BlockSpec((rows, 256), lambda b: (0, b))


def feed_forward_call(pieces, packed, after=()):
    flat_packed = packed.reshape(1536, -1)
    return pl.pallas_call(
        later(feed_forward_kernel, len(after)),
        grid=(4,),
        in_specs=anywhere(after) + PIECES + feed_specs(),
        out_specs=PARTIALS + [column_block(512)] * 3,
        out_shape=PARTIAL_SHAPES
        + [
            jax.ShapeDtypeStruct((512, 1024), F32),
            jax.ShapeDtypeStruct((512, 1024), F32),
            jax.ShapeDtypeStruct((512, 1024), BF16),
        ],
        scratch_shapes=[pltpu.VMEM((512, 1536), BF16), pltpu.VMEM((512, 1536), F32)],
        compiler_params=params(40),
        cost_estimate=cost(4.9e9, 18e6),
        name="feed_forward",
    )(*after, *pieces, flat_packed, flat_packed, packed)


def feed_backward_kernel(*refs):
    pieces, (wg, wu, wd, gate, up), outs = refs[:5], refs[5:10], refs[10:14]
    low_gate, low_up, flat, total = refs[14:]
    step = pl.program_id(0)

    @pl.when(step == 0)
    def _():
        fill(flat, pieces)

    rows = flat[...]
    left, right = down_parts(wd[...])
    grad = nt(rows[:, :1024], left) + nt(rows[:, 1024:], right)
    g = gate[...]
    s = jax.nn.sigmoid(g)
    a = (grad * up[...] * s * (1.0 + g * (1.0 - s))).astype(BF16)
    b = (grad * (g * s)).astype(BF16)
    low_gate[...] = a
    low_up[...] = b
    part = nt(a, wg[...]) + nt(b, wu[...])

    @pl.when(step == 0)
    def _():
        total[...] = part

    @pl.when(step > 0)
    def _():
        total[...] += part

    @pl.when(step == 3)
    def _():
        emit(total, outs)


def feed_backward_call(pieces, packed, gate, up, after=()):
    flat_packed = packed.reshape(1536, -1)
    return pl.pallas_call(
        later(feed_backward_kernel, len(after)),
        grid=(4,),
        in_specs=anywhere(after) + PIECES + feed_specs() + [column_block(512)] * 2,
        out_specs=PARTIALS + [column_block(512)] * 2,
        out_shape=LOW_PARTIAL_SHAPES + [jax.ShapeDtypeStruct((512, 1024), BF16)] * 2,
        scratch_shapes=[pltpu.VMEM((512, 1536), BF16), pltpu.VMEM((512, 1536), F32)],
        compiler_params=params(40),
        cost_estimate=cost(4.9e9, 20e6),
        name="feed_backward",
    )(*after, *pieces, flat_packed, flat_packed, packed, gate, up)


def feed_weights_kernel(*refs):
    flats, grads = refs[:5], refs[5:10]
    low_gate, low_up, hidden, out, flat_t, hidden_t, grad = refs[10:]
    step = pl.program_id(0)

    @pl.when(step == 0)
    def _():
        start = 0
        for ref in flats:
            n = ref.shape[0]
            flat_t[:, start : start + n] = ref[...].T
            start += n

    @pl.when(step == 4)
    def _():
        hidden_t[...] = hidden[...].T
        fill(grad, grads)

    @pl.when(step < 4)
    def _():
        out[...] = nn(flat_t[...], low_gate[...]).astype(BF16).reshape(8, 192, 256)

    @pl.when((step >= 4) & (step < 8))
    def _():
        out[...] = nn(flat_t[...], low_up[...]).astype(BF16).reshape(8, 192, 256)

    for q in range(4):

        @pl.when(step == 8 + q)
        def _():
            top = nn(hidden_t[...], grad[:, 256 * q : 256 * (q + 1)]).astype(BF16)
            out[:, 0:128, :] = top.reshape(8, 128, 256)
            half = 64 * (q // 2)
            some = hidden_t[...].reshape(8, 128, 512)[:, half : half + 64].reshape(512, 512)
            start = 1024 + 256 * (q % 2)
            low = nn(some, grad[:, start : start + 256]).astype(BF16)
            out[:, 128:192, :] = low.reshape(8, 64, 256)


def feed_weights_call(flats, grads, low_gate, low_up, hidden):
    return pl.pallas_call(
        feed_weights_kernel,
        grid=(12,),
        in_specs=PIECES
        + PIECES
        + [
            pl.BlockSpec((512, 256), lambda b: (0, jnp.minimum(b, 3))),
            pl.BlockSpec((512, 256), lambda b: (0, jnp.clip(b - 4, 0, 3))),
            whole((512, 1024)),
        ],
        out_specs=pl.BlockSpec((8, 192, 256), lambda b: (0, 0, b)),
        out_shape=jax.ShapeDtypeStruct((8, 192, 3072), BF16),
        scratch_shapes=[
            pltpu.VMEM((1536, 512), BF16),
            pltpu.VMEM((1024, 512), BF16),
            pltpu.VMEM((512, 1536), BF16),
        ],
        compiler_params=params(40),
        cost_estimate=cost(4.9e9, 18e6),
        name="feed_weights",
    )(*flats, *grads, low_gate, low_up, hidden)


def piece_specs(pieces):
    return [whole(item.shape) for item in pieces]


def turn_columns(block, cosine, sine):
    out = []
    for start in range(0, block.shape[1], HEAD_DIM):
        a = block[:, start : start + 48]
        b = block[:, start + 48 : start + HEAD_DIM]
        out.append(a * cosine - b * sine)
        out.append(b * cosine + a * sine)
    return jnp.concatenate(out, axis=1)


def project_kernel(raw, count, *refs):
    pieces, (gain, weight, cosine, sine, queries, pair) = refs[:count], refs[count : count + 6]
    if raw:
        flat = refs[-1]
        start = 0
        for ref in pieces:
            n = ref.shape[0]
            rows = ref[...].astype(F32)
            scale = lax.rsqrt(jnp.mean(rows * rows, axis=-1, keepdims=True) + 1e-05)
            flat[start : start + n, :] = (rows * scale * gain[...]).astype(BF16)
            start += n
    else:
        flat = refs[-1]
        fill(flat, pieces)
    both = nn(flat[...], weight[...])
    cos, sin = cosine[...], sine[...]
    queries[...] = turn_columns(both[:, :384], cos, sin).astype(BF16)
    keys = turn_columns(both[:, 384:576], cos, sin)
    pair[...] = jnp.concatenate([keys, both[:, 576:768]], axis=1).astype(BF16)


def project_call(raw, pieces, gain, packed, cosine, sine, after=()):
    wide = packed.shape[-1]
    shape = jax.ShapeDtypeStruct((512, 384), BF16)
    flat_shape = jax.ShapeDtypeStruct((512, 1536), BF16)
    return pl.pallas_call(
        later(functools.partial(project_kernel, raw, len(pieces)), len(after)),
        grid=(1,),
        in_specs=anywhere(after)
        + piece_specs(pieces)
        + [whole((1, 1536)), projection_spec(), whole((512, 48)), whole((512, 48))],
        out_specs=[whole((512, 384))] * 2 + ([whole((512, 1536))] if raw else []),
        out_shape=[shape, shape] + ([flat_shape] if raw else []),
        scratch_shapes=[] if raw else [pltpu.VMEM((512, 1536), BF16)],
        compiler_params=params(40),
        cost_estimate=cost(1.3e9, 6e6),
        name="project",
    )(*after, *pieces, gain.reshape(1, 1536), packed.reshape(1536, wide), cosine, sine)


def fill_bias(bias, length, places, key_places, window):
    gap = places[...] - key_places[...]
    inside = (key_places[...] < length) & (gap >= 0) & (gap < window)
    bias[...] = jnp.where(inside | (gap == 0), 0.0, NEGATIVE)


def both_rows(own, other, start):
    return jnp.concatenate(
        [own[:, start : start + HEAD_DIM], other[:, start : start + HEAD_DIM]], axis=0
    )


def attend_kernel(window, length, queries, own, other, places, key_places, w_out, *refs):
    outs, (mixed, log_total, total, bias) = refs[:4], refs[4:]
    fill_bias(bias, length[0], places, key_places, window)
    sums = []
    stats = []
    for head in range(4):
        if head % 2 == 0:
            keys = both_rows(own[...], other[...], HEAD_DIM * (head // 2))
            values = both_rows(own[...], other[...], 192 + HEAD_DIM * (head // 2)).T
        query = queries[:, HEAD_DIM * head : HEAD_DIM * (head + 1)]
        scores = nt(keys, query) * HEAD_DIM ** (-0.5) + bias[...]
        peak = jnp.max(scores, axis=0, keepdims=True)
        probs = jnp.exp(scores - peak)
        totals = jnp.sum(probs, axis=0, keepdims=True)
        part = nn(values, probs.astype(BF16)) / totals
        sums.append(part.astype(BF16).astype(F32).T.astype(BF16))
        stats.append(peak + jnp.log(totals))
        for block in range(4):
            cols = slice(384 * block, 384 * (block + 1))
            value = nn(sums[-1], out_block(w_out, head, block))
            if head == 0:
                total[:, cols] = value
            else:
                total[:, cols] += value
    mixed[...] = jnp.concatenate(sums, axis=1)
    log_total[...] = jnp.concatenate(stats + stats, axis=0)
    emit(total, outs)


def line_specs():
    return [whole((512, 384))] * 3 + [whole((1, 512)), whole((1024, 1))]


def out_spec():
    return pl.BlockSpec((8, 192, 384), lambda *_: (0, 0, 2))


def out_block(w_out, head, block):
    start = 96 * (head % 2)
    return w_out[2 * block + head // 2, start : start + 96, :]


def projection_spec():
    return pl.BlockSpec((1536, 768), lambda *_: (0, 0))


def attend_call(window, length, queries, own, other, places, key_places, packed, after=()):
    return pl.pallas_call(
        later(functools.partial(attend_kernel, window), len(after)),
        grid=(1,),
        in_specs=anywhere(after)
        + [pl.BlockSpec(memory_space=pltpu.SMEM)] + line_specs() + [out_spec()],
        out_specs=PARTIALS + [whole((512, 384)), whole((8, 512))],
        out_shape=PARTIAL_SHAPES
        + [jax.ShapeDtypeStruct((512, 384), BF16), jax.ShapeDtypeStruct((8, 512), F32)],
        scratch_shapes=[pltpu.VMEM((512, 1536), F32), pltpu.VMEM((1024, 512), F32)],
        compiler_params=params(48),
        cost_estimate=cost(3e9, 6e6, 2e6),
        name="attend",
    )(*after, length, queries, own, other, places, key_places, packed)


def attend_backward_kernel(window, length, *refs):
    pieces, refs = refs[:5], refs[5:]
    queries, own, other, places, key_places, w_out, log_total, cosine, sine = refs[:9]
    low_queries, pair_own, pair_other, grad, bias = refs[9:]
    fill(grad, pieces)
    fill_bias(bias, length[0], places, key_places, window)
    cos, sin = cosine[...], sine[...]
    lows = []
    key_sums = []
    value_sums = []
    for head in range(4):
        if head % 2 == 0:
            keys = both_rows(own[...], other[...], HEAD_DIM * (head // 2))
            values = both_rows(own[...], other[...], 192 + HEAD_DIM * (head // 2))
            keys_t = keys.T
        query = queries[:, HEAD_DIM * head : HEAD_DIM * (head + 1)]
        mixed = nt(grad[:, :384], out_block(w_out, head, 0))
        for block in range(1, 4):
            mixed += nt(
                grad[:, 384 * block : 384 * (block + 1)], out_block(w_out, head, block)
            )
        mixed = mixed.astype(BF16)
        scores = nt(keys, query) * HEAD_DIM ** (-0.5) + bias[...]
        probs = jnp.exp(scores - log_total[head : head + 1, :])
        slopes = nt(values, mixed)
        inner = jnp.sum(probs * slopes, axis=0, keepdims=True)
        raw = (probs * (slopes - inner) * HEAD_DIM ** (-0.5)).astype(BF16)
        key_part = nn(raw, query)
        value_part = nn(probs.astype(BF16), mixed)
        if head % 2 == 0:
            key_sums.append(key_part)
            value_sums.append(value_part)
        else:
            key_sums[-1] += key_part
            value_sums[-1] += value_part
        turned = nn(keys_t, raw)
        a, b = turned[:48], turned[48:]
        turned = jnp.concatenate([a * cos + b * sin, b * cos - a * sin], axis=0)
        lows.append(turned.T.astype(BF16))
    low_queries[...] = jnp.concatenate(lows, axis=1)
    both = jnp.concatenate(key_sums + value_sums, axis=1)
    pair_own[...] = both[:512]
    pair_other[...] = both[512:].astype(BF16)


def attend_backward_call(
    window,
    length,
    pieces,
    queries,
    own,
    other,
    places,
    key_places,
    packed,
    log_total,
    cosine,
    sine,
    after=(),
):
    return pl.pallas_call(
        later(functools.partial(attend_backward_kernel, window), len(after)),
        grid=(1,),
        in_specs=anywhere(after)
        + [pl.BlockSpec(memory_space=pltpu.SMEM)]
        + PIECES
        + line_specs()
        + [out_spec(), whole((8, 512)), whole((48, 512)), whole((48, 512))],
        out_specs=[whole((512, 384))] * 3,
        out_shape=[
            jax.ShapeDtypeStruct((512, 384), BF16),
            jax.ShapeDtypeStruct((512, 384), F32),
            jax.ShapeDtypeStruct((512, 384), BF16),
        ],
        scratch_shapes=[pltpu.VMEM((512, 1536), BF16), pltpu.VMEM((1024, 512), F32)],
        compiler_params=params(52),
        cost_estimate=cost(6e9, 6e6, 2e6),
        name="attend_backward",
    )(
        *after,
        length,
        *pieces,
        queries,
        own,
        other,
        places,
        key_places,
        packed,
        log_total,
        cosine,
        sine,
    )


def unproject_kernel(low_queries, pair_own, pair_came, cosine, sine, weight, *refs):
    outs, low = refs[:4], refs[4]
    both = pair_own[...] + pair_came[...].astype(F32)
    keys = turn_columns(both[:, :192], cosine[...], -sine[...])
    rows = jnp.concatenate(
        [low_queries[...], keys.astype(BF16), both[:, 192:].astype(BF16)], axis=1
    )
    low[...] = rows
    emit(nt(rows, weight[...]), outs)


def unproject_call(low_queries, pair_own, pair_came, cosine, sine, packed, after=()):
    wide = packed.shape[-1]
    return pl.pallas_call(
        later(unproject_kernel, len(after)),
        grid=(1,),
        in_specs=anywhere(after)
        + [whole((512, 384))] * 3
        + [whole((512, 48))] * 2
        + [projection_spec()],
        out_specs=PARTIALS + [whole((512, 768))],
        out_shape=LOW_PARTIAL_SHAPES + [jax.ShapeDtypeStruct((512, 768), BF16)],
        compiler_params=params(40),
        cost_estimate=cost(1.3e9, 7e6),
        name="unproject",
    )(*after, low_queries, pair_own, pair_came, cosine, sine, packed.reshape(1536, wide))


def attend_weights_kernel(count, *refs):
    flats, grads, (low, mixed) = refs[:count], refs[count : count + 5], refs[count + 5 : count + 7]
    out, flat_t, grad = refs[count + 7 :]
    start = 0
    for ref in flats:
        n = ref.shape[0]
        flat_t[:, start : start + n] = ref[...].T
        start += n
    fill(grad, grads)
    for block in range(3):
        cols = slice(256 * block, 256 * (block + 1))
        out[:, :, cols] = nn(flat_t[...], low[:, cols]).astype(BF16).reshape(8, 192, 256)
    mixed_t = mixed[...].T
    for block in range(4):
        part = nn(mixed_t, grad[:, 384 * block : 384 * (block + 1)]).astype(BF16)
        out[2 * block : 2 * block + 2, :, 768:1152] = part.reshape(2, 192, 384)


def attend_weights_call(flats, grads, low, mixed):
    return pl.pallas_call(
        functools.partial(attend_weights_kernel, len(flats)),
        grid=(1,),
        in_specs=piece_specs(flats) + PIECES + [whole((512, 768)), whole((512, 384))],
        out_specs=whole((8, 192, 1152)),
        out_shape=jax.ShapeDtypeStruct((8, 192, 1152), BF16),
        scratch_shapes=[pltpu.VMEM((1536, 512), BF16), pltpu.VMEM((512, 1536), BF16)],
        compiler_params=params(40),
        cost_estimate=cost(1.9e9, 10e6),
        name="attend_weights",
    )(*flats, *grads, low, mixed)


def unpack_kernel(*refs):
    every, wq, wk, wv, wo, gate, up, down = refs
    side = pl.program_id(0)
    blocks = [every[x, 0] for x in range(4)]
    for x, block in enumerate(blocks):
        wq[:, 384 * x : 384 * (x + 1)] = block[:, 3072:3456].astype(F32)
        wo[:, 384 * x : 384 * (x + 1)] = block[:, 3840:4224].astype(F32)
        for s in range(8):
            cols = slice(512 * s + 128 * x, 512 * s + 128 * (x + 1))
            gate[:, cols] = block[:, 128 * s : 128 * (s + 1)].astype(F32)
            up[:, cols] = block[:, 1024 + 128 * s : 1024 + 128 * (s + 1)].astype(F32)

        @pl.when(side == 0)
        def _(x=x, block=block):
            down[x, 0:96, :1024] = block[:, 2048:3072].astype(F32)

        @pl.when(side == 1)
        def _(x=x, block=block):
            down[x, 96:128, :1024] = block[0:32, 2048:3072].astype(F32)
            down[x, 0:64, 1024:] = block[32:96, 2048:2560].astype(F32)
            down[x, 64:128, 1024:] = block[32:96, 2560:3072].astype(F32)

    wk[...] = jnp.concatenate([block[:, 3456:3648].astype(F32) for block in blocks], axis=1)
    wv[...] = jnp.concatenate([block[:, 3648:3840].astype(F32) for block in blocks], axis=1)


def unpack_call(every):
    widths = (1536, 768, 768, 1536, 4096, 4096)
    out = pl.pallas_call(
        unpack_kernel,
        grid=(2,),
        in_specs=[pl.BlockSpec((4, 1, 96, every.shape[-1]), lambda b: (0, b, 0, 0))],
        out_specs=[pl.BlockSpec((96, width), lambda b: (b, 0)) for width in widths]
        + [whole((4, 128, 1536))],
        out_shape=[jax.ShapeDtypeStruct((192, width), F32) for width in widths]
        + [jax.ShapeDtypeStruct((4, 128, 1536), F32)],
        compiler_params=params(48),
        cost_estimate=cost(1e6, 30e6),
        name="unpack",
    )(every)
    return out[:4], (out[4], out[5], out[6].reshape(512, 1536))


def pack_feed_kernel(where, w_gate, w_up, w_down, out):
    x = where[0]
    for s in range(8):
        cols = pl.ds(pl.multiple_of(512 * s + 128 * x, 128), 128)
        out[:, 128 * s : 128 * (s + 1)] = w_gate[:, cols]
        out[:, 1024 + 128 * s : 1024 + 128 * (s + 1)] = w_up[:, cols]
    out[0:128, 2048:3072] = w_down[:, 0:1024]
    out[128:192, 2048:2560] = w_down[0:64, 1024:1536]
    out[128:192, 2560:3072] = w_down[64:128, 1024:1536]


def pack_feed_call(where, w_gate, w_up, w_down, after=()):
    return pl.pallas_call(
        later(pack_feed_kernel, len(after), 1),
        grid_spec=pltpu.PrefetchScalarGridSpec(
            num_scalar_prefetch=1,
            grid=(1,),
            in_specs=anywhere(after)
            + [
                pl.BlockSpec((192, 4096), lambda b, w: (0, 0)),
                pl.BlockSpec((192, 4096), lambda b, w: (0, 0)),
                pl.BlockSpec((128, 1536), lambda b, w: (w[0], 0)),
            ],
            out_specs=pl.BlockSpec((192, 3072), lambda b, w: (0, 0)),
        ),
        out_shape=jax.ShapeDtypeStruct((192, 3072), BF16),
        compiler_params=params(24),
        cost_estimate=cost(1e3, 5e6),
        name="pack_feed",
    )(where, *after, w_gate, w_up, w_down)


WINDOW = 512
EPSILON = 1e-05
ROPE_BASE = 100000.0

AXES = ("ylo", "x", "core", "z", "yhi")
SIZES = (2, 4, 2, 4, 2)
REP = ("ylo", "x", "core")
SHARD = ("z", "yhi")
SPREAD = ("z", "core")

RIGHT = [(i, (i + 1) % 4) for i in range(4)]
LEFT = [(i, (i - 1) % 4) for i in range(4)]
ACROSS = [(i, (i + 2) % 4) for i in range(4)]
SWAP = [(0, 1), (1, 0)]


def number(ylo, x, core, z, yhi):
    return (((ylo * 4 + x) * 2 + core) * 4 + z) * 2 + yhi


def permutation(place, taken=None):
    pairs = []
    for ylo in range(2):
        for x in range(4):
            for core in range(2):
                for z in range(4):
                    for yhi in range(2):
                        here = (ylo, x, core, z, yhi)
                        if taken is None or taken(*here):
                            pairs.append((number(*here), number(*place(*here))))
    return pairs


def inverse(pairs):
    return [(there, here) for here, there in pairs]


def at_home(ylo, x, core, z, yhi):
    return core == yhi


LINES = [
    permutation(lambda l, x, c, z, h, k=k: (l, (z + k) % 4, h, x, c)) for k in range(4)
]
TURN = permutation(lambda l, x, c, z, h: (l, z, h, x, c))
SHARE = permutation(lambda l, x, c, z, h: (l, x, c, z, 1 - h), at_home)
CROSS = permutation(lambda l, x, c, z, h: (l, z, c, x, h))


def to_lines(block, z):
    part = block.shape[0] // 4
    out = []
    for k in range(4):
        piece = lax.dynamic_slice_in_dim(block, ((z + k) % 4) * part, part, axis=0)
        out.append(lax.ppermute(piece, AXES, LINES[k]))
    return out


def from_lines(block, z):
    part = block.shape[0] // 4
    out = jnp.zeros_like(block)
    for k in range(4):
        piece = lax.ppermute(block[part * k : part * (k + 1)], AXES, inverse(LINES[k]))
        out = lax.dynamic_update_slice_in_dim(out, piece, ((z + k) % 4) * part, axis=0)
    return out


def interleave(first, second):
    parts = [item[32 * k : 32 * (k + 1)] for k in range(4) for item in (first, second)]
    return jnp.concatenate(parts, axis=0)


def separate(block):
    parts = [block[32 * k : 32 * (k + 1)] for k in range(8)]
    return jnp.concatenate(parts[::2], axis=0), jnp.concatenate(parts[1::2], axis=0)


def ring_gather(block):
    half = block.shape[0] // 2
    from_left = lax.ppermute(block, "x", RIGHT)
    from_right = lax.ppermute(block, "x", LEFT)
    far_first = lax.ppermute(from_left[:half], "x", RIGHT)
    far_second = lax.ppermute(from_right[half:], "x", LEFT)
    return block, from_left, from_right, far_first, far_second


def ring_scatter(own, left, right, far):
    half = far.shape[0] // 2
    first = lax.ppermute(far[:half], "x", RIGHT).astype(F32)
    second = lax.ppermute(far[half:], "x", LEFT).astype(F32)
    right = jnp.concatenate([right[:half] + first, right[half:]], axis=0).astype(BF16)
    left = jnp.concatenate([left[:half], left[half:] + second], axis=0).astype(BF16)
    from_left = lax.ppermute(right, "x", RIGHT).astype(F32)
    from_right = lax.ppermute(left, "x", LEFT).astype(F32)
    return own + from_left + from_right


def ring_scatter_direct(own, left, right, far):
    from_left = lax.ppermute(right, "x", RIGHT).astype(F32)
    from_right = lax.ppermute(left, "x", LEFT).astype(F32)
    from_far = lax.ppermute(far, "x", ACROSS).astype(F32)
    return own + from_left + from_right + from_far


def tie(value, *others):
    return lax.optimization_barrier((value, *others))[0]


def rms_norm(values, gain):
    return values * lax.rsqrt(jnp.mean(values * values, axis=-1, keepdims=True) + EPSILON) * gain


def add_low(mine, came):
    return (mine.astype(F32) + came.astype(F32)).astype(BF16)


def yhi_sum(rows, core, yhi):
    mine = lax.dynamic_slice_in_dim(rows, 96 * core, 96, axis=0)
    theirs = lax.dynamic_slice_in_dim(rows, 96 * (1 - core), 96, axis=0)
    came = lax.ppermute(theirs, "core", SWAP)
    home = core == yhi
    kept = jnp.where(home, mine, came)
    away = jnp.where(home, came, mine)
    return add_low(kept, lax.ppermute(away, "yhi", SWAP))


def ylo_sum(piece):
    return add_low(piece, lax.ppermute(piece, "ylo", SWAP))


def cross(piece, start):
    first, last = start + 768, start + 1152
    moved = lax.ppermute(piece[:, first:last], AXES, CROSS)
    return jnp.concatenate([piece[:, :first], moved, piece[:, last:]], axis=1)


def gain_rows(grads):
    tall = grads.astype(BF16).T.reshape(8, 192, 4)
    return jnp.pad(tall, ((0, 0), (0, 0), (0, 124)))


def norm_back(grad, own_normed, state, gain):
    grad_state, grad_gain = jax.vjp(rms_norm, state, gain)[1](own_normed)
    return grad + grad_state, grad_gain


def body(tokens, lengths, grad_output, *weights):
    stretch, width = tokens.shape[1:]
    x = lax.axis_index("x")
    core = lax.axis_index("core")
    z = lax.axis_index("z")
    yhi = lax.axis_index("yhi")
    member = x.astype(jnp.int32).reshape(1)
    home = core == yhi

    gains = jnp.stack([weights[0], weights[5], weights[9], weights[14]]).T
    gains = jnp.pad(gains, ((0, 0), (0, 124)))

    def shared(block, *joined):
        return jnp.where(home, block, tie(lax.ppermute(block, AXES, SHARE), *joined))

    def attention_part(base, extra, after):
        block = lax.dynamic_slice(tie(weights[base + 4], *after), (0, 384 * x), (192, 384))
        block = lax.ppermute(block, AXES, TURN)
        parts = [
            lax.dynamic_slice(w, (0, x * (w.shape[1] // 4)), (192, w.shape[1] // 4))
            for w in weights[base + 1 : base + 4]
        ]
        parts = shared(jnp.concatenate(parts + extra, axis=1))
        return jnp.concatenate([parts[:, :768], block, parts[:, 768:]], axis=1)

    def feed_part(base, after, joined):
        part = pack_feed_call(member, *weights[base + 6 : base + 9], after=after)
        return shared(part, *joined)

    def line_weights(piece, *after):
        return lax.all_gather(tie(piece, *after), SPREAD, axis=0, tiled=False)

    here = (2 * z + yhi) * stretch + jnp.arange(stretch, dtype=jnp.int32)
    valid = (here < lengths[0])[:, None]
    grad_start = jnp.where(valid, grad_output[0], 0).astype(BF16)
    length = lax.ppermute(lengths, AXES, TURN)
    moved = to_lines(interleave(tokens[0], grad_start), z)
    rows, grad_rows = separate(jnp.concatenate(moved, axis=0))

    attn_one = line_weights(attention_part(0, [gains], ()))
    feed_one = feed_part(0, (), moved)
    gains = attn_one[:, :, 1152:1156].transpose(2, 0, 1).reshape(4, width).astype(F32)
    pieces = ring_gather(rows)
    state = rows.astype(F32)
    feed_one = line_weights(feed_one, *pieces[3:])
    grad_pieces = ring_gather(grad_rows)
    grad = grad_rows.astype(F32)

    part = stretch // 4

    def member_places(member, side_index):
        block = jnp.arange(4, dtype=jnp.int32)
        inner = jnp.arange(part, dtype=jnp.int32)
        home = (member - block + 4) % 4
        return (
            home[:, None] * (2 * stretch) + side_index * stretch + member * part + inner[None, :]
        ).reshape(-1)

    def line_places(side_index):
        return jnp.concatenate([member_places((x + step) % 4, side_index) for step in (0, 3, 1, 2)])

    places = line_places(core)
    key_places = jnp.concatenate([places, line_places(1 - core)]).reshape(1024, 1)
    half = HEAD_DIM // 2
    freq = ROPE_BASE ** (-jnp.arange(half, dtype=F32) * (2.0 / HEAD_DIM))
    angle = places.astype(F32)[:, None] * freq[None, :]
    cosine, sine = jnp.cos(angle), jnp.sin(angle)
    cosine_t, sine_t = cosine.T, sine.T
    places = places.reshape(1, 512)

    records = []
    for index, window in enumerate((WINDOW, 8 * stretch)):
        if index == 0:
            attn, feed = attn_one, feed_one
        else:
            attn, feed = attn_two, feed_two
        gain_attn, gain_feed = gains[2 * index], gains[2 * index + 1]
        if index == 0:
            queries, own, flat = project_call(True, pieces, gain_attn, attn, cosine, sine)
            flats = (flat,)
        else:
            flats = ring_gather(rms_norm(state, gain_attn).astype(BF16))
            feed_two = feed = line_weights(feed_two, *flats[3:])
            queries, own = project_call(False, flats, gain_attn, attn, cosine, sine)
        other = lax.ppermute(own, "core", SWAP)
        line = (queries, own, other, places, key_places)
        after = grad_pieces[3:] if index else ()
        *partial, mixed, log_total = attend_call(window, length, *line, attn, after=after)
        saved_attn = (state, flats, line, mixed, log_total)
        state = state + ring_scatter(*partial)
        if index == 0:
            attn_two = attention_part(9, [], (mixed,))
            feed_two = feed_part(9, (mixed,), ())
        flats = ring_gather(rms_norm(state, gain_feed).astype(BF16))
        if index == 0:
            attn_two = line_weights(attn_two, *flats[3:])
        *partial, gate, up, hidden = feed_forward_call(flats, feed)
        saved_feed = (state, flats, gate, up, hidden)
        state = state + ring_scatter(*partial)
        records.append((saved_attn, saved_feed, window))
    last_rows = state.astype(BF16)
    packed = ((attn_one, feed_one), (attn_two, feed_two))

    results = [None] * 18
    gain_grads = [None] * 4

    def feed_back(index, grad, pieces, after):
        state, flats, gate, up, hidden = records[index][1]
        *partial, low_gate, low_up = feed_backward_call(
            pieces, packed[index][1], gate, up, after=after
        )
        own_normed = ring_scatter_direct(*partial)
        grad, gain_grads[2 * index + 1] = norm_back(
            grad, own_normed, state, gains[2 * index + 1]
        )
        return grad, feed_weights_call(flats, pieces, low_gate, low_up, hidden)

    def attention_back(index, grad, pieces, after, late):
        state, flats, line, mixed, log_total = records[index][0]
        window = records[index][2]
        attn = packed[index][0]
        low_queries, pair_own, pair_other = attend_backward_call(
            window, length, pieces, *line, attn, log_total, cosine_t, sine_t, after=after
        )
        came = lax.ppermute(pair_other, "core", SWAP)
        *partial, low = unproject_call(
            low_queries, pair_own, came, cosine, sine, attn, after=late
        )
        own_normed = ring_scatter_direct(*partial)
        grad, gain_grads[2 * index] = norm_back(grad, own_normed, state, gains[2 * index])
        return grad, attend_weights_call(flats, pieces, low, mixed)

    def scatter(block, *others):
        return lax.psum_scatter(
            tie(block, *others), SPREAD, scatter_dimension=0, tiled=True
        )[0]

    grad, feed_grad = feed_back(1, grad, grad_pieces, ())
    low = tie(grad.astype(BF16), feed_grad)
    second_feed = scatter(feed_grad, low)
    grad, attn_grad = attention_back(1, grad, ring_gather(low), (last_rows,), ())
    low = tie(grad.astype(BF16), attn_grad)
    second_attn = scatter(attn_grad, low, second_feed)

    grad, feed_grad = feed_back(0, grad, ring_gather(low), (second_feed,))
    low = tie(grad.astype(BF16), feed_grad)
    first_feed = scatter(feed_grad, low, second_attn)
    second = yhi_sum(jnp.concatenate([second_feed, second_attn], axis=1), core, yhi)
    grad, attn_grad = attention_back(0, grad, ring_gather(low), (), (second,))
    low = grad.astype(BF16)
    attn_grad = jnp.concatenate([attn_grad, gain_rows(jnp.stack(gain_grads))], axis=2)
    first_attn = scatter(attn_grad, first_feed, low)
    second_piece = cross(ylo_sum(second), 3072)
    feed_piece = ylo_sum(yhi_sum(first_feed, core, yhi))
    back = from_lines(interleave(last_rows, low), z)
    output, input_grad = separate(back)
    output, input_grad = output[None], input_grad.astype(F32)[None]

    every = lax.all_gather(tie(second_piece, first_attn), ("x", "core"), axis=0, tiled=False)
    results[10:14], results[15:18] = unpack_call(every.reshape(4, 2, 96, -1))
    attn_piece = ylo_sum(yhi_sum(tie(first_attn, feed_piece), core, yhi))
    first_piece = jnp.concatenate([feed_piece, cross(attn_piece, 0)], axis=1)
    every = lax.all_gather(first_piece, ("x", "core"), axis=0, tiled=False)
    every = every.reshape(4, 2, 96, -1)
    results[1:5], results[6:9] = unpack_call(every)
    gain_sums = every[..., 4224:4228].astype(F32).sum(axis=0).reshape(192, 4).T
    for index, slot in enumerate((0, 5, 9, 14)):
        results[slot] = gain_sums[index]
    return (output, input_grad, *results)


def solution(mesh):
    fine = Mesh(mesh.devices.reshape(SIZES), AXES)
    token = P(REP, SHARD, None)
    vector = P(SHARD)
    matrix = P(SHARD, None)
    layer = (vector, matrix, matrix, matrix, matrix, vector, matrix, matrix, matrix)
    return jax.shard_map(
        body,
        mesh=fine,
        in_specs=(token, P(REP), token) + layer + layer,
        out_specs=(token, token) + layer + layer,
        check_vma=False,
    )
```

```python
import functools
import jax
import jax.numpy as jnp
from jax import lax
from jax.experimental import pallas as pl
from jax.experimental.pallas import tpu as pltpu
from jax.sharding import Mesh
from jax.sharding import PartitionSpec as P

F32 = jnp.float32
BF16 = jnp.bfloat16
HEAD_DIM = 96
NEGATIVE = -1e30
MIB = 1 << 20

OFFSETS = (0, 128, 256, 384, 448)
SIZES_OF = (128, 128, 128, 64, 64)


def params(mib, semantics=None):
    return pltpu.CompilerParams(vmem_limit_bytes=mib * MIB, dimension_semantics=semantics)


def cost(flops, nbytes, transcendentals=0):
    return pl.CostEstimate(
        flops=int(flops), bytes_accessed=int(nbytes), transcendentals=int(transcendentals)
    )


def fill(target, refs):
    start = 0
    for ref in refs:
        rows = ref.shape[0]
        target[start : start + rows, :] = ref[...]
        start += rows


def nn(a, b):
    return lax.dot_general(a, b, (((1,), (0,)), ((), ())), preferred_element_type=F32)


def nt(a, b):
    return lax.dot_general(a, b, (((1,), (1,)), ((), ())), preferred_element_type=F32)


def tn(a, b):
    return lax.dot_general(a, b, (((0,), (0,)), ((), ())), preferred_element_type=F32)


def later(kernel, count, lead=0):
    if not count:
        return kernel

    def wrapped(*refs):
        return kernel(*refs[:lead], *refs[lead + count :])

    return wrapped


def anywhere(after):
    return [pl.BlockSpec(memory_space=pl.ANY)] * len(after)


def whole(shape):
    return pl.BlockSpec(shape, lambda *_: (0,) * len(shape))


PIECES = [whole((rows, 1536)) for rows in SIZES_OF]
PARTIAL_SHAPES = [
    jax.ShapeDtypeStruct((128, 1536), F32),
    jax.ShapeDtypeStruct((128, 1536), F32),
    jax.ShapeDtypeStruct((128, 1536), F32),
    jax.ShapeDtypeStruct((128, 1536), BF16),
]
LOW_PARTIAL_SHAPES = PARTIAL_SHAPES[:1] + [jax.ShapeDtypeStruct((128, 1536), BF16)] * 3
PARTIALS = [whole((128, 1536))] * 4


def emit(total, outs):
    for place, out in enumerate(outs):
        out[...] = total[128 * place : 128 * (place + 1), :].astype(out.dtype)


def down_parts(block):
    left = block[:, 0:128, :].reshape(256, 1024)
    right = jnp.concatenate([block[:, 128:192, 0:512], block[:, 128:192, 512:1024]], axis=1)
    return left, right.reshape(256, 512)


def feed_forward_kernel(*refs):
    pieces, (wg, wu, wd), outs = refs[:5], refs[5:8], refs[8:12]
    gate, up, hidden, flat, total = refs[12:]
    step = pl.program_id(0)

    @pl.when(step == 0)
    def _():
        fill(flat, pieces)

    rows = flat[...]
    g = nn(rows, wg[...])
    u = nn(rows, wu[...])
    gate[...] = g
    up[...] = u
    h = (g * jax.nn.sigmoid(g) * u).astype(BF16)
    hidden[...] = h
    left, right = down_parts(wd[...])
    left, right = nn(h, left), nn(h, right)

    @pl.when(step == 0)
    def _():
        total[:, :1024] = left
        total[:, 1024:] = right

    @pl.when(step > 0)
    def _():
        total[:, :1024] += left
        total[:, 1024:] += right

    @pl.when(step == 3)
    def _():
        emit(total, outs)


def feed_specs():
    return [
        pl.BlockSpec((1536, 256), lambda b: (0, b)),
        pl.BlockSpec((1536, 256), lambda b: (0, 4 + b)),
        pl.BlockSpec((2, 192, 1024), lambda b: (b, 0, 2)),
    ]


def column_block(rows):
    return pl.BlockSpec((rows, 256), lambda b: (0, b))


def feed_forward_call(pieces, packed, after=()):
    flat_packed = packed.reshape(1536, -1)
    return pl.pallas_call(
        later(feed_forward_kernel, len(after)),
        grid=(4,),
        in_specs=anywhere(after) + PIECES + feed_specs(),
        out_specs=PARTIALS + [column_block(512)] * 3,
        out_shape=PARTIAL_SHAPES
        + [
            jax.ShapeDtypeStruct((512, 1024), F32),
            jax.ShapeDtypeStruct((512, 1024), F32),
            jax.ShapeDtypeStruct((512, 1024), BF16),
        ],
        scratch_shapes=[pltpu.VMEM((512, 1536), BF16), pltpu.VMEM((512, 1536), F32)],
        compiler_params=params(40),
        cost_estimate=cost(4.9e9, 18e6),
        name="feed_forward",
    )(*after, *pieces, flat_packed, flat_packed, packed)


def feed_backward_kernel(*refs):
    pieces, (wg, wu, wd, gate, up), outs = refs[:5], refs[5:10], refs[10:14]
    low_gate, low_up, flat, total = refs[14:]
    step = pl.program_id(0)

    @pl.when(step == 0)
    def _():
        fill(flat, pieces)

    rows = flat[...]
    left, right = down_parts(wd[...])
    grad = nt(rows[:, :1024], left) + nt(rows[:, 1024:], right)
    g = gate[...]
    s = jax.nn.sigmoid(g)
    a = (grad * up[...] * s * (1.0 + g * (1.0 - s))).astype(BF16)
    b = (grad * (g * s)).astype(BF16)
    low_gate[...] = a
    low_up[...] = b
    part = nt(a, wg[...]) + nt(b, wu[...])

    @pl.when(step == 0)
    def _():
        total[...] = part

    @pl.when(step > 0)
    def _():
        total[...] += part

    @pl.when(step == 3)
    def _():
        emit(total, outs)


def feed_backward_call(pieces, packed, gate, up, after=()):
    flat_packed = packed.reshape(1536, -1)
    return pl.pallas_call(
        later(feed_backward_kernel, len(after)),
        grid=(4,),
        in_specs=anywhere(after) + PIECES + feed_specs() + [column_block(512)] * 2,
        out_specs=PARTIALS + [column_block(512)] * 2,
        out_shape=LOW_PARTIAL_SHAPES + [jax.ShapeDtypeStruct((512, 1024), BF16)] * 2,
        scratch_shapes=[pltpu.VMEM((512, 1536), BF16), pltpu.VMEM((512, 1536), F32)],
        compiler_params=params(40),
        cost_estimate=cost(4.9e9, 20e6),
        name="feed_backward",
    )(*after, *pieces, flat_packed, flat_packed, packed, gate, up)


def feed_weights_kernel(*refs):
    flats, grads = refs[:5], refs[5:10]
    low_gate, low_up, hidden, out, flat_t, hidden_t, grad = refs[10:]
    step = pl.program_id(0)

    @pl.when(step == 0)
    def _():
        start = 0
        for ref in flats:
            n = ref.shape[0]
            flat_t[:, start : start + n] = ref[...].T
            start += n

    @pl.when(step == 4)
    def _():
        hidden_t[...] = hidden[...].T
        fill(grad, grads)

    @pl.when(step < 4)
    def _():
        out[...] = nn(flat_t[...], low_gate[...]).astype(BF16).reshape(8, 192, 256)

    @pl.when((step >= 4) & (step < 8))
    def _():
        out[...] = nn(flat_t[...], low_up[...]).astype(BF16).reshape(8, 192, 256)

    for q in range(4):

        @pl.when(step == 8 + q)
        def _():
            top = nn(hidden_t[...], grad[:, 256 * q : 256 * (q + 1)]).astype(BF16)
            out[:, 0:128, :] = top.reshape(8, 128, 256)
            half = 64 * (q // 2)
            some = hidden_t[...].reshape(8, 128, 512)[:, half : half + 64].reshape(512, 512)
            start = 1024 + 256 * (q % 2)
            low = nn(some, grad[:, start : start + 256]).astype(BF16)
            out[:, 128:192, :] = low.reshape(8, 64, 256)


def feed_weights_call(flats, grads, low_gate, low_up, hidden):
    return pl.pallas_call(
        feed_weights_kernel,
        grid=(12,),
        in_specs=PIECES
        + PIECES
        + [
            pl.BlockSpec((512, 256), lambda b: (0, jnp.minimum(b, 3))),
            pl.BlockSpec((512, 256), lambda b: (0, jnp.clip(b - 4, 0, 3))),
            whole((512, 1024)),
        ],
        out_specs=pl.BlockSpec((8, 192, 256), lambda b: (0, 0, b)),
        out_shape=jax.ShapeDtypeStruct((8, 192, 3072), BF16),
        scratch_shapes=[
            pltpu.VMEM((1536, 512), BF16),
            pltpu.VMEM((1024, 512), BF16),
            pltpu.VMEM((512, 1536), BF16),
        ],
        compiler_params=params(40),
        cost_estimate=cost(4.9e9, 18e6),
        name="feed_weights",
    )(*flats, *grads, low_gate, low_up, hidden)


def piece_specs(pieces):
    return [whole(item.shape) for item in pieces]


def turn_columns(block, cosine, sine):
    out = []
    for start in range(0, block.shape[1], HEAD_DIM):
        a = block[:, start : start + 48]
        b = block[:, start + 48 : start + HEAD_DIM]
        out.append(a * cosine - b * sine)
        out.append(b * cosine + a * sine)
    return jnp.concatenate(out, axis=1)


def project_kernel(raw, count, *refs):
    pieces, (gain, weight, cosine, sine, queries, pair) = refs[:count], refs[count : count + 6]
    if raw:
        flat = refs[-1]
        start = 0
        for ref in pieces:
            n = ref.shape[0]
            rows = ref[...].astype(F32)
            scale = lax.rsqrt(jnp.mean(rows * rows, axis=-1, keepdims=True) + 1e-05)
            flat[start : start + n, :] = (rows * scale * gain[...]).astype(BF16)
            start += n
    else:
        flat = refs[-1]
        fill(flat, pieces)
    both = nn(flat[...], weight[...])
    cos, sin = cosine[...], sine[...]
    queries[...] = turn_columns(both[:, :384], cos, sin).astype(BF16)
    keys = turn_columns(both[:, 384:576], cos, sin)
    pair[...] = jnp.concatenate([keys, both[:, 576:768]], axis=1).astype(BF16)


def project_call(raw, pieces, gain, packed, cosine, sine, after=()):
    wide = packed.shape[-1]
    shape = jax.ShapeDtypeStruct((512, 384), BF16)
    flat_shape = jax.ShapeDtypeStruct((512, 1536), BF16)
    return pl.pallas_call(
        later(functools.partial(project_kernel, raw, len(pieces)), len(after)),
        grid=(1,),
        in_specs=anywhere(after)
        + piece_specs(pieces)
        + [whole((1, 1536)), projection_spec(), whole((512, 48)), whole((512, 48))],
        out_specs=[whole((512, 384))] * 2 + ([whole((512, 1536))] if raw else []),
        out_shape=[shape, shape] + ([flat_shape] if raw else []),
        scratch_shapes=[] if raw else [pltpu.VMEM((512, 1536), BF16)],
        compiler_params=params(40),
        cost_estimate=cost(1.3e9, 6e6),
        name="project",
    )(*after, *pieces, gain.reshape(1, 1536), packed.reshape(1536, wide), cosine, sine)


def fill_bias(bias, length, places, key_places, window):
    gap = places[...] - key_places[...]
    inside = (key_places[...] < length) & (gap >= 0) & (gap < window)
    bias[...] = jnp.where(inside | (gap == 0), 0.0, NEGATIVE)


def both_rows(own, other, start):
    return jnp.concatenate(
        [own[:, start : start + HEAD_DIM], other[:, start : start + HEAD_DIM]], axis=0
    )


def attend_kernel(window, length, queries, own, other, places, key_places, w_out, *refs):
    outs, (mixed, log_total, total, bias) = refs[:4], refs[4:]
    fill_bias(bias, length[0], places, key_places, window)
    sums = []
    stats = []
    for head in range(4):
        if head % 2 == 0:
            keys = both_rows(own[...], other[...], HEAD_DIM * (head // 2))
            values = both_rows(own[...], other[...], 192 + HEAD_DIM * (head // 2)).T
        query = queries[:, HEAD_DIM * head : HEAD_DIM * (head + 1)]
        scores = nt(keys, query) * HEAD_DIM ** (-0.5) + bias[...]
        peak = jnp.max(scores, axis=0, keepdims=True)
        probs = jnp.exp(scores - peak)
        totals = jnp.sum(probs, axis=0, keepdims=True)
        part = nn(values, probs.astype(BF16)) / totals
        sums.append(part.astype(BF16).astype(F32).T.astype(BF16))
        stats.append(peak + jnp.log(totals))
        for block in range(4):
            cols = slice(384 * block, 384 * (block + 1))
            value = nn(sums[-1], out_block(w_out, head, block))
            if head == 0:
                total[:, cols] = value
            else:
                total[:, cols] += value
    mixed[...] = jnp.concatenate(sums, axis=1)
    log_total[...] = jnp.concatenate(stats + stats, axis=0)
    emit(total, outs)


def line_specs():
    return [whole((512, 384))] * 3 + [whole((1, 512)), whole((1024, 1))]


def out_spec():
    return pl.BlockSpec((8, 192, 384), lambda *_: (0, 0, 2))


def out_block(w_out, head, block):
    start = 96 * (head % 2)
    return w_out[2 * block + head // 2, start : start + 96, :]


def projection_spec():
    return pl.BlockSpec((1536, 768), lambda *_: (0, 0))


def attend_call(window, length, queries, own, other, places, key_places, packed, after=()):
    return pl.pallas_call(
        later(functools.partial(attend_kernel, window), len(after)),
        grid=(1,),
        in_specs=anywhere(after)
        + [pl.BlockSpec(memory_space=pltpu.SMEM)] + line_specs() + [out_spec()],
        out_specs=PARTIALS + [whole((512, 384)), whole((8, 512))],
        out_shape=PARTIAL_SHAPES
        + [jax.ShapeDtypeStruct((512, 384), BF16), jax.ShapeDtypeStruct((8, 512), F32)],
        scratch_shapes=[pltpu.VMEM((512, 1536), F32), pltpu.VMEM((1024, 512), F32)],
        compiler_params=params(48),
        cost_estimate=cost(3e9, 6e6, 2e6),
        name="attend",
    )(*after, length, queries, own, other, places, key_places, packed)


def attend_backward_kernel(window, length, *refs):
    pieces, refs = refs[:5], refs[5:]
    queries, own, other, places, key_places, w_out, log_total, cosine, sine = refs[:9]
    low_queries, pair_own, pair_other, grad, bias = refs[9:]
    fill(grad, pieces)
    fill_bias(bias, length[0], places, key_places, window)
    cos, sin = cosine[...], sine[...]
    lows = []
    key_sums = []
    value_sums = []
    for head in range(4):
        if head % 2 == 0:
            keys = both_rows(own[...], other[...], HEAD_DIM * (head // 2))
            values = both_rows(own[...], other[...], 192 + HEAD_DIM * (head // 2))
            keys_t = keys.T
        query = queries[:, HEAD_DIM * head : HEAD_DIM * (head + 1)]
        mixed = nt(grad[:, :384], out_block(w_out, head, 0))
        for block in range(1, 4):
            mixed += nt(
                grad[:, 384 * block : 384 * (block + 1)], out_block(w_out, head, block)
            )
        mixed = mixed.astype(BF16)
        scores = nt(keys, query) * HEAD_DIM ** (-0.5) + bias[...]
        probs = jnp.exp(scores - log_total[head : head + 1, :])
        slopes = nt(values, mixed)
        inner = jnp.sum(probs * slopes, axis=0, keepdims=True)
        raw = (probs * (slopes - inner) * HEAD_DIM ** (-0.5)).astype(BF16)
        key_part = nn(raw, query)
        value_part = nn(probs.astype(BF16), mixed)
        if head % 2 == 0:
            key_sums.append(key_part)
            value_sums.append(value_part)
        else:
            key_sums[-1] += key_part
            value_sums[-1] += value_part
        turned = nn(keys_t, raw)
        a, b = turned[:48], turned[48:]
        turned = jnp.concatenate([a * cos + b * sin, b * cos - a * sin], axis=0)
        lows.append(turned.T.astype(BF16))
    low_queries[...] = jnp.concatenate(lows, axis=1)
    both = jnp.concatenate(key_sums + value_sums, axis=1)
    pair_own[...] = both[:512]
    pair_other[...] = both[512:].astype(BF16)


def attend_backward_call(
    window,
    length,
    pieces,
    queries,
    own,
    other,
    places,
    key_places,
    packed,
    log_total,
    cosine,
    sine,
    after=(),
):
    return pl.pallas_call(
        later(functools.partial(attend_backward_kernel, window), len(after)),
        grid=(1,),
        in_specs=anywhere(after)
        + [pl.BlockSpec(memory_space=pltpu.SMEM)]
        + PIECES
        + line_specs()
        + [out_spec(), whole((8, 512)), whole((48, 512)), whole((48, 512))],
        out_specs=[whole((512, 384))] * 3,
        out_shape=[
            jax.ShapeDtypeStruct((512, 384), BF16),
            jax.ShapeDtypeStruct((512, 384), F32),
            jax.ShapeDtypeStruct((512, 384), BF16),
        ],
        scratch_shapes=[pltpu.VMEM((512, 1536), BF16), pltpu.VMEM((1024, 512), F32)],
        compiler_params=params(52),
        cost_estimate=cost(6e9, 6e6, 2e6),
        name="attend_backward",
    )(
        *after,
        length,
        *pieces,
        queries,
        own,
        other,
        places,
        key_places,
        packed,
        log_total,
        cosine,
        sine,
    )


def unproject_kernel(low_queries, pair_own, pair_came, cosine, sine, weight, *refs):
    outs, low = refs[:4], refs[4]
    both = pair_own[...] + pair_came[...].astype(F32)
    keys = turn_columns(both[:, :192], cosine[...], -sine[...])
    rows = jnp.concatenate(
        [low_queries[...], keys.astype(BF16), both[:, 192:].astype(BF16)], axis=1
    )
    low[...] = rows
    emit(nt(rows, weight[...]), outs)


def unproject_call(low_queries, pair_own, pair_came, cosine, sine, packed, after=()):
    wide = packed.shape[-1]
    return pl.pallas_call(
        later(unproject_kernel, len(after)),
        grid=(1,),
        in_specs=anywhere(after)
        + [whole((512, 384))] * 3
        + [whole((512, 48))] * 2
        + [projection_spec()],
        out_specs=PARTIALS + [whole((512, 768))],
        out_shape=LOW_PARTIAL_SHAPES + [jax.ShapeDtypeStruct((512, 768), BF16)],
        compiler_params=params(40),
        cost_estimate=cost(1.3e9, 7e6),
        name="unproject",
    )(*after, low_queries, pair_own, pair_came, cosine, sine, packed.reshape(1536, wide))


def attend_weights_kernel(count, *refs):
    flats, grads, (low, mixed) = refs[:count], refs[count : count + 5], refs[count + 5 : count + 7]
    out, flat_t, grad = refs[count + 7 :]
    start = 0
    for ref in flats:
        n = ref.shape[0]
        flat_t[:, start : start + n] = ref[...].T
        start += n
    fill(grad, grads)
    for block in range(3):
        cols = slice(256 * block, 256 * (block + 1))
        out[:, :, cols] = nn(flat_t[...], low[:, cols]).astype(BF16).reshape(8, 192, 256)
    mixed_t = mixed[...].T
    for block in range(4):
        part = nn(mixed_t, grad[:, 384 * block : 384 * (block + 1)]).astype(BF16)
        out[2 * block : 2 * block + 2, :, 768:1152] = part.reshape(2, 192, 384)


def attend_weights_call(flats, grads, low, mixed):
    return pl.pallas_call(
        functools.partial(attend_weights_kernel, len(flats)),
        grid=(1,),
        in_specs=piece_specs(flats) + PIECES + [whole((512, 768)), whole((512, 384))],
        out_specs=whole((8, 192, 1152)),
        out_shape=jax.ShapeDtypeStruct((8, 192, 1152), BF16),
        scratch_shapes=[pltpu.VMEM((1536, 512), BF16), pltpu.VMEM((512, 1536), BF16)],
        compiler_params=params(40),
        cost_estimate=cost(1.9e9, 10e6),
        name="attend_weights",
    )(*flats, *grads, low, mixed)


def unpack_kernel(*refs):
    every, wq, wk, wv, wo, gate, up, down = refs
    side = pl.program_id(0)
    blocks = [every[x, 0] for x in range(4)]
    for x, block in enumerate(blocks):
        wq[:, 384 * x : 384 * (x + 1)] = block[:, 3072:3456].astype(F32)
        wo[:, 384 * x : 384 * (x + 1)] = block[:, 3840:4224].astype(F32)
        for s in range(8):
            cols = slice(512 * s + 128 * x, 512 * s + 128 * (x + 1))
            gate[:, cols] = block[:, 128 * s : 128 * (s + 1)].astype(F32)
            up[:, cols] = block[:, 1024 + 128 * s : 1024 + 128 * (s + 1)].astype(F32)

        @pl.when(side == 0)
        def _(x=x, block=block):
            down[x, 0:96, :1024] = block[:, 2048:3072].astype(F32)

        @pl.when(side == 1)
        def _(x=x, block=block):
            down[x, 96:128, :1024] = block[0:32, 2048:3072].astype(F32)
            down[x, 0:64, 1024:] = block[32:96, 2048:2560].astype(F32)
            down[x, 64:128, 1024:] = block[32:96, 2560:3072].astype(F32)

    wk[...] = jnp.concatenate([block[:, 3456:3648].astype(F32) for block in blocks], axis=1)
    wv[...] = jnp.concatenate([block[:, 3648:3840].astype(F32) for block in blocks], axis=1)


def unpack_call(every):
    widths = (1536, 768, 768, 1536, 4096, 4096)
    out = pl.pallas_call(
        unpack_kernel,
        grid=(2,),
        in_specs=[pl.BlockSpec((4, 1, 96, every.shape[-1]), lambda b: (0, b, 0, 0))],
        out_specs=[pl.BlockSpec((96, width), lambda b: (b, 0)) for width in widths]
        + [whole((4, 128, 1536))],
        out_shape=[jax.ShapeDtypeStruct((192, width), F32) for width in widths]
        + [jax.ShapeDtypeStruct((4, 128, 1536), F32)],
        compiler_params=params(48),
        cost_estimate=cost(1e6, 30e6),
        name="unpack",
    )(every)
    return out[:4], (out[4], out[5], out[6].reshape(512, 1536))


def pack_feed_kernel(where, w_gate, w_up, w_down, out):
    x = where[0]
    for s in range(8):
        cols = pl.ds(pl.multiple_of(512 * s + 128 * x, 128), 128)
        out[:, 128 * s : 128 * (s + 1)] = w_gate[:, cols]
        out[:, 1024 + 128 * s : 1024 + 128 * (s + 1)] = w_up[:, cols]
    out[0:128, 2048:3072] = w_down[:, 0:1024]
    out[128:192, 2048:2560] = w_down[0:64, 1024:1536]
    out[128:192, 2560:3072] = w_down[64:128, 1024:1536]


def pack_feed_call(where, w_gate, w_up, w_down, after=()):
    return pl.pallas_call(
        later(pack_feed_kernel, len(after), 1),
        grid_spec=pltpu.PrefetchScalarGridSpec(
            num_scalar_prefetch=1,
            grid=(1,),
            in_specs=anywhere(after)
            + [
                pl.BlockSpec((192, 4096), lambda b, w: (0, 0)),
                pl.BlockSpec((192, 4096), lambda b, w: (0, 0)),
                pl.BlockSpec((128, 1536), lambda b, w: (w[0], 0)),
            ],
            out_specs=pl.BlockSpec((192, 3072), lambda b, w: (0, 0)),
        ),
        out_shape=jax.ShapeDtypeStruct((192, 3072), BF16),
        compiler_params=params(24),
        cost_estimate=cost(1e3, 5e6),
        name="pack_feed",
    )(where, *after, w_gate, w_up, w_down)


WINDOW = 512
EPSILON = 1e-05
ROPE_BASE = 100000.0

AXES = ("ylo", "x", "core", "z", "yhi")
SIZES = (2, 4, 2, 4, 2)
REP = ("ylo", "x", "core")
SHARD = ("z", "yhi")
SPREAD = ("z", "core")

RIGHT = [(i, (i + 1) % 4) for i in range(4)]
LEFT = [(i, (i - 1) % 4) for i in range(4)]
ACROSS = [(i, (i + 2) % 4) for i in range(4)]
SWAP = [(0, 1), (1, 0)]


def number(ylo, x, core, z, yhi):
    return (((ylo * 4 + x) * 2 + core) * 4 + z) * 2 + yhi


def permutation(place, taken=None):
    pairs = []
    for ylo in range(2):
        for x in range(4):
            for core in range(2):
                for z in range(4):
                    for yhi in range(2):
                        here = (ylo, x, core, z, yhi)
                        if taken is None or taken(*here):
                            pairs.append((number(*here), number(*place(*here))))
    return pairs


def inverse(pairs):
    return [(there, here) for here, there in pairs]


def at_home(ylo, x, core, z, yhi):
    return core == yhi


LINES = [
    permutation(lambda l, x, c, z, h, k=k: (l, (z + k) % 4, h, x, c)) for k in range(4)
]
TURN = permutation(lambda l, x, c, z, h: (l, z, h, x, c))
SHARE = permutation(lambda l, x, c, z, h: (l, x, c, z, 1 - h), at_home)
CROSS = permutation(lambda l, x, c, z, h: (l, z, c, x, h))


def to_lines(block, z):
    part = block.shape[0] // 4
    out = []
    for k in range(4):
        piece = lax.dynamic_slice_in_dim(block, ((z + k) % 4) * part, part, axis=0)
        out.append(lax.ppermute(piece, AXES, LINES[k]))
    return out


def from_lines(block, z):
    part = block.shape[0] // 4
    out = jnp.zeros_like(block)
    for k in range(4):
        piece = lax.ppermute(block[part * k : part * (k + 1)], AXES, inverse(LINES[k]))
        out = lax.dynamic_update_slice_in_dim(out, piece, ((z + k) % 4) * part, axis=0)
    return out


def interleave(first, second):
    parts = [item[32 * k : 32 * (k + 1)] for k in range(4) for item in (first, second)]
    return jnp.concatenate(parts, axis=0)


def separate(block):
    parts = [block[32 * k : 32 * (k + 1)] for k in range(8)]
    return jnp.concatenate(parts[::2], axis=0), jnp.concatenate(parts[1::2], axis=0)


def ring_gather(block):
    half = block.shape[0] // 2
    from_left = lax.ppermute(block, "x", RIGHT)
    from_right = lax.ppermute(block, "x", LEFT)
    far_first = lax.ppermute(from_left[:half], "x", RIGHT)
    far_second = lax.ppermute(from_right[half:], "x", LEFT)
    return block, from_left, from_right, far_first, far_second


def ring_scatter(own, left, right, far):
    half = far.shape[0] // 2
    first = lax.ppermute(far[:half], "x", RIGHT).astype(F32)
    second = lax.ppermute(far[half:], "x", LEFT).astype(F32)
    right = jnp.concatenate([right[:half] + first, right[half:]], axis=0).astype(BF16)
    left = jnp.concatenate([left[:half], left[half:] + second], axis=0).astype(BF16)
    from_left = lax.ppermute(right, "x", RIGHT).astype(F32)
    from_right = lax.ppermute(left, "x", LEFT).astype(F32)
    return own + from_left + from_right


def ring_scatter_direct(own, left, right, far):
    from_left = lax.ppermute(right, "x", RIGHT).astype(F32)
    from_right = lax.ppermute(left, "x", LEFT).astype(F32)
    from_far = lax.ppermute(far, "x", ACROSS).astype(F32)
    return own + from_left + from_right + from_far


def tie(value, *others):
    return lax.optimization_barrier((value, *others))[0]


def rms_norm(values, gain):
    return values * lax.rsqrt(jnp.mean(values * values, axis=-1, keepdims=True) + EPSILON) * gain


def add_low(mine, came):
    return (mine.astype(F32) + came.astype(F32)).astype(BF16)


def yhi_sum(rows, core, yhi):
    mine = lax.dynamic_slice_in_dim(rows, 96 * core, 96, axis=0)
    theirs = lax.dynamic_slice_in_dim(rows, 96 * (1 - core), 96, axis=0)
    came = lax.ppermute(theirs, "core", SWAP)
    home = core == yhi
    kept = jnp.where(home, mine, came)
    away = jnp.where(home, came, mine)
    return add_low(kept, lax.ppermute(away, "yhi", SWAP))


def ylo_sum(piece):
    return add_low(piece, lax.ppermute(piece, "ylo", SWAP))


def cross(piece, start, *others):
    first, last = start + 768, start + 1152
    moved = lax.ppermute(piece[:, first:last], AXES, CROSS)
    if others:
        piece, moved = lax.optimization_barrier((piece, moved, *others))[:2]
    return jnp.concatenate([piece[:, :first], moved, piece[:, last:]], axis=1)


def gain_rows(grads):
    tall = grads.astype(BF16).T.reshape(8, 192, 4)
    return jnp.pad(tall, ((0, 0), (0, 0), (0, 124)))


def norm_back(grad, own_normed, state, gain):
    grad_state, grad_gain = jax.vjp(rms_norm, state, gain)[1](own_normed)
    return grad + grad_state, grad_gain


def body(tokens, lengths, grad_output, *weights):
    stretch, width = tokens.shape[1:]
    x = lax.axis_index("x")
    core = lax.axis_index("core")
    z = lax.axis_index("z")
    yhi = lax.axis_index("yhi")
    member = x.astype(jnp.int32).reshape(1)
    home = core == yhi

    gains = jnp.stack([weights[0], weights[5], weights[9], weights[14]]).T
    gains = jnp.pad(gains, ((0, 0), (0, 124)))

    def shared(block, *joined):
        return jnp.where(home, block, tie(lax.ppermute(block, AXES, SHARE), *joined))

    def attention_part(base, extra, after):
        block = lax.dynamic_slice(tie(weights[base + 4], *after), (0, 384 * x), (192, 384))
        block = lax.ppermute(block, AXES, TURN)
        parts = [
            lax.dynamic_slice(w, (0, x * (w.shape[1] // 4)), (192, w.shape[1] // 4))
            for w in weights[base + 1 : base + 4]
        ]
        parts = shared(jnp.concatenate(parts + extra, axis=1))
        return jnp.concatenate([parts[:, :768], block, parts[:, 768:]], axis=1)

    def feed_part(base, after, joined):
        part = pack_feed_call(member, *weights[base + 6 : base + 9], after=after)
        return shared(part, *joined)

    def line_weights(piece, *after):
        return lax.all_gather(tie(piece, *after), SPREAD, axis=0, tiled=False)

    here = (2 * z + yhi) * stretch + jnp.arange(stretch, dtype=jnp.int32)
    valid = (here < lengths[0])[:, None]
    grad_start = jnp.where(valid, grad_output[0], 0).astype(BF16)
    length = lax.ppermute(lengths, AXES, TURN)
    moved = to_lines(interleave(tokens[0], grad_start), z)
    rows, grad_rows = separate(jnp.concatenate(moved, axis=0))

    attn_one = line_weights(attention_part(0, [gains], ()))
    feed_one = feed_part(0, (), moved)
    gains = attn_one[:, :, 1152:1156].transpose(2, 0, 1).reshape(4, width).astype(F32)
    pieces = ring_gather(rows)
    state = rows.astype(F32)
    feed_one = line_weights(feed_one, *pieces[3:])
    grad_pieces = ring_gather(grad_rows)
    grad = grad_rows.astype(F32)

    part = stretch // 4

    def member_places(member, side_index):
        block = jnp.arange(4, dtype=jnp.int32)
        inner = jnp.arange(part, dtype=jnp.int32)
        home = (member - block + 4) % 4
        return (
            home[:, None] * (2 * stretch) + side_index * stretch + member * part + inner[None, :]
        ).reshape(-1)

    def line_places(side_index):
        return jnp.concatenate([member_places((x + step) % 4, side_index) for step in (0, 3, 1, 2)])

    places = line_places(core)
    key_places = jnp.concatenate([places, line_places(1 - core)]).reshape(1024, 1)
    half = HEAD_DIM // 2
    freq = ROPE_BASE ** (-jnp.arange(half, dtype=F32) * (2.0 / HEAD_DIM))
    angle = places.astype(F32)[:, None] * freq[None, :]
    cosine, sine = jnp.cos(angle), jnp.sin(angle)
    cosine_t, sine_t = cosine.T, sine.T
    places = places.reshape(1, 512)

    records = []
    for index, window in enumerate((WINDOW, 8 * stretch)):
        if index == 0:
            attn, feed = attn_one, feed_one
        else:
            attn, feed = attn_two, feed_two
        gain_attn, gain_feed = gains[2 * index], gains[2 * index + 1]
        if index == 0:
            queries, own, flat = project_call(True, pieces, gain_attn, attn, cosine, sine)
            flats = (flat,)
        else:
            flats = ring_gather(rms_norm(state, gain_attn).astype(BF16))
            feed_two = feed = line_weights(feed_two, *flats[1:3])
            queries, own = project_call(False, flats, gain_attn, attn, cosine, sine)
        other = lax.ppermute(own, "core", SWAP)
        line = (queries, own, other, places, key_places)
        after = grad_pieces[3:] if index else ()
        *partial, mixed, log_total = attend_call(window, length, *line, attn, after=after)
        saved_attn = (state, flats, line, mixed, log_total)
        state = state + ring_scatter(*partial)
        if index == 0:
            attn_two = attention_part(9, [], (mixed,))
            feed_two = feed_part(9, (mixed,), ())
        flats = ring_gather(rms_norm(state, gain_feed).astype(BF16))
        if index == 0:
            attn_two = line_weights(attn_two, *flats[1:3])
        *partial, gate, up, hidden = feed_forward_call(flats, feed)
        saved_feed = (state, flats, gate, up, hidden)
        state = state + ring_scatter(*partial)
        records.append((saved_attn, saved_feed, window))
    last_rows = state.astype(BF16)
    packed = ((attn_one, feed_one), (attn_two, feed_two))

    results = [None] * 18
    gain_grads = [None] * 4

    def feed_back(index, grad, pieces, after):
        state, flats, gate, up, hidden = records[index][1]
        *partial, low_gate, low_up = feed_backward_call(
            pieces, packed[index][1], gate, up, after=after
        )
        own_normed = ring_scatter_direct(*partial)
        grad, gain_grads[2 * index + 1] = norm_back(
            grad, own_normed, state, gains[2 * index + 1]
        )
        return grad, feed_weights_call(flats, pieces, low_gate, low_up, hidden)

    def attention_back(index, grad, pieces, after, late):
        state, flats, line, mixed, log_total = records[index][0]
        window = records[index][2]
        attn = packed[index][0]
        low_queries, pair_own, pair_other = attend_backward_call(
            window, length, pieces, *line, attn, log_total, cosine_t, sine_t, after=after
        )
        came = lax.ppermute(pair_other, "core", SWAP)
        *partial, low = unproject_call(
            low_queries, pair_own, came, cosine, sine, attn, after=late
        )
        own_normed = ring_scatter_direct(*partial)
        grad, gain_grads[2 * index] = norm_back(grad, own_normed, state, gains[2 * index])
        return grad, attend_weights_call(flats, pieces, low, mixed)

    def scatter(block):
        return lax.psum_scatter(block, SPREAD, scatter_dimension=0, tiled=True)[0]

    grad, feed_grad = feed_back(1, grad, grad_pieces, ())
    low = tie(grad.astype(BF16), feed_grad)
    second_feed = scatter(tie(feed_grad, low))
    grad, attn_grad = attention_back(1, grad, ring_gather(low), (last_rows,), ())
    low = tie(grad.astype(BF16), attn_grad)
    second_attn = scatter(tie(attn_grad, low, second_feed))

    grad, feed_grad = feed_back(0, grad, ring_gather(low), (second_feed,))
    low = tie(grad.astype(BF16), feed_grad)
    first_feed = scatter(tie(feed_grad, low, second_attn))
    second = yhi_sum(jnp.concatenate([second_feed, second_attn], axis=1), core, yhi)
    grad, attn_grad = attention_back(0, grad, ring_gather(low), (), (second,))
    low = grad.astype(BF16)
    attn_grad = tie(attn_grad, first_feed, low)
    attn_grad = jnp.concatenate([attn_grad, gain_rows(jnp.stack(gain_grads))], axis=2)
    first_attn = scatter(attn_grad)
    second_piece = cross(ylo_sum(second), 3072, first_attn)
    feed_piece = ylo_sum(yhi_sum(first_feed, core, yhi))
    back = from_lines(interleave(last_rows, low), z)
    output, input_grad = separate(back)
    output, input_grad = output[None], input_grad.astype(F32)[None]

    every = lax.all_gather(second_piece, ("x", "core"), axis=0, tiled=False)
    results[10:14], results[15:18] = unpack_call(every.reshape(4, 2, 96, -1))
    attn_piece = ylo_sum(yhi_sum(first_attn, core, yhi))
    first_piece = jnp.concatenate([feed_piece, cross(attn_piece, 0)], axis=1)
    every = lax.all_gather(first_piece, ("x", "core"), axis=0, tiled=False)
    every = every.reshape(4, 2, 96, -1)
    results[1:5], results[6:9] = unpack_call(every)
    gain_sums = every[..., 4224:4228].astype(F32).sum(axis=0).reshape(192, 4).T
    for index, slot in enumerate((0, 5, 9, 14)):
        results[slot] = gain_sums[index]
    return (output, input_grad, *results)


def solution(mesh):
    fine = Mesh(mesh.devices.reshape(SIZES), AXES)
    token = P(REP, SHARD, None)
    vector = P(SHARD)
    matrix = P(SHARD, None)
    layer = (vector, matrix, matrix, matrix, matrix, vector, matrix, matrix, matrix)
    return jax.shard_map(
        body,
        mesh=fine,
        in_specs=(token, P(REP), token) + layer + layer,
        out_specs=(token, token) + layer + layer,
        check_vma=False,
    )
```

```python
import functools
import jax
import jax.numpy as jnp
from jax import lax
from jax.experimental import pallas as pl
from jax.experimental.pallas import tpu as pltpu
from jax.sharding import Mesh
from jax.sharding import PartitionSpec as P

F32 = jnp.float32
BF16 = jnp.bfloat16
HEAD_DIM = 96
NEGATIVE = -1e30
MIB = 1 << 20

OFFSETS = (0, 128, 256, 384, 448)
SIZES_OF = (128, 128, 128, 64, 64)


def params(mib, semantics=None):
    return pltpu.CompilerParams(vmem_limit_bytes=mib * MIB, dimension_semantics=semantics)


def cost(flops, nbytes, transcendentals=0):
    return pl.CostEstimate(
        flops=int(flops), bytes_accessed=int(nbytes), transcendentals=int(transcendentals)
    )


def fill(target, refs):
    start = 0
    for ref in refs:
        rows = ref.shape[0]
        target[start : start + rows, :] = ref[...]
        start += rows


def nn(a, b):
    return lax.dot_general(a, b, (((1,), (0,)), ((), ())), preferred_element_type=F32)


def nt(a, b):
    return lax.dot_general(a, b, (((1,), (1,)), ((), ())), preferred_element_type=F32)


def tn(a, b):
    return lax.dot_general(a, b, (((0,), (0,)), ((), ())), preferred_element_type=F32)


def later(kernel, count, lead=0):
    if not count:
        return kernel

    def wrapped(*refs):
        return kernel(*refs[:lead], *refs[lead + count :])

    return wrapped


def anywhere(after):
    return [pl.BlockSpec(memory_space=pl.ANY)] * len(after)


def whole(shape):
    return pl.BlockSpec(shape, lambda *_: (0,) * len(shape))


PIECES = [whole((rows, 1536)) for rows in SIZES_OF]
PARTIAL_SHAPES = [
    jax.ShapeDtypeStruct((128, 1536), F32),
    jax.ShapeDtypeStruct((128, 1536), F32),
    jax.ShapeDtypeStruct((128, 1536), F32),
    jax.ShapeDtypeStruct((128, 1536), BF16),
]
LOW_PARTIAL_SHAPES = PARTIAL_SHAPES[:1] + [jax.ShapeDtypeStruct((128, 1536), BF16)] * 3
PARTIALS = [whole((128, 1536))] * 4


def emit(total, outs):
    for place, out in enumerate(outs):
        out[...] = total[128 * place : 128 * (place + 1), :].astype(out.dtype)


def down_parts(block):
    left = block[:, 0:128, :].reshape(256, 1024)
    right = jnp.concatenate([block[:, 128:192, 0:512], block[:, 128:192, 512:1024]], axis=1)
    return left, right.reshape(256, 512)


def feed_forward_kernel(*refs):
    pieces, (wg, wu, wd), outs = refs[:5], refs[5:8], refs[8:12]
    gate, up, hidden, flat, total = refs[12:]
    step = pl.program_id(0)

    @pl.when(step == 0)
    def _():
        fill(flat, pieces)

    rows = flat[...]
    g = nn(rows, wg[...])
    u = nn(rows, wu[...])
    gate[...] = g
    up[...] = u
    h = (g * jax.nn.sigmoid(g) * u).astype(BF16)
    hidden[...] = h
    left, right = down_parts(wd[...])
    left, right = nn(h, left), nn(h, right)

    @pl.when(step == 0)
    def _():
        total[:, :1024] = left
        total[:, 1024:] = right

    @pl.when(step > 0)
    def _():
        total[:, :1024] += left
        total[:, 1024:] += right

    @pl.when(step == 3)
    def _():
        emit(total, outs)


def feed_specs():
    return [
        pl.BlockSpec((1536, 256), lambda b: (0, b)),
        pl.BlockSpec((1536, 256), lambda b: (0, 4 + b)),
        pl.BlockSpec((2, 192, 1024), lambda b: (b, 0, 2)),
    ]


def column_block(rows):
    return pl.BlockSpec((rows, 256), lambda b: (0, b))


def feed_forward_call(pieces, packed, after=()):
    flat_packed = packed.reshape(1536, -1)
    return pl.pallas_call(
        later(feed_forward_kernel, len(after)),
        grid=(4,),
        in_specs=anywhere(after) + PIECES + feed_specs(),
        out_specs=PARTIALS + [column_block(512)] * 3,
        out_shape=PARTIAL_SHAPES
        + [
            jax.ShapeDtypeStruct((512, 1024), F32),
            jax.ShapeDtypeStruct((512, 1024), F32),
            jax.ShapeDtypeStruct((512, 1024), BF16),
        ],
        scratch_shapes=[pltpu.VMEM((512, 1536), BF16), pltpu.VMEM((512, 1536), F32)],
        compiler_params=params(40),
        cost_estimate=cost(4.9e9, 18e6),
        name="feed_forward",
    )(*after, *pieces, flat_packed, flat_packed, packed)


def feed_backward_kernel(*refs):
    pieces, (wg, wu, wd, gate, up), outs = refs[:5], refs[5:10], refs[10:14]
    low_gate, low_up, flat, total = refs[14:]
    step = pl.program_id(0)

    @pl.when(step == 0)
    def _():
        fill(flat, pieces)

    rows = flat[...]
    left, right = down_parts(wd[...])
    grad = nt(rows[:, :1024], left) + nt(rows[:, 1024:], right)
    g = gate[...]
    s = jax.nn.sigmoid(g)
    a = (grad * up[...] * s * (1.0 + g * (1.0 - s))).astype(BF16)
    b = (grad * (g * s)).astype(BF16)
    low_gate[...] = a
    low_up[...] = b
    part = nt(a, wg[...]) + nt(b, wu[...])

    @pl.when(step == 0)
    def _():
        total[...] = part

    @pl.when(step > 0)
    def _():
        total[...] += part

    @pl.when(step == 3)
    def _():
        emit(total, outs)


def feed_backward_call(pieces, packed, gate, up, after=()):
    flat_packed = packed.reshape(1536, -1)
    return pl.pallas_call(
        later(feed_backward_kernel, len(after)),
        grid=(4,),
        in_specs=anywhere(after) + PIECES + feed_specs() + [column_block(512)] * 2,
        out_specs=PARTIALS + [column_block(512)] * 2,
        out_shape=LOW_PARTIAL_SHAPES + [jax.ShapeDtypeStruct((512, 1024), BF16)] * 2,
        scratch_shapes=[pltpu.VMEM((512, 1536), BF16), pltpu.VMEM((512, 1536), F32)],
        compiler_params=params(40),
        cost_estimate=cost(4.9e9, 20e6),
        name="feed_backward",
    )(*after, *pieces, flat_packed, flat_packed, packed, gate, up)


def feed_weights_kernel(*refs):
    flats, grads = refs[:5], refs[5:10]
    low_gate, low_up, hidden, out, flat_t, hidden_t, grad = refs[10:]
    step = pl.program_id(0)

    @pl.when(step == 0)
    def _():
        start = 0
        for ref in flats:
            n = ref.shape[0]
            flat_t[:, start : start + n] = ref[...].T
            start += n

    @pl.when(step == 4)
    def _():
        hidden_t[...] = hidden[...].T
        fill(grad, grads)

    @pl.when(step < 4)
    def _():
        out[...] = nn(flat_t[...], low_gate[...]).astype(BF16).reshape(8, 192, 256)

    @pl.when((step >= 4) & (step < 8))
    def _():
        out[...] = nn(flat_t[...], low_up[...]).astype(BF16).reshape(8, 192, 256)

    for q in range(4):

        @pl.when(step == 8 + q)
        def _():
            top = nn(hidden_t[...], grad[:, 256 * q : 256 * (q + 1)]).astype(BF16)
            out[:, 0:128, :] = top.reshape(8, 128, 256)
            half = 64 * (q // 2)
            some = hidden_t[...].reshape(8, 128, 512)[:, half : half + 64].reshape(512, 512)
            start = 1024 + 256 * (q % 2)
            low = nn(some, grad[:, start : start + 256]).astype(BF16)
            out[:, 128:192, :] = low.reshape(8, 64, 256)


def feed_weights_call(flats, grads, low_gate, low_up, hidden):
    return pl.pallas_call(
        feed_weights_kernel,
        grid=(12,),
        in_specs=PIECES
        + PIECES
        + [
            pl.BlockSpec((512, 256), lambda b: (0, jnp.minimum(b, 3))),
            pl.BlockSpec((512, 256), lambda b: (0, jnp.clip(b - 4, 0, 3))),
            whole((512, 1024)),
        ],
        out_specs=pl.BlockSpec((8, 192, 256), lambda b: (0, 0, b)),
        out_shape=jax.ShapeDtypeStruct((8, 192, 3072), BF16),
        scratch_shapes=[
            pltpu.VMEM((1536, 512), BF16),
            pltpu.VMEM((1024, 512), BF16),
            pltpu.VMEM((512, 1536), BF16),
        ],
        compiler_params=params(40),
        cost_estimate=cost(4.9e9, 18e6),
        name="feed_weights",
    )(*flats, *grads, low_gate, low_up, hidden)


def piece_specs(pieces):
    return [whole(item.shape) for item in pieces]


def turn_columns(block, cosine, sine):
    out = []
    for start in range(0, block.shape[1], HEAD_DIM):
        a = block[:, start : start + 48]
        b = block[:, start + 48 : start + HEAD_DIM]
        out.append(a * cosine - b * sine)
        out.append(b * cosine + a * sine)
    return jnp.concatenate(out, axis=1)


def project_kernel(raw, count, *refs):
    pieces, (gain, weight, cosine, sine, queries, pair) = refs[:count], refs[count : count + 6]
    if raw:
        flat = refs[-1]
        start = 0
        for ref in pieces:
            n = ref.shape[0]
            rows = ref[...].astype(F32)
            scale = lax.rsqrt(jnp.mean(rows * rows, axis=-1, keepdims=True) + 1e-05)
            flat[start : start + n, :] = (rows * scale * gain[...]).astype(BF16)
            start += n
    else:
        flat = refs[-1]
        fill(flat, pieces)
    both = nn(flat[...], weight[...])
    cos, sin = cosine[...], sine[...]
    queries[...] = turn_columns(both[:, :384], cos, sin).astype(BF16)
    keys = turn_columns(both[:, 384:576], cos, sin)
    pair[...] = jnp.concatenate([keys, both[:, 576:768]], axis=1).astype(BF16)


def project_call(raw, pieces, gain, packed, cosine, sine, after=()):
    wide = packed.shape[-1]
    shape = jax.ShapeDtypeStruct((512, 384), BF16)
    flat_shape = jax.ShapeDtypeStruct((512, 1536), BF16)
    return pl.pallas_call(
        later(functools.partial(project_kernel, raw, len(pieces)), len(after)),
        grid=(1,),
        in_specs=anywhere(after)
        + piece_specs(pieces)
        + [whole((1, 1536)), projection_spec(), whole((512, 48)), whole((512, 48))],
        out_specs=[whole((512, 384))] * 2 + ([whole((512, 1536))] if raw else []),
        out_shape=[shape, shape] + ([flat_shape] if raw else []),
        scratch_shapes=[] if raw else [pltpu.VMEM((512, 1536), BF16)],
        compiler_params=params(40),
        cost_estimate=cost(1.3e9, 6e6),
        name="project",
    )(*after, *pieces, gain.reshape(1, 1536), packed.reshape(1536, wide), cosine, sine)


def fill_bias(bias, length, places, key_places, window):
    gap = places[...] - key_places[...]
    inside = (key_places[...] < length) & (gap >= 0) & (gap < window)
    bias[...] = jnp.where(inside | (gap == 0), 0.0, NEGATIVE)


def both_rows(own, other, start):
    return jnp.concatenate(
        [own[:, start : start + HEAD_DIM], other[:, start : start + HEAD_DIM]], axis=0
    )


def attend_kernel(window, length, queries, own, other, places, key_places, w_out, *refs):
    outs, (mixed, log_total, total, bias) = refs[:4], refs[4:]
    fill_bias(bias, length[0], places, key_places, window)
    sums = []
    stats = []
    for head in range(4):
        if head % 2 == 0:
            keys = both_rows(own[...], other[...], HEAD_DIM * (head // 2))
            values = both_rows(own[...], other[...], 192 + HEAD_DIM * (head // 2)).T
        query = queries[:, HEAD_DIM * head : HEAD_DIM * (head + 1)]
        scores = nt(keys, query) * HEAD_DIM ** (-0.5) + bias[...]
        peak = jnp.max(scores, axis=0, keepdims=True)
        probs = jnp.exp(scores - peak)
        totals = jnp.sum(probs, axis=0, keepdims=True)
        part = nn(values, probs.astype(BF16)) / totals
        sums.append(part.astype(BF16).astype(F32).T.astype(BF16))
        stats.append(peak + jnp.log(totals))
        for block in range(4):
            cols = slice(384 * block, 384 * (block + 1))
            value = nn(sums[-1], out_block(w_out, head, block))
            if head == 0:
                total[:, cols] = value
            else:
                total[:, cols] += value
    mixed[...] = jnp.concatenate(sums, axis=1)
    log_total[...] = jnp.concatenate(stats + stats, axis=0)
    emit(total, outs)


def line_specs():
    return [whole((512, 384))] * 3 + [whole((1, 512)), whole((1024, 1))]


def out_spec():
    return pl.BlockSpec((8, 192, 384), lambda *_: (0, 0, 2))


def out_block(w_out, head, block):
    start = 96 * (head % 2)
    return w_out[2 * block + head // 2, start : start + 96, :]


def projection_spec():
    return pl.BlockSpec((1536, 768), lambda *_: (0, 0))


def attend_call(window, length, queries, own, other, places, key_places, packed, after=()):
    return pl.pallas_call(
        later(functools.partial(attend_kernel, window), len(after)),
        grid=(1,),
        in_specs=anywhere(after)
        + [pl.BlockSpec(memory_space=pltpu.SMEM)] + line_specs() + [out_spec()],
        out_specs=PARTIALS + [whole((512, 384)), whole((8, 512))],
        out_shape=PARTIAL_SHAPES
        + [jax.ShapeDtypeStruct((512, 384), BF16), jax.ShapeDtypeStruct((8, 512), F32)],
        scratch_shapes=[pltpu.VMEM((512, 1536), F32), pltpu.VMEM((1024, 512), F32)],
        compiler_params=params(48),
        cost_estimate=cost(3e9, 6e6, 2e6),
        name="attend",
    )(*after, length, queries, own, other, places, key_places, packed)


def attend_backward_kernel(window, length, *refs):
    pieces, refs = refs[:5], refs[5:]
    queries, own, other, places, key_places, w_out, log_total, cosine, sine = refs[:9]
    low_queries, pair_own, pair_other, grad, bias = refs[9:]
    fill(grad, pieces)
    fill_bias(bias, length[0], places, key_places, window)
    cos, sin = cosine[...], sine[...]
    lows = []
    key_sums = []
    value_sums = []
    for head in range(4):
        if head % 2 == 0:
            keys = both_rows(own[...], other[...], HEAD_DIM * (head // 2))
            values = both_rows(own[...], other[...], 192 + HEAD_DIM * (head // 2))
            keys_t = keys.T
        query = queries[:, HEAD_DIM * head : HEAD_DIM * (head + 1)]
        mixed = nt(grad[:, :384], out_block(w_out, head, 0))
        for block in range(1, 4):
            mixed += nt(
                grad[:, 384 * block : 384 * (block + 1)], out_block(w_out, head, block)
            )
        mixed = mixed.astype(BF16)
        scores = nt(keys, query) * HEAD_DIM ** (-0.5) + bias[...]
        probs = jnp.exp(scores - log_total[head : head + 1, :])
        slopes = nt(values, mixed)
        inner = jnp.sum(probs * slopes, axis=0, keepdims=True)
        raw = (probs * (slopes - inner) * HEAD_DIM ** (-0.5)).astype(BF16)
        key_part = nn(raw, query)
        value_part = nn(probs.astype(BF16), mixed)
        if head % 2 == 0:
            key_sums.append(key_part)
            value_sums.append(value_part)
        else:
            key_sums[-1] += key_part
            value_sums[-1] += value_part
        turned = nn(keys_t, raw)
        a, b = turned[:48], turned[48:]
        turned = jnp.concatenate([a * cos + b * sin, b * cos - a * sin], axis=0)
        lows.append(turned.T.astype(BF16))
    low_queries[...] = jnp.concatenate(lows, axis=1)
    both = jnp.concatenate(key_sums + value_sums, axis=1)
    pair_own[...] = both[:512]
    pair_other[...] = both[512:].astype(BF16)


def attend_backward_call(
    window,
    length,
    pieces,
    queries,
    own,
    other,
    places,
    key_places,
    packed,
    log_total,
    cosine,
    sine,
    after=(),
):
    return pl.pallas_call(
        later(functools.partial(attend_backward_kernel, window), len(after)),
        grid=(1,),
        in_specs=anywhere(after)
        + [pl.BlockSpec(memory_space=pltpu.SMEM)]
        + PIECES
        + line_specs()
        + [out_spec(), whole((8, 512)), whole((48, 512)), whole((48, 512))],
        out_specs=[whole((512, 384))] * 3,
        out_shape=[
            jax.ShapeDtypeStruct((512, 384), BF16),
            jax.ShapeDtypeStruct((512, 384), F32),
            jax.ShapeDtypeStruct((512, 384), BF16),
        ],
        scratch_shapes=[pltpu.VMEM((512, 1536), BF16), pltpu.VMEM((1024, 512), F32)],
        compiler_params=params(52),
        cost_estimate=cost(6e9, 6e6, 2e6),
        name="attend_backward",
    )(
        *after,
        length,
        *pieces,
        queries,
        own,
        other,
        places,
        key_places,
        packed,
        log_total,
        cosine,
        sine,
    )


def unproject_kernel(low_queries, pair_own, pair_came, cosine, sine, weight, *refs):
    outs, low = refs[:4], refs[4]
    both = pair_own[...] + pair_came[...].astype(F32)
    keys = turn_columns(both[:, :192], cosine[...], -sine[...])
    rows = jnp.concatenate(
        [low_queries[...], keys.astype(BF16), both[:, 192:].astype(BF16)], axis=1
    )
    low[...] = rows
    emit(nt(rows, weight[...]), outs)


def unproject_call(low_queries, pair_own, pair_came, cosine, sine, packed, after=()):
    wide = packed.shape[-1]
    return pl.pallas_call(
        later(unproject_kernel, len(after)),
        grid=(1,),
        in_specs=anywhere(after)
        + [whole((512, 384))] * 3
        + [whole((512, 48))] * 2
        + [projection_spec()],
        out_specs=PARTIALS + [whole((512, 768))],
        out_shape=LOW_PARTIAL_SHAPES + [jax.ShapeDtypeStruct((512, 768), BF16)],
        compiler_params=params(40),
        cost_estimate=cost(1.3e9, 7e6),
        name="unproject",
    )(*after, low_queries, pair_own, pair_came, cosine, sine, packed.reshape(1536, wide))


def attend_weights_kernel(count, *refs):
    flats, grads, (low, mixed) = refs[:count], refs[count : count + 5], refs[count + 5 : count + 7]
    out, flat_t, grad = refs[count + 7 :]
    start = 0
    for ref in flats:
        n = ref.shape[0]
        flat_t[:, start : start + n] = ref[...].T
        start += n
    fill(grad, grads)
    for block in range(3):
        cols = slice(256 * block, 256 * (block + 1))
        out[:, :, cols] = nn(flat_t[...], low[:, cols]).astype(BF16).reshape(8, 192, 256)
    mixed_t = mixed[...].T
    for block in range(4):
        part = nn(mixed_t, grad[:, 384 * block : 384 * (block + 1)]).astype(BF16)
        out[2 * block : 2 * block + 2, :, 768:1152] = part.reshape(2, 192, 384)


def attend_weights_call(flats, grads, low, mixed):
    return pl.pallas_call(
        functools.partial(attend_weights_kernel, len(flats)),
        grid=(1,),
        in_specs=piece_specs(flats) + PIECES + [whole((512, 768)), whole((512, 384))],
        out_specs=whole((8, 192, 1152)),
        out_shape=jax.ShapeDtypeStruct((8, 192, 1152), BF16),
        scratch_shapes=[pltpu.VMEM((1536, 512), BF16), pltpu.VMEM((512, 1536), BF16)],
        compiler_params=params(40),
        cost_estimate=cost(1.9e9, 10e6),
        name="attend_weights",
    )(*flats, *grads, low, mixed)


def unpack_kernel(*refs):
    every, wq, wk, wv, wo, gate, up, down = refs
    side = pl.program_id(0)
    blocks = [every[x, 0] for x in range(4)]
    for x, block in enumerate(blocks):
        wq[:, 384 * x : 384 * (x + 1)] = block[:, 3072:3456].astype(F32)
        wo[:, 384 * x : 384 * (x + 1)] = block[:, 3840:4224].astype(F32)
        for s in range(8):
            cols = slice(512 * s + 128 * x, 512 * s + 128 * (x + 1))
            gate[:, cols] = block[:, 128 * s : 128 * (s + 1)].astype(F32)
            up[:, cols] = block[:, 1024 + 128 * s : 1024 + 128 * (s + 1)].astype(F32)

        @pl.when(side == 0)
        def _(x=x, block=block):
            down[x, 0:96, :1024] = block[:, 2048:3072].astype(F32)

        @pl.when(side == 1)
        def _(x=x, block=block):
            down[x, 96:128, :1024] = block[0:32, 2048:3072].astype(F32)
            down[x, 0:64, 1024:] = block[32:96, 2048:2560].astype(F32)
            down[x, 64:128, 1024:] = block[32:96, 2560:3072].astype(F32)

    wk[...] = jnp.concatenate([block[:, 3456:3648].astype(F32) for block in blocks], axis=1)
    wv[...] = jnp.concatenate([block[:, 3648:3840].astype(F32) for block in blocks], axis=1)


def unpack_call(every):
    widths = (1536, 768, 768, 1536, 4096, 4096)
    out = pl.pallas_call(
        unpack_kernel,
        grid=(2,),
        in_specs=[pl.BlockSpec((4, 1, 96, every.shape[-1]), lambda b: (0, b, 0, 0))],
        out_specs=[pl.BlockSpec((96, width), lambda b: (b, 0)) for width in widths]
        + [whole((4, 128, 1536))],
        out_shape=[jax.ShapeDtypeStruct((192, width), F32) for width in widths]
        + [jax.ShapeDtypeStruct((4, 128, 1536), F32)],
        compiler_params=params(48),
        cost_estimate=cost(1e6, 30e6),
        name="unpack",
    )(every)
    return out[:4], (out[4], out[5], out[6].reshape(512, 1536))


def pack_feed_kernel(where, w_gate, w_up, w_down, out):
    x = where[0]
    for s in range(8):
        cols = pl.ds(pl.multiple_of(512 * s + 128 * x, 128), 128)
        out[:, 128 * s : 128 * (s + 1)] = w_gate[:, cols]
        out[:, 1024 + 128 * s : 1024 + 128 * (s + 1)] = w_up[:, cols]
    out[0:128, 2048:3072] = w_down[:, 0:1024]
    out[128:192, 2048:2560] = w_down[0:64, 1024:1536]
    out[128:192, 2560:3072] = w_down[64:128, 1024:1536]


def pack_feed_call(where, w_gate, w_up, w_down, after=()):
    return pl.pallas_call(
        later(pack_feed_kernel, len(after), 1),
        grid_spec=pltpu.PrefetchScalarGridSpec(
            num_scalar_prefetch=1,
            grid=(1,),
            in_specs=anywhere(after)
            + [
                pl.BlockSpec((192, 4096), lambda b, w: (0, 0)),
                pl.BlockSpec((192, 4096), lambda b, w: (0, 0)),
                pl.BlockSpec((128, 1536), lambda b, w: (w[0], 0)),
            ],
            out_specs=pl.BlockSpec((192, 3072), lambda b, w: (0, 0)),
        ),
        out_shape=jax.ShapeDtypeStruct((192, 3072), BF16),
        compiler_params=params(24),
        cost_estimate=cost(1e3, 5e6),
        name="pack_feed",
    )(where, *after, w_gate, w_up, w_down)


WINDOW = 512
EPSILON = 1e-05
ROPE_BASE = 100000.0

AXES = ("ylo", "x", "core", "z", "yhi")
SIZES = (2, 4, 2, 4, 2)
REP = ("ylo", "x", "core")
SHARD = ("z", "yhi")
SPREAD = ("z", "core")

RIGHT = [(i, (i + 1) % 4) for i in range(4)]
LEFT = [(i, (i - 1) % 4) for i in range(4)]
ACROSS = [(i, (i + 2) % 4) for i in range(4)]
SWAP = [(0, 1), (1, 0)]


def number(ylo, x, core, z, yhi):
    return (((ylo * 4 + x) * 2 + core) * 4 + z) * 2 + yhi


def permutation(place, taken=None):
    pairs = []
    for ylo in range(2):
        for x in range(4):
            for core in range(2):
                for z in range(4):
                    for yhi in range(2):
                        here = (ylo, x, core, z, yhi)
                        if taken is None or taken(*here):
                            pairs.append((number(*here), number(*place(*here))))
    return pairs


def inverse(pairs):
    return [(there, here) for here, there in pairs]


def at_home(ylo, x, core, z, yhi):
    return core == yhi


LINES = [
    permutation(lambda l, x, c, z, h, k=k: (l, (z + k) % 4, h, x, c)) for k in range(4)
]
TURN = permutation(lambda l, x, c, z, h: (l, z, h, x, c))
SHARE = permutation(lambda l, x, c, z, h: (l, x, c, z, 1 - h), at_home)
CROSS = permutation(lambda l, x, c, z, h: (l, z, c, x, h))


def to_lines(block, z):
    part = block.shape[0] // 4
    out = []
    for k in range(4):
        piece = lax.dynamic_slice_in_dim(block, ((z + k) % 4) * part, part, axis=0)
        out.append(lax.ppermute(piece, AXES, LINES[k]))
    return out


def from_lines(block, z):
    part = block.shape[0] // 4
    out = jnp.zeros_like(block)
    for k in range(4):
        piece = lax.ppermute(block[part * k : part * (k + 1)], AXES, inverse(LINES[k]))
        out = lax.dynamic_update_slice_in_dim(out, piece, ((z + k) % 4) * part, axis=0)
    return out


def interleave(first, second):
    parts = [item[32 * k : 32 * (k + 1)] for k in range(4) for item in (first, second)]
    return jnp.concatenate(parts, axis=0)


def separate(block):
    parts = [block[32 * k : 32 * (k + 1)] for k in range(8)]
    return jnp.concatenate(parts[::2], axis=0), jnp.concatenate(parts[1::2], axis=0)


def ring_gather(block):
    half = block.shape[0] // 2
    from_left = lax.ppermute(block, "x", RIGHT)
    from_right = lax.ppermute(block, "x", LEFT)
    far_first = lax.ppermute(from_left[:half], "x", RIGHT)
    far_second = lax.ppermute(from_right[half:], "x", LEFT)
    return block, from_left, from_right, far_first, far_second


def ring_scatter(own, left, right, far):
    half = far.shape[0] // 2
    first = lax.ppermute(far[:half], "x", RIGHT).astype(F32)
    second = lax.ppermute(far[half:], "x", LEFT).astype(F32)
    right = jnp.concatenate([right[:half] + first, right[half:]], axis=0).astype(BF16)
    left = jnp.concatenate([left[:half], left[half:] + second], axis=0).astype(BF16)
    from_left = lax.ppermute(right, "x", RIGHT).astype(F32)
    from_right = lax.ppermute(left, "x", LEFT).astype(F32)
    return own + from_left + from_right


def ring_scatter_direct(own, left, right, far):
    from_left = lax.ppermute(right, "x", RIGHT).astype(F32)
    from_right = lax.ppermute(left, "x", LEFT).astype(F32)
    from_far = lax.ppermute(far, "x", ACROSS).astype(F32)
    return own + from_left + from_right + from_far


def tie(value, *others):
    return lax.optimization_barrier((value, *others))[0]


def rms_norm(values, gain):
    return values * lax.rsqrt(jnp.mean(values * values, axis=-1, keepdims=True) + EPSILON) * gain


def add_low(mine, came):
    return (mine.astype(F32) + came.astype(F32)).astype(BF16)


def yhi_sum(rows, core, yhi):
    mine = lax.dynamic_slice_in_dim(rows, 96 * core, 96, axis=0)
    theirs = lax.dynamic_slice_in_dim(rows, 96 * (1 - core), 96, axis=0)
    came = lax.ppermute(theirs, "core", SWAP)
    home = core == yhi
    kept = jnp.where(home, mine, came)
    away = jnp.where(home, came, mine)
    return add_low(kept, lax.ppermute(away, "yhi", SWAP))


def ylo_sum(piece):
    return add_low(piece, lax.ppermute(piece, "ylo", SWAP))


def cross(piece, start, *others):
    first, last = start + 768, start + 1152
    moved = lax.ppermute(piece[:, first:last], AXES, CROSS)
    if others:
        piece, moved = lax.optimization_barrier((piece, moved, *others))[:2]
    return jnp.concatenate([piece[:, :first], moved, piece[:, last:]], axis=1)


def gain_rows(grads):
    tall = grads.astype(BF16).T.reshape(8, 192, 4)
    return jnp.pad(tall, ((0, 0), (0, 0), (0, 124)))


def norm_back(grad, own_normed, state, gain):
    grad_state, grad_gain = jax.vjp(rms_norm, state, gain)[1](own_normed)
    return grad + grad_state, grad_gain


def body(tokens, lengths, grad_output, *weights):
    stretch, width = tokens.shape[1:]
    x = lax.axis_index("x")
    core = lax.axis_index("core")
    z = lax.axis_index("z")
    yhi = lax.axis_index("yhi")
    member = x.astype(jnp.int32).reshape(1)
    home = core == yhi

    gains = jnp.stack([weights[0], weights[5], weights[9], weights[14]]).T
    gains = jnp.pad(gains, ((0, 0), (0, 124)))

    def shared(block, *joined):
        return jnp.where(home, block, tie(lax.ppermute(block, AXES, SHARE), *joined))

    def attention_part(base, extra, after):
        block = lax.dynamic_slice(tie(weights[base + 4], *after), (0, 384 * x), (192, 384))
        block = lax.ppermute(block, AXES, TURN)
        parts = [
            lax.dynamic_slice(w, (0, x * (w.shape[1] // 4)), (192, w.shape[1] // 4))
            for w in weights[base + 1 : base + 4]
        ]
        parts = shared(jnp.concatenate(parts + extra, axis=1))
        return jnp.concatenate([parts[:, :768], block, parts[:, 768:]], axis=1)

    def feed_part(base, after, joined):
        part = pack_feed_call(member, *weights[base + 6 : base + 9], after=after)
        return shared(part, *joined)

    def line_weights(piece, *after):
        return lax.all_gather(tie(piece, *after), SPREAD, axis=0, tiled=False)

    here = (2 * z + yhi) * stretch + jnp.arange(stretch, dtype=jnp.int32)
    valid = (here < lengths[0])[:, None]
    grad_start = jnp.where(valid, grad_output[0], 0).astype(BF16)
    length = lax.ppermute(lengths, AXES, TURN)
    moved = to_lines(interleave(tokens[0], grad_start), z)
    rows, grad_rows = separate(jnp.concatenate(moved, axis=0))

    attn_one = line_weights(attention_part(0, [gains], ()))
    feed_one = feed_part(0, (), moved)
    gains = attn_one[:, :, 1152:1156].transpose(2, 0, 1).reshape(4, width).astype(F32)
    pieces = ring_gather(rows)
    state = rows.astype(F32)
    feed_one = line_weights(feed_one, *pieces[3:])
    grad_pieces = ring_gather(grad_rows)
    grad = grad_rows.astype(F32)

    part = stretch // 4

    def member_places(member, side_index):
        block = jnp.arange(4, dtype=jnp.int32)
        inner = jnp.arange(part, dtype=jnp.int32)
        home = (member - block + 4) % 4
        return (
            home[:, None] * (2 * stretch) + side_index * stretch + member * part + inner[None, :]
        ).reshape(-1)

    def line_places(side_index):
        return jnp.concatenate([member_places((x + step) % 4, side_index) for step in (0, 3, 1, 2)])

    places = line_places(core)
    key_places = jnp.concatenate([places, line_places(1 - core)]).reshape(1024, 1)
    half = HEAD_DIM // 2
    freq = ROPE_BASE ** (-jnp.arange(half, dtype=F32) * (2.0 / HEAD_DIM))
    angle = places.astype(F32)[:, None] * freq[None, :]
    cosine, sine = jnp.cos(angle), jnp.sin(angle)
    cosine_t, sine_t = cosine.T, sine.T
    places = places.reshape(1, 512)

    records = []
    for index, window in enumerate((WINDOW, 8 * stretch)):
        if index == 0:
            attn, feed = attn_one, feed_one
        else:
            attn, feed = attn_two, feed_two
        gain_attn, gain_feed = gains[2 * index], gains[2 * index + 1]
        if index == 0:
            queries, own, flat = project_call(True, pieces, gain_attn, attn, cosine, sine)
            flats = (flat,)
        else:
            flats = ring_gather(rms_norm(state, gain_attn).astype(BF16))
            feed_two = feed = line_weights(feed_two, *flats[1:3])
            queries, own = project_call(False, flats, gain_attn, attn, cosine, sine)
        other = lax.ppermute(own, "core", SWAP)
        line = (queries, own, other, places, key_places)
        after = grad_pieces[3:] if index else ()
        *partial, mixed, log_total = attend_call(window, length, *line, attn, after=after)
        saved_attn = (state, flats, line, mixed, log_total)
        state = state + ring_scatter(*partial)
        if index == 0:
            attn_two = attention_part(9, [], (mixed,))
            feed_two = feed_part(9, (mixed,), ())
        flats = ring_gather(rms_norm(state, gain_feed).astype(BF16))
        if index == 0:
            attn_two = line_weights(attn_two, *flats[1:3])
        *partial, gate, up, hidden = feed_forward_call(flats, feed)
        saved_feed = (state, flats, gate, up, hidden)
        state = state + ring_scatter(*partial)
        records.append((saved_attn, saved_feed, window))
    last_rows = state.astype(BF16)
    packed = ((attn_one, feed_one), (attn_two, feed_two))

    results = [None] * 18
    gain_grads = [None] * 4

    def feed_back(index, grad, pieces, after):
        state, flats, gate, up, hidden = records[index][1]
        *partial, low_gate, low_up = feed_backward_call(
            pieces, packed[index][1], gate, up, after=after
        )
        own_normed = ring_scatter_direct(*partial)
        grad, gain_grads[2 * index + 1] = norm_back(
            grad, own_normed, state, gains[2 * index + 1]
        )
        return grad, feed_weights_call(flats, pieces, low_gate, low_up, hidden)

    def attention_back(index, grad, pieces, after, late):
        state, flats, line, mixed, log_total = records[index][0]
        window = records[index][2]
        attn = packed[index][0]
        low_queries, pair_own, pair_other = attend_backward_call(
            window, length, pieces, *line, attn, log_total, cosine_t, sine_t, after=after
        )
        came = lax.ppermute(pair_other, "core", SWAP)
        *partial, low = unproject_call(
            low_queries, pair_own, came, cosine, sine, attn, after=late
        )
        own_normed = ring_scatter_direct(*partial)
        grad, gain_grads[2 * index] = norm_back(grad, own_normed, state, gains[2 * index])
        return grad, attend_weights_call(flats, pieces, low, mixed)

    def scatter(block):
        return lax.psum_scatter(block, SPREAD, scatter_dimension=0, tiled=True)

    grad, feed_grad = feed_back(1, grad, grad_pieces, ())
    low = tie(grad.astype(BF16), feed_grad)
    second_feed = scatter(tie(feed_grad, low))
    grad, attn_grad = attention_back(1, grad, ring_gather(low), (last_rows,), ())
    low = tie(grad.astype(BF16), attn_grad)
    second_attn = scatter(tie(attn_grad, low, second_feed))

    grad, feed_grad = feed_back(0, grad, ring_gather(low), (second_feed,))
    low = tie(grad.astype(BF16), feed_grad)
    first_feed = scatter(tie(feed_grad, low, second_attn))
    second = yhi_sum(jnp.concatenate([second_feed, second_attn], axis=2)[0], core, yhi)
    grad, attn_grad = attention_back(0, grad, ring_gather(low), (), (second,))
    low = grad.astype(BF16)
    attn_grad = tie(attn_grad, first_feed, low)
    attn_grad = jnp.concatenate([attn_grad, gain_rows(jnp.stack(gain_grads))], axis=2)
    first_attn = scatter(attn_grad)
    second_piece = cross(ylo_sum(second), 3072, first_attn)
    feed_piece = ylo_sum(yhi_sum(first_feed[0], core, yhi))
    back = from_lines(interleave(last_rows, low), z)
    output, input_grad = separate(back)
    output, input_grad = output[None], input_grad.astype(F32)[None]

    every = lax.all_gather(second_piece, ("x", "core"), axis=0, tiled=False)
    results[10:14], results[15:18] = unpack_call(every.reshape(4, 2, 96, -1))
    attn_piece = ylo_sum(yhi_sum(tie(first_attn, feed_piece)[0], core, yhi))
    first_piece = jnp.concatenate([feed_piece, cross(attn_piece, 0)], axis=1)
    every = lax.all_gather(first_piece, ("x", "core"), axis=0, tiled=False)
    every = every.reshape(4, 2, 96, -1)
    results[1:5], results[6:9] = unpack_call(every)
    gain_sums = every[..., 4224:4228].astype(F32).sum(axis=0).reshape(192, 4).T
    for index, slot in enumerate((0, 5, 9, 14)):
        results[slot] = gain_sums[index]
    return (output, input_grad, *results)


def solution(mesh):
    fine = Mesh(mesh.devices.reshape(SIZES), AXES)
    token = P(REP, SHARD, None)
    vector = P(SHARD)
    matrix = P(SHARD, None)
    layer = (vector, matrix, matrix, matrix, matrix, vector, matrix, matrix, matrix)
    return jax.shard_map(
        body,
        mesh=fine,
        in_specs=(token, P(REP), token) + layer + layer,
        out_specs=(token, token) + layer + layer,
        check_vma=False,
    )
```

```python
import functools
import jax
import jax.numpy as jnp
from jax import lax
from jax.experimental import pallas as pl
from jax.experimental.pallas import tpu as pltpu
from jax.sharding import Mesh
from jax.sharding import PartitionSpec as P

F32 = jnp.float32
BF16 = jnp.bfloat16
HEAD_DIM = 96
NEGATIVE = -1e30
MIB = 1 << 20

OFFSETS = (0, 128, 256, 384, 448)
SIZES_OF = (128, 128, 128, 64, 64)


def params(mib, semantics=None):
    return pltpu.CompilerParams(vmem_limit_bytes=mib * MIB, dimension_semantics=semantics)


def cost(flops, nbytes, transcendentals=0):
    return pl.CostEstimate(
        flops=int(flops), bytes_accessed=int(nbytes), transcendentals=int(transcendentals)
    )


def fill(target, refs):
    start = 0
    for ref in refs:
        rows = ref.shape[0]
        target[start : start + rows, :] = ref[...]
        start += rows


def nn(a, b):
    return lax.dot_general(a, b, (((1,), (0,)), ((), ())), preferred_element_type=F32)


def nt(a, b):
    return lax.dot_general(a, b, (((1,), (1,)), ((), ())), preferred_element_type=F32)


def tn(a, b):
    return lax.dot_general(a, b, (((0,), (0,)), ((), ())), preferred_element_type=F32)


def later(kernel, count, lead=0):
    if not count:
        return kernel

    def wrapped(*refs):
        return kernel(*refs[:lead], *refs[lead + count :])

    return wrapped


def anywhere(after):
    return [pl.BlockSpec(memory_space=pl.ANY)] * len(after)


def whole(shape):
    return pl.BlockSpec(shape, lambda *_: (0,) * len(shape))


PIECES = [whole((rows, 1536)) for rows in SIZES_OF]
PARTIAL_SHAPES = [
    jax.ShapeDtypeStruct((128, 1536), F32),
    jax.ShapeDtypeStruct((128, 1536), F32),
    jax.ShapeDtypeStruct((128, 1536), F32),
    jax.ShapeDtypeStruct((128, 1536), BF16),
]
LOW_PARTIAL_SHAPES = PARTIAL_SHAPES[:1] + [jax.ShapeDtypeStruct((128, 1536), BF16)] * 3
PARTIALS = [whole((128, 1536))] * 4


def emit(total, outs):
    for place, out in enumerate(outs):
        out[...] = total[128 * place : 128 * (place + 1), :].astype(out.dtype)


def down_parts(block):
    left = block[:, 0:128, :].reshape(256, 1024)
    right = jnp.concatenate([block[:, 128:192, 0:512], block[:, 128:192, 512:1024]], axis=1)
    return left, right.reshape(256, 512)


def feed_forward_kernel(count, parts, *refs):
    pieces, (wg, wu, wd) = refs[:count], refs[count : count + 3]
    outs = refs[count + 3 : count + 3 + parts]
    gate, up, hidden, flat, total = refs[count + 3 + parts :]
    step = pl.program_id(0)

    @pl.when(step == 0)
    def _():
        fill(flat, pieces)

    rows = flat[...]
    g = nn(rows, wg[...])
    u = nn(rows, wu[...])
    gate[...] = g
    up[...] = u
    h = (g * jax.nn.sigmoid(g) * u).astype(BF16)
    hidden[...] = h
    left, right = down_parts(wd[...])
    left, right = nn(h, left), nn(h, right)

    @pl.when(step == 0)
    def _():
        total[:, :1024] = left
        total[:, 1024:] = right

    @pl.when(step > 0)
    def _():
        total[:, :1024] += left
        total[:, 1024:] += right

    @pl.when(step == 3)
    def _():
        emit(total, outs)


def feed_specs():
    return [
        pl.BlockSpec((1536, 256), lambda b: (0, b)),
        pl.BlockSpec((1536, 256), lambda b: (0, 4 + b)),
        pl.BlockSpec((2, 192, 1024), lambda b: (b, 0, 2)),
    ]


def column_block(rows):
    return pl.BlockSpec((rows, 256), lambda b: (0, b))


def chunk_shapes(pieces, own):
    rows = sum(item.shape[0] for item in pieces)
    kind = F32 if own else BF16
    return rows, [jax.ShapeDtypeStruct((128, 1536), kind)] * (rows // 128)


def feed_forward_call(pieces, packed, own):
    flat_packed = packed.reshape(1536, -1)
    rows, partials = chunk_shapes(pieces, own)
    return pl.pallas_call(
        functools.partial(feed_forward_kernel, len(pieces), len(partials)),
        grid=(4,),
        in_specs=piece_specs(pieces) + feed_specs(),
        out_specs=PARTIALS[: len(partials)] + [column_block(rows)] * 3,
        out_shape=partials
        + [
            jax.ShapeDtypeStruct((rows, 1024), F32),
            jax.ShapeDtypeStruct((rows, 1024), F32),
            jax.ShapeDtypeStruct((rows, 1024), BF16),
        ],
        scratch_shapes=[pltpu.VMEM((rows, 1536), BF16), pltpu.VMEM((rows, 1536), F32)],
        compiler_params=params(40),
        cost_estimate=cost(9.6e6 * rows, 10e6 + 12e3 * rows),
        name="feed_forward",
    )(*pieces, flat_packed, flat_packed, packed)


def feed_backward_kernel(count, parts, *refs):
    pieces, (wg, wu, wd, gate, up) = refs[:count], refs[count : count + 5]
    outs = refs[count + 5 : count + 5 + parts]
    low_gate, low_up, flat, total = refs[count + 5 + parts :]
    step = pl.program_id(0)

    @pl.when(step == 0)
    def _():
        fill(flat, pieces)

    rows = flat[...]
    left, right = down_parts(wd[...])
    grad = nt(rows[:, :1024], left) + nt(rows[:, 1024:], right)
    g = gate[...]
    s = jax.nn.sigmoid(g)
    a = (grad * up[...] * s * (1.0 + g * (1.0 - s))).astype(BF16)
    b = (grad * (g * s)).astype(BF16)
    low_gate[...] = a
    low_up[...] = b
    part = nt(a, wg[...]) + nt(b, wu[...])

    @pl.when(step == 0)
    def _():
        total[...] = part

    @pl.when(step > 0)
    def _():
        total[...] += part

    @pl.when(step == 3)
    def _():
        emit(total, outs)


def feed_backward_call(pieces, packed, gate, up, own, after=()):
    flat_packed = packed.reshape(1536, -1)
    rows, partials = chunk_shapes(pieces, own)
    return pl.pallas_call(
        later(functools.partial(feed_backward_kernel, len(pieces), len(partials)), len(after)),
        grid=(4,),
        in_specs=anywhere(after) + piece_specs(pieces) + feed_specs() + [column_block(rows)] * 2,
        out_specs=PARTIALS[: len(partials)] + [column_block(rows)] * 2,
        out_shape=partials + [jax.ShapeDtypeStruct((rows, 1024), BF16)] * 2,
        scratch_shapes=[pltpu.VMEM((rows, 1536), BF16), pltpu.VMEM((rows, 1536), F32)],
        compiler_params=params(40),
        cost_estimate=cost(9.6e6 * rows, 10e6 + 16e3 * rows),
        name="feed_backward",
    )(*after, *pieces, flat_packed, flat_packed, packed, gate, up)


CHUNKS = (128, 256, 128)


def chunked(pieces):
    return pieces[:1], pieces[1:3], pieces[3:]


def feed_weights_kernel(*refs):
    flats, grads = refs[:5], refs[5:10]
    low_gate, low_up, hidden = refs[10:13], refs[13:16], refs[16:19]
    out, flat_t, hidden_t, grad = refs[19:]
    step = pl.program_id(0)

    @pl.when(step == 0)
    def _():
        start = 0
        for ref in flats:
            n = ref.shape[0]
            flat_t[:, start : start + n] = ref[...].T
            start += n

    @pl.when(step == 4)
    def _():
        start = 0
        for ref in hidden:
            n = ref.shape[0]
            hidden_t[:, start : start + n] = ref[...].T
            start += n
        fill(grad, grads)

    def columns(blocks):
        block = jnp.concatenate([ref[...] for ref in blocks], axis=0)
        out[...] = nn(flat_t[...], block).astype(BF16).reshape(8, 192, 256)

    @pl.when(step < 4)
    def _():
        columns(low_gate)

    @pl.when((step >= 4) & (step < 8))
    def _():
        columns(low_up)

    for q in range(4):

        @pl.when(step == 8 + q)
        def _():
            top = nn(hidden_t[...], grad[:, 256 * q : 256 * (q + 1)]).astype(BF16)
            out[:, 0:128, :] = top.reshape(8, 128, 256)
            half = 64 * (q // 2)
            some = hidden_t[...].reshape(8, 128, 512)[:, half : half + 64].reshape(512, 512)
            start = 1024 + 256 * (q % 2)
            low = nn(some, grad[:, start : start + 256]).astype(BF16)
            out[:, 128:192, :] = low.reshape(8, 64, 256)


def feed_weights_call(flats, grads, low_gate, low_up, hidden):
    return pl.pallas_call(
        feed_weights_kernel,
        grid=(12,),
        in_specs=PIECES
        + PIECES
        + [pl.BlockSpec((n, 256), lambda b: (0, jnp.minimum(b, 3))) for n in CHUNKS]
        + [pl.BlockSpec((n, 256), lambda b: (0, jnp.clip(b - 4, 0, 3))) for n in CHUNKS]
        + [whole((n, 1024)) for n in CHUNKS],
        out_specs=pl.BlockSpec((8, 192, 256), lambda b: (0, 0, b)),
        out_shape=jax.ShapeDtypeStruct((8, 192, 3072), BF16),
        scratch_shapes=[
            pltpu.VMEM((1536, 512), BF16),
            pltpu.VMEM((1024, 512), BF16),
            pltpu.VMEM((512, 1536), BF16),
        ],
        compiler_params=params(40),
        cost_estimate=cost(4.9e9, 18e6),
        name="feed_weights",
    )(*flats, *grads, *low_gate, *low_up, *hidden)


def piece_specs(pieces):
    return [whole(item.shape) for item in pieces]


def turn_columns(block, cosine, sine):
    out = []
    for start in range(0, block.shape[1], HEAD_DIM):
        a = block[:, start : start + 48]
        b = block[:, start + 48 : start + HEAD_DIM]
        out.append(a * cosine - b * sine)
        out.append(b * cosine + a * sine)
    return jnp.concatenate(out, axis=1)


def project_kernel(raw, count, *refs):
    pieces, (gain, weight, cosine, sine, queries, pair) = refs[:count], refs[count : count + 6]
    if raw:
        flat = refs[-1]
        start = 0
        for ref in pieces:
            n = ref.shape[0]
            rows = ref[...].astype(F32)
            scale = lax.rsqrt(jnp.mean(rows * rows, axis=-1, keepdims=True) + 1e-05)
            flat[start : start + n, :] = (rows * scale * gain[...]).astype(BF16)
            start += n
    else:
        flat = refs[-1]
        fill(flat, pieces)
    both = nn(flat[...], weight[...])
    cos, sin = cosine[...], sine[...]
    queries[...] = turn_columns(both[:, :384], cos, sin).astype(BF16)
    keys = turn_columns(both[:, 384:576], cos, sin)
    pair[...] = jnp.concatenate([keys, both[:, 576:768]], axis=1).astype(BF16)


def project_call(raw, pieces, gain, packed, cosine, sine, after=()):
    wide = packed.shape[-1]
    shape = jax.ShapeDtypeStruct((512, 384), BF16)
    flat_shape = jax.ShapeDtypeStruct((512, 1536), BF16)
    return pl.pallas_call(
        later(functools.partial(project_kernel, raw, len(pieces)), len(after)),
        grid=(1,),
        in_specs=anywhere(after)
        + piece_specs(pieces)
        + [whole((1, 1536)), projection_spec(), whole((512, 48)), whole((512, 48))],
        out_specs=[whole((512, 384))] * 2 + ([whole((512, 1536))] if raw else []),
        out_shape=[shape, shape] + ([flat_shape] if raw else []),
        scratch_shapes=[] if raw else [pltpu.VMEM((512, 1536), BF16)],
        compiler_params=params(40),
        cost_estimate=cost(1.3e9, 6e6),
        name="project",
    )(*after, *pieces, gain.reshape(1, 1536), packed.reshape(1536, wide), cosine, sine)


def fill_bias(bias, length, places, key_places, window):
    gap = places[...] - key_places[...]
    inside = (key_places[...] < length) & (gap >= 0) & (gap < window)
    bias[...] = jnp.where(inside | (gap == 0), 0.0, NEGATIVE)


def both_rows(own, other, start):
    return jnp.concatenate(
        [own[:, start : start + HEAD_DIM], other[:, start : start + HEAD_DIM]], axis=0
    )


def attend_kernel(window, length, queries, own, other, places, key_places, w_out, *refs):
    outs, (mixed, log_total, total, bias) = refs[:4], refs[4:]
    fill_bias(bias, length[0], places, key_places, window)
    sums = []
    stats = []
    for head in range(4):
        if head % 2 == 0:
            keys = both_rows(own[...], other[...], HEAD_DIM * (head // 2))
            values = both_rows(own[...], other[...], 192 + HEAD_DIM * (head // 2)).T
        query = queries[:, HEAD_DIM * head : HEAD_DIM * (head + 1)]
        scores = nt(keys, query) * HEAD_DIM ** (-0.5) + bias[...]
        peak = jnp.max(scores, axis=0, keepdims=True)
        probs = jnp.exp(scores - peak)
        totals = jnp.sum(probs, axis=0, keepdims=True)
        part = nn(values, probs.astype(BF16)) / totals
        sums.append(part.astype(BF16).astype(F32).T.astype(BF16))
        stats.append(peak + jnp.log(totals))
        for block in range(4):
            cols = slice(384 * block, 384 * (block + 1))
            value = nn(sums[-1], out_block(w_out, head, block))
            if head == 0:
                total[:, cols] = value
            else:
                total[:, cols] += value
    mixed[...] = jnp.concatenate(sums, axis=1)
    log_total[...] = jnp.concatenate(stats + stats, axis=0)
    emit(total, outs)


def line_specs():
    return [whole((512, 384))] * 3 + [whole((1, 512)), whole((1024, 1))]


def out_spec():
    return pl.BlockSpec((8, 192, 384), lambda *_: (0, 0, 2))


def out_block(w_out, head, block):
    start = 96 * (head % 2)
    return w_out[2 * block + head // 2, start : start + 96, :]


def projection_spec():
    return pl.BlockSpec((1536, 768), lambda *_: (0, 0))


def attend_call(window, length, queries, own, other, places, key_places, packed, after=()):
    return pl.pallas_call(
        later(functools.partial(attend_kernel, window), len(after)),
        grid=(1,),
        in_specs=anywhere(after)
        + [pl.BlockSpec(memory_space=pltpu.SMEM)] + line_specs() + [out_spec()],
        out_specs=PARTIALS + [whole((512, 384)), whole((8, 512))],
        out_shape=PARTIAL_SHAPES
        + [jax.ShapeDtypeStruct((512, 384), BF16), jax.ShapeDtypeStruct((8, 512), F32)],
        scratch_shapes=[pltpu.VMEM((512, 1536), F32), pltpu.VMEM((1024, 512), F32)],
        compiler_params=params(48),
        cost_estimate=cost(3e9, 6e6, 2e6),
        name="attend",
    )(*after, length, queries, own, other, places, key_places, packed)


def attend_backward_kernel(window, length, *refs):
    pieces, refs = refs[:5], refs[5:]
    queries, own, other, places, key_places, w_out, log_total, cosine, sine = refs[:9]
    low_queries, pair_own, pair_other, grad, bias = refs[9:]
    fill(grad, pieces)
    fill_bias(bias, length[0], places, key_places, window)
    cos, sin = cosine[...], sine[...]
    lows = []
    key_sums = []
    value_sums = []
    for head in range(4):
        if head % 2 == 0:
            keys = both_rows(own[...], other[...], HEAD_DIM * (head // 2))
            values = both_rows(own[...], other[...], 192 + HEAD_DIM * (head // 2))
            keys_t = keys.T
        query = queries[:, HEAD_DIM * head : HEAD_DIM * (head + 1)]
        mixed = nt(grad[:, :384], out_block(w_out, head, 0))
        for block in range(1, 4):
            mixed += nt(
                grad[:, 384 * block : 384 * (block + 1)], out_block(w_out, head, block)
            )
        mixed = mixed.astype(BF16)
        scores = nt(keys, query) * HEAD_DIM ** (-0.5) + bias[...]
        probs = jnp.exp(scores - log_total[head : head + 1, :])
        slopes = nt(values, mixed)
        inner = jnp.sum(probs * slopes, axis=0, keepdims=True)
        raw = (probs * (slopes - inner) * HEAD_DIM ** (-0.5)).astype(BF16)
        key_part = nn(raw, query)
        value_part = nn(probs.astype(BF16), mixed)
        if head % 2 == 0:
            key_sums.append(key_part)
            value_sums.append(value_part)
        else:
            key_sums[-1] += key_part
            value_sums[-1] += value_part
        turned = nn(keys_t, raw)
        a, b = turned[:48], turned[48:]
        turned = jnp.concatenate([a * cos + b * sin, b * cos - a * sin], axis=0)
        lows.append(turned.T.astype(BF16))
    low_queries[...] = jnp.concatenate(lows, axis=1)
    both = jnp.concatenate(key_sums + value_sums, axis=1)
    pair_own[...] = both[:512]
    pair_other[...] = both[512:].astype(BF16)


def attend_backward_call(
    window,
    length,
    pieces,
    queries,
    own,
    other,
    places,
    key_places,
    packed,
    log_total,
    cosine,
    sine,
    after=(),
):
    return pl.pallas_call(
        later(functools.partial(attend_backward_kernel, window), len(after)),
        grid=(1,),
        in_specs=anywhere(after)
        + [pl.BlockSpec(memory_space=pltpu.SMEM)]
        + PIECES
        + line_specs()
        + [out_spec(), whole((8, 512)), whole((48, 512)), whole((48, 512))],
        out_specs=[whole((512, 384))] * 3,
        out_shape=[
            jax.ShapeDtypeStruct((512, 384), BF16),
            jax.ShapeDtypeStruct((512, 384), F32),
            jax.ShapeDtypeStruct((512, 384), BF16),
        ],
        scratch_shapes=[pltpu.VMEM((512, 1536), BF16), pltpu.VMEM((1024, 512), F32)],
        compiler_params=params(52),
        cost_estimate=cost(6e9, 6e6, 2e6),
        name="attend_backward",
    )(
        *after,
        length,
        *pieces,
        queries,
        own,
        other,
        places,
        key_places,
        packed,
        log_total,
        cosine,
        sine,
    )


def unproject_kernel(low_queries, pair_own, pair_came, cosine, sine, weight, *refs):
    outs, low = refs[:4], refs[4]
    both = pair_own[...] + pair_came[...].astype(F32)
    keys = turn_columns(both[:, :192], cosine[...], -sine[...])
    rows = jnp.concatenate(
        [low_queries[...], keys.astype(BF16), both[:, 192:].astype(BF16)], axis=1
    )
    low[...] = rows
    emit(nt(rows, weight[...]), outs)


def unproject_call(low_queries, pair_own, pair_came, cosine, sine, packed, after=()):
    wide = packed.shape[-1]
    return pl.pallas_call(
        later(unproject_kernel, len(after)),
        grid=(1,),
        in_specs=anywhere(after)
        + [whole((512, 384))] * 3
        + [whole((512, 48))] * 2
        + [projection_spec()],
        out_specs=PARTIALS + [whole((512, 768))],
        out_shape=LOW_PARTIAL_SHAPES + [jax.ShapeDtypeStruct((512, 768), BF16)],
        compiler_params=params(40),
        cost_estimate=cost(1.3e9, 7e6),
        name="unproject",
    )(*after, low_queries, pair_own, pair_came, cosine, sine, packed.reshape(1536, wide))


def attend_weights_kernel(count, *refs):
    flats, grads, (low, mixed) = refs[:count], refs[count : count + 5], refs[count + 5 : count + 7]
    out, flat_t, grad = refs[count + 7 :]
    start = 0
    for ref in flats:
        n = ref.shape[0]
        flat_t[:, start : start + n] = ref[...].T
        start += n
    fill(grad, grads)
    for block in range(3):
        cols = slice(256 * block, 256 * (block + 1))
        out[:, :, cols] = nn(flat_t[...], low[:, cols]).astype(BF16).reshape(8, 192, 256)
    mixed_t = mixed[...].T
    for block in range(4):
        part = nn(mixed_t, grad[:, 384 * block : 384 * (block + 1)]).astype(BF16)
        out[2 * block : 2 * block + 2, :, 768:1152] = part.reshape(2, 192, 384)


def attend_weights_call(flats, grads, low, mixed):
    return pl.pallas_call(
        functools.partial(attend_weights_kernel, len(flats)),
        grid=(1,),
        in_specs=piece_specs(flats) + PIECES + [whole((512, 768)), whole((512, 384))],
        out_specs=whole((8, 192, 1152)),
        out_shape=jax.ShapeDtypeStruct((8, 192, 1152), BF16),
        scratch_shapes=[pltpu.VMEM((1536, 512), BF16), pltpu.VMEM((512, 1536), BF16)],
        compiler_params=params(40),
        cost_estimate=cost(1.9e9, 10e6),
        name="attend_weights",
    )(*flats, *grads, low, mixed)


def unpack_kernel(*refs):
    every, wq, wk, wv, wo, gate, up, down = refs
    side = pl.program_id(0)
    blocks = [every[x, 0] for x in range(4)]
    for x, block in enumerate(blocks):
        wq[:, 384 * x : 384 * (x + 1)] = block[:, 3072:3456].astype(F32)
        wo[:, 384 * x : 384 * (x + 1)] = block[:, 3840:4224].astype(F32)
        for s in range(8):
            cols = slice(512 * s + 128 * x, 512 * s + 128 * (x + 1))
            gate[:, cols] = block[:, 128 * s : 128 * (s + 1)].astype(F32)
            up[:, cols] = block[:, 1024 + 128 * s : 1024 + 128 * (s + 1)].astype(F32)

        @pl.when(side == 0)
        def _(x=x, block=block):
            down[x, 0:96, :1024] = block[:, 2048:3072].astype(F32)

        @pl.when(side == 1)
        def _(x=x, block=block):
            down[x, 96:128, :1024] = block[0:32, 2048:3072].astype(F32)
            down[x, 0:64, 1024:] = block[32:96, 2048:2560].astype(F32)
            down[x, 64:128, 1024:] = block[32:96, 2560:3072].astype(F32)

    wk[...] = jnp.concatenate([block[:, 3456:3648].astype(F32) for block in blocks], axis=1)
    wv[...] = jnp.concatenate([block[:, 3648:3840].astype(F32) for block in blocks], axis=1)


def unpack_call(every):
    widths = (1536, 768, 768, 1536, 4096, 4096)
    out = pl.pallas_call(
        unpack_kernel,
        grid=(2,),
        in_specs=[pl.BlockSpec((4, 1, 96, every.shape[-1]), lambda b: (0, b, 0, 0))],
        out_specs=[pl.BlockSpec((96, width), lambda b: (b, 0)) for width in widths]
        + [whole((4, 128, 1536))],
        out_shape=[jax.ShapeDtypeStruct((192, width), F32) for width in widths]
        + [jax.ShapeDtypeStruct((4, 128, 1536), F32)],
        compiler_params=params(48),
        cost_estimate=cost(1e6, 30e6),
        name="unpack",
    )(every)
    return out[:4], (out[4], out[5], out[6].reshape(512, 1536))


def pack_feed_kernel(where, w_gate, w_up, w_down, out):
    x = where[0]
    for s in range(8):
        cols = pl.ds(pl.multiple_of(512 * s + 128 * x, 128), 128)
        out[:, 128 * s : 128 * (s + 1)] = w_gate[:, cols]
        out[:, 1024 + 128 * s : 1024 + 128 * (s + 1)] = w_up[:, cols]
    out[0:128, 2048:3072] = w_down[:, 0:1024]
    out[128:192, 2048:2560] = w_down[0:64, 1024:1536]
    out[128:192, 2560:3072] = w_down[64:128, 1024:1536]


def pack_feed_call(where, w_gate, w_up, w_down, after=()):
    return pl.pallas_call(
        later(pack_feed_kernel, len(after), 1),
        grid_spec=pltpu.PrefetchScalarGridSpec(
            num_scalar_prefetch=1,
            grid=(1,),
            in_specs=anywhere(after)
            + [
                pl.BlockSpec((192, 4096), lambda b, w: (0, 0)),
                pl.BlockSpec((192, 4096), lambda b, w: (0, 0)),
                pl.BlockSpec((128, 1536), lambda b, w: (w[0], 0)),
            ],
            out_specs=pl.BlockSpec((192, 3072), lambda b, w: (0, 0)),
        ),
        out_shape=jax.ShapeDtypeStruct((192, 3072), BF16),
        compiler_params=params(24),
        cost_estimate=cost(1e3, 5e6),
        name="pack_feed",
    )(where, *after, w_gate, w_up, w_down)


WINDOW = 512
EPSILON = 1e-05
ROPE_BASE = 100000.0

AXES = ("ylo", "x", "core", "z", "yhi")
SIZES = (2, 4, 2, 4, 2)
REP = ("ylo", "x", "core")
SHARD = ("z", "yhi")
SPREAD = ("z", "core")

RIGHT = [(i, (i + 1) % 4) for i in range(4)]
LEFT = [(i, (i - 1) % 4) for i in range(4)]
ACROSS = [(i, (i + 2) % 4) for i in range(4)]
SWAP = [(0, 1), (1, 0)]


def number(ylo, x, core, z, yhi):
    return (((ylo * 4 + x) * 2 + core) * 4 + z) * 2 + yhi


def permutation(place, taken=None):
    pairs = []
    for ylo in range(2):
        for x in range(4):
            for core in range(2):
                for z in range(4):
                    for yhi in range(2):
                        here = (ylo, x, core, z, yhi)
                        if taken is None or taken(*here):
                            pairs.append((number(*here), number(*place(*here))))
    return pairs


def inverse(pairs):
    return [(there, here) for here, there in pairs]


def at_home(ylo, x, core, z, yhi):
    return core == yhi


LINES = [
    permutation(lambda l, x, c, z, h, k=k: (l, (z + k) % 4, h, x, c)) for k in range(4)
]
TURN = permutation(lambda l, x, c, z, h: (l, z, h, x, c))
SHARE = permutation(lambda l, x, c, z, h: (l, x, c, z, 1 - h), at_home)
CROSS = permutation(lambda l, x, c, z, h: (l, z, c, x, h))


def to_lines(block, z):
    part = block.shape[0] // 4
    out = []
    for k in range(4):
        piece = lax.dynamic_slice_in_dim(block, ((z + k) % 4) * part, part, axis=0)
        out.append(lax.ppermute(piece, AXES, LINES[k]))
    return out


def from_lines(block, z):
    part = block.shape[0] // 4
    out = jnp.zeros_like(block)
    for k in range(4):
        piece = lax.ppermute(block[part * k : part * (k + 1)], AXES, inverse(LINES[k]))
        out = lax.dynamic_update_slice_in_dim(out, piece, ((z + k) % 4) * part, axis=0)
    return out


def interleave(first, second):
    parts = [item[32 * k : 32 * (k + 1)] for k in range(4) for item in (first, second)]
    return jnp.concatenate(parts, axis=0)


def separate(block):
    parts = [block[32 * k : 32 * (k + 1)] for k in range(8)]
    return jnp.concatenate(parts[::2], axis=0), jnp.concatenate(parts[1::2], axis=0)


def ring_gather(block):
    half = block.shape[0] // 2
    from_left = lax.ppermute(block, "x", RIGHT)
    from_right = lax.ppermute(block, "x", LEFT)
    far_first = lax.ppermute(from_left[:half], "x", RIGHT)
    far_second = lax.ppermute(from_right[half:], "x", LEFT)
    return block, from_left, from_right, far_first, far_second


def ring_scatter(own, left, right, far):
    half = far.shape[0] // 2
    first = lax.ppermute(far[:half], "x", RIGHT).astype(F32)
    second = lax.ppermute(far[half:], "x", LEFT).astype(F32)
    right = jnp.concatenate([right[:half] + first, right[half:]], axis=0).astype(BF16)
    left = jnp.concatenate([left[:half], left[half:] + second], axis=0).astype(BF16)
    from_left = lax.ppermute(right, "x", RIGHT).astype(F32)
    from_right = lax.ppermute(left, "x", LEFT).astype(F32)
    return own + from_left + from_right


def ring_scatter_direct(own, left, right, far):
    from_left = lax.ppermute(right, "x", RIGHT).astype(F32)
    from_right = lax.ppermute(left, "x", LEFT).astype(F32)
    from_far = lax.ppermute(far, "x", ACROSS).astype(F32)
    return own + from_left + from_right + from_far


def tie(value, *others):
    return lax.optimization_barrier((value, *others))[0]


def rms_norm(values, gain):
    return values * lax.rsqrt(jnp.mean(values * values, axis=-1, keepdims=True) + EPSILON) * gain


def add_low(mine, came):
    return (mine.astype(F32) + came.astype(F32)).astype(BF16)


def yhi_sum(rows, core, yhi):
    mine = lax.dynamic_slice_in_dim(rows, 96 * core, 96, axis=0)
    theirs = lax.dynamic_slice_in_dim(rows, 96 * (1 - core), 96, axis=0)
    came = lax.ppermute(theirs, "core", SWAP)
    home = core == yhi
    kept = jnp.where(home, mine, came)
    away = jnp.where(home, came, mine)
    return add_low(kept, lax.ppermute(away, "yhi", SWAP))


def ylo_sum(piece):
    return add_low(piece, lax.ppermute(piece, "ylo", SWAP))


def cross(piece, start, *others):
    first, last = start + 768, start + 1152
    moved = lax.ppermute(piece[:, first:last], AXES, CROSS)
    if others:
        piece, moved = lax.optimization_barrier((piece, moved, *others))[:2]
    return jnp.concatenate([piece[:, :first], moved, piece[:, last:]], axis=1)


def gain_rows(grads):
    tall = grads.astype(BF16).T.reshape(8, 192, 4)
    return jnp.pad(tall, ((0, 0), (0, 0), (0, 124)))


def norm_back(grad, own_normed, state, gain):
    grad_state, grad_gain = jax.vjp(rms_norm, state, gain)[1](own_normed)
    return grad + grad_state, grad_gain


def body(tokens, lengths, grad_output, *weights):
    stretch, width = tokens.shape[1:]
    x = lax.axis_index("x")
    core = lax.axis_index("core")
    z = lax.axis_index("z")
    yhi = lax.axis_index("yhi")
    member = x.astype(jnp.int32).reshape(1)
    home = core == yhi

    gains = jnp.stack([weights[0], weights[5], weights[9], weights[14]]).T
    gains = jnp.pad(gains, ((0, 0), (0, 124)))

    def shared(block, *joined):
        return jnp.where(home, block, tie(lax.ppermute(block, AXES, SHARE), *joined))

    def attention_part(base, extra, after):
        block = lax.dynamic_slice(tie(weights[base + 4], *after), (0, 384 * x), (192, 384))
        block = lax.ppermute(block, AXES, TURN)
        parts = [
            lax.dynamic_slice(w, (0, x * (w.shape[1] // 4)), (192, w.shape[1] // 4))
            for w in weights[base + 1 : base + 4]
        ]
        parts = shared(jnp.concatenate(parts + extra, axis=1))
        return jnp.concatenate([parts[:, :768], block, parts[:, 768:]], axis=1)

    def feed_part(base, after, joined):
        part = pack_feed_call(member, *weights[base + 6 : base + 9], after=after)
        return shared(part, *joined)

    def line_weights(piece, *after):
        return lax.all_gather(tie(piece, *after), SPREAD, axis=0, tiled=False)

    here = (2 * z + yhi) * stretch + jnp.arange(stretch, dtype=jnp.int32)
    valid = (here < lengths[0])[:, None]
    grad_start = jnp.where(valid, grad_output[0], 0).astype(BF16)
    length = lax.ppermute(lengths, AXES, TURN)
    moved = to_lines(interleave(tokens[0], grad_start), z)
    rows, grad_rows = separate(jnp.concatenate(moved, axis=0))

    attn_one = line_weights(attention_part(0, [gains], ()))
    feed_one = feed_part(0, (), moved)
    gains = attn_one[:, :, 1152:1156].transpose(2, 0, 1).reshape(4, width).astype(F32)
    pieces = ring_gather(rows)
    state = rows.astype(F32)
    feed_one = line_weights(feed_one, *pieces[3:])
    grad_pieces = ring_gather(grad_rows)
    grad = grad_rows.astype(F32)

    part = stretch // 4

    def member_places(member, side_index):
        block = jnp.arange(4, dtype=jnp.int32)
        inner = jnp.arange(part, dtype=jnp.int32)
        home = (member - block + 4) % 4
        return (
            home[:, None] * (2 * stretch) + side_index * stretch + member * part + inner[None, :]
        ).reshape(-1)

    def line_places(side_index):
        return jnp.concatenate([member_places((x + step) % 4, side_index) for step in (0, 3, 1, 2)])

    places = line_places(core)
    key_places = jnp.concatenate([places, line_places(1 - core)]).reshape(1024, 1)
    half = HEAD_DIM // 2
    freq = ROPE_BASE ** (-jnp.arange(half, dtype=F32) * (2.0 / HEAD_DIM))
    angle = places.astype(F32)[:, None] * freq[None, :]
    cosine, sine = jnp.cos(angle), jnp.sin(angle)
    cosine_t, sine_t = cosine.T, sine.T
    places = places.reshape(1, 512)

    records = []
    for index, window in enumerate((WINDOW, 8 * stretch)):
        if index == 0:
            attn, feed = attn_one, feed_one
        else:
            attn, feed = attn_two, feed_two
        gain_attn, gain_feed = gains[2 * index], gains[2 * index + 1]
        if index == 0:
            queries, own, flat = project_call(True, pieces, gain_attn, attn, cosine, sine)
            flats = (flat,)
        else:
            flats = ring_gather(rms_norm(state, gain_attn).astype(BF16))
            feed_two = feed = line_weights(feed_two, *flats[1:3])
            queries, own = project_call(False, flats, gain_attn, attn, cosine, sine)
        other = lax.ppermute(own, "core", SWAP)
        line = (queries, own, other, places, key_places)
        after = grad_pieces[3:] if index else ()
        *partial, mixed, log_total = attend_call(window, length, *line, attn, after=after)
        saved_attn = (state, flats, line, mixed, log_total)
        state = state + ring_scatter(*partial)
        if index == 0:
            attn_two = attention_part(9, [], (mixed,))
            feed_two = feed_part(9, (mixed,), ())
        flats = ring_gather(rms_norm(state, gain_feed).astype(BF16))
        if index == 0:
            attn_two = line_weights(attn_two, *flats[1:3])
        partial = []
        saved = []
        for number_of, chunk in enumerate(chunked(flats)):
            *sums, gate, up, hidden = feed_forward_call(chunk, feed, number_of == 0)
            partial += sums
            saved.append((gate, up, hidden))
        saved_feed = (state, flats, saved)
        state = state + ring_scatter_direct(*partial)
        records.append((saved_attn, saved_feed, window))
    last_rows = state.astype(BF16)
    packed = ((attn_one, feed_one), (attn_two, feed_two))

    results = [None] * 18
    gain_grads = [None] * 4

    def feed_back(index, grad, pieces, after):
        state, flats, saved = records[index][1]
        partial = []
        lows = []
        for number_of, chunk in enumerate(chunked(pieces)):
            gate, up, _ = saved[number_of]
            last = number_of == 2
            *sums, low_gate, low_up = feed_backward_call(
                chunk, packed[index][1], gate, up, number_of == 0, after=after if last else ()
            )
            partial += sums
            lows.append((low_gate, low_up))
        own_normed = ring_scatter_direct(*partial)
        grad, gain_grads[2 * index + 1] = norm_back(
            grad, own_normed, state, gains[2 * index + 1]
        )
        low_gates, low_ups = zip(*lows)
        return grad, feed_weights_call(
            flats, pieces, low_gates, low_ups, [item[2] for item in saved]
        )

    def attention_back(index, grad, pieces, after, late):
        state, flats, line, mixed, log_total = records[index][0]
        window = records[index][2]
        attn = packed[index][0]
        low_queries, pair_own, pair_other = attend_backward_call(
            window, length, pieces, *line, attn, log_total, cosine_t, sine_t, after=after
        )
        came = lax.ppermute(pair_other, "core", SWAP)
        *partial, low = unproject_call(
            low_queries, pair_own, came, cosine, sine, attn, after=late
        )
        own_normed = ring_scatter_direct(*partial)
        grad, gain_grads[2 * index] = norm_back(grad, own_normed, state, gains[2 * index])
        return grad, attend_weights_call(flats, pieces, low, mixed)

    def scatter(block):
        return lax.psum_scatter(block, SPREAD, scatter_dimension=0, tiled=True)

    grad, feed_grad = feed_back(1, grad, grad_pieces, ())
    low = tie(grad.astype(BF16), feed_grad)
    second_feed = scatter(tie(feed_grad, low))
    grad, attn_grad = attention_back(1, grad, ring_gather(low), (last_rows,), ())
    low = tie(grad.astype(BF16), attn_grad)
    second_attn = scatter(tie(attn_grad, low, second_feed))

    grad, feed_grad = feed_back(0, grad, ring_gather(low), (second_feed,))
    low = tie(grad.astype(BF16), feed_grad)
    first_feed = scatter(tie(feed_grad, low, second_attn))
    second = yhi_sum(jnp.concatenate([second_feed, second_attn], axis=2)[0], core, yhi)
    grad, attn_grad = attention_back(0, grad, ring_gather(low), (), (second,))
    low = grad.astype(BF16)
    attn_grad = tie(attn_grad, first_feed, low)
    attn_grad = jnp.concatenate([attn_grad, gain_rows(jnp.stack(gain_grads))], axis=2)
    first_attn = scatter(attn_grad)
    feed_piece = ylo_sum(yhi_sum(first_feed[0], core, yhi))
    second_piece = cross(ylo_sum(second), 3072, first_attn, feed_piece)
    back = from_lines(interleave(last_rows, low), z)
    output, input_grad = separate(back)
    output, input_grad = output[None], input_grad.astype(F32)[None]

    every = lax.all_gather(second_piece, ("x", "core"), axis=0, tiled=False)
    results[10:14], results[15:18] = unpack_call(every.reshape(4, 2, 96, -1))
    attn_piece = ylo_sum(yhi_sum(tie(first_attn, feed_piece)[0], core, yhi))
    first_piece = jnp.concatenate([feed_piece, cross(attn_piece, 0)], axis=1)
    every = lax.all_gather(first_piece, ("x", "core"), axis=0, tiled=False)
    every = every.reshape(4, 2, 96, -1)
    results[1:5], results[6:9] = unpack_call(every)
    gain_sums = every[..., 4224:4228].astype(F32).sum(axis=0).reshape(192, 4).T
    for index, slot in enumerate((0, 5, 9, 14)):
        results[slot] = gain_sums[index]
    return (output, input_grad, *results)


def solution(mesh):
    fine = Mesh(mesh.devices.reshape(SIZES), AXES)
    token = P(REP, SHARD, None)
    vector = P(SHARD)
    matrix = P(SHARD, None)
    layer = (vector, matrix, matrix, matrix, matrix, vector, matrix, matrix, matrix)
    return jax.shard_map(
        body,
        mesh=fine,
        in_specs=(token, P(REP), token) + layer + layer,
        out_specs=(token, token) + layer + layer,
        check_vma=False,
    )
```

```python
import functools
import jax
import jax.numpy as jnp
from jax import lax
from jax.experimental import pallas as pl
from jax.experimental.pallas import tpu as pltpu
from jax.sharding import Mesh
from jax.sharding import PartitionSpec as P

F32 = jnp.float32
BF16 = jnp.bfloat16
HEAD_DIM = 96
NEGATIVE = -1e30
MIB = 1 << 20

OFFSETS = (0, 128, 256, 384, 448)
SIZES_OF = (128, 128, 128, 64, 64)


def params(mib, semantics=None):
    return pltpu.CompilerParams(vmem_limit_bytes=mib * MIB, dimension_semantics=semantics)


def cost(flops, nbytes, transcendentals=0):
    return pl.CostEstimate(
        flops=int(flops), bytes_accessed=int(nbytes), transcendentals=int(transcendentals)
    )


def fill(target, refs):
    start = 0
    for ref in refs:
        rows = ref.shape[0]
        target[start : start + rows, :] = ref[...]
        start += rows


def nn(a, b):
    return lax.dot_general(a, b, (((1,), (0,)), ((), ())), preferred_element_type=F32)


def nt(a, b):
    return lax.dot_general(a, b, (((1,), (1,)), ((), ())), preferred_element_type=F32)


def tn(a, b):
    return lax.dot_general(a, b, (((0,), (0,)), ((), ())), preferred_element_type=F32)


def later(kernel, count, lead=0):
    if not count:
        return kernel

    def wrapped(*refs):
        return kernel(*refs[:lead], *refs[lead + count :])

    return wrapped


def anywhere(after):
    return [pl.BlockSpec(memory_space=pl.ANY)] * len(after)


def whole(shape):
    return pl.BlockSpec(shape, lambda *_: (0,) * len(shape))


PIECES = [whole((rows, 1536)) for rows in SIZES_OF]
PARTIAL_SHAPES = [
    jax.ShapeDtypeStruct((128, 1536), F32),
    jax.ShapeDtypeStruct((128, 1536), F32),
    jax.ShapeDtypeStruct((128, 1536), F32),
    jax.ShapeDtypeStruct((128, 1536), BF16),
]
LOW_PARTIAL_SHAPES = PARTIAL_SHAPES[:1] + [jax.ShapeDtypeStruct((128, 1536), BF16)] * 3
PARTIALS = [whole((128, 1536))] * 4


def emit(total, outs):
    for place, out in enumerate(outs):
        out[...] = total[128 * place : 128 * (place + 1), :].astype(out.dtype)


def down_parts(block):
    left = block[:, 0:128, :].reshape(256, 1024)
    right = jnp.concatenate([block[:, 128:192, 0:512], block[:, 128:192, 512:1024]], axis=1)
    return left, right.reshape(256, 512)


def feed_forward_kernel(*refs):
    pieces, (wg, wu, wd), outs = refs[:5], refs[5:8], refs[8:12]
    gate, up, hidden, flat, total = refs[12:]
    step = pl.program_id(0)

    @pl.when(step == 0)
    def _():
        fill(flat, pieces)

    rows = flat[...]
    g = nn(rows, wg[...])
    u = nn(rows, wu[...])
    gate[...] = g
    up[...] = u
    h = (g * jax.nn.sigmoid(g) * u).astype(BF16)
    hidden[...] = h
    left, right = down_parts(wd[...])
    left, right = nn(h, left), nn(h, right)

    @pl.when(step == 0)
    def _():
        total[:, :1024] = left
        total[:, 1024:] = right

    @pl.when(step > 0)
    def _():
        total[:, :1024] += left
        total[:, 1024:] += right

    @pl.when(step == 3)
    def _():
        emit(total, outs)


def feed_specs():
    return [
        pl.BlockSpec((1536, 256), lambda b: (0, b)),
        pl.BlockSpec((1536, 256), lambda b: (0, 4 + b)),
        pl.BlockSpec((2, 192, 1024), lambda b: (b, 0, 2)),
    ]


def column_block(rows):
    return pl.BlockSpec((rows, 256), lambda b: (0, b))


def feed_forward_call(pieces, packed, after=()):
    flat_packed = packed.reshape(1536, -1)
    return pl.pallas_call(
        later(feed_forward_kernel, len(after)),
        grid=(4,),
        in_specs=anywhere(after) + PIECES + feed_specs(),
        out_specs=PARTIALS + [column_block(512)] * 3,
        out_shape=PARTIAL_SHAPES
        + [
            jax.ShapeDtypeStruct((512, 1024), F32),
            jax.ShapeDtypeStruct((512, 1024), F32),
            jax.ShapeDtypeStruct((512, 1024), BF16),
        ],
        scratch_shapes=[pltpu.VMEM((512, 1536), BF16), pltpu.VMEM((512, 1536), F32)],
        compiler_params=params(40),
        cost_estimate=cost(4.9e9, 18e6),
        name="feed_forward",
    )(*after, *pieces, flat_packed, flat_packed, packed)


def feed_backward_kernel(*refs):
    pieces, (wg, wu, wd, gate, up), outs = refs[:5], refs[5:10], refs[10:14]
    low_gate, low_up, flat, total = refs[14:]
    step = pl.program_id(0)

    @pl.when(step == 0)
    def _():
        fill(flat, pieces)

    rows = flat[...]
    left, right = down_parts(wd[...])
    grad = nt(rows[:, :1024], left) + nt(rows[:, 1024:], right)
    g = gate[...]
    s = jax.nn.sigmoid(g)
    a = (grad * up[...] * s * (1.0 + g * (1.0 - s))).astype(BF16)
    b = (grad * (g * s)).astype(BF16)
    low_gate[...] = a
    low_up[...] = b
    part = nt(a, wg[...]) + nt(b, wu[...])

    @pl.when(step == 0)
    def _():
        total[...] = part

    @pl.when(step > 0)
    def _():
        total[...] += part

    @pl.when(step == 3)
    def _():
        emit(total, outs)


def feed_backward_call(pieces, packed, gate, up, after=()):
    flat_packed = packed.reshape(1536, -1)
    return pl.pallas_call(
        later(feed_backward_kernel, len(after)),
        grid=(4,),
        in_specs=anywhere(after) + PIECES + feed_specs() + [column_block(512)] * 2,
        out_specs=PARTIALS + [column_block(512)] * 2,
        out_shape=LOW_PARTIAL_SHAPES + [jax.ShapeDtypeStruct((512, 1024), BF16)] * 2,
        scratch_shapes=[pltpu.VMEM((512, 1536), BF16), pltpu.VMEM((512, 1536), F32)],
        compiler_params=params(40),
        cost_estimate=cost(4.9e9, 20e6),
        name="feed_backward",
    )(*after, *pieces, flat_packed, flat_packed, packed, gate, up)


def feed_weights_kernel(*refs):
    flats, grads = refs[:5], refs[5:10]
    low_gate, low_up, hidden, out, flat_t, hidden_t, grad = refs[10:]
    step = pl.program_id(0)

    @pl.when(step == 0)
    def _():
        start = 0
        for ref in flats:
            n = ref.shape[0]
            flat_t[:, start : start + n] = ref[...].T
            start += n

    @pl.when(step == 4)
    def _():
        hidden_t[...] = hidden[...].T
        fill(grad, grads)

    @pl.when(step < 4)
    def _():
        out[...] = nn(flat_t[...], low_gate[...]).astype(BF16).reshape(8, 192, 256)

    @pl.when((step >= 4) & (step < 8))
    def _():
        out[...] = nn(flat_t[...], low_up[...]).astype(BF16).reshape(8, 192, 256)

    for q in range(4):

        @pl.when(step == 8 + q)
        def _():
            top = nn(hidden_t[...], grad[:, 256 * q : 256 * (q + 1)]).astype(BF16)
            out[:, 0:128, :] = top.reshape(8, 128, 256)
            half = 64 * (q // 2)
            some = hidden_t[...].reshape(8, 128, 512)[:, half : half + 64].reshape(512, 512)
            start = 1024 + 256 * (q % 2)
            low = nn(some, grad[:, start : start + 256]).astype(BF16)
            out[:, 128:192, :] = low.reshape(8, 64, 256)


def feed_weights_call(flats, grads, low_gate, low_up, hidden):
    return pl.pallas_call(
        feed_weights_kernel,
        grid=(12,),
        in_specs=PIECES
        + PIECES
        + [
            pl.BlockSpec((512, 256), lambda b: (0, jnp.minimum(b, 3))),
            pl.BlockSpec((512, 256), lambda b: (0, jnp.clip(b - 4, 0, 3))),
            whole((512, 1024)),
        ],
        out_specs=pl.BlockSpec((8, 192, 256), lambda b: (0, 0, b)),
        out_shape=jax.ShapeDtypeStruct((8, 192, 3072), BF16),
        scratch_shapes=[
            pltpu.VMEM((1536, 512), BF16),
            pltpu.VMEM((1024, 512), BF16),
            pltpu.VMEM((512, 1536), BF16),
        ],
        compiler_params=params(40),
        cost_estimate=cost(4.9e9, 18e6),
        name="feed_weights",
    )(*flats, *grads, low_gate, low_up, hidden)


def piece_specs(pieces):
    return [whole(item.shape) for item in pieces]


def turn_columns(block, cosine, sine):
    out = []
    for start in range(0, block.shape[1], HEAD_DIM):
        a = block[:, start : start + 48]
        b = block[:, start + 48 : start + HEAD_DIM]
        out.append(a * cosine - b * sine)
        out.append(b * cosine + a * sine)
    return jnp.concatenate(out, axis=1)


def project_kernel(raw, count, *refs):
    pieces, (gain, weight, cosine, sine, queries, pair) = refs[:count], refs[count : count + 6]
    if raw:
        flat = refs[-1]
        start = 0
        for ref in pieces:
            n = ref.shape[0]
            rows = ref[...].astype(F32)
            scale = lax.rsqrt(jnp.mean(rows * rows, axis=-1, keepdims=True) + 1e-05)
            flat[start : start + n, :] = (rows * scale * gain[...]).astype(BF16)
            start += n
    else:
        flat = refs[-1]
        fill(flat, pieces)
    both = nn(flat[...], weight[...])
    cos, sin = cosine[...], sine[...]
    queries[...] = turn_columns(both[:, :384], cos, sin).astype(BF16)
    keys = turn_columns(both[:, 384:576], cos, sin)
    pair[...] = jnp.concatenate([keys, both[:, 576:768]], axis=1).astype(BF16)


def project_call(raw, pieces, gain, packed, cosine, sine, after=()):
    wide = packed.shape[-1]
    shape = jax.ShapeDtypeStruct((512, 384), BF16)
    flat_shape = jax.ShapeDtypeStruct((512, 1536), BF16)
    return pl.pallas_call(
        later(functools.partial(project_kernel, raw, len(pieces)), len(after)),
        grid=(1,),
        in_specs=anywhere(after)
        + piece_specs(pieces)
        + [whole((1, 1536)), projection_spec(), whole((512, 48)), whole((512, 48))],
        out_specs=[whole((512, 384))] * 2 + ([whole((512, 1536))] if raw else []),
        out_shape=[shape, shape] + ([flat_shape] if raw else []),
        scratch_shapes=[] if raw else [pltpu.VMEM((512, 1536), BF16)],
        compiler_params=params(40),
        cost_estimate=cost(1.3e9, 6e6),
        name="project",
    )(*after, *pieces, gain.reshape(1, 1536), packed.reshape(1536, wide), cosine, sine)


def fill_bias(bias, length, places, key_places, window):
    gap = places[...] - key_places[...]
    inside = (key_places[...] < length) & (gap >= 0) & (gap < window)
    bias[...] = jnp.where(inside | (gap == 0), 0.0, NEGATIVE)


def both_rows(own, other, start):
    return jnp.concatenate(
        [own[:, start : start + HEAD_DIM], other[:, start : start + HEAD_DIM]], axis=0
    )


def attend_kernel(window, length, queries, own, other, places, key_places, w_out, *refs):
    outs, (mixed, log_total, total, bias) = refs[:4], refs[4:]
    fill_bias(bias, length[0], places, key_places, window)
    sums = []
    stats = []
    for head in range(4):
        if head % 2 == 0:
            keys = both_rows(own[...], other[...], HEAD_DIM * (head // 2))
            values = both_rows(own[...], other[...], 192 + HEAD_DIM * (head // 2)).T
        query = queries[:, HEAD_DIM * head : HEAD_DIM * (head + 1)]
        scores = nt(keys, query) * HEAD_DIM ** (-0.5) + bias[...]
        peak = jnp.max(scores, axis=0, keepdims=True)
        probs = jnp.exp(scores - peak)
        totals = jnp.sum(probs, axis=0, keepdims=True)
        part = nn(values, probs.astype(BF16)) / totals
        sums.append(part.astype(BF16).astype(F32).T.astype(BF16))
        stats.append(peak + jnp.log(totals))
        for block in range(4):
            cols = slice(384 * block, 384 * (block + 1))
            value = nn(sums[-1], out_block(w_out, head, block))
            if head == 0:
                total[:, cols] = value
            else:
                total[:, cols] += value
    mixed[...] = jnp.concatenate(sums, axis=1)
    log_total[...] = jnp.concatenate(stats + stats, axis=0)
    emit(total, outs)


def line_specs():
    return [whole((512, 384))] * 3 + [whole((1, 512)), whole((1024, 1))]


def out_spec():
    return pl.BlockSpec((8, 192, 384), lambda *_: (0, 0, 2))


def out_block(w_out, head, block):
    start = 96 * (head % 2)
    return w_out[2 * block + head // 2, start : start + 96, :]


def projection_spec():
    return pl.BlockSpec((1536, 768), lambda *_: (0, 0))


def attend_call(window, length, queries, own, other, places, key_places, packed, after=()):
    return pl.pallas_call(
        later(functools.partial(attend_kernel, window), len(after)),
        grid=(1,),
        in_specs=anywhere(after)
        + [pl.BlockSpec(memory_space=pltpu.SMEM)] + line_specs() + [out_spec()],
        out_specs=PARTIALS + [whole((512, 384)), whole((8, 512))],
        out_shape=PARTIAL_SHAPES
        + [jax.ShapeDtypeStruct((512, 384), BF16), jax.ShapeDtypeStruct((8, 512), F32)],
        scratch_shapes=[pltpu.VMEM((512, 1536), F32), pltpu.VMEM((1024, 512), F32)],
        compiler_params=params(48),
        cost_estimate=cost(3e9, 6e6, 2e6),
        name="attend",
    )(*after, length, queries, own, other, places, key_places, packed)


def attend_backward_kernel(window, length, *refs):
    pieces, refs = refs[:5], refs[5:]
    queries, own, other, places, key_places, w_out, log_total, cosine, sine = refs[:9]
    low_queries, pair_own, pair_other, grad, bias = refs[9:]
    fill(grad, pieces)
    fill_bias(bias, length[0], places, key_places, window)
    cos, sin = cosine[...], sine[...]
    lows = []
    key_sums = []
    value_sums = []
    for head in range(4):
        if head % 2 == 0:
            keys = both_rows(own[...], other[...], HEAD_DIM * (head // 2))
            values = both_rows(own[...], other[...], 192 + HEAD_DIM * (head // 2))
            keys_t = keys.T
        query = queries[:, HEAD_DIM * head : HEAD_DIM * (head + 1)]
        mixed = nt(grad[:, :384], out_block(w_out, head, 0))
        for block in range(1, 4):
            mixed += nt(
                grad[:, 384 * block : 384 * (block + 1)], out_block(w_out, head, block)
            )
        mixed = mixed.astype(BF16)
        scores = nt(keys, query) * HEAD_DIM ** (-0.5) + bias[...]
        probs = jnp.exp(scores - log_total[head : head + 1, :])
        slopes = nt(values, mixed)
        inner = jnp.sum(probs * slopes, axis=0, keepdims=True)
        raw = (probs * (slopes - inner) * HEAD_DIM ** (-0.5)).astype(BF16)
        key_part = nn(raw, query)
        value_part = nn(probs.astype(BF16), mixed)
        if head % 2 == 0:
            key_sums.append(key_part)
            value_sums.append(value_part)
        else:
            key_sums[-1] += key_part
            value_sums[-1] += value_part
        turned = nn(keys_t, raw)
        a, b = turned[:48], turned[48:]
        turned = jnp.concatenate([a * cos + b * sin, b * cos - a * sin], axis=0)
        lows.append(turned.T.astype(BF16))
    low_queries[...] = jnp.concatenate(lows, axis=1)
    both = jnp.concatenate(key_sums + value_sums, axis=1)
    pair_own[...] = both[:512]
    pair_other[...] = both[512:].astype(BF16)


def attend_backward_call(
    window,
    length,
    pieces,
    queries,
    own,
    other,
    places,
    key_places,
    packed,
    log_total,
    cosine,
    sine,
    after=(),
):
    return pl.pallas_call(
        later(functools.partial(attend_backward_kernel, window), len(after)),
        grid=(1,),
        in_specs=anywhere(after)
        + [pl.BlockSpec(memory_space=pltpu.SMEM)]
        + PIECES
        + line_specs()
        + [out_spec(), whole((8, 512)), whole((48, 512)), whole((48, 512))],
        out_specs=[whole((512, 384))] * 3,
        out_shape=[
            jax.ShapeDtypeStruct((512, 384), BF16),
            jax.ShapeDtypeStruct((512, 384), F32),
            jax.ShapeDtypeStruct((512, 384), BF16),
        ],
        scratch_shapes=[pltpu.VMEM((512, 1536), BF16), pltpu.VMEM((1024, 512), F32)],
        compiler_params=params(52),
        cost_estimate=cost(6e9, 6e6, 2e6),
        name="attend_backward",
    )(
        *after,
        length,
        *pieces,
        queries,
        own,
        other,
        places,
        key_places,
        packed,
        log_total,
        cosine,
        sine,
    )


def unproject_kernel(low_queries, pair_own, pair_came, cosine, sine, weight, *refs):
    outs, low = refs[:4], refs[4]
    both = pair_own[...] + pair_came[...].astype(F32)
    keys = turn_columns(both[:, :192], cosine[...], -sine[...])
    rows = jnp.concatenate(
        [low_queries[...], keys.astype(BF16), both[:, 192:].astype(BF16)], axis=1
    )
    low[...] = rows
    emit(nt(rows, weight[...]), outs)


def unproject_call(low_queries, pair_own, pair_came, cosine, sine, packed, after=()):
    wide = packed.shape[-1]
    return pl.pallas_call(
        later(unproject_kernel, len(after)),
        grid=(1,),
        in_specs=anywhere(after)
        + [whole((512, 384))] * 3
        + [whole((512, 48))] * 2
        + [projection_spec()],
        out_specs=PARTIALS + [whole((512, 768))],
        out_shape=LOW_PARTIAL_SHAPES + [jax.ShapeDtypeStruct((512, 768), BF16)],
        compiler_params=params(40),
        cost_estimate=cost(1.3e9, 7e6),
        name="unproject",
    )(*after, low_queries, pair_own, pair_came, cosine, sine, packed.reshape(1536, wide))


def attend_weights_kernel(count, *refs):
    flats, grads, (low, mixed) = refs[:count], refs[count : count + 5], refs[count + 5 : count + 7]
    out, flat_t, grad = refs[count + 7 :]
    start = 0
    for ref in flats:
        n = ref.shape[0]
        flat_t[:, start : start + n] = ref[...].T
        start += n
    fill(grad, grads)
    for block in range(3):
        cols = slice(256 * block, 256 * (block + 1))
        out[:, :, cols] = nn(flat_t[...], low[:, cols]).astype(BF16).reshape(8, 192, 256)
    mixed_t = mixed[...].T
    for block in range(4):
        part = nn(mixed_t, grad[:, 384 * block : 384 * (block + 1)]).astype(BF16)
        out[2 * block : 2 * block + 2, :, 768:1152] = part.reshape(2, 192, 384)


def attend_weights_call(flats, grads, low, mixed):
    return pl.pallas_call(
        functools.partial(attend_weights_kernel, len(flats)),
        grid=(1,),
        in_specs=piece_specs(flats) + PIECES + [whole((512, 768)), whole((512, 384))],
        out_specs=whole((8, 192, 1152)),
        out_shape=jax.ShapeDtypeStruct((8, 192, 1152), BF16),
        scratch_shapes=[pltpu.VMEM((1536, 512), BF16), pltpu.VMEM((512, 1536), BF16)],
        compiler_params=params(40),
        cost_estimate=cost(1.9e9, 10e6),
        name="attend_weights",
    )(*flats, *grads, low, mixed)


def unpack_kernel(*refs):
    every, wq, wk, wv, wo, gate, up, down = refs
    side = pl.program_id(0)
    blocks = [every[x, 0] for x in range(4)]
    for x, block in enumerate(blocks):
        wq[:, 384 * x : 384 * (x + 1)] = block[:, 3072:3456].astype(F32)
        wo[:, 384 * x : 384 * (x + 1)] = block[:, 3840:4224].astype(F32)
        for s in range(8):
            cols = slice(512 * s + 128 * x, 512 * s + 128 * (x + 1))
            gate[:, cols] = block[:, 128 * s : 128 * (s + 1)].astype(F32)
            up[:, cols] = block[:, 1024 + 128 * s : 1024 + 128 * (s + 1)].astype(F32)

        @pl.when(side == 0)
        def _(x=x, block=block):
            down[x, 0:96, :1024] = block[:, 2048:3072].astype(F32)

        @pl.when(side == 1)
        def _(x=x, block=block):
            down[x, 96:128, :1024] = block[0:32, 2048:3072].astype(F32)
            down[x, 0:64, 1024:] = block[32:96, 2048:2560].astype(F32)
            down[x, 64:128, 1024:] = block[32:96, 2560:3072].astype(F32)

    wk[...] = jnp.concatenate([block[:, 3456:3648].astype(F32) for block in blocks], axis=1)
    wv[...] = jnp.concatenate([block[:, 3648:3840].astype(F32) for block in blocks], axis=1)


def unpack_call(every):
    widths = (1536, 768, 768, 1536, 4096, 4096)
    out = pl.pallas_call(
        unpack_kernel,
        grid=(2,),
        in_specs=[pl.BlockSpec((4, 1, 96, every.shape[-1]), lambda b: (0, b, 0, 0))],
        out_specs=[pl.BlockSpec((96, width), lambda b: (b, 0)) for width in widths]
        + [whole((4, 128, 1536))],
        out_shape=[jax.ShapeDtypeStruct((192, width), F32) for width in widths]
        + [jax.ShapeDtypeStruct((4, 128, 1536), F32)],
        compiler_params=params(48),
        cost_estimate=cost(1e6, 30e6),
        name="unpack",
    )(every)
    return out[:4], (out[4], out[5], out[6].reshape(512, 1536))


def pack_feed_kernel(where, w_gate, w_up, w_down, out):
    x = where[0]
    for s in range(8):
        cols = pl.ds(pl.multiple_of(512 * s + 128 * x, 128), 128)
        out[:, 128 * s : 128 * (s + 1)] = w_gate[:, cols]
        out[:, 1024 + 128 * s : 1024 + 128 * (s + 1)] = w_up[:, cols]
    out[0:128, 2048:3072] = w_down[:, 0:1024]
    out[128:192, 2048:2560] = w_down[0:64, 1024:1536]
    out[128:192, 2560:3072] = w_down[64:128, 1024:1536]


def pack_feed_call(where, w_gate, w_up, w_down, after=()):
    return pl.pallas_call(
        later(pack_feed_kernel, len(after), 1),
        grid_spec=pltpu.PrefetchScalarGridSpec(
            num_scalar_prefetch=1,
            grid=(1,),
            in_specs=anywhere(after)
            + [
                pl.BlockSpec((192, 4096), lambda b, w: (0, 0)),
                pl.BlockSpec((192, 4096), lambda b, w: (0, 0)),
                pl.BlockSpec((128, 1536), lambda b, w: (w[0], 0)),
            ],
            out_specs=pl.BlockSpec((192, 3072), lambda b, w: (0, 0)),
        ),
        out_shape=jax.ShapeDtypeStruct((192, 3072), BF16),
        compiler_params=params(24),
        cost_estimate=cost(1e3, 5e6),
        name="pack_feed",
    )(where, *after, w_gate, w_up, w_down)


WINDOW = 512
EPSILON = 1e-05
ROPE_BASE = 100000.0

AXES = ("ylo", "x", "core", "z", "yhi")
SIZES = (2, 4, 2, 4, 2)
REP = ("ylo", "x", "core")
SHARD = ("z", "yhi")
SPREAD = ("z", "core")

RIGHT = [(i, (i + 1) % 4) for i in range(4)]
LEFT = [(i, (i - 1) % 4) for i in range(4)]
ACROSS = [(i, (i + 2) % 4) for i in range(4)]
SWAP = [(0, 1), (1, 0)]


def number(ylo, x, core, z, yhi):
    return (((ylo * 4 + x) * 2 + core) * 4 + z) * 2 + yhi


def permutation(place, taken=None):
    pairs = []
    for ylo in range(2):
        for x in range(4):
            for core in range(2):
                for z in range(4):
                    for yhi in range(2):
                        here = (ylo, x, core, z, yhi)
                        if taken is None or taken(*here):
                            pairs.append((number(*here), number(*place(*here))))
    return pairs


def inverse(pairs):
    return [(there, here) for here, there in pairs]


def at_home(ylo, x, core, z, yhi):
    return core == yhi


LINES = [
    permutation(lambda l, x, c, z, h, k=k: (l, (z + k) % 4, h, x, c)) for k in range(4)
]
TURN = permutation(lambda l, x, c, z, h: (l, z, h, x, c))
SHARE = permutation(lambda l, x, c, z, h: (l, x, c, z, 1 - h), at_home)
CROSS = permutation(lambda l, x, c, z, h: (l, z, c, x, h))


def to_lines(block, z):
    part = block.shape[0] // 4
    out = []
    for k in range(4):
        piece = lax.dynamic_slice_in_dim(block, ((z + k) % 4) * part, part, axis=0)
        out.append(lax.ppermute(piece, AXES, LINES[k]))
    return out


def send_home(block):
    part = block.shape[0] // 4
    return [
        lax.ppermute(block[part * k : part * (k + 1)], AXES, inverse(LINES[k])) for k in range(4)
    ]


def place_home(parts, z):
    rows = parts[0].shape[0]
    out = jnp.zeros((4 * rows,) + parts[0].shape[1:], parts[0].dtype)
    for k in range(4):
        out = lax.dynamic_update_slice_in_dim(out, parts[k], ((z + k) % 4) * rows, axis=0)
    return out


def interleave(first, second):
    parts = [item[32 * k : 32 * (k + 1)] for k in range(4) for item in (first, second)]
    return jnp.concatenate(parts, axis=0)


def separate(block):
    parts = [block[32 * k : 32 * (k + 1)] for k in range(8)]
    return jnp.concatenate(parts[::2], axis=0), jnp.concatenate(parts[1::2], axis=0)


def ring_gather(block):
    half = block.shape[0] // 2
    from_left = lax.ppermute(block, "x", RIGHT)
    from_right = lax.ppermute(block, "x", LEFT)
    far_first = lax.ppermute(from_left[:half], "x", RIGHT)
    far_second = lax.ppermute(from_right[half:], "x", LEFT)
    return block, from_left, from_right, far_first, far_second


def ring_scatter(own, left, right, far):
    half = far.shape[0] // 2
    first = lax.ppermute(far[:half], "x", RIGHT).astype(F32)
    second = lax.ppermute(far[half:], "x", LEFT).astype(F32)
    right = jnp.concatenate([right[:half] + first, right[half:]], axis=0).astype(BF16)
    left = jnp.concatenate([left[:half], left[half:] + second], axis=0).astype(BF16)
    from_left = lax.ppermute(right, "x", RIGHT).astype(F32)
    from_right = lax.ppermute(left, "x", LEFT).astype(F32)
    return own + from_left + from_right


def ring_scatter_direct(own, left, right, far):
    from_left = lax.ppermute(right, "x", RIGHT).astype(F32)
    from_right = lax.ppermute(left, "x", LEFT).astype(F32)
    from_far = lax.ppermute(far, "x", ACROSS).astype(F32)
    return own + from_left + from_right + from_far


def tie(value, *others):
    return lax.optimization_barrier((value, *others))[0]


def rms_norm(values, gain):
    return values * lax.rsqrt(jnp.mean(values * values, axis=-1, keepdims=True) + EPSILON) * gain


def add_low(mine, came):
    return (mine.astype(F32) + came.astype(F32)).astype(BF16)


def yhi_sum(rows, core, yhi):
    mine = lax.dynamic_slice_in_dim(rows, 96 * core, 96, axis=0)
    theirs = lax.dynamic_slice_in_dim(rows, 96 * (1 - core), 96, axis=0)
    came = lax.ppermute(theirs, "core", SWAP)
    home = core == yhi
    kept = jnp.where(home, mine, came)
    away = jnp.where(home, came, mine)
    return add_low(kept, lax.ppermute(away, "yhi", SWAP))


def ylo_sum(piece):
    return add_low(piece, lax.ppermute(piece, "ylo", SWAP))


def cross(piece, start, *others):
    first, last = start + 768, start + 1152
    moved = lax.ppermute(piece[:, first:last], AXES, CROSS)
    if others:
        piece, moved = lax.optimization_barrier((piece, moved, *others))[:2]
    return jnp.concatenate([piece[:, :first], moved, piece[:, last:]], axis=1)


def gain_rows(grads):
    tall = grads.astype(BF16).T.reshape(8, 192, 4)
    return jnp.pad(tall, ((0, 0), (0, 0), (0, 124)))


def norm_back(grad, own_normed, state, gain):
    grad_state, grad_gain = jax.vjp(rms_norm, state, gain)[1](own_normed)
    return grad + grad_state, grad_gain


def body(tokens, lengths, grad_output, *weights):
    stretch, width = tokens.shape[1:]
    x = lax.axis_index("x")
    core = lax.axis_index("core")
    z = lax.axis_index("z")
    yhi = lax.axis_index("yhi")
    member = x.astype(jnp.int32).reshape(1)
    home = core == yhi

    gains = jnp.stack([weights[0], weights[5], weights[9], weights[14]]).T
    gains = jnp.pad(gains, ((0, 0), (0, 124)))

    def shared(block, *joined):
        return jnp.where(home, block, tie(lax.ppermute(block, AXES, SHARE), *joined))

    def attention_part(base, extra, after):
        block = lax.dynamic_slice(tie(weights[base + 4], *after), (0, 384 * x), (192, 384))
        block = lax.ppermute(block, AXES, TURN)
        parts = [
            lax.dynamic_slice(w, (0, x * (w.shape[1] // 4)), (192, w.shape[1] // 4))
            for w in weights[base + 1 : base + 4]
        ]
        parts = shared(jnp.concatenate(parts + extra, axis=1))
        return jnp.concatenate([parts[:, :768], block, parts[:, 768:]], axis=1)

    def feed_part(base, after, joined):
        part = pack_feed_call(member, *weights[base + 6 : base + 9], after=after)
        return shared(part, *joined)

    def line_weights(piece, *after):
        return lax.all_gather(tie(piece, *after), SPREAD, axis=0, tiled=False)

    here = (2 * z + yhi) * stretch + jnp.arange(stretch, dtype=jnp.int32)
    valid = (here < lengths[0])[:, None]
    grad_start = jnp.where(valid, grad_output[0], 0).astype(BF16)
    length = lax.ppermute(lengths, AXES, TURN)
    moved = to_lines(interleave(tokens[0], grad_start), z)
    rows, grad_rows = separate(jnp.concatenate(moved, axis=0))

    attn_one = line_weights(attention_part(0, [gains], ()))
    feed_one = feed_part(0, (), moved)
    gains = attn_one[:, :, 1152:1156].transpose(2, 0, 1).reshape(4, width).astype(F32)
    pieces = ring_gather(rows)
    state = rows.astype(F32)
    feed_one = line_weights(feed_one, *pieces[3:])
    grad_pieces = ring_gather(grad_rows)
    grad = grad_rows.astype(F32)

    part = stretch // 4

    def member_places(member, side_index):
        block = jnp.arange(4, dtype=jnp.int32)
        inner = jnp.arange(part, dtype=jnp.int32)
        home = (member - block + 4) % 4
        return (
            home[:, None] * (2 * stretch) + side_index * stretch + member * part + inner[None, :]
        ).reshape(-1)

    def line_places(side_index):
        return jnp.concatenate([member_places((x + step) % 4, side_index) for step in (0, 3, 1, 2)])

    places = line_places(core)
    key_places = jnp.concatenate([places, line_places(1 - core)]).reshape(1024, 1)
    half = HEAD_DIM // 2
    freq = ROPE_BASE ** (-jnp.arange(half, dtype=F32) * (2.0 / HEAD_DIM))
    angle = places.astype(F32)[:, None] * freq[None, :]
    cosine, sine = jnp.cos(angle), jnp.sin(angle)
    cosine_t, sine_t = cosine.T, sine.T
    places = places.reshape(1, 512)

    records = []
    for index, window in enumerate((WINDOW, 8 * stretch)):
        if index == 0:
            attn, feed = attn_one, feed_one
        else:
            attn, feed = attn_two, feed_two
        gain_attn, gain_feed = gains[2 * index], gains[2 * index + 1]
        if index == 0:
            queries, own, flat = project_call(True, pieces, gain_attn, attn, cosine, sine)
            flats = (flat,)
        else:
            flats = ring_gather(rms_norm(state, gain_attn).astype(BF16))
            feed_two = feed = line_weights(feed_two, *flats[1:3])
            queries, own = project_call(False, flats, gain_attn, attn, cosine, sine)
        other = lax.ppermute(own, "core", SWAP)
        line = (queries, own, other, places, key_places)
        after = grad_pieces[3:] if index else ()
        *partial, mixed, log_total = attend_call(window, length, *line, attn, after=after)
        saved_attn = (state, flats, line, mixed, log_total)
        state = state + ring_scatter(*partial)
        if index == 0:
            attn_two = attention_part(9, [], (mixed,))
            feed_two = feed_part(9, (mixed,), ())
        flats = ring_gather(rms_norm(state, gain_feed).astype(BF16))
        if index == 0:
            attn_two = line_weights(attn_two, *flats[1:3])
        *partial, gate, up, hidden = feed_forward_call(flats, feed)
        saved_feed = (state, flats, gate, up, hidden)
        state = state + ring_scatter(*partial)
        records.append((saved_attn, saved_feed, window))
    last_rows = state.astype(BF16)
    packed = ((attn_one, feed_one), (attn_two, feed_two))

    results = [None] * 18
    gain_grads = [None] * 4

    def feed_back(index, grad, pieces, after):
        state, flats, gate, up, hidden = records[index][1]
        *partial, low_gate, low_up = feed_backward_call(
            pieces, packed[index][1], gate, up, after=after
        )
        own_normed = ring_scatter_direct(*partial)
        grad, gain_grads[2 * index + 1] = norm_back(
            grad, own_normed, state, gains[2 * index + 1]
        )
        return grad, feed_weights_call(flats, pieces, low_gate, low_up, hidden)

    def attention_back(index, grad, pieces, after, late):
        state, flats, line, mixed, log_total = records[index][0]
        window = records[index][2]
        attn = packed[index][0]
        low_queries, pair_own, pair_other = attend_backward_call(
            window, length, pieces, *line, attn, log_total, cosine_t, sine_t, after=after
        )
        came = lax.ppermute(pair_other, "core", SWAP)
        *partial, low = unproject_call(
            low_queries, pair_own, came, cosine, sine, attn, after=late
        )
        own_normed = ring_scatter_direct(*partial)
        grad, gain_grads[2 * index] = norm_back(grad, own_normed, state, gains[2 * index])
        return grad, attend_weights_call(flats, pieces, low, mixed)

    def scatter(block):
        return lax.psum_scatter(block, SPREAD, scatter_dimension=0, tiled=True)

    grad, feed_grad = feed_back(1, grad, grad_pieces, ())
    low = tie(grad.astype(BF16), feed_grad)
    second_feed = scatter(tie(feed_grad, low))
    grad, attn_grad = attention_back(1, grad, ring_gather(low), (last_rows,), ())
    low = tie(grad.astype(BF16), attn_grad)
    second_attn = scatter(tie(attn_grad, low, second_feed))

    grad, feed_grad = feed_back(0, grad, ring_gather(low), (second_feed,))
    low = tie(grad.astype(BF16), feed_grad)
    first_feed = scatter(tie(feed_grad, low, second_attn))
    second = yhi_sum(jnp.concatenate([second_feed, second_attn], axis=2)[0], core, yhi)
    second_piece = ylo_sum(second)
    grad, attn_grad = attention_back(0, grad, ring_gather(low), (second,), (second_piece,))
    low = grad.astype(BF16)
    attn_grad = tie(attn_grad, first_feed, low)
    attn_grad = jnp.concatenate([attn_grad, gain_rows(jnp.stack(gain_grads))], axis=2)
    first_attn = scatter(attn_grad)
    back = send_home(interleave(last_rows, low))
    feed_piece = tie(yhi_sum(first_feed[0], core, yhi), back[0])
    feed_piece = tie(ylo_sum(feed_piece), back[1])
    every = cross(second_piece, 3072, first_attn, feed_piece)
    every = lax.all_gather(every, ("x", "core"), axis=0, tiled=False)
    results[10:14], results[15:18] = unpack_call(every.reshape(4, 2, 96, -1))
    attn_piece = tie(yhi_sum(tie(first_attn, feed_piece)[0], core, yhi), back[2])
    attn_piece = tie(ylo_sum(attn_piece), back[3])
    first_piece = jnp.concatenate([feed_piece, cross(attn_piece, 0)], axis=1)
    every = lax.all_gather(first_piece, ("x", "core"), axis=0, tiled=False)
    every = every.reshape(4, 2, 96, -1)
    results[1:5], results[6:9] = unpack_call(every)
    gain_sums = every[..., 4224:4228].astype(F32).sum(axis=0).reshape(192, 4).T
    output, input_grad = separate(place_home(back, z))
    output, input_grad = output[None], input_grad.astype(F32)[None]
    for index, slot in enumerate((0, 5, 9, 14)):
        results[slot] = gain_sums[index]
    return (output, input_grad, *results)


def solution(mesh):
    fine = Mesh(mesh.devices.reshape(SIZES), AXES)
    token = P(REP, SHARD, None)
    vector = P(SHARD)
    matrix = P(SHARD, None)
    layer = (vector, matrix, matrix, matrix, matrix, vector, matrix, matrix, matrix)
    return jax.shard_map(
        body,
        mesh=fine,
        in_specs=(token, P(REP), token) + layer + layer,
        out_specs=(token, token) + layer + layer,
        check_vma=False,
    )
```

```python
import functools
import jax
import jax.numpy as jnp
from jax import lax
from jax.experimental import pallas as pl
from jax.experimental.pallas import tpu as pltpu
from jax.sharding import Mesh
from jax.sharding import PartitionSpec as P

F32 = jnp.float32
BF16 = jnp.bfloat16
HEAD_DIM = 96
NEGATIVE = -1e30
MIB = 1 << 20

OFFSETS = (0, 128, 256, 384, 448)
SIZES_OF = (128, 128, 128, 64, 64)


def params(mib, semantics=None):
    return pltpu.CompilerParams(vmem_limit_bytes=mib * MIB, dimension_semantics=semantics)


def cost(flops, nbytes, transcendentals=0):
    return pl.CostEstimate(
        flops=int(flops), bytes_accessed=int(nbytes), transcendentals=int(transcendentals)
    )


def fill(target, refs):
    start = 0
    for ref in refs:
        rows = ref.shape[0]
        target[start : start + rows, :] = ref[...]
        start += rows


def nn(a, b):
    return lax.dot_general(a, b, (((1,), (0,)), ((), ())), preferred_element_type=F32)


def nt(a, b):
    return lax.dot_general(a, b, (((1,), (1,)), ((), ())), preferred_element_type=F32)


def tn(a, b):
    return lax.dot_general(a, b, (((0,), (0,)), ((), ())), preferred_element_type=F32)


def later(kernel, count, lead=0):
    if not count:
        return kernel

    def wrapped(*refs):
        return kernel(*refs[:lead], *refs[lead + count :])

    return wrapped


def anywhere(after):
    return [pl.BlockSpec(memory_space=pl.ANY)] * len(after)


def whole(shape):
    return pl.BlockSpec(shape, lambda *_: (0,) * len(shape))


PIECES = [whole((rows, 1536)) for rows in SIZES_OF]
PARTIAL_SHAPES = [
    jax.ShapeDtypeStruct((128, 1536), F32),
    jax.ShapeDtypeStruct((128, 1536), F32),
    jax.ShapeDtypeStruct((128, 1536), F32),
    jax.ShapeDtypeStruct((128, 1536), BF16),
]
LOW_PARTIAL_SHAPES = PARTIAL_SHAPES[:1] + [jax.ShapeDtypeStruct((128, 1536), BF16)] * 3
PARTIALS = [whole((128, 1536))] * 4


def emit(total, outs):
    for place, out in enumerate(outs):
        out[...] = total[128 * place : 128 * (place + 1), :].astype(out.dtype)


def down_parts(block):
    left = block[:, 0:128, :].reshape(256, 1024)
    right = jnp.concatenate([block[:, 128:192, 0:512], block[:, 128:192, 512:1024]], axis=1)
    return left, right.reshape(256, 512)


def feed_forward_kernel(*refs):
    pieces, (wg, wu, wd), outs = refs[:5], refs[5:8], refs[8:12]
    gate, up, hidden, flat, total = refs[12:]
    step = pl.program_id(0)

    @pl.when(step == 0)
    def _():
        fill(flat, pieces)

    rows = flat[...]
    g = nn(rows, wg[...])
    u = nn(rows, wu[...])
    gate[...] = g
    up[...] = u
    h = (g * jax.nn.sigmoid(g) * u).astype(BF16)
    hidden[...] = h
    left, right = down_parts(wd[...])
    left, right = nn(h, left), nn(h, right)

    @pl.when(step == 0)
    def _():
        total[:, :1024] = left
        total[:, 1024:] = right

    @pl.when(step > 0)
    def _():
        total[:, :1024] += left
        total[:, 1024:] += right

    @pl.when(step == 3)
    def _():
        emit(total, outs)


def feed_specs():
    return [
        pl.BlockSpec((1536, 256), lambda b: (0, b)),
        pl.BlockSpec((1536, 256), lambda b: (0, 4 + b)),
        pl.BlockSpec((2, 192, 1024), lambda b: (b, 0, 2)),
    ]


def column_block(rows):
    return pl.BlockSpec((rows, 256), lambda b: (0, b))


def feed_forward_call(pieces, packed, after=()):
    flat_packed = packed.reshape(1536, -1)
    return pl.pallas_call(
        later(feed_forward_kernel, len(after)),
        grid=(4,),
        in_specs=anywhere(after) + PIECES + feed_specs(),
        out_specs=PARTIALS + [column_block(512)] * 3,
        out_shape=PARTIAL_SHAPES
        + [
            jax.ShapeDtypeStruct((512, 1024), F32),
            jax.ShapeDtypeStruct((512, 1024), F32),
            jax.ShapeDtypeStruct((512, 1024), BF16),
        ],
        scratch_shapes=[pltpu.VMEM((512, 1536), BF16), pltpu.VMEM((512, 1536), F32)],
        compiler_params=params(40),
        cost_estimate=cost(4.9e9, 18e6),
        name="feed_forward",
    )(*after, *pieces, flat_packed, flat_packed, packed)


def feed_backward_kernel(*refs):
    pieces, (wg, wu, wd, gate, up), outs = refs[:5], refs[5:10], refs[10:14]
    low_gate, low_up, flat, total = refs[14:]
    step = pl.program_id(0)

    @pl.when(step == 0)
    def _():
        fill(flat, pieces)

    rows = flat[...]
    left, right = down_parts(wd[...])
    grad = nt(rows[:, :1024], left) + nt(rows[:, 1024:], right)
    g = gate[...]
    s = jax.nn.sigmoid(g)
    a = (grad * up[...] * s * (1.0 + g * (1.0 - s))).astype(BF16)
    b = (grad * (g * s)).astype(BF16)
    low_gate[...] = a
    low_up[...] = b
    part = nt(a, wg[...]) + nt(b, wu[...])

    @pl.when(step == 0)
    def _():
        total[...] = part

    @pl.when(step > 0)
    def _():
        total[...] += part

    @pl.when(step == 3)
    def _():
        emit(total, outs)


def feed_backward_call(pieces, packed, gate, up, after=()):
    flat_packed = packed.reshape(1536, -1)
    return pl.pallas_call(
        later(feed_backward_kernel, len(after)),
        grid=(4,),
        in_specs=anywhere(after) + PIECES + feed_specs() + [column_block(512)] * 2,
        out_specs=PARTIALS + [column_block(512)] * 2,
        out_shape=LOW_PARTIAL_SHAPES + [jax.ShapeDtypeStruct((512, 1024), BF16)] * 2,
        scratch_shapes=[pltpu.VMEM((512, 1536), BF16), pltpu.VMEM((512, 1536), F32)],
        compiler_params=params(40),
        cost_estimate=cost(4.9e9, 20e6),
        name="feed_backward",
    )(*after, *pieces, flat_packed, flat_packed, packed, gate, up)


def feed_weights_kernel(*refs):
    flats, grads = refs[:5], refs[5:10]
    low_gate, low_up, hidden, out, flat_t, hidden_t, grad = refs[10:]
    step = pl.program_id(0)

    @pl.when(step == 0)
    def _():
        start = 0
        for ref in flats:
            n = ref.shape[0]
            flat_t[:, start : start + n] = ref[...].T
            start += n

    @pl.when(step == 4)
    def _():
        hidden_t[...] = hidden[...].T
        fill(grad, grads)

    @pl.when(step < 4)
    def _():
        out[...] = nn(flat_t[...], low_gate[...]).astype(BF16).reshape(8, 192, 256)

    @pl.when((step >= 4) & (step < 8))
    def _():
        out[...] = nn(flat_t[...], low_up[...]).astype(BF16).reshape(8, 192, 256)

    for q in range(4):

        @pl.when(step == 8 + q)
        def _():
            top = nn(hidden_t[...], grad[:, 256 * q : 256 * (q + 1)]).astype(BF16)
            out[:, 0:128, :] = top.reshape(8, 128, 256)
            half = 64 * (q // 2)
            some = hidden_t[...].reshape(8, 128, 512)[:, half : half + 64].reshape(512, 512)
            start = 1024 + 256 * (q % 2)
            low = nn(some, grad[:, start : start + 256]).astype(BF16)
            out[:, 128:192, :] = low.reshape(8, 64, 256)


def feed_weights_call(flats, grads, low_gate, low_up, hidden):
    return pl.pallas_call(
        feed_weights_kernel,
        grid=(12,),
        in_specs=PIECES
        + PIECES
        + [
            pl.BlockSpec((512, 256), lambda b: (0, jnp.minimum(b, 3))),
            pl.BlockSpec((512, 256), lambda b: (0, jnp.clip(b - 4, 0, 3))),
            whole((512, 1024)),
        ],
        out_specs=pl.BlockSpec((8, 192, 256), lambda b: (0, 0, b)),
        out_shape=jax.ShapeDtypeStruct((8, 192, 3072), BF16),
        scratch_shapes=[
            pltpu.VMEM((1536, 512), BF16),
            pltpu.VMEM((1024, 512), BF16),
            pltpu.VMEM((512, 1536), BF16),
        ],
        compiler_params=params(40),
        cost_estimate=cost(4.9e9, 18e6),
        name="feed_weights",
    )(*flats, *grads, low_gate, low_up, hidden)


def piece_specs(pieces):
    return [whole(item.shape) for item in pieces]


def turn_columns(block, cosine, sine):
    out = []
    for start in range(0, block.shape[1], HEAD_DIM):
        a = block[:, start : start + 48]
        b = block[:, start + 48 : start + HEAD_DIM]
        out.append(a * cosine - b * sine)
        out.append(b * cosine + a * sine)
    return jnp.concatenate(out, axis=1)


def project_kernel(raw, count, *refs):
    pieces, (gain, weight, cosine, sine, queries, pair) = refs[:count], refs[count : count + 6]
    if raw:
        flat = refs[-1]
        start = 0
        for ref in pieces:
            n = ref.shape[0]
            rows = ref[...].astype(F32)
            scale = lax.rsqrt(jnp.mean(rows * rows, axis=-1, keepdims=True) + 1e-05)
            flat[start : start + n, :] = (rows * scale * gain[...]).astype(BF16)
            start += n
    else:
        flat = refs[-1]
        fill(flat, pieces)
    both = nn(flat[...], weight[...])
    cos, sin = cosine[...], sine[...]
    queries[...] = turn_columns(both[:, :384], cos, sin).astype(BF16)
    keys = turn_columns(both[:, 384:576], cos, sin)
    pair[...] = jnp.concatenate([keys, both[:, 576:768]], axis=1).astype(BF16)


def project_call(raw, pieces, gain, packed, cosine, sine, after=()):
    wide = packed.shape[-1]
    shape = jax.ShapeDtypeStruct((512, 384), BF16)
    flat_shape = jax.ShapeDtypeStruct((512, 1536), BF16)
    return pl.pallas_call(
        later(functools.partial(project_kernel, raw, len(pieces)), len(after)),
        grid=(1,),
        in_specs=anywhere(after)
        + piece_specs(pieces)
        + [whole((1, 1536)), projection_spec(), whole((512, 48)), whole((512, 48))],
        out_specs=[whole((512, 384))] * 2 + ([whole((512, 1536))] if raw else []),
        out_shape=[shape, shape] + ([flat_shape] if raw else []),
        scratch_shapes=[] if raw else [pltpu.VMEM((512, 1536), BF16)],
        compiler_params=params(40),
        cost_estimate=cost(1.3e9, 6e6),
        name="project",
    )(*after, *pieces, gain.reshape(1, 1536), packed.reshape(1536, wide), cosine, sine)


def fill_bias(bias, length, places, key_places, window):
    gap = places[...] - key_places[...]
    inside = (key_places[...] < length) & (gap >= 0) & (gap < window)
    bias[...] = jnp.where(inside | (gap == 0), 0.0, NEGATIVE)


def both_rows(own, other, start):
    return jnp.concatenate(
        [own[:, start : start + HEAD_DIM], other[:, start : start + HEAD_DIM]], axis=0
    )


def attend_kernel(window, length, queries, own, other, places, key_places, w_out, *refs):
    outs, (mixed, log_total, total, bias) = refs[:4], refs[4:]
    fill_bias(bias, length[0], places, key_places, window)
    sums = []
    stats = []
    for head in range(4):
        if head % 2 == 0:
            keys = both_rows(own[...], other[...], HEAD_DIM * (head // 2))
            values = both_rows(own[...], other[...], 192 + HEAD_DIM * (head // 2)).T
        query = queries[:, HEAD_DIM * head : HEAD_DIM * (head + 1)]
        scores = nt(keys, query) * HEAD_DIM ** (-0.5) + bias[...]
        peak = jnp.max(scores, axis=0, keepdims=True)
        probs = jnp.exp(scores - peak)
        totals = jnp.sum(probs, axis=0, keepdims=True)
        part = nn(values, probs.astype(BF16)) / totals
        sums.append(part.astype(BF16).astype(F32).T.astype(BF16))
        stats.append(peak + jnp.log(totals))
        for block in range(4):
            cols = slice(384 * block, 384 * (block + 1))
            value = nn(sums[-1], out_block(w_out, head, block))
            if head == 0:
                total[:, cols] = value
            else:
                total[:, cols] += value
    mixed[...] = jnp.concatenate(sums, axis=1)
    log_total[...] = jnp.concatenate(stats + stats, axis=0)
    emit(total, outs)


def line_specs():
    return [whole((512, 384))] * 3 + [whole((1, 512)), whole((1024, 1))]


def out_spec():
    return pl.BlockSpec((8, 192, 384), lambda *_: (0, 0, 2))


def out_block(w_out, head, block):
    start = 96 * (head % 2)
    return w_out[2 * block + head // 2, start : start + 96, :]


def projection_spec():
    return pl.BlockSpec((1536, 768), lambda *_: (0, 0))


def attend_call(window, length, queries, own, other, places, key_places, packed, after=()):
    return pl.pallas_call(
        later(functools.partial(attend_kernel, window), len(after)),
        grid=(1,),
        in_specs=anywhere(after)
        + [pl.BlockSpec(memory_space=pltpu.SMEM)] + line_specs() + [out_spec()],
        out_specs=PARTIALS + [whole((512, 384)), whole((8, 512))],
        out_shape=PARTIAL_SHAPES
        + [jax.ShapeDtypeStruct((512, 384), BF16), jax.ShapeDtypeStruct((8, 512), F32)],
        scratch_shapes=[pltpu.VMEM((512, 1536), F32), pltpu.VMEM((1024, 512), F32)],
        compiler_params=params(48),
        cost_estimate=cost(3e9, 6e6, 2e6),
        name="attend",
    )(*after, length, queries, own, other, places, key_places, packed)


def attend_backward_kernel(window, length, *refs):
    pieces, refs = refs[:5], refs[5:]
    queries, own, other, places, key_places, w_out, log_total, cosine, sine = refs[:9]
    low_queries, pair_own, pair_other, grad, bias = refs[9:]
    fill(grad, pieces)
    fill_bias(bias, length[0], places, key_places, window)
    cos, sin = cosine[...], sine[...]
    lows = []
    key_sums = []
    value_sums = []
    for head in range(4):
        if head % 2 == 0:
            keys = both_rows(own[...], other[...], HEAD_DIM * (head // 2))
            values = both_rows(own[...], other[...], 192 + HEAD_DIM * (head // 2))
            keys_t = keys.T
        query = queries[:, HEAD_DIM * head : HEAD_DIM * (head + 1)]
        mixed = nt(grad[:, :384], out_block(w_out, head, 0))
        for block in range(1, 4):
            mixed += nt(
                grad[:, 384 * block : 384 * (block + 1)], out_block(w_out, head, block)
            )
        mixed = mixed.astype(BF16)
        scores = nt(keys, query) * HEAD_DIM ** (-0.5) + bias[...]
        probs = jnp.exp(scores - log_total[head : head + 1, :])
        slopes = nt(values, mixed)
        inner = jnp.sum(probs * slopes, axis=0, keepdims=True)
        raw = (probs * (slopes - inner) * HEAD_DIM ** (-0.5)).astype(BF16)
        key_part = nn(raw, query)
        value_part = nn(probs.astype(BF16), mixed)
        if head % 2 == 0:
            key_sums.append(key_part)
            value_sums.append(value_part)
        else:
            key_sums[-1] += key_part
            value_sums[-1] += value_part
        turned = nn(keys_t, raw)
        a, b = turned[:48], turned[48:]
        turned = jnp.concatenate([a * cos + b * sin, b * cos - a * sin], axis=0)
        lows.append(turned.T.astype(BF16))
    low_queries[...] = jnp.concatenate(lows, axis=1)
    both = jnp.concatenate(key_sums + value_sums, axis=1)
    pair_own[...] = both[:512]
    pair_other[...] = both[512:].astype(BF16)


def attend_backward_call(
    window,
    length,
    pieces,
    queries,
    own,
    other,
    places,
    key_places,
    packed,
    log_total,
    cosine,
    sine,
    after=(),
):
    return pl.pallas_call(
        later(functools.partial(attend_backward_kernel, window), len(after)),
        grid=(1,),
        in_specs=anywhere(after)
        + [pl.BlockSpec(memory_space=pltpu.SMEM)]
        + PIECES
        + line_specs()
        + [out_spec(), whole((8, 512)), whole((48, 512)), whole((48, 512))],
        out_specs=[whole((512, 384))] * 3,
        out_shape=[
            jax.ShapeDtypeStruct((512, 384), BF16),
            jax.ShapeDtypeStruct((512, 384), F32),
            jax.ShapeDtypeStruct((512, 384), BF16),
        ],
        scratch_shapes=[pltpu.VMEM((512, 1536), BF16), pltpu.VMEM((1024, 512), F32)],
        compiler_params=params(52),
        cost_estimate=cost(6e9, 6e6, 2e6),
        name="attend_backward",
    )(
        *after,
        length,
        *pieces,
        queries,
        own,
        other,
        places,
        key_places,
        packed,
        log_total,
        cosine,
        sine,
    )


def unproject_kernel(low_queries, pair_own, pair_came, cosine, sine, weight, *refs):
    outs, low = refs[:4], refs[4]
    both = pair_own[...] + pair_came[...].astype(F32)
    keys = turn_columns(both[:, :192], cosine[...], -sine[...])
    rows = jnp.concatenate(
        [low_queries[...], keys.astype(BF16), both[:, 192:].astype(BF16)], axis=1
    )
    low[...] = rows
    emit(nt(rows, weight[...]), outs)


def unproject_call(low_queries, pair_own, pair_came, cosine, sine, packed, after=()):
    wide = packed.shape[-1]
    return pl.pallas_call(
        later(unproject_kernel, len(after)),
        grid=(1,),
        in_specs=anywhere(after)
        + [whole((512, 384))] * 3
        + [whole((512, 48))] * 2
        + [projection_spec()],
        out_specs=PARTIALS + [whole((512, 768))],
        out_shape=LOW_PARTIAL_SHAPES + [jax.ShapeDtypeStruct((512, 768), BF16)],
        compiler_params=params(40),
        cost_estimate=cost(1.3e9, 7e6),
        name="unproject",
    )(*after, low_queries, pair_own, pair_came, cosine, sine, packed.reshape(1536, wide))


def attend_weights_kernel(count, *refs):
    flats, grads, (low, mixed) = refs[:count], refs[count : count + 5], refs[count + 5 : count + 7]
    out, flat_t, grad = refs[count + 7 :]
    start = 0
    for ref in flats:
        n = ref.shape[0]
        flat_t[:, start : start + n] = ref[...].T
        start += n
    fill(grad, grads)
    for block in range(3):
        cols = slice(256 * block, 256 * (block + 1))
        out[:, :, cols] = nn(flat_t[...], low[:, cols]).astype(BF16).reshape(8, 192, 256)
    mixed_t = mixed[...].T
    for block in range(4):
        part = nn(mixed_t, grad[:, 384 * block : 384 * (block + 1)]).astype(BF16)
        out[2 * block : 2 * block + 2, :, 768:1152] = part.reshape(2, 192, 384)


def attend_weights_call(flats, grads, low, mixed):
    return pl.pallas_call(
        functools.partial(attend_weights_kernel, len(flats)),
        grid=(1,),
        in_specs=piece_specs(flats) + PIECES + [whole((512, 768)), whole((512, 384))],
        out_specs=whole((8, 192, 1152)),
        out_shape=jax.ShapeDtypeStruct((8, 192, 1152), BF16),
        scratch_shapes=[pltpu.VMEM((1536, 512), BF16), pltpu.VMEM((512, 1536), BF16)],
        compiler_params=params(40),
        cost_estimate=cost(1.9e9, 10e6),
        name="attend_weights",
    )(*flats, *grads, low, mixed)


def unpack_kernel(*refs):
    every, wq, wk, wv, wo, gate, up, down = refs
    side = pl.program_id(0)
    blocks = [every[x, 0] for x in range(4)]
    for x, block in enumerate(blocks):
        wq[:, 384 * x : 384 * (x + 1)] = block[:, 3072:3456].astype(F32)
        wo[:, 384 * x : 384 * (x + 1)] = block[:, 3840:4224].astype(F32)
        for s in range(8):
            cols = slice(512 * s + 128 * x, 512 * s + 128 * (x + 1))
            gate[:, cols] = block[:, 128 * s : 128 * (s + 1)].astype(F32)
            up[:, cols] = block[:, 1024 + 128 * s : 1024 + 128 * (s + 1)].astype(F32)

        @pl.when(side == 0)
        def _(x=x, block=block):
            down[x, 0:96, :1024] = block[:, 2048:3072].astype(F32)

        @pl.when(side == 1)
        def _(x=x, block=block):
            down[x, 96:128, :1024] = block[0:32, 2048:3072].astype(F32)
            down[x, 0:64, 1024:] = block[32:96, 2048:2560].astype(F32)
            down[x, 64:128, 1024:] = block[32:96, 2560:3072].astype(F32)

    wk[...] = jnp.concatenate([block[:, 3456:3648].astype(F32) for block in blocks], axis=1)
    wv[...] = jnp.concatenate([block[:, 3648:3840].astype(F32) for block in blocks], axis=1)


def unpack_call(every):
    widths = (1536, 768, 768, 1536, 4096, 4096)
    out = pl.pallas_call(
        unpack_kernel,
        grid=(2,),
        in_specs=[pl.BlockSpec((4, 1, 96, every.shape[-1]), lambda b: (0, b, 0, 0))],
        out_specs=[pl.BlockSpec((96, width), lambda b: (b, 0)) for width in widths]
        + [whole((4, 128, 1536))],
        out_shape=[jax.ShapeDtypeStruct((192, width), F32) for width in widths]
        + [jax.ShapeDtypeStruct((4, 128, 1536), F32)],
        compiler_params=params(48),
        cost_estimate=cost(1e6, 30e6),
        name="unpack",
    )(every)
    return out[:4], (out[4], out[5], out[6].reshape(512, 1536))


def pack_feed_kernel(where, w_gate, w_up, w_down, out):
    x = where[0]
    for s in range(8):
        cols = pl.ds(pl.multiple_of(512 * s + 128 * x, 128), 128)
        out[:, 128 * s : 128 * (s + 1)] = w_gate[:, cols]
        out[:, 1024 + 128 * s : 1024 + 128 * (s + 1)] = w_up[:, cols]
    out[0:128, 2048:3072] = w_down[:, 0:1024]
    out[128:192, 2048:2560] = w_down[0:64, 1024:1536]
    out[128:192, 2560:3072] = w_down[64:128, 1024:1536]


def pack_feed_call(where, w_gate, w_up, w_down, after=()):
    return pl.pallas_call(
        later(pack_feed_kernel, len(after), 1),
        grid_spec=pltpu.PrefetchScalarGridSpec(
            num_scalar_prefetch=1,
            grid=(1,),
            in_specs=anywhere(after)
            + [
                pl.BlockSpec((192, 4096), lambda b, w: (0, 0)),
                pl.BlockSpec((192, 4096), lambda b, w: (0, 0)),
                pl.BlockSpec((128, 1536), lambda b, w: (w[0], 0)),
            ],
            out_specs=pl.BlockSpec((192, 3072), lambda b, w: (0, 0)),
        ),
        out_shape=jax.ShapeDtypeStruct((192, 3072), BF16),
        compiler_params=params(24),
        cost_estimate=cost(1e3, 5e6),
        name="pack_feed",
    )(where, *after, w_gate, w_up, w_down)


WINDOW = 512
EPSILON = 1e-05
ROPE_BASE = 100000.0

AXES = ("ylo", "x", "core", "z", "yhi")
SIZES = (2, 4, 2, 4, 2)
REP = ("ylo", "x", "core")
SHARD = ("z", "yhi")
SPREAD = ("z", "core")

RIGHT = [(i, (i + 1) % 4) for i in range(4)]
LEFT = [(i, (i - 1) % 4) for i in range(4)]
ACROSS = [(i, (i + 2) % 4) for i in range(4)]
SWAP = [(0, 1), (1, 0)]


def number(ylo, x, core, z, yhi):
    return (((ylo * 4 + x) * 2 + core) * 4 + z) * 2 + yhi


def permutation(place, taken=None):
    pairs = []
    for ylo in range(2):
        for x in range(4):
            for core in range(2):
                for z in range(4):
                    for yhi in range(2):
                        here = (ylo, x, core, z, yhi)
                        if taken is None or taken(*here):
                            pairs.append((number(*here), number(*place(*here))))
    return pairs


def inverse(pairs):
    return [(there, here) for here, there in pairs]


def at_home(ylo, x, core, z, yhi):
    return core == yhi


LINES = [
    permutation(lambda l, x, c, z, h, k=k: (l, (z + k) % 4, h, x, c)) for k in range(4)
]
TURN = permutation(lambda l, x, c, z, h: (l, z, h, x, c))
SHARE = permutation(lambda l, x, c, z, h: (l, x, c, z, 1 - h), at_home)
CROSS = permutation(lambda l, x, c, z, h: (l, z, c, x, h))


def to_lines(block, z):
    part = block.shape[0] // 4
    out = []
    for k in range(4):
        piece = lax.dynamic_slice_in_dim(block, ((z + k) % 4) * part, part, axis=0)
        out.append(lax.ppermute(piece, AXES, LINES[k]))
    return out


def from_lines(block, z):
    part = block.shape[0] // 4
    out = jnp.zeros_like(block)
    for k in range(4):
        piece = lax.ppermute(block[part * k : part * (k + 1)], AXES, inverse(LINES[k]))
        out = lax.dynamic_update_slice_in_dim(out, piece, ((z + k) % 4) * part, axis=0)
    return out


def interleave(first, second):
    parts = [item[32 * k : 32 * (k + 1)] for k in range(4) for item in (first, second)]
    return jnp.concatenate(parts, axis=0)


def separate(block):
    parts = [block[32 * k : 32 * (k + 1)] for k in range(8)]
    return jnp.concatenate(parts[::2], axis=0), jnp.concatenate(parts[1::2], axis=0)


def ring_gather(block):
    half = block.shape[0] // 2
    from_left = lax.ppermute(block, "x", RIGHT)
    from_right = lax.ppermute(block, "x", LEFT)
    far_first = lax.ppermute(from_left[:half], "x", RIGHT)
    far_second = lax.ppermute(from_right[half:], "x", LEFT)
    return block, from_left, from_right, far_first, far_second


def ring_scatter(own, left, right, far):
    half = far.shape[0] // 2
    first = lax.ppermute(far[:half], "x", RIGHT).astype(F32)
    second = lax.ppermute(far[half:], "x", LEFT).astype(F32)
    right = jnp.concatenate([right[:half] + first, right[half:]], axis=0).astype(BF16)
    left = jnp.concatenate([left[:half], left[half:] + second], axis=0).astype(BF16)
    from_left = lax.ppermute(right, "x", RIGHT).astype(F32)
    from_right = lax.ppermute(left, "x", LEFT).astype(F32)
    return own + from_left + from_right


def ring_scatter_direct(own, left, right, far):
    from_left = lax.ppermute(right, "x", RIGHT).astype(F32)
    from_right = lax.ppermute(left, "x", LEFT).astype(F32)
    from_far = lax.ppermute(far, "x", ACROSS).astype(F32)
    return own + from_left + from_right + from_far


def tie(value, *others):
    return lax.optimization_barrier((value, *others))[0]


def rms_norm(values, gain):
    return values * lax.rsqrt(jnp.mean(values * values, axis=-1, keepdims=True) + EPSILON) * gain


def add_low(mine, came):
    return (mine.astype(F32) + came.astype(F32)).astype(BF16)


def yhi_sum(rows, core, yhi):
    mine = lax.dynamic_slice_in_dim(rows, 96 * core, 96, axis=0)
    theirs = lax.dynamic_slice_in_dim(rows, 96 * (1 - core), 96, axis=0)
    came = lax.ppermute(theirs, "core", SWAP)
    home = core == yhi
    kept = jnp.where(home, mine, came)
    away = jnp.where(home, came, mine)
    return add_low(kept, lax.ppermute(away, "yhi", SWAP))


def ylo_sum(piece):
    return add_low(piece, lax.ppermute(piece, "ylo", SWAP))


def cross(piece, start, *others):
    first, last = start + 768, start + 1152
    moved = lax.ppermute(piece[:, first:last], AXES, CROSS)
    if others:
        piece, moved = lax.optimization_barrier((piece, moved, *others))[:2]
    return jnp.concatenate([piece[:, :first], moved, piece[:, last:]], axis=1)


def butterfly(values):
    for axis, size in (("core", 2), ("x", 4), ("z", 4), ("yhi", 2), ("ylo", 2)):
        step = 1
        while step < size:
            pairs = [(i, i ^ step) for i in range(size)]
            values = values + lax.ppermute(values, axis, pairs)
            step *= 2
    return values


def norm_back(grad, own_normed, state, gain):
    grad_state, grad_gain = jax.vjp(rms_norm, state, gain)[1](own_normed)
    return grad + grad_state, grad_gain


def body(tokens, lengths, grad_output, *weights):
    stretch, width = tokens.shape[1:]
    x = lax.axis_index("x")
    core = lax.axis_index("core")
    z = lax.axis_index("z")
    yhi = lax.axis_index("yhi")
    member = x.astype(jnp.int32).reshape(1)
    home = core == yhi

    gains = jnp.stack([weights[0], weights[5], weights[9], weights[14]]).T
    gains = jnp.pad(gains, ((0, 0), (0, 124)))

    def shared(block, *joined):
        return jnp.where(home, block, tie(lax.ppermute(block, AXES, SHARE), *joined))

    def attention_part(base, extra, after):
        block = lax.dynamic_slice(tie(weights[base + 4], *after), (0, 384 * x), (192, 384))
        block = lax.ppermute(block, AXES, TURN)
        parts = [
            lax.dynamic_slice(w, (0, x * (w.shape[1] // 4)), (192, w.shape[1] // 4))
            for w in weights[base + 1 : base + 4]
        ]
        parts = shared(jnp.concatenate(parts + extra, axis=1))
        return jnp.concatenate([parts[:, :768], block, parts[:, 768:]], axis=1)

    def feed_part(base, after, joined):
        part = pack_feed_call(member, *weights[base + 6 : base + 9], after=after)
        return shared(part, *joined)

    def line_weights(piece, *after):
        return lax.all_gather(tie(piece, *after), SPREAD, axis=0, tiled=False)

    here = (2 * z + yhi) * stretch + jnp.arange(stretch, dtype=jnp.int32)
    valid = (here < lengths[0])[:, None]
    grad_start = jnp.where(valid, grad_output[0], 0).astype(BF16)
    length = lax.ppermute(lengths, AXES, TURN)
    moved = to_lines(interleave(tokens[0], grad_start), z)
    rows, grad_rows = separate(jnp.concatenate(moved, axis=0))

    attn_one = line_weights(attention_part(0, [gains], ()))
    feed_one = feed_part(0, (), moved)
    gains = attn_one[:, :, 1152:1156].transpose(2, 0, 1).reshape(4, width).astype(F32)
    pieces = ring_gather(rows)
    state = rows.astype(F32)
    feed_one = line_weights(feed_one, *pieces[3:])
    grad_pieces = ring_gather(grad_rows)
    grad = grad_rows.astype(F32)

    part = stretch // 4

    def member_places(member, side_index):
        block = jnp.arange(4, dtype=jnp.int32)
        inner = jnp.arange(part, dtype=jnp.int32)
        home = (member - block + 4) % 4
        return (
            home[:, None] * (2 * stretch) + side_index * stretch + member * part + inner[None, :]
        ).reshape(-1)

    def line_places(side_index):
        return jnp.concatenate([member_places((x + step) % 4, side_index) for step in (0, 3, 1, 2)])

    places = line_places(core)
    key_places = jnp.concatenate([places, line_places(1 - core)]).reshape(1024, 1)
    half = HEAD_DIM // 2
    freq = ROPE_BASE ** (-jnp.arange(half, dtype=F32) * (2.0 / HEAD_DIM))
    angle = places.astype(F32)[:, None] * freq[None, :]
    cosine, sine = jnp.cos(angle), jnp.sin(angle)
    cosine_t, sine_t = cosine.T, sine.T
    places = places.reshape(1, 512)

    records = []
    for index, window in enumerate((WINDOW, 8 * stretch)):
        if index == 0:
            attn, feed = attn_one, feed_one
        else:
            attn, feed = attn_two, feed_two
        gain_attn, gain_feed = gains[2 * index], gains[2 * index + 1]
        if index == 0:
            queries, own, flat = project_call(True, pieces, gain_attn, attn, cosine, sine)
            flats = (flat,)
        else:
            flats = ring_gather(rms_norm(state, gain_attn).astype(BF16))
            feed_two = feed = line_weights(feed_two, *flats[1:3])
            queries, own = project_call(False, flats, gain_attn, attn, cosine, sine)
        other = lax.ppermute(own, "core", SWAP)
        line = (queries, own, other, places, key_places)
        after = grad_pieces[3:] if index else ()
        *partial, mixed, log_total = attend_call(window, length, *line, attn, after=after)
        saved_attn = (state, flats, line, mixed, log_total)
        state = state + ring_scatter(*partial)
        if index == 0:
            attn_two = attention_part(9, [], (mixed,))
            feed_two = feed_part(9, (mixed,), ())
        flats = ring_gather(rms_norm(state, gain_feed).astype(BF16))
        if index == 0:
            attn_two = line_weights(attn_two, *flats[1:3])
        *partial, gate, up, hidden = feed_forward_call(flats, feed)
        saved_feed = (state, flats, gate, up, hidden)
        state = state + ring_scatter(*partial)
        records.append((saved_attn, saved_feed, window))
    last_rows = state.astype(BF16)
    packed = ((attn_one, feed_one), (attn_two, feed_two))

    results = [None] * 18
    gain_grads = [None] * 4

    def feed_back(index, grad, pieces, after):
        state, flats, gate, up, hidden = records[index][1]
        *partial, low_gate, low_up = feed_backward_call(
            pieces, packed[index][1], gate, up, after=after
        )
        own_normed = ring_scatter_direct(*partial)
        grad, gain_grads[2 * index + 1] = norm_back(
            grad, own_normed, state, gains[2 * index + 1]
        )
        return grad, feed_weights_call(flats, pieces, low_gate, low_up, hidden)

    def attention_back(index, grad, pieces, after, late):
        state, flats, line, mixed, log_total = records[index][0]
        window = records[index][2]
        attn = packed[index][0]
        low_queries, pair_own, pair_other = attend_backward_call(
            window, length, pieces, *line, attn, log_total, cosine_t, sine_t, after=after
        )
        came = lax.ppermute(pair_other, "core", SWAP)
        *partial, low = unproject_call(
            low_queries, pair_own, came, cosine, sine, attn, after=late
        )
        own_normed = ring_scatter_direct(*partial)
        grad, gain_grads[2 * index] = norm_back(grad, own_normed, state, gains[2 * index])
        return grad, attend_weights_call(flats, pieces, low, mixed)

    def scatter(block):
        return lax.psum_scatter(block, SPREAD, scatter_dimension=0, tiled=True)

    grad, feed_grad = feed_back(1, grad, grad_pieces, ())
    low = tie(grad.astype(BF16), feed_grad)
    second_feed = scatter(tie(feed_grad, low))
    grad, attn_grad = attention_back(1, grad, ring_gather(low), (last_rows,), ())
    low = tie(grad.astype(BF16), attn_grad)
    second_attn = scatter(tie(attn_grad, low, second_feed))

    grad, feed_grad = feed_back(0, grad, ring_gather(low), (second_feed,))
    low = tie(grad.astype(BF16), feed_grad)
    first_feed = scatter(tie(feed_grad, low, second_attn))
    second = yhi_sum(jnp.concatenate([second_feed, second_attn], axis=2)[0], core, yhi)
    grad, attn_grad = attention_back(0, grad, ring_gather(low), (), (second,))
    low = grad.astype(BF16)
    first_attn = scatter(tie(attn_grad, first_feed))
    second_piece = cross(ylo_sum(second), 3072, first_attn, low)
    feed_piece = ylo_sum(yhi_sum(tie(first_feed, low)[0], core, yhi))
    gain_sums = butterfly(jnp.stack(gain_grads))
    back = from_lines(interleave(last_rows, low), z)
    output, input_grad = separate(back)
    output, input_grad = output[None], input_grad.astype(F32)[None]

    every = lax.all_gather(second_piece, ("x", "core"), axis=0, tiled=False)
    results[10:14], results[15:18] = unpack_call(every.reshape(4, 2, 96, -1))
    attn_piece = ylo_sum(yhi_sum(tie(first_attn, feed_piece, gain_sums)[0], core, yhi))
    first_piece = jnp.concatenate([feed_piece, cross(attn_piece, 0)], axis=1)
    every = lax.all_gather(first_piece, ("x", "core"), axis=0, tiled=False)
    every = every.reshape(4, 2, 96, -1)
    results[1:5], results[6:9] = unpack_call(every)
    gain_sums = lax.dynamic_slice_in_dim(gain_sums, (2 * z + yhi) * 192, 192, axis=1)
    for index, slot in enumerate((0, 5, 9, 14)):
        results[slot] = gain_sums[index]
    return (output, input_grad, *results)


def solution(mesh):
    fine = Mesh(mesh.devices.reshape(SIZES), AXES)
    token = P(REP, SHARD, None)
    vector = P(SHARD)
    matrix = P(SHARD, None)
    layer = (vector, matrix, matrix, matrix, matrix, vector, matrix, matrix, matrix)
    return jax.shard_map(
        body,
        mesh=fine,
        in_specs=(token, P(REP), token) + layer + layer,
        out_specs=(token, token) + layer + layer,
        check_vma=False,
    )
```

```python
import functools
import jax
import jax.numpy as jnp
from jax import lax
from jax.experimental import pallas as pl
from jax.experimental.pallas import tpu as pltpu
from jax.sharding import Mesh
from jax.sharding import PartitionSpec as P

F32 = jnp.float32
BF16 = jnp.bfloat16
HEAD_DIM = 96
NEGATIVE = -1e30
MIB = 1 << 20

OFFSETS = (0, 128, 256, 384, 448)
SIZES_OF = (128, 128, 128, 64, 64)


def params(mib, semantics=None):
    return pltpu.CompilerParams(vmem_limit_bytes=mib * MIB, dimension_semantics=semantics)


def cost(flops, nbytes, transcendentals=0):
    return pl.CostEstimate(
        flops=int(flops), bytes_accessed=int(nbytes), transcendentals=int(transcendentals)
    )


def fill(target, refs):
    start = 0
    for ref in refs:
        rows = ref.shape[0]
        target[start : start + rows, :] = ref[...]
        start += rows


def nn(a, b):
    return lax.dot_general(a, b, (((1,), (0,)), ((), ())), preferred_element_type=F32)


def nt(a, b):
    return lax.dot_general(a, b, (((1,), (1,)), ((), ())), preferred_element_type=F32)


def tn(a, b):
    return lax.dot_general(a, b, (((0,), (0,)), ((), ())), preferred_element_type=F32)


def later(kernel, count, lead=0):
    if not count:
        return kernel

    def wrapped(*refs):
        return kernel(*refs[:lead], *refs[lead + count :])

    return wrapped


def anywhere(after):
    return [pl.BlockSpec(memory_space=pl.ANY)] * len(after)


def whole(shape):
    return pl.BlockSpec(shape, lambda *_: (0,) * len(shape))


PIECES = [whole((rows, 1536)) for rows in SIZES_OF]
PARTIAL_SHAPES = [
    jax.ShapeDtypeStruct((128, 1536), F32),
    jax.ShapeDtypeStruct((128, 1536), F32),
    jax.ShapeDtypeStruct((128, 1536), F32),
    jax.ShapeDtypeStruct((128, 1536), BF16),
]
LOW_PARTIAL_SHAPES = PARTIAL_SHAPES[:1] + [jax.ShapeDtypeStruct((128, 1536), BF16)] * 3
PARTIALS = [whole((128, 1536))] * 4


def emit(total, outs):
    for place, out in enumerate(outs):
        out[...] = total[128 * place : 128 * (place + 1), :].astype(out.dtype)


def down_parts(block):
    left = block[:, 0:128, :].reshape(256, 1024)
    right = jnp.concatenate([block[:, 128:192, 0:512], block[:, 128:192, 512:1024]], axis=1)
    return left, right.reshape(256, 512)


def feed_forward_kernel(*refs):
    pieces, (wg, wu, wd), outs = refs[:5], refs[5:8], refs[8:12]
    gate, up, hidden, flat, total = refs[12:]
    step = pl.program_id(0)

    @pl.when(step == 0)
    def _():
        fill(flat, pieces)

    rows = flat[...]
    g = nn(rows, wg[...])
    u = nn(rows, wu[...])
    gate[...] = g
    up[...] = u
    h = (g * jax.nn.sigmoid(g) * u).astype(BF16)
    hidden[...] = h
    left, right = down_parts(wd[...])
    left, right = nn(h, left), nn(h, right)

    @pl.when(step == 0)
    def _():
        total[:, :1024] = left
        total[:, 1024:] = right

    @pl.when(step > 0)
    def _():
        total[:, :1024] += left
        total[:, 1024:] += right

    @pl.when(step == 3)
    def _():
        emit(total, outs)


def feed_specs():
    return [
        pl.BlockSpec((1536, 256), lambda b: (0, b)),
        pl.BlockSpec((1536, 256), lambda b: (0, 4 + b)),
        pl.BlockSpec((2, 192, 1024), lambda b: (b, 0, 2)),
    ]


def column_block(rows):
    return pl.BlockSpec((rows, 256), lambda b: (0, b))


def feed_forward_call(pieces, packed, after=()):
    flat_packed = packed.reshape(1536, -1)
    return pl.pallas_call(
        later(feed_forward_kernel, len(after)),
        grid=(4,),
        in_specs=anywhere(after) + PIECES + feed_specs(),
        out_specs=PARTIALS + [column_block(512)] * 3,
        out_shape=PARTIAL_SHAPES
        + [
            jax.ShapeDtypeStruct((512, 1024), F32),
            jax.ShapeDtypeStruct((512, 1024), F32),
            jax.ShapeDtypeStruct((512, 1024), BF16),
        ],
        scratch_shapes=[pltpu.VMEM((512, 1536), BF16), pltpu.VMEM((512, 1536), F32)],
        compiler_params=params(40),
        cost_estimate=cost(4.9e9, 18e6),
        name="feed_forward",
    )(*after, *pieces, flat_packed, flat_packed, packed)


def feed_backward_kernel(*refs):
    pieces, (wg, wu, wd, gate, up), outs = refs[:5], refs[5:10], refs[10:14]
    low_gate, low_up, flat, total = refs[14:]
    step = pl.program_id(0)

    @pl.when(step == 0)
    def _():
        fill(flat, pieces)

    rows = flat[...]
    left, right = down_parts(wd[...])
    grad = nt(rows[:, :1024], left) + nt(rows[:, 1024:], right)
    g = gate[...]
    s = jax.nn.sigmoid(g)
    a = (grad * up[...] * s * (1.0 + g * (1.0 - s))).astype(BF16)
    b = (grad * (g * s)).astype(BF16)
    low_gate[...] = a
    low_up[...] = b
    part = nt(a, wg[...]) + nt(b, wu[...])

    @pl.when(step == 0)
    def _():
        total[...] = part

    @pl.when(step > 0)
    def _():
        total[...] += part

    @pl.when(step == 3)
    def _():
        emit(total, outs)


def feed_backward_call(pieces, packed, gate, up, after=()):
    flat_packed = packed.reshape(1536, -1)
    return pl.pallas_call(
        later(feed_backward_kernel, len(after)),
        grid=(4,),
        in_specs=anywhere(after) + PIECES + feed_specs() + [column_block(512)] * 2,
        out_specs=PARTIALS + [column_block(512)] * 2,
        out_shape=LOW_PARTIAL_SHAPES + [jax.ShapeDtypeStruct((512, 1024), BF16)] * 2,
        scratch_shapes=[pltpu.VMEM((512, 1536), BF16), pltpu.VMEM((512, 1536), F32)],
        compiler_params=params(40),
        cost_estimate=cost(4.9e9, 20e6),
        name="feed_backward",
    )(*after, *pieces, flat_packed, flat_packed, packed, gate, up)


def feed_weights_kernel(*refs):
    flats, grads = refs[:5], refs[5:10]
    low_gate, low_up, hidden, out, flat_t, hidden_t, grad = refs[10:]
    step = pl.program_id(0)

    @pl.when(step == 0)
    def _():
        start = 0
        for ref in flats:
            n = ref.shape[0]
            flat_t[:, start : start + n] = ref[...].T
            start += n

    @pl.when(step == 4)
    def _():
        hidden_t[...] = hidden[...].T
        fill(grad, grads)

    @pl.when(step < 4)
    def _():
        out[...] = nn(flat_t[...], low_gate[...]).astype(BF16).reshape(8, 192, 256)

    @pl.when((step >= 4) & (step < 8))
    def _():
        out[...] = nn(flat_t[...], low_up[...]).astype(BF16).reshape(8, 192, 256)

    for q in range(4):

        @pl.when(step == 8 + q)
        def _():
            top = nn(hidden_t[...], grad[:, 256 * q : 256 * (q + 1)]).astype(BF16)
            out[:, 0:128, :] = top.reshape(8, 128, 256)
            half = 64 * (q // 2)
            some = hidden_t[...].reshape(8, 128, 512)[:, half : half + 64].reshape(512, 512)
            start = 1024 + 256 * (q % 2)
            low = nn(some, grad[:, start : start + 256]).astype(BF16)
            out[:, 128:192, :] = low.reshape(8, 64, 256)


def feed_weights_call(flats, grads, low_gate, low_up, hidden):
    return pl.pallas_call(
        feed_weights_kernel,
        grid=(12,),
        in_specs=PIECES
        + PIECES
        + [
            pl.BlockSpec((512, 256), lambda b: (0, jnp.minimum(b, 3))),
            pl.BlockSpec((512, 256), lambda b: (0, jnp.clip(b - 4, 0, 3))),
            whole((512, 1024)),
        ],
        out_specs=pl.BlockSpec((8, 192, 256), lambda b: (0, 0, b)),
        out_shape=jax.ShapeDtypeStruct((8, 192, 3072), BF16),
        scratch_shapes=[
            pltpu.VMEM((1536, 512), BF16),
            pltpu.VMEM((1024, 512), BF16),
            pltpu.VMEM((512, 1536), BF16),
        ],
        compiler_params=params(40),
        cost_estimate=cost(4.9e9, 18e6),
        name="feed_weights",
    )(*flats, *grads, low_gate, low_up, hidden)


def piece_specs(pieces):
    return [whole(item.shape) for item in pieces]


def turn_columns(block, cosine, sine):
    out = []
    for start in range(0, block.shape[1], HEAD_DIM):
        a = block[:, start : start + 48]
        b = block[:, start + 48 : start + HEAD_DIM]
        out.append(a * cosine - b * sine)
        out.append(b * cosine + a * sine)
    return jnp.concatenate(out, axis=1)


def project_kernel(raw, count, *refs):
    pieces, (gain, weight, cosine, sine, queries, pair) = refs[:count], refs[count : count + 6]
    if raw:
        flat = refs[-1]
        start = 0
        for ref in pieces:
            n = ref.shape[0]
            rows = ref[...].astype(F32)
            scale = lax.rsqrt(jnp.mean(rows * rows, axis=-1, keepdims=True) + 1e-05)
            flat[start : start + n, :] = (rows * scale * gain[...]).astype(BF16)
            start += n
    else:
        flat = refs[-1]
        fill(flat, pieces)
    both = nn(flat[...], weight[...])
    cos, sin = cosine[...], sine[...]
    queries[...] = turn_columns(both[:, :384], cos, sin).astype(BF16)
    keys = turn_columns(both[:, 384:576], cos, sin)
    pair[...] = jnp.concatenate([keys, both[:, 576:768]], axis=1).astype(BF16)


def project_call(raw, pieces, gain, packed, cosine, sine, after=()):
    wide = packed.shape[-1]
    shape = jax.ShapeDtypeStruct((512, 384), BF16)
    flat_shape = jax.ShapeDtypeStruct((512, 1536), BF16)
    return pl.pallas_call(
        later(functools.partial(project_kernel, raw, len(pieces)), len(after)),
        grid=(1,),
        in_specs=anywhere(after)
        + piece_specs(pieces)
        + [whole((1, 1536)), projection_spec(), whole((512, 48)), whole((512, 48))],
        out_specs=[whole((512, 384))] * 2 + ([whole((512, 1536))] if raw else []),
        out_shape=[shape, shape] + ([flat_shape] if raw else []),
        scratch_shapes=[] if raw else [pltpu.VMEM((512, 1536), BF16)],
        compiler_params=params(40),
        cost_estimate=cost(1.3e9, 6e6),
        name="project",
    )(*after, *pieces, gain.reshape(1, 1536), packed.reshape(1536, wide), cosine, sine)


def fill_bias(bias, length, places, key_places, window):
    gap = places[...] - key_places[...]
    inside = (key_places[...] < length) & (gap >= 0) & (gap < window)
    bias[...] = jnp.where(inside | (gap == 0), 0.0, NEGATIVE)


def both_rows(own, other, start):
    return jnp.concatenate(
        [own[:, start : start + HEAD_DIM], other[:, start : start + HEAD_DIM]], axis=0
    )


def attend_kernel(window, length, queries, own, other, places, key_places, w_out, *refs):
    outs, (mixed, log_total, total, bias) = refs[:4], refs[4:]
    fill_bias(bias, length[0], places, key_places, window)
    sums = []
    stats = []
    for head in range(4):
        if head % 2 == 0:
            keys = both_rows(own[...], other[...], HEAD_DIM * (head // 2))
            values = both_rows(own[...], other[...], 192 + HEAD_DIM * (head // 2)).T
        query = queries[:, HEAD_DIM * head : HEAD_DIM * (head + 1)]
        scores = nt(keys, query) * HEAD_DIM ** (-0.5) + bias[...]
        peak = jnp.max(scores, axis=0, keepdims=True)
        probs = jnp.exp(scores - peak)
        totals = jnp.sum(probs, axis=0, keepdims=True)
        part = nn(values, probs.astype(BF16)) / totals
        sums.append(part.astype(BF16).astype(F32).T.astype(BF16))
        stats.append(peak + jnp.log(totals))
        for block in range(4):
            cols = slice(384 * block, 384 * (block + 1))
            value = nn(sums[-1], out_block(w_out, head, block))
            if head == 0:
                total[:, cols] = value
            else:
                total[:, cols] += value
    mixed[...] = jnp.concatenate(sums, axis=1)
    log_total[...] = jnp.concatenate(stats + stats, axis=0)
    emit(total, outs)


def line_specs():
    return [whole((512, 384))] * 3 + [whole((1, 512)), whole((1024, 1))]


def out_spec():
    return pl.BlockSpec((8, 192, 384), lambda *_: (0, 0, 2))


def out_block(w_out, head, block):
    start = 96 * (head % 2)
    return w_out[2 * block + head // 2, start : start + 96, :]


def projection_spec():
    return pl.BlockSpec((1536, 768), lambda *_: (0, 0))


def attend_call(window, length, queries, own, other, places, key_places, packed, after=()):
    return pl.pallas_call(
        later(functools.partial(attend_kernel, window), len(after)),
        grid=(1,),
        in_specs=anywhere(after)
        + [pl.BlockSpec(memory_space=pltpu.SMEM)] + line_specs() + [out_spec()],
        out_specs=PARTIALS + [whole((512, 384)), whole((8, 512))],
        out_shape=PARTIAL_SHAPES
        + [jax.ShapeDtypeStruct((512, 384), BF16), jax.ShapeDtypeStruct((8, 512), F32)],
        scratch_shapes=[pltpu.VMEM((512, 1536), F32), pltpu.VMEM((1024, 512), F32)],
        compiler_params=params(48),
        cost_estimate=cost(3e9, 6e6, 2e6),
        name="attend",
    )(*after, length, queries, own, other, places, key_places, packed)


def attend_backward_kernel(window, length, *refs):
    pieces, refs = refs[:5], refs[5:]
    queries, own, other, places, key_places, w_out, log_total, cosine, sine = refs[:9]
    low_queries, pair_own, pair_other, grad, bias = refs[9:]
    fill(grad, pieces)
    fill_bias(bias, length[0], places, key_places, window)
    cos, sin = cosine[...], sine[...]
    lows = []
    key_sums = []
    value_sums = []
    for head in range(4):
        if head % 2 == 0:
            keys = both_rows(own[...], other[...], HEAD_DIM * (head // 2))
            values = both_rows(own[...], other[...], 192 + HEAD_DIM * (head // 2))
            keys_t = keys.T
        query = queries[:, HEAD_DIM * head : HEAD_DIM * (head + 1)]
        mixed = nt(grad[:, :384], out_block(w_out, head, 0))
        for block in range(1, 4):
            mixed += nt(
                grad[:, 384 * block : 384 * (block + 1)], out_block(w_out, head, block)
            )
        mixed = mixed.astype(BF16)
        scores = nt(keys, query) * HEAD_DIM ** (-0.5) + bias[...]
        probs = jnp.exp(scores - log_total[head : head + 1, :])
        slopes = nt(values, mixed)
        inner = jnp.sum(probs * slopes, axis=0, keepdims=True)
        raw = (probs * (slopes - inner) * HEAD_DIM ** (-0.5)).astype(BF16)
        key_part = nn(raw, query)
        value_part = nn(probs.astype(BF16), mixed)
        if head % 2 == 0:
            key_sums.append(key_part)
            value_sums.append(value_part)
        else:
            key_sums[-1] += key_part
            value_sums[-1] += value_part
        turned = nn(keys_t, raw)
        a, b = turned[:48], turned[48:]
        turned = jnp.concatenate([a * cos + b * sin, b * cos - a * sin], axis=0)
        lows.append(turned.T.astype(BF16))
    low_queries[...] = jnp.concatenate(lows, axis=1)
    both = jnp.concatenate(key_sums + value_sums, axis=1)
    pair_own[...] = both[:512]
    pair_other[...] = both[512:].astype(BF16)


def attend_backward_call(
    window,
    length,
    pieces,
    queries,
    own,
    other,
    places,
    key_places,
    packed,
    log_total,
    cosine,
    sine,
    after=(),
):
    return pl.pallas_call(
        later(functools.partial(attend_backward_kernel, window), len(after)),
        grid=(1,),
        in_specs=anywhere(after)
        + [pl.BlockSpec(memory_space=pltpu.SMEM)]
        + PIECES
        + line_specs()
        + [out_spec(), whole((8, 512)), whole((48, 512)), whole((48, 512))],
        out_specs=[whole((512, 384))] * 3,
        out_shape=[
            jax.ShapeDtypeStruct((512, 384), BF16),
            jax.ShapeDtypeStruct((512, 384), F32),
            jax.ShapeDtypeStruct((512, 384), BF16),
        ],
        scratch_shapes=[pltpu.VMEM((512, 1536), BF16), pltpu.VMEM((1024, 512), F32)],
        compiler_params=params(52),
        cost_estimate=cost(6e9, 6e6, 2e6),
        name="attend_backward",
    )(
        *after,
        length,
        *pieces,
        queries,
        own,
        other,
        places,
        key_places,
        packed,
        log_total,
        cosine,
        sine,
    )


def unproject_kernel(low_queries, pair_own, pair_came, cosine, sine, weight, *refs):
    outs, low = refs[:4], refs[4]
    both = pair_own[...] + pair_came[...].astype(F32)
    keys = turn_columns(both[:, :192], cosine[...], -sine[...])
    rows = jnp.concatenate(
        [low_queries[...], keys.astype(BF16), both[:, 192:].astype(BF16)], axis=1
    )
    low[...] = rows
    emit(nt(rows, weight[...]), outs)


def unproject_call(low_queries, pair_own, pair_came, cosine, sine, packed, after=()):
    wide = packed.shape[-1]
    return pl.pallas_call(
        later(unproject_kernel, len(after)),
        grid=(1,),
        in_specs=anywhere(after)
        + [whole((512, 384))] * 3
        + [whole((512, 48))] * 2
        + [projection_spec()],
        out_specs=PARTIALS + [whole((512, 768))],
        out_shape=LOW_PARTIAL_SHAPES + [jax.ShapeDtypeStruct((512, 768), BF16)],
        compiler_params=params(40),
        cost_estimate=cost(1.3e9, 7e6),
        name="unproject",
    )(*after, low_queries, pair_own, pair_came, cosine, sine, packed.reshape(1536, wide))


def attend_weights_kernel(count, *refs):
    flats, grads, (low, mixed) = refs[:count], refs[count : count + 5], refs[count + 5 : count + 7]
    out, flat_t, grad = refs[count + 7 :]
    start = 0
    for ref in flats:
        n = ref.shape[0]
        flat_t[:, start : start + n] = ref[...].T
        start += n
    fill(grad, grads)
    for block in range(3):
        cols = slice(256 * block, 256 * (block + 1))
        out[:, :, cols] = nn(flat_t[...], low[:, cols]).astype(BF16).reshape(8, 192, 256)
    mixed_t = mixed[...].T
    for block in range(4):
        part = nn(mixed_t, grad[:, 384 * block : 384 * (block + 1)]).astype(BF16)
        out[2 * block : 2 * block + 2, :, 768:1152] = part.reshape(2, 192, 384)


def attend_weights_call(flats, grads, low, mixed):
    return pl.pallas_call(
        functools.partial(attend_weights_kernel, len(flats)),
        grid=(1,),
        in_specs=piece_specs(flats) + PIECES + [whole((512, 768)), whole((512, 384))],
        out_specs=whole((8, 192, 1152)),
        out_shape=jax.ShapeDtypeStruct((8, 192, 1152), BF16),
        scratch_shapes=[pltpu.VMEM((1536, 512), BF16), pltpu.VMEM((512, 1536), BF16)],
        compiler_params=params(40),
        cost_estimate=cost(1.9e9, 10e6),
        name="attend_weights",
    )(*flats, *grads, low, mixed)


def unpack_kernel(*refs):
    every, wq, wk, wv, wo, gate, up, down = refs
    side = pl.program_id(0)
    blocks = [every[x, 0] for x in range(4)]
    for x, block in enumerate(blocks):
        wq[:, 384 * x : 384 * (x + 1)] = block[:, 3072:3456].astype(F32)
        wo[:, 384 * x : 384 * (x + 1)] = block[:, 3840:4224].astype(F32)
        for s in range(8):
            cols = slice(512 * s + 128 * x, 512 * s + 128 * (x + 1))
            gate[:, cols] = block[:, 128 * s : 128 * (s + 1)].astype(F32)
            up[:, cols] = block[:, 1024 + 128 * s : 1024 + 128 * (s + 1)].astype(F32)

        @pl.when(side == 0)
        def _(x=x, block=block):
            down[x, 0:96, :1024] = block[:, 2048:3072].astype(F32)

        @pl.when(side == 1)
        def _(x=x, block=block):
            down[x, 96:128, :1024] = block[0:32, 2048:3072].astype(F32)
            down[x, 0:64, 1024:] = block[32:96, 2048:2560].astype(F32)
            down[x, 64:128, 1024:] = block[32:96, 2560:3072].astype(F32)

    wk[...] = jnp.concatenate([block[:, 3456:3648].astype(F32) for block in blocks], axis=1)
    wv[...] = jnp.concatenate([block[:, 3648:3840].astype(F32) for block in blocks], axis=1)


def unpack_call(every):
    widths = (1536, 768, 768, 1536, 4096, 4096)
    out = pl.pallas_call(
        unpack_kernel,
        grid=(2,),
        in_specs=[pl.BlockSpec((4, 1, 96, every.shape[-1]), lambda b: (0, b, 0, 0))],
        out_specs=[pl.BlockSpec((96, width), lambda b: (b, 0)) for width in widths]
        + [whole((4, 128, 1536))],
        out_shape=[jax.ShapeDtypeStruct((192, width), F32) for width in widths]
        + [jax.ShapeDtypeStruct((4, 128, 1536), F32)],
        compiler_params=params(48),
        cost_estimate=cost(1e6, 30e6),
        name="unpack",
    )(every)
    return out[:4], (out[4], out[5], out[6].reshape(512, 1536))


def pack_feed_kernel(where, w_gate, w_up, w_down, out):
    x = where[0]
    for s in range(8):
        cols = pl.ds(pl.multiple_of(512 * s + 128 * x, 128), 128)
        out[:, 128 * s : 128 * (s + 1)] = w_gate[:, cols]
        out[:, 1024 + 128 * s : 1024 + 128 * (s + 1)] = w_up[:, cols]
    out[0:128, 2048:3072] = w_down[:, 0:1024]
    out[128:192, 2048:2560] = w_down[0:64, 1024:1536]
    out[128:192, 2560:3072] = w_down[64:128, 1024:1536]


def pack_feed_call(where, w_gate, w_up, w_down, after=()):
    return pl.pallas_call(
        later(pack_feed_kernel, len(after), 1),
        grid_spec=pltpu.PrefetchScalarGridSpec(
            num_scalar_prefetch=1,
            grid=(1,),
            in_specs=anywhere(after)
            + [
                pl.BlockSpec((192, 4096), lambda b, w: (0, 0)),
                pl.BlockSpec((192, 4096), lambda b, w: (0, 0)),
                pl.BlockSpec((128, 1536), lambda b, w: (w[0], 0)),
            ],
            out_specs=pl.BlockSpec((192, 3072), lambda b, w: (0, 0)),
        ),
        out_shape=jax.ShapeDtypeStruct((192, 3072), BF16),
        compiler_params=params(24),
        cost_estimate=cost(1e3, 5e6),
        name="pack_feed",
    )(where, *after, w_gate, w_up, w_down)


WINDOW = 512
EPSILON = 1e-05
ROPE_BASE = 100000.0

AXES = ("ylo", "x", "core", "z", "yhi")
SIZES = (2, 4, 2, 4, 2)
REP = ("ylo", "x", "core")
SHARD = ("z", "yhi")
SPREAD = ("z", "core")

RIGHT = [(i, (i + 1) % 4) for i in range(4)]
LEFT = [(i, (i - 1) % 4) for i in range(4)]
ACROSS = [(i, (i + 2) % 4) for i in range(4)]
SWAP = [(0, 1), (1, 0)]


def number(ylo, x, core, z, yhi):
    return (((ylo * 4 + x) * 2 + core) * 4 + z) * 2 + yhi


def permutation(place, taken=None):
    pairs = []
    for ylo in range(2):
        for x in range(4):
            for core in range(2):
                for z in range(4):
                    for yhi in range(2):
                        here = (ylo, x, core, z, yhi)
                        if taken is None or taken(*here):
                            pairs.append((number(*here), number(*place(*here))))
    return pairs


def inverse(pairs):
    return [(there, here) for here, there in pairs]


def at_home(ylo, x, core, z, yhi):
    return core == yhi


LINES = [
    permutation(lambda l, x, c, z, h, k=k: (l, (z + k) % 4, h, x, c)) for k in range(4)
]
TURN = permutation(lambda l, x, c, z, h: (l, z, h, x, c))
SHARE = permutation(lambda l, x, c, z, h: (l, x, c, z, 1 - h), at_home)
CROSS = permutation(lambda l, x, c, z, h: (l, z, c, x, h))


def to_lines(block, z):
    part = block.shape[0] // 4
    out = []
    for k in range(4):
        piece = lax.dynamic_slice_in_dim(block, ((z + k) % 4) * part, part, axis=0)
        out.append(lax.ppermute(piece, AXES, LINES[k]))
    return out


def send_home(block):
    part = block.shape[0] // 4
    return [
        lax.ppermute(block[part * k : part * (k + 1)], AXES, inverse(LINES[k])) for k in range(4)
    ]


def place_home(parts, z):
    rows = parts[0].shape[0]
    out = jnp.zeros((4 * rows,) + parts[0].shape[1:], parts[0].dtype)
    for k in range(4):
        out = lax.dynamic_update_slice_in_dim(out, parts[k], ((z + k) % 4) * rows, axis=0)
    return out


def interleave(first, second):
    parts = [item[32 * k : 32 * (k + 1)] for k in range(4) for item in (first, second)]
    return jnp.concatenate(parts, axis=0)


def separate(block):
    parts = [block[32 * k : 32 * (k + 1)] for k in range(8)]
    return jnp.concatenate(parts[::2], axis=0), jnp.concatenate(parts[1::2], axis=0)


def ring_gather(block):
    half = block.shape[0] // 2
    from_left = lax.ppermute(block, "x", RIGHT)
    from_right = lax.ppermute(block, "x", LEFT)
    far_first = lax.ppermute(from_left[:half], "x", RIGHT)
    far_second = lax.ppermute(from_right[half:], "x", LEFT)
    return block, from_left, from_right, far_first, far_second


def ring_scatter(own, left, right, far):
    half = far.shape[0] // 2
    first = lax.ppermute(far[:half], "x", RIGHT).astype(F32)
    second = lax.ppermute(far[half:], "x", LEFT).astype(F32)
    right = jnp.concatenate([right[:half] + first, right[half:]], axis=0).astype(BF16)
    left = jnp.concatenate([left[:half], left[half:] + second], axis=0).astype(BF16)
    from_left = lax.ppermute(right, "x", RIGHT).astype(F32)
    from_right = lax.ppermute(left, "x", LEFT).astype(F32)
    return own + from_left + from_right


def ring_scatter_direct(own, left, right, far):
    from_left = lax.ppermute(right, "x", RIGHT).astype(F32)
    from_right = lax.ppermute(left, "x", LEFT).astype(F32)
    from_far = lax.ppermute(far, "x", ACROSS).astype(F32)
    return own + from_left + from_right + from_far


def tie(value, *others):
    return lax.optimization_barrier((value, *others))[0]


def rms_norm(values, gain):
    return values * lax.rsqrt(jnp.mean(values * values, axis=-1, keepdims=True) + EPSILON) * gain


def add_low(mine, came):
    return (mine.astype(F32) + came.astype(F32)).astype(BF16)


def yhi_sum(rows, core, yhi):
    mine = lax.dynamic_slice_in_dim(rows, 96 * core, 96, axis=0)
    theirs = lax.dynamic_slice_in_dim(rows, 96 * (1 - core), 96, axis=0)
    came = lax.ppermute(theirs, "core", SWAP)
    home = core == yhi
    kept = jnp.where(home, mine, came)
    away = jnp.where(home, came, mine)
    return add_low(kept, lax.ppermute(away, "yhi", SWAP))


def ylo_sum(piece):
    return add_low(piece, lax.ppermute(piece, "ylo", SWAP))


def cross(piece, start, *others):
    first, last = start + 768, start + 1152
    moved = lax.ppermute(piece[:, first:last], AXES, CROSS)
    if others:
        piece, moved = lax.optimization_barrier((piece, moved, *others))[:2]
    return jnp.concatenate([piece[:, :first], moved, piece[:, last:]], axis=1)


def butterfly(values):
    for axis, size in (("core", 2), ("x", 4), ("z", 4), ("yhi", 2), ("ylo", 2)):
        step = 1
        while step < size:
            pairs = [(i, i ^ step) for i in range(size)]
            values = values + lax.ppermute(values, axis, pairs)
            step *= 2
    return values


def norm_back(grad, own_normed, state, gain):
    grad_state, grad_gain = jax.vjp(rms_norm, state, gain)[1](own_normed)
    return grad + grad_state, grad_gain


def body(tokens, lengths, grad_output, *weights):
    stretch, width = tokens.shape[1:]
    x = lax.axis_index("x")
    core = lax.axis_index("core")
    z = lax.axis_index("z")
    yhi = lax.axis_index("yhi")
    member = x.astype(jnp.int32).reshape(1)
    home = core == yhi

    gains = jnp.stack([weights[0], weights[5], weights[9], weights[14]]).T
    gains = jnp.pad(gains, ((0, 0), (0, 124)))

    def shared(block, *joined):
        return jnp.where(home, block, tie(lax.ppermute(block, AXES, SHARE), *joined))

    def attention_part(base, extra, after):
        block = lax.dynamic_slice(tie(weights[base + 4], *after), (0, 384 * x), (192, 384))
        block = lax.ppermute(block, AXES, TURN)
        parts = [
            lax.dynamic_slice(w, (0, x * (w.shape[1] // 4)), (192, w.shape[1] // 4))
            for w in weights[base + 1 : base + 4]
        ]
        parts = shared(jnp.concatenate(parts + extra, axis=1))
        return jnp.concatenate([parts[:, :768], block, parts[:, 768:]], axis=1)

    def feed_part(base, after, joined):
        part = pack_feed_call(member, *weights[base + 6 : base + 9], after=after)
        return shared(part, *joined)

    def line_weights(piece, *after):
        return lax.all_gather(tie(piece, *after), SPREAD, axis=0, tiled=False)

    here = (2 * z + yhi) * stretch + jnp.arange(stretch, dtype=jnp.int32)
    valid = (here < lengths[0])[:, None]
    grad_start = jnp.where(valid, grad_output[0], 0).astype(BF16)
    length = lax.ppermute(lengths, AXES, TURN)
    moved = to_lines(interleave(tokens[0], grad_start), z)
    rows, grad_rows = separate(jnp.concatenate(moved, axis=0))

    attn_one = line_weights(attention_part(0, [gains], ()))
    feed_one = feed_part(0, (), moved)
    gains = attn_one[:, :, 1152:1156].transpose(2, 0, 1).reshape(4, width).astype(F32)
    pieces = ring_gather(rows)
    state = rows.astype(F32)
    feed_one = line_weights(feed_one, *pieces[3:])
    grad_pieces = ring_gather(grad_rows)
    grad = grad_rows.astype(F32)

    part = stretch // 4

    def member_places(member, side_index):
        block = jnp.arange(4, dtype=jnp.int32)
        inner = jnp.arange(part, dtype=jnp.int32)
        home = (member - block + 4) % 4
        return (
            home[:, None] * (2 * stretch) + side_index * stretch + member * part + inner[None, :]
        ).reshape(-1)

    def line_places(side_index):
        return jnp.concatenate([member_places((x + step) % 4, side_index) for step in (0, 3, 1, 2)])

    places = line_places(core)
    key_places = jnp.concatenate([places, line_places(1 - core)]).reshape(1024, 1)
    half = HEAD_DIM // 2
    freq = ROPE_BASE ** (-jnp.arange(half, dtype=F32) * (2.0 / HEAD_DIM))
    angle = places.astype(F32)[:, None] * freq[None, :]
    cosine, sine = jnp.cos(angle), jnp.sin(angle)
    cosine_t, sine_t = cosine.T, sine.T
    places = places.reshape(1, 512)

    records = []
    for index, window in enumerate((WINDOW, 8 * stretch)):
        if index == 0:
            attn, feed = attn_one, feed_one
        else:
            attn, feed = attn_two, feed_two
        gain_attn, gain_feed = gains[2 * index], gains[2 * index + 1]
        if index == 0:
            queries, own, flat = project_call(True, pieces, gain_attn, attn, cosine, sine)
            flats = (flat,)
        else:
            flats = ring_gather(rms_norm(state, gain_attn).astype(BF16))
            feed_two = feed = line_weights(feed_two, *flats[1:3])
            queries, own = project_call(False, flats, gain_attn, attn, cosine, sine)
        other = lax.ppermute(own, "core", SWAP)
        line = (queries, own, other, places, key_places)
        after = grad_pieces[3:] if index else ()
        *partial, mixed, log_total = attend_call(window, length, *line, attn, after=after)
        saved_attn = (state, flats, line, mixed, log_total)
        state = state + ring_scatter(*partial)
        if index == 0:
            attn_two = attention_part(9, [], (mixed,))
            feed_two = feed_part(9, (mixed,), ())
        flats = ring_gather(rms_norm(state, gain_feed).astype(BF16))
        if index == 0:
            attn_two = line_weights(attn_two, *flats[1:3])
        *partial, gate, up, hidden = feed_forward_call(flats, feed)
        saved_feed = (state, flats, gate, up, hidden)
        state = state + ring_scatter(*partial)
        records.append((saved_attn, saved_feed, window))
    last_rows = state.astype(BF16)
    packed = ((attn_one, feed_one), (attn_two, feed_two))

    results = [None] * 18
    gain_grads = [None] * 4

    def feed_back(index, grad, pieces, after):
        state, flats, gate, up, hidden = records[index][1]
        *partial, low_gate, low_up = feed_backward_call(
            pieces, packed[index][1], gate, up, after=after
        )
        own_normed = ring_scatter_direct(*partial)
        grad, gain_grads[2 * index + 1] = norm_back(
            grad, own_normed, state, gains[2 * index + 1]
        )
        return grad, feed_weights_call(flats, pieces, low_gate, low_up, hidden)

    def attention_back(index, grad, pieces, after, late):
        state, flats, line, mixed, log_total = records[index][0]
        window = records[index][2]
        attn = packed[index][0]
        low_queries, pair_own, pair_other = attend_backward_call(
            window, length, pieces, *line, attn, log_total, cosine_t, sine_t, after=after
        )
        came = lax.ppermute(pair_other, "core", SWAP)
        *partial, low = unproject_call(
            low_queries, pair_own, came, cosine, sine, attn, after=late
        )
        own_normed = ring_scatter_direct(*partial)
        grad, gain_grads[2 * index] = norm_back(grad, own_normed, state, gains[2 * index])
        return grad, attend_weights_call(flats, pieces, low, mixed)

    def scatter(block):
        return lax.psum_scatter(block, SPREAD, scatter_dimension=0, tiled=True)

    grad, feed_grad = feed_back(1, grad, grad_pieces, ())
    low = tie(grad.astype(BF16), feed_grad)
    second_feed = scatter(tie(feed_grad, low))
    grad, attn_grad = attention_back(1, grad, ring_gather(low), (last_rows,), ())
    low = tie(grad.astype(BF16), attn_grad)
    second_attn = scatter(tie(attn_grad, low, second_feed))

    grad, feed_grad = feed_back(0, grad, ring_gather(low), (second_feed,))
    low = tie(grad.astype(BF16), feed_grad)
    first_feed = scatter(tie(feed_grad, low, second_attn))
    second = yhi_sum(jnp.concatenate([second_feed, second_attn], axis=2)[0], core, yhi)
    grad, attn_grad = attention_back(0, grad, ring_gather(low), (), (second,))
    low = grad.astype(BF16)
    first_attn = scatter(tie(attn_grad, first_feed))
    second_piece = cross(ylo_sum(second), 3072, first_attn, low)
    back = send_home(interleave(last_rows, low))
    feed_piece = tie(yhi_sum(tie(first_feed, low)[0], core, yhi), back[0])
    feed_piece = tie(ylo_sum(feed_piece), back[1])
    gain_sums = butterfly(jnp.stack(gain_grads))
    output, input_grad = separate(place_home(back, z))
    output, input_grad = output[None], input_grad.astype(F32)[None]

    every = lax.all_gather(second_piece, ("x", "core"), axis=0, tiled=False)
    results[10:14], results[15:18] = unpack_call(every.reshape(4, 2, 96, -1))
    attn_piece = yhi_sum(tie(first_attn, feed_piece, gain_sums)[0], core, yhi)
    attn_piece = tie(ylo_sum(tie(attn_piece, back[2])), back[3])
    first_piece = jnp.concatenate([feed_piece, cross(attn_piece, 0)], axis=1)
    every = lax.all_gather(first_piece, ("x", "core"), axis=0, tiled=False)
    every = every.reshape(4, 2, 96, -1)
    results[1:5], results[6:9] = unpack_call(every)
    gain_sums = lax.dynamic_slice_in_dim(gain_sums, (2 * z + yhi) * 192, 192, axis=1)
    for index, slot in enumerate((0, 5, 9, 14)):
        results[slot] = gain_sums[index]
    return (output, input_grad, *results)


def solution(mesh):
    fine = Mesh(mesh.devices.reshape(SIZES), AXES)
    token = P(REP, SHARD, None)
    vector = P(SHARD)
    matrix = P(SHARD, None)
    layer = (vector, matrix, matrix, matrix, matrix, vector, matrix, matrix, matrix)
    return jax.shard_map(
        body,
        mesh=fine,
        in_specs=(token, P(REP), token) + layer + layer,
        out_specs=(token, token) + layer + layer,
        check_vma=False,
    )
```
